32 devices in a mesh: ctx: 8 (over y, x, core), tp: 4 (over z).
Axes of the slice: x: 2, y: 2, z: 4, core: 2. Of those that a mesh axis runs over, the one named last changes fastest.
Arguments:
- tokens: bfloat16 [8192, 2048], P(('ctx', 'tp')), may hold values from -6 to 6
- cotangent: bfloat16 [8192, 2048], P(('ctx', 'tp')), may hold values from -6 to 6
- block_order: int32 [4, 16], replicated, may hold values from 0 to 15, each once within a row
- gain_one: float32 [2048], replicated, may hold values from 0.5 to 1.5
- shift_one: float32 [2048], replicated, may hold values from -1 to 1
- query_w: bfloat16 [2048, 2048], P(None, 'tp'), may hold values from -0.125 to 0.125
- key_w: bfloat16 [2048, 2048], P(None, 'tp'), may hold values from -0.125 to 0.125
- value_w: bfloat16 [2048, 2048], P(None, 'tp'), may hold values from -0.125 to 0.125
- query_b: float32 [2048], P('tp'), may hold values from -1.5 to 1.5
- key_b: float32 [32, 16], P('tp'), may hold values from -1.5 to 1.5
- value_b: float32 [2048], P('tp'), may hold values from -0.1 to 0.1
- output_w: bfloat16 [2048, 2048], P('tp'), may hold values from -3 to 3
- gain_two: float32 [2048], replicated, may hold values from 0.5 to 1.5
- shift_two: float32 [2048], replicated, may hold values from -1 to 1
- gate_w: bfloat16 [2048, 5632], P(None, 'tp'), may hold values from -0.125 to 0.125
- up_w: bfloat16 [2048, 5632], P(None, 'tp'), may hold values from -0.125 to 0.125
- down_w: bfloat16 [5632, 2048], P('tp'), may hold values from -0.078125 to 0.078125
Outputs:
- out_tokens: bfloat16 [8192, 2048], P(('ctx', 'tp'))
- grad_tokens: bfloat16 [8192, 2048], P(('ctx', 'tp'))
- grad_gain_one: float32 [2048], replicated
- grad_shift_one: float32 [2048], replicated
- grad_query_w: float32 [2048, 2048], P(None, 'tp')
- grad_key_w: float32 [2048, 2048], P(None, 'tp')
- grad_value_w: float32 [2048, 2048], P(None, 'tp')
- grad_query_b: float32 [2048], P('tp')
- grad_key_b: float32 [32, 16], P('tp')
- grad_value_b: float32 [2048], P('tp')
- grad_output_w: float32 [2048, 2048], P('tp')
- grad_gain_two: float32 [2048], replicated
- grad_shift_two: float32 [2048], replicated
- grad_gate_w: float32 [2048, 5632], P(None, 'tp')
- grad_up_w: float32 [2048, 5632], P(None, 'tp')
- grad_down_w: float32 [5632, 2048], P('tp')
The draws below stay inside these ranges and needn't reach their ends.
Inputs may be any that keep to these rules, and one draw needn't show every extreme that they name: `block_order`: each row is a permutation of the (16) block numbers of one sequence.
All inputs are finite; a program needn't handle non-finite values.
Results may differ from the reference program's by a relative error of at most 0.03.
Values may be sent and summed in bfloat16 or wider, within the bound.
No kernel may reach another device: no remote copies, remote signals or barrier semaphores. Data moves between devices by JAX's collectives and lax.ppermute only.
A program may use at most 256 MiB of HBM per device.

```python
import math
import jax
import jax.numpy as jnp
from jax import lax

D = 2048
HEADS = 32
HEAD_DIM = 64
ROT = 16
FF = 5632
SEQS = 4
HALF_BLOCK = 128
LENGTH = 2048
TOKENS = 8192
N_CTX = 8


def steps_of(own_key, dims, pieces, smallest, top_value):
    factor_of, own = 1.0, jax.random.fold_in(own_key, 6)
    for axis_at, blocks in pieces:
        draws = jnp.exp(jax.random.uniform(jax.random.fold_in(own, axis_at), (blocks,), jnp.float32, smallest / len(pieces), top_value / len(pieces)))
        factor_of = factor_of * jnp.repeat(draws, dims[axis_at] // blocks).reshape([-1 if axis == axis_at else 1 for axis in range(len(dims))])
    return factor_of


def gaussian(stream_key, extent, scale, most, pieces=(), kind=jnp.bfloat16):
    array = jax.random.normal(stream_key, extent, jnp.float32) * scale
    if len(pieces) > 0:
        array = steps_of(stream_key, extent, pieces, -0.22, 0.18) * array
    return jnp.clip(array, min=-most, max=most).astype(kind)


def setup_inputs(seed: int = 0) -> dict:
    seeds = jax.random.split(jax.random.key(seed), 18)
    tokens = gaussian(seeds[0], (TOKENS, D), 1.0, 6.0, ((0, 32),))
    cotangent = gaussian(seeds[1], (TOKENS, D), 1.0, 6.0, ((0, 32),))
    block_order = jax.vmap(lambda own: jax.random.permutation(own, 2 * N_CTX))(jax.random.split(seeds[2], SEQS)).reshape((SEQS, 2 * N_CTX)).astype(jnp.int32)
    gain_one = jnp.clip(1.0 + 0.1 * jax.random.normal(seeds[3], (D,), jnp.float32), 0.5, 1.5)
    shift_one = gaussian(seeds[4], (D,), 0.2, 1.0, (), jnp.float32)
    query_w = gaussian(seeds[5], (D, D), D ** -0.5, 0.125, ((1, 4),))
    key_w = gaussian(seeds[6], (D, D), D ** -0.5, 0.125, ((1, 4),))
    value_w = gaussian(seeds[7], (D, D), D ** -0.5, 0.125, ((1, 4),))
    query_b = gaussian(seeds[8], (D,), 0.3, 1.5, ((0, 4),), jnp.float32)
    key_b = gaussian(seeds[9], (HEADS, ROT), 0.3, 1.5, ((0, 4),), jnp.float32)
    value_b = gaussian(seeds[10], (D,), 0.02, 0.1, ((0, 4),), jnp.float32)
    output_w = gaussian(seeds[11], (D, D), (max(1, 4 * D // LENGTH)) ** -0.5, 3.0, ((0, 4),))
    gain_two = jnp.clip(1.0 + 0.1 * jax.random.normal(seeds[12], (D,), jnp.float32), 0.5, 1.5)
    shift_two = gaussian(seeds[13], (D,), 0.2, 1.0, (), jnp.float32)
    gate_w = gaussian(seeds[14], (D, FF), D ** -0.5, 0.125, ((1, 4),))
    up_w = gaussian(seeds[15], (D, FF), D ** -0.5, 0.125, ((1, 4),))
    down_w = gaussian(seeds[16], (FF, D), FF ** -0.5, 0.078125, ((0, 4),))
    return {"tokens": tokens, "cotangent": cotangent, "block_order": block_order, "gain_one": gain_one, "shift_one": shift_one, "query_w": query_w, "key_w": key_w, "value_w": value_w, "query_b": query_b, "key_b": key_b, "value_b": value_b, "output_w": output_w, "gain_two": gain_two, "shift_two": shift_two, "gate_w": gate_w, "up_w": up_w, "down_w": down_w}


@jax.custom_vjp
def low(v):
    return lax.optimization_barrier(v.astype(jnp.bfloat16)).astype(jnp.float32)

@jax.custom_vjp
def low_back(v):
    return v

def low_keep(v):
    return (low(v), None)

def low_pass(kept, grad):
    return (grad,)

def back_keep(v):
    return (v, None)

def back_low(kept, grad):
    return (low(grad),)
low.defvjp(low_keep, low_pass)
low_back.defvjp(back_keep, back_low)
norm_eps = 1e-05
masked_score = -1e+30
highest = lax.Precision.HIGHEST

def matmul(left, right):
    return jnp.dot(left, right, precision=highest, preferred_element_type=jnp.float32)

def layer_norm(values, gain_vec, shift_vec):
    row_mean = lax.optimization_barrier(jnp.mean(values, axis=-1, keepdims=True))
    centred = values - row_mean
    variance = lax.optimization_barrier(jnp.mean(centred * centred, axis=-1, keepdims=True))
    return centred * lax.rsqrt(variance + norm_eps) * gain_vec + shift_vec

def rotary(values, positions):
    half_rot = ROT // 2
    frequencies = 10000.0 ** (-2.0 * jnp.arange(half_rot, dtype=jnp.float32) / ROT)
    angles = positions.astype(jnp.float32)[:, None] * frequencies[None, :]
    cosine = jnp.cos(angles)[:, None, :]
    sine_vals = jnp.sin(angles)[:, None, :]
    first_part = values[..., :half_rot]
    second_part = values[..., half_rot:ROT]
    return jnp.concatenate([first_part * cosine - second_part * sine_vals, second_part * cosine + first_part * sine_vals, values[..., ROT:]], axis=-1)

def attend(queries, key_rows, value_rows, positions):
    length = queries.shape[0]
    block_size = math.gcd(512, length)
    query_blocks = queries.reshape(length // block_size, block_size, HEADS, HEAD_DIM)
    position_blocks = positions.reshape(length // block_size, block_size)
    score_scale = 1.0 / math.sqrt(HEAD_DIM)

    def one_block(parts):
        query_part, query_pos = parts
        scores = jnp.einsum('qhd,khd->hqk', query_part, key_rows, precision=highest) * score_scale
        scores = low_back(scores)
        allowed = positions[None, None, :] <= query_pos[None, :, None]
        probabilities = low(jax.nn.softmax(jnp.where(allowed, scores, masked_score), axis=-1))
        return jnp.einsum('hqk,khd->qhd', probabilities, value_rows, precision=highest)
    outputs = lax.map(jax.checkpoint(one_block), (query_blocks, position_blocks))
    return outputs.reshape(length, HEADS, HEAD_DIM)

def reference(tokens, cotangent, block_order, gain_one, shift_one, query_w, key_w, value_w, query_b, key_b, value_b, output_w, gain_two, shift_two, gate_w, up_w, down_w):
    slot_index = jnp.arange(LENGTH, dtype=jnp.int32)
    seq_positions = (block_order[:, slot_index // HALF_BLOCK] * HALF_BLOCK + slot_index % HALF_BLOCK).astype(jnp.int32)
    row_positions = jnp.transpose(seq_positions.reshape(SEQS, N_CTX, 2 * HALF_BLOCK), (1, 0, 2)).reshape(TOKENS)

    def to_sequences(rows):
        shaped = rows.reshape(N_CTX, SEQS, 2 * HALF_BLOCK, HEADS, HEAD_DIM)
        return jnp.transpose(shaped, (1, 0, 2, 3, 4)).reshape(SEQS, LENGTH, HEADS, HEAD_DIM)

    def from_sequences(seq_rows):
        shaped = seq_rows.reshape(SEQS, N_CTX, 2 * HALF_BLOCK, D)
        return jnp.transpose(shaped, (1, 0, 2, 3)).reshape(TOKENS, D)

    def forward(x_float, gain_one, shift_one, query_w, key_w, value_w, query_b, key_b, value_b, output_w, gain_two, shift_two, gate_w, up_w, down_w):
        normed_one = low(layer_norm(x_float, gain_one, shift_one))
        key_bias = jnp.concatenate([key_b, jnp.zeros((HEADS, HEAD_DIM - ROT), jnp.float32)], axis=1).reshape(D)
        query_lin = low_back(matmul(normed_one, query_w) + query_b)
        key_lin = low_back(matmul(normed_one, key_w) + key_bias)
        value_rows = low(low_back(matmul(normed_one, value_w) + value_b))
        queries = low(rotary(query_lin.reshape(TOKENS, HEADS, HEAD_DIM), row_positions))
        key_rows = low(rotary(key_lin.reshape(TOKENS, HEADS, HEAD_DIM), row_positions))
        value_heads = value_rows.reshape(TOKENS, HEADS, HEAD_DIM)
        attended = lax.map(lambda parts: attend(parts[0], parts[1], parts[2], parts[3]), (to_sequences(queries), to_sequences(key_rows), to_sequences(value_heads), seq_positions))
        attention = low(low_back(from_sequences(attended)))
        mixed = x_float + low_back(matmul(attention, output_w))
        normed_two = low(layer_norm(mixed, gain_two, shift_two))
        gate_lin = low_back(matmul(normed_two, gate_w))
        up_lin = low_back(matmul(normed_two, up_w))
        activation = low(jax.nn.silu(gate_lin) * up_lin)
        return mixed + low_back(matmul(activation, down_w))
    primals = tuple((arg.astype(jnp.float32) for arg in (tokens, gain_one, shift_one, query_w, key_w, value_w, query_b, key_b, value_b, output_w, gain_two, shift_two, gate_w, up_w, down_w)))
    out_float, pullback = jax.vjp(forward, *primals)
    grads = pullback(cotangent.astype(jnp.float32))
    return (out_float.astype(jnp.bfloat16), grads[0].astype(jnp.bfloat16), grads[1], grads[2], grads[3], grads[4], grads[5], grads[6], grads[7], grads[8], grads[9], grads[10], grads[11], grads[12], grads[13], grads[14])
```

```python
import functools
import jax, jax.numpy as jnp
from jax import lax
from jax.experimental import pallas as pl
from jax.experimental.pallas import tpu as pltpu

BLK = 128
CB = 4
CH = BLK * CB
NEG = -1e30
SCALE = 0.125

def nt(a, b):
    return lax.dot_general(a, b, (((1,), (1,)), ((), ())), preferred_element_type=jnp.float32)

def nn(a, b):
    return lax.dot_general(a, b, (((1,), (0,)), ((), ())), preferred_element_type=jnp.float32)

def lane_of(shape):
    return lax.broadcasted_iota(jnp.int32, shape, 1)

def row_of(shape):
    return lax.broadcasted_iota(jnp.int32, shape, 0)

def split_heads(x):
    low = lane_of(x.shape) < 64
    zero = jnp.zeros_like(x)
    return jnp.concatenate([jnp.where(low, x, zero), jnp.where(low, zero, x)], axis=0)

def join_heads(x):
    low = lane_of((BLK, 128)) < 64
    return jnp.where(low, x[:BLK], x[BLK:])

def sort_rows(order_ref, s, src_ref, dst_ref, count):
    for p in range(count):
        slot = order_ref[s, p]
        dst_ref[p * BLK:(p + 1) * BLK, 0:128] = src_ref[slot // 2, 0, slot % 2]

def fwd_kernel(order_ref, own_ref, q_ref, k_ref, v_ref, o_ref, lse_ref, ks, vs, scr, acc, *, blocks):
    s = pl.program_id(0)
    @pl.when((s == 0) & (pl.program_id(1) == 0))
    def _():
        vs[:, 128:256] = jnp.ones((blocks * BLK, 128), jnp.bfloat16)
    sort_rows(order_ref, s, k_ref, ks, blocks)
    sort_rows(order_ref, s, v_ref, vs, blocks)
    for w in range(2):
        pos = own_ref[s, w]
        last = pos // CB
        qs = split_heads(q_ref[0, w * BLK:(w + 1) * BLK, :] * jnp.bfloat16(SCALE))

        def tiles_max(run, sc):
            for t in range(CB):
                run = jnp.maximum(run, sc[:, t * 128:(t + 1) * 128])
            return run

        def score(c, run):
            at = pl.multiple_of(c * CH, CH)
            sc = nt(qs, ks[pl.ds(at, CH), :])
            scr[c] = sc
            return tiles_max(run, sc)

        run = lax.fori_loop(0, last, score, jnp.full((2 * BLK, 128), NEG, jnp.float32))
        at = pl.multiple_of(last * CH, CH)
        sc = nt(qs, ks[pl.ds(at, CH), :])
        qpos = pos * BLK + row_of((2 * BLK, CH)) % BLK
        kpos = last * CH + lane_of((2 * BLK, CH))
        sc = jnp.where(kpos <= qpos, sc, NEG)
        scr[last] = sc
        run = tiles_max(run, sc)
        top = jnp.max(run, axis=1, keepdims=True)
        topb = jnp.broadcast_to(top, (2 * BLK, 128))
        topc = jnp.concatenate([topb] * CB, axis=1)
        acc[...] = jnp.zeros_like(acc)

        def weigh(c, carry):
            at = pl.multiple_of(c * CH, CH)
            p = jnp.exp(scr[c] - topc).astype(jnp.bfloat16)
            acc[...] += nn(p, vs[pl.ds(at, CH), :])
            return carry

        lax.fori_loop(0, last + 1, weigh, 0)
        total = acc[:, 128:256]
        out = acc[:, 0:128] / total
        o_ref[0, w * BLK:(w + 1) * BLK, :] = join_heads(out).astype(jnp.bfloat16)
        lse = topb + jnp.log(total)
        for h in range(2):
            lse_ref[0, 0, w, h:h + 1, :] = lse[h * BLK:(h + 1) * BLK].T[0:1, :]

def dq_kernel(order_ref, own_ref, q_ref, do_ref, lse_ref, delta_ref, k_ref, v_ref, c_ref, a_ref, b_ref, dq_ref, ks, vs, acc, *, blocks):
    s = pl.program_id(0)
    sort_rows(order_ref, s, k_ref, ks, blocks)
    sort_rows(order_ref, s, v_ref, vs, blocks)
    for w in range(2):
        pos = own_ref[s, w]
        last = pos // CB
        qs = split_heads(q_ref[0, w * BLK:(w + 1) * BLK, :] * jnp.bfloat16(SCALE))
        dos = split_heads(do_ref[0, w * BLK:(w + 1) * BLK, :])
        cols = []
        for ref in (lse_ref, delta_ref):
            both = [jnp.broadcast_to(ref[0, 0, w, h:h + 1, :], (BLK, 128)).T for h in range(2)]
            cols.append(jnp.concatenate([jnp.concatenate(both, axis=0)] * CB, axis=1))
        lse, delta = cols
        acc[...] = jnp.zeros_like(acc)

        def step(c, mask):
            at = pl.multiple_of(c * CH, CH)
            kc = ks[pl.ds(at, CH), :]
            p = jnp.exp(nt(qs, kc) - lse)
            if mask is not None:
                p = jnp.where(mask, p, 0.0)
            dp = nt(dos, vs[pl.ds(at, CH), :])
            ds = (p * (dp - delta)).astype(jnp.bfloat16)
            acc[...] += nn(ds, kc)

        def body(c, carry):
            step(c, None)
            return carry

        lax.fori_loop(0, last, body, 0)
        qpos = pos * BLK + row_of((2 * BLK, CH)) % BLK
        kpos = last * CH + lane_of((2 * BLK, CH))
        step(last, kpos <= qpos)
        rows = slice(w * BLK, (w + 1) * BLK)
        grad = join_heads(acc[...]) * SCALE
        dq_ref[0, rows, :] = turn(grad, c_ref[rows], a_ref[rows], b_ref[rows], -1.0).astype(jnp.bfloat16)

def dkv_kernel(order_ref, own_ref, k_ref, v_ref, q_ref, do_ref, lse_ref, delta_ref, c_ref, a_ref, b_ref, dk_ref, dv_ref,
               qs, dos, lses, deltas, acck, accv, *, blocks):
    s = pl.program_id(0)
    sort_rows(order_ref, s, q_ref, qs, blocks)
    sort_rows(order_ref, s, do_ref, dos, blocks)
    for p in range(blocks):
        slot = order_ref[s, p]
        at = (p % CB) * BLK
        lses[p // CB, :, at:at + BLK] = lse_ref[slot // 2, 0, 0, slot % 2]
        deltas[p // CB, :, at:at + BLK] = delta_ref[slot // 2, 0, 0, slot % 2]
    for w in range(2):
        pos = own_ref[s, w]
        first = pos // CB
        kw = split_heads(k_ref[0, w * BLK:(w + 1) * BLK, :] * jnp.bfloat16(SCALE))
        vw = split_heads(v_ref[0, w * BLK:(w + 1) * BLK, :])
        acck[...] = jnp.zeros_like(acck)
        accv[...] = jnp.zeros_like(accv)

        def step(c, mask):
            at = pl.multiple_of(c * CH, CH)
            qc = qs[pl.ds(at, CH), :]
            doc = dos[pl.ds(at, CH), :]
            lse2, delta2 = lses[c], deltas[c]
            lse = jnp.concatenate([jnp.broadcast_to(lse2[h:h + 1], (BLK, CH)) for h in range(2)], axis=0)
            delta = jnp.concatenate([jnp.broadcast_to(delta2[h:h + 1], (BLK, CH)) for h in range(2)], axis=0)
            p = jnp.exp(nt(kw, qc) - lse)
            if mask is not None:
                p = jnp.where(mask, p, 0.0)
            accv[...] += nn(p.astype(jnp.bfloat16), doc)
            ds = (p * (nt(vw, doc) - delta)).astype(jnp.bfloat16)
            acck[...] += nn(ds, qc)

        def body(c, carry):
            step(c, None)
            return carry

        kpos = pos * BLK + row_of((2 * BLK, CH)) % BLK
        qpos = first * CH + lane_of((2 * BLK, CH))
        step(first, kpos <= qpos)
        lax.fori_loop(first + 1, blocks // CB, body, 0)
        rows = slice(w * BLK, (w + 1) * BLK)
        grad = join_heads(acck[...]) * SCALE
        dk_ref[0, rows, :] = turn(grad, c_ref[rows], a_ref[rows], b_ref[rows], -1.0).astype(jnp.bfloat16)
        dv_ref[0, rows, :] = join_heads(accv[...]).astype(jnp.bfloat16)

def specs(n_ctx):
    own = pl.BlockSpec((1, 2 * BLK, 128), lambda s, h, *_: (s, 0, h))
    whole = pl.BlockSpec((n_ctx, 1, 2, BLK, 128), lambda s, h, *_: (0, s, 0, 0, h))
    row = pl.BlockSpec((1, 1, 2, 2, BLK), lambda s, h, *_: (s, h, 0, 0, 0))
    rows = pl.BlockSpec((n_ctx, 1, 1, 2, 2, BLK), lambda s, h, *_: (0, s, h, 0, 0, 0))
    table = pl.BlockSpec((2 * BLK, 128), lambda s, h, *_: (s, 0))
    return own, whole, row, rows, table

def cost(seqs, pairs, blocks, mats, n_bytes):
    work = seqs * pairs * 2 * 2 * BLK * blocks * BLK // 2
    return pl.CostEstimate(flops=work * 128 * 2 * mats, bytes_accessed=n_bytes, transcendentals=work)

def attend(order, own_order, q, k_all, v_all):
    n_ctx, seqs = k_all.shape[:2]
    pairs = q.shape[2] // 128
    blocks = 2 * n_ctx
    own, whole, row, rows, table = specs(n_ctx)
    return pl.pallas_call(
        functools.partial(fwd_kernel, blocks=blocks),
        grid_spec=pltpu.PrefetchScalarGridSpec(
            num_scalar_prefetch=2, grid=(seqs, pairs),
            in_specs=[own, whole, whole], out_specs=[own, row],
            scratch_shapes=[pltpu.VMEM((blocks * BLK, 128), jnp.bfloat16), pltpu.VMEM((blocks * BLK, 256), jnp.bfloat16),
                            pltpu.VMEM((blocks // CB, 2 * BLK, CH), jnp.float32), pltpu.VMEM((2 * BLK, 256), jnp.float32)]),
        out_shape=[jax.ShapeDtypeStruct(q.shape, jnp.bfloat16), jax.ShapeDtypeStruct((seqs, pairs, 2, 2, BLK), jnp.float32)],
        compiler_params=pltpu.CompilerParams(vmem_limit_bytes=40 * 2**20),
        cost_estimate=cost(seqs, pairs, blocks, 2, 4 * k_all.size),
        name="attend",
    )(order, own_order, q, k_all, v_all)

def query_grad(order, own_order, q, do, lse, delta, k_all, v_all, tabs):
    n_ctx, seqs = k_all.shape[:2]
    pairs = q.shape[2] // 128
    blocks = 2 * n_ctx
    own, whole, row, rows, table = specs(n_ctx)
    return pl.pallas_call(
        functools.partial(dq_kernel, blocks=blocks),
        grid_spec=pltpu.PrefetchScalarGridSpec(
            num_scalar_prefetch=2, grid=(seqs, pairs),
            in_specs=[own, own, row, row, whole, whole, table, table, table], out_specs=own,
            scratch_shapes=[pltpu.VMEM((blocks * BLK, 128), jnp.bfloat16), pltpu.VMEM((blocks * BLK, 128), jnp.bfloat16),
                            pltpu.VMEM((2 * BLK, 128), jnp.float32)]),
        out_shape=jax.ShapeDtypeStruct(q.shape, jnp.bfloat16),
        compiler_params=pltpu.CompilerParams(vmem_limit_bytes=40 * 2**20),
        cost_estimate=cost(seqs, pairs, blocks, 3, 4 * k_all.size),
        name="query_grad",
    )(order, own_order, q, do, lse, delta, k_all, v_all, *tabs)

def key_value_grad(order, own_order, k, v, q_all, do_all, lse_all, delta_all, tabs):
    n_ctx, seqs = q_all.shape[:2]
    pairs = k.shape[2] // 128
    blocks = 2 * n_ctx
    own, whole, row, rows, table = specs(n_ctx)
    return pl.pallas_call(
        functools.partial(dkv_kernel, blocks=blocks),
        grid_spec=pltpu.PrefetchScalarGridSpec(
            num_scalar_prefetch=2, grid=(seqs, pairs),
            in_specs=[own, own, whole, whole, rows, rows, table, table, table], out_specs=[own, own],
            scratch_shapes=[pltpu.VMEM((blocks * BLK, 128), jnp.bfloat16), pltpu.VMEM((blocks * BLK, 128), jnp.bfloat16),
                            pltpu.VMEM((blocks // CB, 2, CH), jnp.float32), pltpu.VMEM((blocks // CB, 2, CH), jnp.float32),
                            pltpu.VMEM((2 * BLK, 128), jnp.float32), pltpu.VMEM((2 * BLK, 128), jnp.float32)]),
        out_shape=[jax.ShapeDtypeStruct(k.shape, jnp.bfloat16)] * 2,
        compiler_params=pltpu.CompilerParams(vmem_limit_bytes=40 * 2**20),
        cost_estimate=cost(seqs, pairs, blocks, 4, 4 * q_all.size),
        name="key_value_grad",
    )(order, own_order, k, v, q_all, do_all, lse_all, delta_all, *tabs)


import math
from jax.sharding import PartitionSpec as P

HEAD_DIM = 64
ROT = 16
SEQS = 4
EPS = 1e-05
F32 = jnp.float32
BF16 = jnp.bfloat16


def rc(left, right):
    return lax.dot_general(left, right, (((0,), (0,)), ((), ())), preferred_element_type=F32)


def layer_stats(values, gain, shift):
    mean = jnp.mean(values, axis=-1, keepdims=True)
    centred = values - mean
    inverse = lax.rsqrt(jnp.mean(centred * centred, axis=-1, keepdims=True) + EPS)
    unit = centred * inverse
    return unit * gain + shift, unit, inverse


def layer_back(grad, unit, inverse, gain):
    scaled = grad * gain
    grad_in = inverse * (
        scaled
        - jnp.mean(scaled, axis=-1, keepdims=True)
        - unit * jnp.mean(scaled * unit, axis=-1, keepdims=True)
    )
    return grad_in, jnp.sum(grad * unit, axis=0), jnp.sum(grad, axis=0)


def rotary_tables(positions):
    half = ROT // 2
    freq = 10000.0 ** (-2.0 * jnp.arange(half, dtype=F32) / ROT)
    angles = positions.astype(F32)[:, None] * freq[None, :]
    cos, sin = jnp.cos(angles), jnp.sin(angles)
    rows = positions.shape[0]
    one, none = jnp.ones((rows, HEAD_DIM - ROT), F32), jnp.zeros((rows, HEAD_DIM - ROT), F32)
    zero = jnp.zeros_like(sin)
    ctab = jnp.concatenate([cos, cos, one] * 2, axis=1)
    above = jnp.concatenate([sin, zero, none] * 2, axis=1)
    below = jnp.concatenate([zero, sin, none] * 2, axis=1)
    return ctab, above, below


def turn(x, ctab, above, below, sign):
    up = pltpu.roll(x, 128 - ROT // 2, axis=1)
    down = pltpu.roll(x, ROT // 2, axis=1)
    return x * ctab + sign * (down * below - up * above)


def project_kernel(h_ref, wq_ref, wk_ref, wv_ref, bias_ref, c_ref, a_ref, b_ref, q_ref, kv_ref):
    h = h_ref[...]
    width = wq_ref.shape[1]
    tabs = c_ref[...], a_ref[...], b_ref[...]
    for at, (w_ref, out) in enumerate(((wq_ref, q_ref.at[0]), (wk_ref, kv_ref.at[0, 0]), (wv_ref, kv_ref.at[1, 0]))):
        lin = nn(h, w_ref[...]) + bias_ref[at:at + 1, :]
        for p in range(width // 128):
            part = lin[:, p * 128:(p + 1) * 128]
            if at < 2:
                part = turn(part, *tabs, 1.0)
            out[:, p * 128:(p + 1) * 128] = part.astype(BF16)


def project(rows, wq, wk, wv, bias, tabs):
    total, depth = rows.shape
    width = wq.shape[1]
    step = total // SEQS
    weight = pl.BlockSpec((depth, width), lambda i: (0, 0))
    table = pl.BlockSpec((step, 128), lambda i: (i, 0))
    return pl.pallas_call(
        project_kernel,
        grid=(SEQS,),
        in_specs=[pl.BlockSpec((step, depth), lambda i: (i, 0)), weight, weight, weight,
                  pl.BlockSpec((3, width), lambda i: (0, 0)), table, table, table],
        out_specs=[pl.BlockSpec((1, step, width), lambda i: (i, 0, 0)),
                   pl.BlockSpec((2, 1, step, width), lambda i: (0, i, 0, 0))],
        out_shape=[jax.ShapeDtypeStruct((SEQS, step, width), BF16), jax.ShapeDtypeStruct((2, SEQS, step, width), BF16)],
        compiler_params=pltpu.CompilerParams(vmem_limit_bytes=48 * 2**20),
        cost_estimate=pl.CostEstimate(flops=6 * total * depth * width, bytes_accessed=6 * depth * width, transcendentals=0),
        name="project",
    )(rows, wq, wk, wv, bias, *tabs)


def ctx_swap(x, mask):
    n = lax.axis_size("ctx")
    return lax.ppermute(x, "ctx", [(i, i ^ mask) for i in range(n)])


def add16(a, b):
    return (a.astype(F32) + b.astype(F32)).astype(BF16)


def reduce_step(x, bit):
    mine = (lax.axis_index("ctx") >> bit) & 1
    r = x.shape[0] // 2
    keep = lax.dynamic_slice_in_dim(x, mine * r, r, 0)
    send = lax.dynamic_slice_in_dim(x, (1 - mine) * r, r, 0)
    return add16(keep, ctx_swap(send, 1 << bit))


def gather_step(x, bit):
    mine = (lax.axis_index("ctx") >> bit) & 1
    other = ctx_swap(x, 1 << bit)
    return jnp.where(mine == 0, jnp.concatenate([x, other]), jnp.concatenate([other, x]))


def sum_over_ctx(half):
    bits = list(range(1, int(math.log2(lax.axis_size("ctx")))))
    orders = [bits, bits[::-1]]
    r = half.shape[0] // 2
    streams = [half[:r], half[r:]]
    for i in range(len(bits)):
        streams = [reduce_step(x, order[i]) for x, order in zip(streams, orders)]
    for i in reversed(range(len(bits))):
        streams = [gather_step(x, order[i]) for x, order in zip(streams, orders)]
    return jnp.concatenate(streams)


def weight_grad(left, right, split_left):
    core = lax.axis_index("ctx") & 1
    split = left if split_left else right
    w = split.shape[1] // 2

    def part(which):
        cut = lax.dynamic_slice_in_dim(split, which * w, w, 1)
        return rc(cut, right) if split_left else rc(left, cut)

    got = ctx_swap(part(1 - core).astype(BF16), 1)
    half = sum_over_ctx((part(core) + got.astype(F32)).astype(BF16))
    other = ctx_swap(half, 1)
    axis = 0 if split_left else 1
    return jnp.where(core == 0, jnp.concatenate([half, other], axis=axis), jnp.concatenate([other, half], axis=axis)).astype(F32)


def all_rows(x):
    return lax.all_gather(x, "tp", axis=0, tiled=True)


def sum_rows(x):
    return lax.psum_scatter(x, "tp", scatter_dimension=0, tiled=True).astype(F32)


def local(tokens, cotangent, block_order, gain_one, shift_one, query_w, key_w, value_w, query_b, key_b, value_b,
          output_w, gain_two, shift_two, gate_w, up_w, down_w):
    heads = key_b.shape[0]
    width = heads * HEAD_DIM
    n_ctx = lax.axis_size("ctx")
    ctx = lax.axis_index("ctx")
    blocks = 2 * n_ctx
    own_order = lax.dynamic_slice_in_dim(block_order, 2 * ctx, 2, 1)
    slots = jnp.arange(blocks, dtype=jnp.int32)
    order = jnp.sum(jnp.where(block_order[:, :, None] == slots[None, None, :], slots[None, :, None], 0), axis=1).astype(jnp.int32)
    positions = (own_order[:, :, None] * BLK + jnp.arange(BLK, dtype=jnp.int32)).reshape(-1)
    tabs = rotary_tables(positions)

    x = tokens.astype(F32)
    normed_one, unit_one, inverse_one = layer_stats(x, gain_one, shift_one)
    rows_one = all_rows(normed_one.astype(BF16))
    dy_rows = all_rows(cotangent)
    key_bias = jnp.concatenate([key_b, jnp.zeros((heads, HEAD_DIM - ROT), F32)], axis=1).reshape(-1)
    bias = jnp.stack([query_b, key_bias, value_b])
    q, kv = project(rows_one, query_w, key_w, value_w, bias, tabs)
    shape = (SEQS, 2, BLK, width)
    kv_all = lax.all_gather(kv.reshape((2,) + shape), "ctx", axis=0)
    k_all, v_all = kv_all[:, 0], kv_all[:, 1]
    attn, lse = attend(order, own_order, q, k_all, v_all)
    q_all = lax.all_gather(q.reshape(shape), "ctx", axis=0)
    lse_all = lax.all_gather(lse, "ctx", axis=0)
    attn_rows = attn.reshape(-1, width)
    mixed = x + sum_rows(nn(attn_rows, output_w).astype(BF16))
    normed_two, unit_two, inverse_two = layer_stats(mixed, gain_two, shift_two)
    rows_two = all_rows(normed_two.astype(BF16))
    gate = nn(rows_two, gate_w)
    up = nn(rows_two, up_w)
    sig = jax.nn.sigmoid(gate)
    silu = gate * sig
    act = (silu * up).astype(BF16)
    grad_act = nt(dy_rows, down_w)
    grad_gate = (grad_act * up * sig * (1.0 + gate * (1.0 - sig))).astype(BF16)
    grad_up = (grad_act * silu).astype(BF16)
    grad_two = sum_rows((nt(grad_gate, gate_w) + nt(grad_up, up_w)).astype(BF16))
    out_tokens = (mixed + sum_rows(nn(act, down_w).astype(BF16))).astype(BF16)
    grad_down_w = weight_grad(act, dy_rows, False)
    grad_gate_w = weight_grad(rows_two, grad_gate, True)
    grad_up_w = weight_grad(rows_two, grad_up, True)

    norm_two, grad_gain_two, grad_shift_two = layer_back(grad_two, unit_two, inverse_two, gain_two)
    grad_mixed = cotangent.astype(F32) + norm_two
    branch = all_rows(grad_mixed.astype(BF16))
    grad_attn = nt(branch, output_w).astype(BF16)
    ind = (jnp.arange(heads)[:, None] == (jnp.arange(width) // HEAD_DIM)[None, :]).astype(F32)
    delta = lax.dot_general(ind, grad_attn.astype(F32) * attn_rows.astype(F32), (((1,), (1,)), ((), ())),
                            precision=lax.Precision.HIGHEST, preferred_element_type=F32)
    delta = jnp.transpose(delta.reshape(heads // 2, 2, SEQS, 2, BLK), (2, 0, 3, 1, 4))
    do_all = lax.all_gather(grad_attn.reshape(shape), "ctx", axis=0)
    delta_all = lax.all_gather(delta, "ctx", axis=0)
    grad_output_w = weight_grad(attn_rows, branch, False)
    grad_q = query_grad(order, own_order, q, grad_attn.reshape(q.shape), lse, delta, k_all, v_all, tabs)
    grad_k, grad_v = key_value_grad(order, own_order, kv[0], kv[1], q_all, do_all, lse_all, delta_all, tabs)
    grad_q, grad_k, grad_v = (g.reshape(-1, width) for g in (grad_q, grad_k, grad_v))
    grad_one = sum_rows((nt(grad_q, query_w) + nt(grad_k, key_w) + nt(grad_v, value_w)).astype(BF16))
    grad_qkv = jnp.concatenate([grad_q, grad_k, grad_v], axis=1)
    grad_qkv_w = weight_grad(rows_one, grad_qkv, True)
    bias_sum = lax.psum(jnp.sum(grad_qkv.astype(F32), axis=0), "ctx")
    norm_one, grad_gain_one, grad_shift_one = layer_back(grad_one, unit_one, inverse_one, gain_one)
    grad_tokens = (grad_mixed + norm_one).astype(BF16)
    norms = lax.psum((grad_gain_one, grad_shift_one, grad_gain_two, grad_shift_two), ("ctx", "tp"))
    return (
        out_tokens, grad_tokens, norms[0], norms[1],
        grad_qkv_w[:, :width], grad_qkv_w[:, width:2 * width], grad_qkv_w[:, 2 * width:],
        bias_sum[:width], bias_sum[width:2 * width].reshape(heads, HEAD_DIM)[:, :ROT], bias_sum[2 * width:],
        grad_output_w, norms[2], norms[3], grad_gate_w, grad_up_w, grad_down_w,
    )


def solution(mesh):
    rows, cols, depth, flat = P(("ctx", "tp"), None), P(None, "tp"), P("tp", None), P("tp")
    in_specs = (rows, rows, P(), P(), P(), cols, cols, cols, flat, depth, flat, depth, P(), P(), cols, cols, depth)
    out_specs = (rows, rows, P(), P(), cols, cols, cols, flat, depth, flat, depth, P(), P(), cols, cols, depth)
    return jax.shard_map(local, mesh=mesh, in_specs=in_specs, out_specs=out_specs, check_vma=False)
```

```python
import functools
import jax, jax.numpy as jnp
from jax import lax
from jax.experimental import pallas as pl
from jax.experimental.pallas import tpu as pltpu

BLK = 128
CB = 4
CH = BLK * CB
NEG = -1e30
SCALE = 0.125


def nt(a, b):
    return lax.dot_general(a, b, (((1,), (1,)), ((), ())), preferred_element_type=jnp.float32)


def nn(a, b):
    return lax.dot_general(a, b, (((1,), (0,)), ((), ())), preferred_element_type=jnp.float32)


def lane_of(shape):
    return lax.broadcasted_iota(jnp.int32, shape, 1)


def row_of(shape):
    return lax.broadcasted_iota(jnp.int32, shape, 0)


def split_heads(x):
    low = lane_of(x.shape) < 64
    zero = jnp.zeros_like(x)
    return jnp.concatenate([jnp.where(low, x, zero), jnp.where(low, zero, x)], axis=0)


def join_heads(x):
    low = lane_of((BLK, 128)) < 64
    return jnp.where(low, x[:BLK], x[BLK:])


def own_lanes(pair):
    shape = (2 * BLK, 128)
    return lane_of(shape) // 3 == 2 * pair + row_of(shape) // BLK


def terms(x, lane):
    first = x.astype(jnp.bfloat16).astype(jnp.float32)
    second = (x - first).astype(jnp.bfloat16).astype(jnp.float32)
    return jnp.where(lane % 3 == 0, first, jnp.where(lane % 3 == 1, second, x - first - second))


def place_rows(place_ref, s, refs, dst_ref, lane=0):
    at = 0
    for ref in refs:
        for j in range(ref.shape[0]):
            for w in range(2):
                row = pl.multiple_of(place_ref[s, at] * BLK, BLK)
                dst_ref[pl.ds(row, BLK), lane:lane + 128] = ref[j, 0, w]
                at += 1


def fwd_kernel(place_ref, own_ref, q_ref, *refs, blocks, n):
    k_refs, v_refs, (o_ref, ext_ref, ks, vs, scr, acc) = refs[:n], refs[n:2 * n], refs[2 * n:]
    s, pair = pl.program_id(0), pl.program_id(1)

    @pl.when((s == 0) & (pair == 0))
    def _():
        vs[:, 128:256] = jnp.ones((blocks * BLK, 128), jnp.bfloat16)

    @pl.when(pair == 0)
    def _():
        ext_ref[...] = jnp.zeros_like(ext_ref)

    place_rows(place_ref, s, k_refs, ks)
    place_rows(place_ref, s, v_refs, vs)
    for w in range(2):
        rows = slice(w * BLK, (w + 1) * BLK)
        pos = own_ref[s, w]
        last = pos // CB
        qs = split_heads(q_ref[0, rows, :] * jnp.bfloat16(SCALE))

        def tiles_max(run, sc):
            for t in range(CB):
                run = jnp.maximum(run, sc[:, t * 128:(t + 1) * 128])
            return run

        def score(c, run):
            at = pl.multiple_of(c * CH, CH)
            sc = nt(qs, ks[pl.ds(at, CH), :])
            scr[c] = sc
            return tiles_max(run, sc)

        run = lax.fori_loop(0, last, score, jnp.full((2 * BLK, 128), NEG, jnp.float32))
        at = pl.multiple_of(last * CH, CH)
        sc = nt(qs, ks[pl.ds(at, CH), :])
        qpos = pos * BLK + row_of((2 * BLK, CH)) % BLK
        kpos = last * CH + lane_of((2 * BLK, CH))
        sc = jnp.where(kpos <= qpos, sc, NEG)
        scr[last] = sc
        run = tiles_max(run, sc)
        top = jnp.broadcast_to(jnp.max(run, axis=1, keepdims=True), (2 * BLK, 128))
        topc = jnp.concatenate([top] * CB, axis=1)
        acc[...] = jnp.zeros_like(acc)

        def weigh(c, carry):
            at = pl.multiple_of(c * CH, CH)
            p = jnp.exp(scr[c] - topc).astype(jnp.bfloat16)
            acc[...] += nn(p, vs[pl.ds(at, CH), :])
            return carry

        lax.fori_loop(0, last + 1, weigh, 0)
        total = acc[:, 128:256]
        o_ref[0, rows, :] = join_heads(acc[:, 0:128] / total).astype(jnp.bfloat16)
        lane = lane_of((2 * BLK, 128))
        mine = jnp.where(own_lanes(pair), terms(-(top + jnp.log(total)), lane), 0.0)
        ext_ref[0, rows, :] = (ext_ref[0, rows, :].astype(jnp.float32) + mine[:BLK] + mine[BLK:]).astype(jnp.bfloat16)


def dq_kernel(place_ref, own_ref, q_ref, do_ref, qx_ref, dox_ref, c_ref, a_ref, b_ref, *refs, blocks, n):
    k_refs, v_refs, (dq_ref, ks, vs, acc) = refs[:n], refs[n:2 * n], refs[2 * n:]
    s, pair = pl.program_id(0), pl.program_id(1)

    @pl.when((s == 0) & (pair == 0))
    def _():
        ks[:, 128:256] = jnp.ones((blocks * BLK, 128), jnp.bfloat16)
        vs[:, 128:256] = jnp.ones((blocks * BLK, 128), jnp.bfloat16)

    place_rows(place_ref, s, k_refs, ks)
    place_rows(place_ref, s, v_refs, vs)
    mine = own_lanes(pair)
    for w in range(2):
        rows = slice(w * BLK, (w + 1) * BLK)
        pos = own_ref[s, w]
        last = pos // CB

        def extend(tile, ext):
            both = jnp.concatenate([ext, ext], axis=0)
            return jnp.concatenate([split_heads(tile), jnp.where(mine, both, jnp.zeros_like(both))], axis=1)

        qs = extend(q_ref[0, rows, :] * jnp.bfloat16(SCALE), qx_ref[0, rows, :])
        dos = extend(do_ref[0, rows, :], dox_ref[0, rows, :])
        acc[...] = jnp.zeros_like(acc)

        def step(c, mask):
            at = pl.multiple_of(c * CH, CH)
            p = jnp.exp(nt(qs, ks[pl.ds(at, CH), :]))
            if mask is not None:
                p = jnp.where(mask, p, 0.0)
            ds = (p * nt(dos, vs[pl.ds(at, CH), :])).astype(jnp.bfloat16)
            acc[...] += nn(ds, ks[pl.ds(at, CH), 0:128])

        def body(c, carry):
            step(c, None)
            return carry

        lax.fori_loop(0, last, body, 0)
        qpos = pos * BLK + row_of((2 * BLK, CH)) % BLK
        kpos = last * CH + lane_of((2 * BLK, CH))
        step(last, kpos <= qpos)
        grad = join_heads(acc[...]) * SCALE
        dq_ref[0, rows, :] = turn(grad, c_ref[rows], a_ref[rows], b_ref[rows], -1.0).astype(jnp.bfloat16)


def dkv_kernel(place_ref, own_ref, k_ref, v_ref, c_ref, a_ref, b_ref, *refs, blocks, n):
    q_refs, do_refs, qx_refs, dox_refs = (refs[i * n:(i + 1) * n] for i in range(4))
    dk_ref, dv_ref, qs, dos, acck, accv = refs[4 * n:]
    s, pair = pl.program_id(0), pl.program_id(1)
    place_rows(place_ref, s, q_refs, qs)
    place_rows(place_ref, s, do_refs, dos)

    @pl.when(pair == 0)
    def _():
        place_rows(place_ref, s, qx_refs, qs, 128)
        place_rows(place_ref, s, dox_refs, dos, 128)

    ones = own_lanes(pair).astype(jnp.bfloat16)
    for w in range(2):
        rows = slice(w * BLK, (w + 1) * BLK)
        pos = own_ref[s, w]
        first = pos // CB
        kw = jnp.concatenate([split_heads(k_ref[0, 0, rows, :] * jnp.bfloat16(SCALE)), ones], axis=1)
        vw = jnp.concatenate([split_heads(v_ref[0, 0, rows, :]), ones], axis=1)
        acck[...] = jnp.zeros_like(acck)
        accv[...] = jnp.zeros_like(accv)

        def step(c, mask):
            at = pl.multiple_of(c * CH, CH)
            p = jnp.exp(nt(kw, qs[pl.ds(at, CH), :]))
            if mask is not None:
                p = jnp.where(mask, p, 0.0)
            accv[...] += nn(p.astype(jnp.bfloat16), dos[pl.ds(at, CH), 0:128])
            ds = (p * nt(vw, dos[pl.ds(at, CH), :])).astype(jnp.bfloat16)
            acck[...] += nn(ds, qs[pl.ds(at, CH), 0:128])

        def body(c, carry):
            step(c, None)
            return carry

        kpos = pos * BLK + row_of((2 * BLK, CH)) % BLK
        qpos = first * CH + lane_of((2 * BLK, CH))
        step(first, kpos <= qpos)
        lax.fori_loop(first + 1, blocks // CB, body, 0)
        grad = join_heads(acck[...]) * SCALE
        dk_ref[0, rows, :] = turn(grad, c_ref[rows], a_ref[rows], b_ref[rows], -1.0).astype(jnp.bfloat16)
        dv_ref[0, rows, :] = join_heads(accv[...]).astype(jnp.bfloat16)


OWN = pl.BlockSpec((1, 2 * BLK, 128), lambda s, h, *_: (s, 0, h))
EXT = pl.BlockSpec((1, 2 * BLK, 128), lambda s, h, *_: (s, 0, 0))
TABLE = pl.BlockSpec((2 * BLK, 128), lambda s, h, *_: (s, 0))


def piece(x, first=0, lane=None):
    count = x.shape[0] if first is None else 1
    lead = 0 if first is None else first
    if lane is None:
        return pl.BlockSpec((count, 1, 2, BLK, 128), lambda s, h, *_: (lead, s, 0, 0, h))
    return pl.BlockSpec((count, 1, 2, BLK, 128), lambda s, h, *_: (lead, s, 0, 0, lane))


def attention_call(kernel, name, mats, seqs, pairs, blocks, in_specs, out_specs, out_shape, scratch, args):
    work = seqs * pairs * 2 * 2 * BLK * blocks * BLK // 2
    return pl.pallas_call(
        kernel,
        grid_spec=pltpu.PrefetchScalarGridSpec(
            num_scalar_prefetch=2, grid=(seqs, pairs), in_specs=in_specs, out_specs=out_specs, scratch_shapes=scratch),
        out_shape=out_shape,
        compiler_params=pltpu.CompilerParams(vmem_limit_bytes=40 * 2**20),
        cost_estimate=pl.CostEstimate(flops=work * 512 * mats, bytes_accessed=4 * seqs * pairs * blocks * BLK * 128, transcendentals=work),
        name=name,
    )(*args)


def rows_of(blocks, lanes):
    return pltpu.VMEM((blocks * BLK, lanes), jnp.bfloat16)


def acc_of(lanes):
    return pltpu.VMEM((2 * BLK, lanes), jnp.float32)


def attend(place, own, q, keys, values):
    seqs, pairs, blocks = q.shape[0], q.shape[2] // 128, place.shape[1]
    return attention_call(
        functools.partial(fwd_kernel, blocks=blocks, n=len(keys)), "attend", 2, seqs, pairs, blocks,
        [OWN] + [piece(*e) for e in keys + values], [OWN, EXT],
        [jax.ShapeDtypeStruct(q.shape, jnp.bfloat16), jax.ShapeDtypeStruct(q.shape[:2] + (128,), jnp.bfloat16)],
        [rows_of(blocks, 128), rows_of(blocks, 256), pltpu.VMEM((blocks // CB, 2 * BLK, CH), jnp.float32), acc_of(256)],
        [place, own, q] + [e[0] for e in keys + values])


def query_grad(place, own, q, do, q_ext, do_ext, tabs, keys, values):
    seqs, pairs, blocks = q.shape[0], q.shape[2] // 128, place.shape[1]
    return attention_call(
        functools.partial(dq_kernel, blocks=blocks, n=len(keys)), "query_grad", 3, seqs, pairs, blocks,
        [OWN, OWN, EXT, EXT, TABLE, TABLE, TABLE] + [piece(*e) for e in keys + values], OWN,
        jax.ShapeDtypeStruct(q.shape, jnp.bfloat16),
        [rows_of(blocks, 256), rows_of(blocks, 256), acc_of(128)],
        [place, own, q, do, q_ext, do_ext, *tabs] + [e[0] for e in keys + values])


def key_value_grad(place, own, kv, tabs, queries, grads):
    seqs, pairs, blocks = kv.shape[1], kv.shape[3] // 128, place.shape[1]
    shape = kv.shape[1:]

    def own_part(i):
        return pl.BlockSpec((1, 1, 2 * BLK, 128), lambda s, h, *_: (i, s, 0, h))

    return attention_call(
        functools.partial(dkv_kernel, blocks=blocks, n=len(queries)), "key_value_grad", 4, seqs, pairs, blocks,
        [own_part(0), own_part(1), TABLE, TABLE, TABLE] + [piece(*e) for e in queries + grads]
        + [piece(*e, lane=pairs) for e in queries + grads], [OWN, OWN],
        [jax.ShapeDtypeStruct(shape, jnp.bfloat16)] * 2,
        [rows_of(blocks, 256), rows_of(blocks, 256), acc_of(128), acc_of(128)],
        [place, own, kv, kv, *tabs] + [e[0] for e in queries + grads] * 2)


import math
from jax.sharding import PartitionSpec as P

HEAD_DIM = 64
ROT = 16
SEQS = 4
EPS = 1e-05
F32 = jnp.float32
BF16 = jnp.bfloat16


def rc(left, right):
    return lax.dot_general(left, right, (((0,), (0,)), ((), ())), preferred_element_type=F32)


def layer_stats(values, gain, shift):
    mean = jnp.mean(values, axis=-1, keepdims=True)
    centred = values - mean
    inverse = lax.rsqrt(jnp.mean(centred * centred, axis=-1, keepdims=True) + EPS)
    unit = centred * inverse
    return unit * gain + shift, unit, inverse


def layer_back(grad, unit, inverse, gain):
    scaled = grad * gain
    grad_in = inverse * (
        scaled
        - jnp.mean(scaled, axis=-1, keepdims=True)
        - unit * jnp.mean(scaled * unit, axis=-1, keepdims=True)
    )
    return grad_in, jnp.sum(grad * unit, axis=0), jnp.sum(grad, axis=0)


def rotary_tables(positions):
    half = ROT // 2
    freq = 10000.0 ** (-2.0 * jnp.arange(half, dtype=F32) / ROT)
    angles = positions.astype(F32)[:, None] * freq[None, :]
    cos, sin = jnp.cos(angles), jnp.sin(angles)
    rows = positions.shape[0]
    one, none = jnp.ones((rows, HEAD_DIM - ROT), F32), jnp.zeros((rows, HEAD_DIM - ROT), F32)
    zero = jnp.zeros_like(sin)
    ctab = jnp.concatenate([cos, cos, one] * 2, axis=1)
    above = jnp.concatenate([sin, zero, none] * 2, axis=1)
    below = jnp.concatenate([zero, sin, none] * 2, axis=1)
    return ctab, above, below


def turn(x, ctab, above, below, sign):
    up = pltpu.roll(x, 128 - ROT // 2, axis=1)
    down = pltpu.roll(x, ROT // 2, axis=1)
    return x * ctab + sign * (down * below - up * above)


def project_kernel(h_ref, wq_ref, wk_ref, wv_ref, bias_ref, c_ref, a_ref, b_ref, q_ref, kv_ref):
    h = h_ref[...]
    width = wq_ref.shape[1]
    tabs = c_ref[...], a_ref[...], b_ref[...]
    for at, (w_ref, out) in enumerate(((wq_ref, q_ref.at[0]), (wk_ref, kv_ref.at[0, 0]), (wv_ref, kv_ref.at[1, 0]))):
        lin = nn(h, w_ref[...]) + bias_ref[at:at + 1, :]
        for p in range(width // 128):
            part = lin[:, p * 128:(p + 1) * 128]
            if at < 2:
                part = turn(part, *tabs, 1.0)
            out[:, p * 128:(p + 1) * 128] = part.astype(BF16)


def project(rows, wq, wk, wv, bias, tabs):
    total, depth = rows.shape
    width = wq.shape[1]
    step = total // SEQS
    weight = pl.BlockSpec((depth, width), lambda i: (0, 0))
    table = pl.BlockSpec((step, 128), lambda i: (i, 0))
    return pl.pallas_call(
        project_kernel,
        grid=(SEQS,),
        in_specs=[pl.BlockSpec((step, depth), lambda i: (i, 0)), weight, weight, weight,
                  pl.BlockSpec((3, width), lambda i: (0, 0)), table, table, table],
        out_specs=[pl.BlockSpec((1, step, width), lambda i: (i, 0, 0)),
                   pl.BlockSpec((2, 1, step, width), lambda i: (0, i, 0, 0))],
        out_shape=[jax.ShapeDtypeStruct((SEQS, step, width), BF16), jax.ShapeDtypeStruct((2, SEQS, step, width), BF16)],
        compiler_params=pltpu.CompilerParams(vmem_limit_bytes=48 * 2**20),
        cost_estimate=pl.CostEstimate(flops=6 * total * depth * width, bytes_accessed=6 * depth * width, transcendentals=0),
        name="project",
    )(rows, wq, wk, wv, bias, *tabs)


def mlp_kernel(h_ref, dy_ref, gate_ref, up_ref, down_ref, act_ref, *grad_refs):
    width = gate_ref.shape[1]
    gate = nn(h_ref[...], gate_ref[...])
    up = nn(h_ref[...], up_ref[...])
    grad = nt(dy_ref[...], down_ref[...])
    sig = 1.0 / (1.0 + jnp.exp(-gate))
    silu = gate * sig
    act_ref[...] = (silu * up).astype(BF16)
    outs = grad_refs if len(grad_refs) == 2 else (grad_refs[0].at[:, :width], grad_refs[0].at[:, width:])
    outs[0][...] = (grad * up * (sig + silu * (1.0 - sig))).astype(BF16)
    outs[1][...] = (grad * silu).astype(BF16)


def mlp(rows, dy, gate_w, up_w, down_w, step=256):
    total, depth = rows.shape
    width = gate_w.shape[1]
    joined = width % 128 == 0
    block = pl.BlockSpec((step, depth), lambda i: (i, 0))

    def whole(x):
        return pl.BlockSpec(x.shape, lambda i: (0, 0), pipeline_mode=pl.Buffered(1))

    def out(n):
        return pl.BlockSpec((step, n), lambda i: (i, 0)), jax.ShapeDtypeStruct((total, n), BF16)

    outs = [out(width), out(2 * width)] if joined else [out(width)] * 3
    act, *grads = pl.pallas_call(
        mlp_kernel,
        grid=(total // step,),
        in_specs=[block, block, whole(gate_w), whole(up_w), whole(down_w)],
        out_specs=[o[0] for o in outs],
        out_shape=[o[1] for o in outs],
        compiler_params=pltpu.CompilerParams(vmem_limit_bytes=56 * 2**20),
        cost_estimate=pl.CostEstimate(flops=6 * total * depth * width, bytes_accessed=6 * depth * width + 10 * total * depth,
                                      transcendentals=total * width),
        name="mlp",
    )(rows, dy, gate_w, up_w, down_w)
    return act, grads[0] if joined else jnp.concatenate(grads, axis=1)


def ctx_swap(x, mask):
    n = lax.axis_size("ctx")
    return lax.ppermute(x, "ctx", [(i, i ^ mask) for i in range(n)])


def add16(a, b):
    return (a.astype(F32) + b.astype(F32)).astype(BF16)


def after(x, *deps):
    return lax.optimization_barrier((x, deps))[0]


def half_of(x, bit, mine):
    side = (lax.axis_index("ctx") >> bit) & 1
    r = x.shape[0] // 2
    return lax.dynamic_slice_in_dim(x, (side if mine else 1 - side) * r, r, 0)


def weight_grad(left, right, split_left):
    core = lax.axis_index("ctx") & 1
    split = left if split_left else right
    w = split.shape[1] // 2

    def part(which):
        cut = lax.dynamic_slice_in_dim(split, which * w, w, 1)
        return rc(cut, right) if split_left else rc(left, cut)

    got = ctx_swap(part(1 - core).astype(BF16), 1)
    gate = yield [got]
    half = (part(core) + got.astype(F32)).astype(BF16)
    bits = list(range(1, int(math.log2(lax.axis_size("ctx")))))
    orders = [bits, bits[::-1]]
    r = half.shape[0] // 2
    streams = [half[:r], half[r:]]
    for i in range(len(bits)):
        streams = after(streams, gate)
        got = [ctx_swap(half_of(x, o[i], False), 1 << o[i]) for x, o in zip(streams, orders)]
        gate = yield got
        streams = [add16(half_of(x, o[i], True), g) for x, o, g in zip(streams, orders, got)]
    for i in reversed(range(len(bits))):
        streams = after(streams, gate)
        got = [ctx_swap(x, 1 << o[i]) for x, o in zip(streams, orders)]
        gate = yield got
        streams = [
            jnp.where(((lax.axis_index("ctx") >> o[i]) & 1) == 0, jnp.concatenate([x, g]), jnp.concatenate([g, x]))
            for x, o, g in zip(streams, orders, got)
        ]
    half = after(jnp.concatenate(streams), gate)
    other = ctx_swap(half, 1)
    yield [other]
    yield half, other


def advance(chains, gate=None):
    fly = []
    for chain in chains:
        fly += chain.send(gate)
    return fly


def begin(*args):
    chain = weight_grad(*args)
    return chain, next(chain)


def finish(chain):
    for got in chain:
        pass
    return got


def unpack_rows_kernel(core_ref, half_ref, other_ref, *out_refs):
    def put(src):
        at = 0
        for out in out_refs:
            out[...] = src[:, at:at + out.shape[1]].astype(F32)
            at += out.shape[1]

    @pl.when(pl.program_id(0) == core_ref[0])
    def _():
        put(half_ref)

    @pl.when(pl.program_id(0) != core_ref[0])
    def _():
        put(other_ref)


def unpack_rows(half, other, parts):
    r, c = half.shape
    step = math.gcd(r, 256)
    blocks = r // step
    core = lax.axis_index("ctx") & 1

    def mine(i, j, core_ref):
        return jnp.where(i == core_ref[0], j, jnp.where(core_ref[0] == 0, blocks - 1, 0)), 0

    def theirs(i, j, core_ref):
        return jnp.where(i != core_ref[0], j, jnp.where(core_ref[0] == 1, blocks - 1, 0)), 0

    return pl.pallas_call(
        unpack_rows_kernel,
        grid_spec=pltpu.PrefetchScalarGridSpec(
            num_scalar_prefetch=1, grid=(2, blocks),
            in_specs=[pl.BlockSpec((step, c), mine), pl.BlockSpec((step, c), theirs)],
            out_specs=[pl.BlockSpec((step, c // parts), lambda i, j, _: (i * blocks + j, 0))] * parts),
        out_shape=[jax.ShapeDtypeStruct((2 * r, c // parts), F32)] * parts,
        compiler_params=pltpu.CompilerParams(vmem_limit_bytes=40 * 2**20),
        cost_estimate=pl.CostEstimate(flops=0, bytes_accessed=12 * r * c, transcendentals=0),
        name="unpack_rows",
    )(core[None], half, other)


def unpack_cols_kernel(core_ref, half_ref, other_ref, out_ref):
    c = half_ref.shape[1]
    core = core_ref[0]
    out_ref[:, pl.ds(pl.multiple_of(core * c, 128), c)] = half_ref[...].astype(F32)
    out_ref[:, pl.ds(pl.multiple_of((1 - core) * c, 128), c)] = other_ref[...].astype(F32)


def unpack_cols(half, other):
    r, c = half.shape
    step = math.gcd(r, 256)
    block = pl.BlockSpec((step, c), lambda i, _: (i, 0))
    return pl.pallas_call(
        unpack_cols_kernel,
        grid_spec=pltpu.PrefetchScalarGridSpec(
            num_scalar_prefetch=1, grid=(r // step,), in_specs=[block, block],
            out_specs=pl.BlockSpec((step, 2 * c), lambda i, _: (i, 0))),
        out_shape=jax.ShapeDtypeStruct((r, 2 * c), F32),
        compiler_params=pltpu.CompilerParams(vmem_limit_bytes=40 * 2**20),
        cost_estimate=pl.CostEstimate(flops=0, bytes_accessed=12 * r * c, transcendentals=0),
        name="unpack_cols",
    )((lax.axis_index("ctx") & 1)[None], half, other)


def all_rows(x):
    return lax.all_gather(x, "tp", axis=0, tiled=True)


def sum_rows(x):
    return lax.psum_scatter(x, "tp", scatter_dimension=0, tiled=True).astype(F32)


def gather_pair(kv):
    n = lax.axis_size("ctx")
    held = {0: ((kv, 0), (kv, 1))}
    for bit in range(1, int(math.log2(n))):
        mask = 1 << bit
        for j in list(held):
            if j == 0:
                got = ctx_swap(kv, mask)
                held[mask] = (got, 0), (got, 1)
            elif mask == 4 and j == 2:
                held[6] = (ctx_swap(held[2][0][0][0:1], 4), 0), (ctx_swap(held[4][1][0][1:2], 2), 0)
            else:
                (k, i), (v, t) = held[j]
                if k is v:
                    got = ctx_swap(k, mask)
                    held[j | mask] = (got, i), (got, t)
                else:
                    held[j | mask] = (ctx_swap(k, mask), i), (ctx_swap(v, mask), t)
    for j in list(held):
        (k, i), (v, t) = held[j]
        got = ctx_swap(k, 1)
        held[j | 1] = (got, i), (got if k is v else ctx_swap(v, 1), t)
    return [held[j][0] for j in range(n)], [held[j][1] for j in range(n)]


def gather_ctx(x):
    n = lax.axis_size("ctx")
    held = [x] + [None] * (n - 1)
    for j in range(2, n, 2):
        held[j] = ctx_swap(x, j)
    for j in range(0, n, 2):
        held[j + 1] = ctx_swap(held[j], 1)
    return held


def local(tokens, cotangent, block_order, gain_one, shift_one, query_w, key_w, value_w, query_b, key_b, value_b,
          output_w, gain_two, shift_two, gate_w, up_w, down_w):
    heads = key_b.shape[0]
    width = heads * HEAD_DIM
    n_ctx, n_tp = lax.axis_size("ctx"), lax.axis_size("tp")
    ctx = lax.axis_index("ctx")
    own = lax.dynamic_slice_in_dim(block_order, 2 * ctx, 2, 1)
    picked = (jnp.arange(n_ctx, dtype=jnp.int32) ^ ctx)[:, None] == jnp.arange(n_ctx, dtype=jnp.int32)[None, :]
    by_ctx = block_order.reshape(SEQS, 1, n_ctx, 2)
    place = jnp.sum(jnp.where(picked[None, :, :, None], by_ctx, 0), axis=2).astype(jnp.int32).reshape(SEQS, 2 * n_ctx)
    positions = (own[:, :, None] * BLK + jnp.arange(BLK, dtype=jnp.int32)).reshape(-1)
    tabs = rotary_tables(positions)

    x = tokens.astype(F32)
    normed_one, unit_one, inverse_one = layer_stats(x, gain_one, shift_one)
    rows_one = all_rows(normed_one.astype(BF16))
    key_bias = jnp.concatenate([key_b, jnp.zeros((heads, HEAD_DIM - ROT), F32)], axis=1).reshape(-1)
    bias = jnp.stack([query_b, key_bias, value_b])
    q, kv = project(rows_one, query_w, key_w, value_w, bias, tabs)
    keys, values = gather_pair(kv.reshape(2, SEQS, 2, BLK, width))

    rows_w = output_w.shape[0] // n_ctx
    part = lax.dynamic_slice_in_dim(output_w, ctx * rows_w, rows_w, 0)
    part = lax.all_gather(after(part, rows_one), "tp", axis=0)
    dy_rows = all_rows(after(cotangent, kv))
    whole_w = lax.all_gather(after(part, dy_rows), "ctx", axis=1).reshape(n_tp * output_w.shape[0], -1)

    attn, q_ext = attend(place, own, q, keys, values)
    attn_rows = attn.reshape(-1, width)
    attn_own = lax.all_to_all(attn_rows, "tp", split_axis=0, concat_axis=1, tiled=True)
    mixed = x + nn(attn_own, whole_w)
    normed_two, unit_two, inverse_two = layer_stats(mixed, gain_two, shift_two)
    rows_two = all_rows(after(normed_two.astype(BF16), dy_rows, whole_w))
    shape = (1, SEQS, 2, BLK, width + 128)
    queries = gather_ctx(after(jnp.concatenate([q, q_ext], axis=2).reshape(shape), attn_own))
    rows_two = after(rows_two, queries)

    act, grad_gu = mlp(rows_two, dy_rows, gate_w, up_w, down_w)
    ff = gate_w.shape[1]
    part_two = (nt(grad_gu[:, :ff], gate_w) + nt(grad_gu[:, ff:], up_w)).astype(BF16)
    grad_two = sum_rows(part_two)
    act, rows_two, dy_rows, grad_gu = after((act, rows_two, dy_rows, grad_gu), part_two)
    down_chain, fly = begin(act, dy_rows, False)
    gu_chain, more = begin(rows_two, grad_gu, True)
    down = nn(act, down_w).astype(BF16)
    fly = advance([down_chain, gu_chain], fly + more)
    grad_two = after(grad_two, fly, down)

    norm_two, grad_gain_two, grad_shift_two = layer_back(grad_two, unit_two, inverse_two, gain_two)
    grad_mixed = cotangent.astype(F32) + norm_two
    branch_own = grad_mixed.astype(BF16)
    grad_attn = nt(branch_own, whole_w).astype(BF16)
    for _ in range(int(math.log2(n_ctx)) - 2):
        fly = advance([down_chain, gu_chain])
    grad_attn = lax.all_to_all(grad_attn, "tp", split_axis=1, concat_axis=0, tiled=True)
    branch = all_rows(after(branch_own, grad_attn))
    out_tokens = (mixed + sum_rows(after(down, branch))).astype(BF16)
    lane = jnp.arange(128)[None, :]
    ind = ((jnp.arange(width) // HEAD_DIM)[:, None] == lane // 3).astype(F32)
    delta = lax.dot_general(grad_attn.astype(F32) * attn_rows.astype(F32), ind, (((1,), (0,)), ((), ())),
                            precision=lax.Precision.HIGHEST, preferred_element_type=F32)
    do_ext = terms(-delta, lane).astype(BF16)
    grads = gather_ctx(jnp.concatenate([grad_attn, do_ext], axis=1).reshape(shape))
    grad_attn = after(grad_attn, fly)
    fly = advance([down_chain, gu_chain])
    grad_q = query_grad(place, own, q, grad_attn.reshape(q.shape), q_ext, do_ext.reshape(q_ext.shape), tabs, keys, values)
    grad_q = grad_q.reshape(-1, width)
    q_part = nt(grad_q, query_w)
    branch, grads = after((branch, grads), fly, q_part)
    for _ in range(int(math.log2(n_ctx)) - 2):
        fly = advance([down_chain, gu_chain], grads)
    out_chain, more = begin(attn_rows, branch, False)
    grad_k, grad_v = key_value_grad(place, own, kv, tabs, [(x, 0) for x in queries], [(x, 0) for x in grads])
    grad_k, grad_v = after((grad_k, grad_v), fly, more)
    grad_k, grad_v = (g.reshape(-1, width) for g in (grad_k, grad_v))
    part_one = q_part + nt(grad_k, key_w) + nt(grad_v, value_w)
    part_sent = part_one.astype(BF16)
    grad_one = sum_rows(part_sent)

    rows_one, grad_q, grad_k, grad_v = after((rows_one, grad_q, grad_k, grad_v), part_sent)
    unit_rows = (rows_one.astype(F32) - shift_one) / gain_one
    grad_qkv = jnp.concatenate([grad_q, grad_k, grad_v], axis=1)
    bias_grad = jnp.sum(grad_qkv.astype(F32), axis=0)
    tp_row = (jnp.arange(n_tp) == lax.axis_index("tp"))[:, None]
    small = jnp.concatenate([
        jnp.sum(part_one * unit_rows, axis=0), jnp.sum(part_one, axis=0), grad_gain_two, grad_shift_two,
        jnp.where(tp_row, bias_grad[None, :], 0.0).reshape(-1)])
    qkv_chain, more = begin(rows_one, grad_qkv, True)
    fly = advance([down_chain, gu_chain, out_chain])
    small = lax.psum(small, ("ctx", "tp"))
    depth = x.shape[1]
    norms = small[:4 * depth].reshape(4, depth)
    bias_sum = jnp.sum(jnp.where(tp_row, small[4 * depth:].reshape(n_tp, -1), 0.0), axis=0)
    grad_gate_w, grad_up_w = unpack_rows(*finish(gu_chain), 2)
    grad_query_w, grad_key_w, grad_value_w = unpack_rows(*finish(qkv_chain), 3)
    grad_down_w, grad_output_w = unpack_cols(*finish(down_chain)), unpack_cols(*finish(out_chain))
    norm_one, _, _ = layer_back(grad_one, unit_one, inverse_one, gain_one)
    grad_tokens = (grad_mixed + norm_one).astype(BF16)
    return (
        out_tokens, grad_tokens, norms[0], norms[1], grad_query_w, grad_key_w, grad_value_w,
        bias_sum[:width], bias_sum[width:2 * width].reshape(heads, HEAD_DIM)[:, :ROT], bias_sum[2 * width:],
        grad_output_w, norms[2], norms[3], grad_gate_w, grad_up_w, grad_down_w,
    )


def solution(mesh):
    rows, cols, depth, flat = P(("ctx", "tp"), None), P(None, "tp"), P("tp", None), P("tp")
    in_specs = (rows, rows, P(), P(), P(), cols, cols, cols, flat, depth, flat, depth, P(), P(), cols, cols, depth)
    out_specs = (rows, rows, P(), P(), cols, cols, cols, flat, depth, flat, depth, P(), P(), cols, cols, depth)
    return jax.shard_map(local, mesh=mesh, in_specs=in_specs, out_specs=out_specs, check_vma=False)
```

```python
import functools
import jax, jax.numpy as jnp
from jax import lax
from jax.experimental import pallas as pl
from jax.experimental.pallas import tpu as pltpu

BLK = 128
CB = 4
CH = BLK * CB
NEG = -1e30
SCALE = 0.125


def nt(a, b):
    return lax.dot_general(a, b, (((1,), (1,)), ((), ())), preferred_element_type=jnp.float32)


def nn(a, b):
    return lax.dot_general(a, b, (((1,), (0,)), ((), ())), preferred_element_type=jnp.float32)


def lane_of(shape):
    return lax.broadcasted_iota(jnp.int32, shape, 1)


def row_of(shape):
    return lax.broadcasted_iota(jnp.int32, shape, 0)


def split_heads(x):
    low = lane_of(x.shape) < 64
    zero = jnp.zeros_like(x)
    return jnp.concatenate([jnp.where(low, x, zero), jnp.where(low, zero, x)], axis=0)


def join_heads(x):
    low = lane_of((BLK, 128)) < 64
    return jnp.where(low, x[:BLK], x[BLK:])


def own_lanes(pair):
    shape = (2 * BLK, 128)
    return lane_of(shape) // 3 == 2 * pair + row_of(shape) // BLK


def terms(x, lane):
    first = x.astype(jnp.bfloat16).astype(jnp.float32)
    second = (x - first).astype(jnp.bfloat16).astype(jnp.float32)
    return jnp.where(lane % 3 == 0, first, jnp.where(lane % 3 == 1, second, x - first - second))


def place_rows(place_ref, s, refs, dst_ref, lane=0):
    at = 0
    for ref in refs:
        for j in range(ref.shape[0]):
            for w in range(2):
                row = pl.multiple_of(place_ref[s, at] * BLK, BLK)
                dst_ref[pl.ds(row, BLK), lane:lane + 128] = ref[j, 0, w]
                at += 1


def fwd_kernel(place_ref, own_ref, q_ref, *refs, blocks, n):
    k_refs, v_refs, (o_ref, ext_ref, ks, vs, scr, acc) = refs[:n], refs[n:2 * n], refs[2 * n:]
    s, pair = pl.program_id(0), pl.program_id(1)

    @pl.when((s == 0) & (pair == 0))
    def _():
        vs[:, 128:256] = jnp.ones((blocks * BLK, 128), jnp.bfloat16)

    @pl.when(pair == 0)
    def _():
        ext_ref[...] = jnp.zeros_like(ext_ref)

    place_rows(place_ref, s, k_refs, ks)
    place_rows(place_ref, s, v_refs, vs)
    for w in range(2):
        rows = slice(w * BLK, (w + 1) * BLK)
        pos = own_ref[s, w]
        last = pos // CB
        qs = split_heads(q_ref[0, rows, :] * jnp.bfloat16(SCALE))

        def tiles_max(run, sc):
            for t in range(CB):
                run = jnp.maximum(run, sc[:, t * 128:(t + 1) * 128])
            return run

        def score(c, run):
            at = pl.multiple_of(c * CH, CH)
            sc = nt(qs, ks[pl.ds(at, CH), :])
            scr[c] = sc
            return tiles_max(run, sc)

        run = lax.fori_loop(0, last, score, jnp.full((2 * BLK, 128), NEG, jnp.float32))
        at = pl.multiple_of(last * CH, CH)
        sc = nt(qs, ks[pl.ds(at, CH), :])
        qpos = pos * BLK + row_of((2 * BLK, CH)) % BLK
        kpos = last * CH + lane_of((2 * BLK, CH))
        sc = jnp.where(kpos <= qpos, sc, NEG)
        scr[last] = sc
        run = tiles_max(run, sc)
        top = jnp.broadcast_to(jnp.max(run, axis=1, keepdims=True), (2 * BLK, 128))
        topc = jnp.concatenate([top] * CB, axis=1)
        acc[...] = jnp.zeros_like(acc)

        def weigh(c, carry):
            at = pl.multiple_of(c * CH, CH)
            p = jnp.exp(scr[c] - topc).astype(jnp.bfloat16)
            acc[...] += nn(p, vs[pl.ds(at, CH), :])
            return carry

        lax.fori_loop(0, last + 1, weigh, 0)
        total = acc[:, 128:256]
        o_ref[0, rows, :] = join_heads(acc[:, 0:128] / total).astype(jnp.bfloat16)
        lane = lane_of((2 * BLK, 128))
        mine = jnp.where(own_lanes(pair), terms(-(top + jnp.log(total)), lane), 0.0)
        ext_ref[0, rows, :] = (ext_ref[0, rows, :].astype(jnp.float32) + mine[:BLK] + mine[BLK:]).astype(jnp.bfloat16)


def dq_kernel(place_ref, own_ref, q_ref, do_ref, qx_ref, dox_ref, c_ref, a_ref, b_ref, *refs, blocks, n):
    k_refs, v_refs, (dq_ref, ks, vs, acc) = refs[:n], refs[n:2 * n], refs[2 * n:]
    s, pair = pl.program_id(0), pl.program_id(1)

    @pl.when((s == 0) & (pair == 0))
    def _():
        ks[:, 128:256] = jnp.ones((blocks * BLK, 128), jnp.bfloat16)
        vs[:, 128:256] = jnp.ones((blocks * BLK, 128), jnp.bfloat16)

    place_rows(place_ref, s, k_refs, ks)
    place_rows(place_ref, s, v_refs, vs)
    mine = own_lanes(pair)
    for w in range(2):
        rows = slice(w * BLK, (w + 1) * BLK)
        pos = own_ref[s, w]
        last = pos // CB

        def extend(tile, ext):
            both = jnp.concatenate([ext, ext], axis=0)
            return jnp.concatenate([split_heads(tile), jnp.where(mine, both, jnp.zeros_like(both))], axis=1)

        qs = extend(q_ref[0, rows, :] * jnp.bfloat16(SCALE), qx_ref[0, rows, :])
        dos = extend(do_ref[0, rows, :], dox_ref[0, rows, :])
        acc[...] = jnp.zeros_like(acc)

        def step(c, mask):
            at = pl.multiple_of(c * CH, CH)
            p = jnp.exp(nt(qs, ks[pl.ds(at, CH), :]))
            if mask is not None:
                p = jnp.where(mask, p, 0.0)
            ds = (p * nt(dos, vs[pl.ds(at, CH), :])).astype(jnp.bfloat16)
            acc[...] += nn(ds, ks[pl.ds(at, CH), 0:128])

        def body(c, carry):
            step(c, None)
            return carry

        lax.fori_loop(0, last, body, 0)
        qpos = pos * BLK + row_of((2 * BLK, CH)) % BLK
        kpos = last * CH + lane_of((2 * BLK, CH))
        step(last, kpos <= qpos)
        grad = join_heads(acc[...]) * SCALE
        dq_ref[0, rows, :] = turn(grad, c_ref[rows], a_ref[rows], b_ref[rows], -1.0).astype(jnp.bfloat16)


def dkv_kernel(place_ref, own_ref, k_ref, v_ref, c_ref, a_ref, b_ref, *refs, blocks, n):
    q_refs, do_refs, qx_refs, dox_refs = (refs[i * n:(i + 1) * n] for i in range(4))
    dk_ref, dv_ref, qs, dos, acck, accv = refs[4 * n:]
    s, pair = pl.program_id(0), pl.program_id(1)
    place_rows(place_ref, s, q_refs, qs)
    place_rows(place_ref, s, do_refs, dos)

    @pl.when(pair == 0)
    def _():
        place_rows(place_ref, s, qx_refs, qs, 128)
        place_rows(place_ref, s, dox_refs, dos, 128)

    ones = own_lanes(pair).astype(jnp.bfloat16)
    for w in range(2):
        rows = slice(w * BLK, (w + 1) * BLK)
        pos = own_ref[s, w]
        first = pos // CB
        kw = jnp.concatenate([split_heads(k_ref[0, 0, rows, :] * jnp.bfloat16(SCALE)), ones], axis=1)
        vw = jnp.concatenate([split_heads(v_ref[0, 0, rows, :]), ones], axis=1)
        acck[...] = jnp.zeros_like(acck)
        accv[...] = jnp.zeros_like(accv)

        def step(c, mask):
            at = pl.multiple_of(c * CH, CH)
            p = jnp.exp(nt(kw, qs[pl.ds(at, CH), :]))
            if mask is not None:
                p = jnp.where(mask, p, 0.0)
            accv[...] += nn(p.astype(jnp.bfloat16), dos[pl.ds(at, CH), 0:128])
            ds = (p * nt(vw, dos[pl.ds(at, CH), :])).astype(jnp.bfloat16)
            acck[...] += nn(ds, qs[pl.ds(at, CH), 0:128])

        def body(c, carry):
            step(c, None)
            return carry

        kpos = pos * BLK + row_of((2 * BLK, CH)) % BLK
        qpos = first * CH + lane_of((2 * BLK, CH))
        step(first, kpos <= qpos)
        lax.fori_loop(first + 1, blocks // CB, body, 0)
        grad = join_heads(acck[...]) * SCALE
        dk_ref[0, rows, :] = turn(grad, c_ref[rows], a_ref[rows], b_ref[rows], -1.0).astype(jnp.bfloat16)
        dv_ref[0, rows, :] = join_heads(accv[...]).astype(jnp.bfloat16)


OWN = pl.BlockSpec((1, 2 * BLK, 128), lambda s, h, *_: (s, 0, h))
EXT = pl.BlockSpec((1, 2 * BLK, 128), lambda s, h, *_: (s, 0, 0))
TABLE = pl.BlockSpec((2 * BLK, 128), lambda s, h, *_: (s, 0))


def piece(x, first=0, lane=None):
    count = x.shape[0] if first is None else 1
    lead = 0 if first is None else first
    if lane is None:
        return pl.BlockSpec((count, 1, 2, BLK, 128), lambda s, h, *_: (lead, s, 0, 0, h))
    return pl.BlockSpec((count, 1, 2, BLK, 128), lambda s, h, *_: (lead, s, 0, 0, lane))


def attention_call(kernel, name, mats, seqs, pairs, blocks, in_specs, out_specs, out_shape, scratch, args):
    work = seqs * pairs * 2 * 2 * BLK * blocks * BLK // 2
    return pl.pallas_call(
        kernel,
        grid_spec=pltpu.PrefetchScalarGridSpec(
            num_scalar_prefetch=2, grid=(seqs, pairs), in_specs=in_specs, out_specs=out_specs, scratch_shapes=scratch),
        out_shape=out_shape,
        compiler_params=pltpu.CompilerParams(vmem_limit_bytes=40 * 2**20),
        cost_estimate=pl.CostEstimate(flops=work * 512 * mats, bytes_accessed=4 * seqs * pairs * blocks * BLK * 128, transcendentals=work),
        name=name,
    )(*args)


def rows_of(blocks, lanes):
    return pltpu.VMEM((blocks * BLK, lanes), jnp.bfloat16)


def acc_of(lanes):
    return pltpu.VMEM((2 * BLK, lanes), jnp.float32)


def attend(place, own, q, keys, values):
    seqs, pairs, blocks = q.shape[0], q.shape[2] // 128, place.shape[1]
    return attention_call(
        functools.partial(fwd_kernel, blocks=blocks, n=len(keys)), "attend", 2, seqs, pairs, blocks,
        [OWN] + [piece(*e) for e in keys + values], [OWN, EXT],
        [jax.ShapeDtypeStruct(q.shape, jnp.bfloat16), jax.ShapeDtypeStruct(q.shape[:2] + (128,), jnp.bfloat16)],
        [rows_of(blocks, 128), rows_of(blocks, 256), pltpu.VMEM((blocks // CB, 2 * BLK, CH), jnp.float32), acc_of(256)],
        [place, own, q] + [e[0] for e in keys + values])


def query_grad(place, own, q, do, q_ext, do_ext, tabs, keys, values):
    seqs, pairs, blocks = q.shape[0], q.shape[2] // 128, place.shape[1]
    return attention_call(
        functools.partial(dq_kernel, blocks=blocks, n=len(keys)), "query_grad", 3, seqs, pairs, blocks,
        [OWN, OWN, EXT, EXT, TABLE, TABLE, TABLE] + [piece(*e) for e in keys + values], OWN,
        jax.ShapeDtypeStruct(q.shape, jnp.bfloat16),
        [rows_of(blocks, 256), rows_of(blocks, 256), acc_of(128)],
        [place, own, q, do, q_ext, do_ext, *tabs] + [e[0] for e in keys + values])


def key_value_grad(place, own, kv, tabs, queries, grads):
    seqs, pairs, blocks = kv.shape[1], kv.shape[3] // 128, place.shape[1]
    shape = kv.shape[1:]

    def own_part(i):
        return pl.BlockSpec((1, 1, 2 * BLK, 128), lambda s, h, *_: (i, s, 0, h))

    return attention_call(
        functools.partial(dkv_kernel, blocks=blocks, n=len(queries)), "key_value_grad", 4, seqs, pairs, blocks,
        [own_part(0), own_part(1), TABLE, TABLE, TABLE] + [piece(*e) for e in queries + grads]
        + [piece(*e, lane=pairs) for e in queries + grads], [OWN, OWN],
        [jax.ShapeDtypeStruct(shape, jnp.bfloat16)] * 2,
        [rows_of(blocks, 256), rows_of(blocks, 256), acc_of(128), acc_of(128)],
        [place, own, kv, kv, *tabs] + [e[0] for e in queries + grads] * 2)


import math
from jax.sharding import PartitionSpec as P

HEAD_DIM = 64
ROT = 16
SEQS = 4
EPS = 1e-05
F32 = jnp.float32
BF16 = jnp.bfloat16


def rc(left, right):
    return lax.dot_general(left, right, (((0,), (0,)), ((), ())), preferred_element_type=F32)


def layer_stats(values, gain, shift):
    mean = jnp.mean(values, axis=-1, keepdims=True)
    centred = values - mean
    inverse = lax.rsqrt(jnp.mean(centred * centred, axis=-1, keepdims=True) + EPS)
    unit = centred * inverse
    return unit * gain + shift, unit, inverse


def layer_back(grad, unit, inverse, gain):
    scaled = grad * gain
    grad_in = inverse * (
        scaled
        - jnp.mean(scaled, axis=-1, keepdims=True)
        - unit * jnp.mean(scaled * unit, axis=-1, keepdims=True)
    )
    return grad_in, jnp.sum(grad * unit, axis=0), jnp.sum(grad, axis=0)


def rotary_tables(positions):
    half = ROT // 2
    freq = 10000.0 ** (-2.0 * jnp.arange(half, dtype=F32) / ROT)
    angles = positions.astype(F32)[:, None] * freq[None, :]
    cos, sin = jnp.cos(angles), jnp.sin(angles)
    rows = positions.shape[0]
    one, none = jnp.ones((rows, HEAD_DIM - ROT), F32), jnp.zeros((rows, HEAD_DIM - ROT), F32)
    zero = jnp.zeros_like(sin)
    ctab = jnp.concatenate([cos, cos, one] * 2, axis=1)
    above = jnp.concatenate([sin, zero, none] * 2, axis=1)
    below = jnp.concatenate([zero, sin, none] * 2, axis=1)
    return ctab, above, below


def turn(x, ctab, above, below, sign):
    up = pltpu.roll(x, 128 - ROT // 2, axis=1)
    down = pltpu.roll(x, ROT // 2, axis=1)
    return x * ctab + sign * (down * below - up * above)


def project_kernel(h_ref, wq_ref, wk_ref, wv_ref, bias_ref, c_ref, a_ref, b_ref, q_ref, kv_ref):
    h = h_ref[...]
    width = wq_ref.shape[1]
    tabs = c_ref[...], a_ref[...], b_ref[...]
    for at, (w_ref, out) in enumerate(((wq_ref, q_ref.at[0]), (wk_ref, kv_ref.at[0, 0]), (wv_ref, kv_ref.at[1, 0]))):
        lin = nn(h, w_ref[...]) + bias_ref[at:at + 1, :]
        for p in range(width // 128):
            part = lin[:, p * 128:(p + 1) * 128]
            if at < 2:
                part = turn(part, *tabs, 1.0)
            out[:, p * 128:(p + 1) * 128] = part.astype(BF16)


def project(rows, wq, wk, wv, bias, tabs):
    total, depth = rows.shape
    width = wq.shape[1]
    step = total // SEQS
    weight = pl.BlockSpec((depth, width), lambda i: (0, 0))
    table = pl.BlockSpec((step, 128), lambda i: (i, 0))
    return pl.pallas_call(
        project_kernel,
        grid=(SEQS,),
        in_specs=[pl.BlockSpec((step, depth), lambda i: (i, 0)), weight, weight, weight,
                  pl.BlockSpec((3, width), lambda i: (0, 0)), table, table, table],
        out_specs=[pl.BlockSpec((1, step, width), lambda i: (i, 0, 0)),
                   pl.BlockSpec((2, 1, step, width), lambda i: (0, i, 0, 0))],
        out_shape=[jax.ShapeDtypeStruct((SEQS, step, width), BF16), jax.ShapeDtypeStruct((2, SEQS, step, width), BF16)],
        compiler_params=pltpu.CompilerParams(vmem_limit_bytes=48 * 2**20),
        cost_estimate=pl.CostEstimate(flops=6 * total * depth * width, bytes_accessed=6 * depth * width, transcendentals=0),
        name="project",
    )(rows, wq, wk, wv, bias, *tabs)


def mlp_kernel(h_ref, dy_ref, gate_ref, up_ref, down_ref, act_ref, *grad_refs):
    width = gate_ref.shape[1]
    gate = nn(h_ref[...], gate_ref[...])
    up = nn(h_ref[...], up_ref[...])
    grad = nt(dy_ref[...], down_ref[...])
    sig = 1.0 / (1.0 + jnp.exp(-gate))
    silu = gate * sig
    act_ref[...] = (silu * up).astype(BF16)
    outs = grad_refs if len(grad_refs) == 2 else (grad_refs[0].at[:, :width], grad_refs[0].at[:, width:])
    outs[0][...] = (grad * up * (sig + silu * (1.0 - sig))).astype(BF16)
    outs[1][...] = (grad * silu).astype(BF16)


def mlp(rows, dy, gate_w, up_w, down_w, step=256):
    total, depth = rows.shape
    width = gate_w.shape[1]
    joined = width % 128 == 0
    block = pl.BlockSpec((step, depth), lambda i: (i, 0))

    def whole(x):
        return pl.BlockSpec(x.shape, lambda i: (0, 0), pipeline_mode=pl.Buffered(1))

    def out(n):
        return pl.BlockSpec((step, n), lambda i: (i, 0)), jax.ShapeDtypeStruct((total, n), BF16)

    outs = [out(width), out(2 * width)] if joined else [out(width)] * 3
    act, *grads = pl.pallas_call(
        mlp_kernel,
        grid=(total // step,),
        in_specs=[block, block, whole(gate_w), whole(up_w), whole(down_w)],
        out_specs=[o[0] for o in outs],
        out_shape=[o[1] for o in outs],
        compiler_params=pltpu.CompilerParams(vmem_limit_bytes=56 * 2**20),
        cost_estimate=pl.CostEstimate(flops=6 * total * depth * width, bytes_accessed=6 * depth * width + 10 * total * depth,
                                      transcendentals=total * width),
        name="mlp",
    )(rows, dy, gate_w, up_w, down_w)
    return act, grads[0] if joined else jnp.concatenate(grads, axis=1)


def ctx_swap(x, mask):
    n = lax.axis_size("ctx")
    return lax.ppermute(x, "ctx", [(i, i ^ mask) for i in range(n)])


def add16(a, b):
    return (a.astype(F32) + b.astype(F32)).astype(BF16)


def after(x, *deps):
    return lax.optimization_barrier((x, deps))[0]


def half_of(x, bit, mine):
    side = (lax.axis_index("ctx") >> bit) & 1
    r = x.shape[0] // 2
    return lax.dynamic_slice_in_dim(x, (side if mine else 1 - side) * r, r, 0)


def weight_grad(left, right, split_left):
    core = lax.axis_index("ctx") & 1
    split = left if split_left else right
    w = split.shape[1] // 2

    def part(which):
        cut = lax.dynamic_slice_in_dim(split, which * w, w, 1)
        return rc(cut, right) if split_left else rc(left, cut)

    got = ctx_swap(part(1 - core).astype(BF16), 1)
    gate = yield [got]
    half = (part(core) + after(got, gate).astype(F32)).astype(BF16)
    bits = list(range(1, int(math.log2(lax.axis_size("ctx")))))
    orders = [bits, bits[::-1]]
    r = half.shape[0] // 2
    streams = [half[:r], half[r:]]
    yield streams
    for i in range(len(bits)):
        got = [ctx_swap(half_of(x, o[i], False), 1 << o[i]) for x, o in zip(streams, orders)]
        gate = yield got
        streams, got = after((streams, got), gate)
        streams = [add16(half_of(x, o[i], True), g) for x, o, g in zip(streams, orders, got)]
        yield streams
    for i in reversed(range(len(bits))):
        got = [ctx_swap(x, 1 << o[i]) for x, o in zip(streams, orders)]
        gate = yield got
        streams, got = after((streams, got), gate)
        streams = [
            jnp.where(((lax.axis_index("ctx") >> o[i]) & 1) == 0, jnp.concatenate([x, g]), jnp.concatenate([g, x]))
            for x, o, g in zip(streams, orders, got)
        ]
        if i == 0:
            streams = jnp.concatenate(streams)
        yield streams
    other = ctx_swap(streams, 1)
    gate = yield [other]
    yield after((streams, other), gate)


def advance(chain, gate=None):
    held = chain.send(gate)
    next(chain)
    return held


def begin(*args):
    chain = weight_grad(*args)
    next(chain)
    return chain


def finish(chain, gate=None):
    return chain.send(gate)


def unpack_rows_kernel(core_ref, half_ref, other_ref, *out_refs):
    def put(src):
        at = 0
        for out in out_refs:
            out[...] = src[:, at:at + out.shape[1]].astype(F32)
            at += out.shape[1]

    @pl.when(pl.program_id(0) == core_ref[0])
    def _():
        put(half_ref)

    @pl.when(pl.program_id(0) != core_ref[0])
    def _():
        put(other_ref)


def unpack_rows(half, other, parts):
    r, c = half.shape
    step = math.gcd(r, 256)
    blocks = r // step
    core = lax.axis_index("ctx") & 1

    def mine(i, j, core_ref):
        return jnp.where(i == core_ref[0], j, jnp.where(core_ref[0] == 0, blocks - 1, 0)), 0

    def theirs(i, j, core_ref):
        return jnp.where(i != core_ref[0], j, jnp.where(core_ref[0] == 1, blocks - 1, 0)), 0

    return pl.pallas_call(
        unpack_rows_kernel,
        grid_spec=pltpu.PrefetchScalarGridSpec(
            num_scalar_prefetch=1, grid=(2, blocks),
            in_specs=[pl.BlockSpec((step, c), mine), pl.BlockSpec((step, c), theirs)],
            out_specs=[pl.BlockSpec((step, c // parts), lambda i, j, _: (i * blocks + j, 0))] * parts),
        out_shape=[jax.ShapeDtypeStruct((2 * r, c // parts), F32)] * parts,
        compiler_params=pltpu.CompilerParams(vmem_limit_bytes=40 * 2**20),
        cost_estimate=pl.CostEstimate(flops=0, bytes_accessed=12 * r * c, transcendentals=0),
        name="unpack_rows",
    )(core[None], half, other)


def unpack_cols_kernel(core_ref, half_ref, other_ref, out_ref):
    c = half_ref.shape[1]
    core = core_ref[0]
    out_ref[:, pl.ds(pl.multiple_of(core * c, 128), c)] = half_ref[...].astype(F32)
    out_ref[:, pl.ds(pl.multiple_of((1 - core) * c, 128), c)] = other_ref[...].astype(F32)


def unpack_cols(half, other):
    r, c = half.shape
    step = math.gcd(r, 256)
    block = pl.BlockSpec((step, c), lambda i, _: (i, 0))
    return pl.pallas_call(
        unpack_cols_kernel,
        grid_spec=pltpu.PrefetchScalarGridSpec(
            num_scalar_prefetch=1, grid=(r // step,), in_specs=[block, block],
            out_specs=pl.BlockSpec((step, 2 * c), lambda i, _: (i, 0))),
        out_shape=jax.ShapeDtypeStruct((r, 2 * c), F32),
        compiler_params=pltpu.CompilerParams(vmem_limit_bytes=40 * 2**20),
        cost_estimate=pl.CostEstimate(flops=0, bytes_accessed=12 * r * c, transcendentals=0),
        name="unpack_cols",
    )((lax.axis_index("ctx") & 1)[None], half, other)


def all_rows(x):
    return lax.all_gather(x, "tp", axis=0, tiled=True)


def sum_rows(x):
    return lax.psum_scatter(x, "tp", scatter_dimension=0, tiled=True).astype(F32)


def gather_pair(kv):
    n = lax.axis_size("ctx")
    held = {0: ((kv, 0), (kv, 1))}
    for bit in range(1, int(math.log2(n))):
        mask = 1 << bit
        for j in list(held):
            if j == 0:
                got = ctx_swap(kv, mask)
                held[mask] = (got, 0), (got, 1)
            elif mask == 4 and j == 2:
                held[6] = (ctx_swap(held[2][0][0][0:1], 4), 0), (ctx_swap(held[4][1][0][1:2], 2), 0)
            else:
                (k, i), (v, t) = held[j]
                if k is v:
                    got = ctx_swap(k, mask)
                    held[j | mask] = (got, i), (got, t)
                else:
                    held[j | mask] = (ctx_swap(k, mask), i), (ctx_swap(v, mask), t)
    for j in list(held):
        (k, i), (v, t) = held[j]
        got = ctx_swap(k, 1)
        held[j | 1] = (got, i), (got if k is v else ctx_swap(v, 1), t)
    return [held[j][0] for j in range(n)], [held[j][1] for j in range(n)]


def gather_ctx(x):
    n = lax.axis_size("ctx")
    held = [x] + [None] * (n - 1)
    for j in range(2, n, 2):
        held[j] = ctx_swap(x, j)
    for j in range(0, n, 2):
        held[j + 1] = ctx_swap(held[j], 1)
    return held


def local(tokens, cotangent, block_order, gain_one, shift_one, query_w, key_w, value_w, query_b, key_b, value_b,
          output_w, gain_two, shift_two, gate_w, up_w, down_w):
    heads = key_b.shape[0]
    width = heads * HEAD_DIM
    n_ctx, n_tp = lax.axis_size("ctx"), lax.axis_size("tp")
    ctx = lax.axis_index("ctx")
    own = lax.dynamic_slice_in_dim(block_order, 2 * ctx, 2, 1)
    picked = (jnp.arange(n_ctx, dtype=jnp.int32) ^ ctx)[:, None] == jnp.arange(n_ctx, dtype=jnp.int32)[None, :]
    by_ctx = block_order.reshape(SEQS, 1, n_ctx, 2)
    place = jnp.sum(jnp.where(picked[None, :, :, None], by_ctx, 0), axis=2).astype(jnp.int32).reshape(SEQS, 2 * n_ctx)
    positions = (own[:, :, None] * BLK + jnp.arange(BLK, dtype=jnp.int32)).reshape(-1)
    tabs = rotary_tables(positions)

    x = tokens.astype(F32)
    normed_one, unit_one, inverse_one = layer_stats(x, gain_one, shift_one)
    rows_one = all_rows(normed_one.astype(BF16))
    key_bias = jnp.concatenate([key_b, jnp.zeros((heads, HEAD_DIM - ROT), F32)], axis=1).reshape(-1)
    bias = jnp.stack([query_b, key_bias, value_b])
    q, kv = project(rows_one, query_w, key_w, value_w, bias, tabs)
    keys, values = gather_pair(kv.reshape(2, SEQS, 2, BLK, width))
    arrived = [e[0] for e in keys + values]

    rows_w = output_w.shape[0] // n_ctx
    part = lax.dynamic_slice_in_dim(output_w, ctx * rows_w, rows_w, 0)
    part = lax.all_gather(after(part, rows_one), "tp", axis=0)
    dy_rows = all_rows(after(cotangent, kv))
    whole_w = lax.all_gather(after(part, dy_rows, arrived), "ctx", axis=1).reshape(n_tp * output_w.shape[0], -1)

    attn, q_ext = attend(place, own, q, keys, values)
    attn_rows = attn.reshape(-1, width)
    attn_own = lax.all_to_all(attn_rows, "tp", split_axis=0, concat_axis=1, tiled=True)
    mixed = x + nn(attn_own, whole_w)
    normed_two, unit_two, inverse_two = layer_stats(mixed, gain_two, shift_two)
    rows_two = all_rows(after(normed_two.astype(BF16), dy_rows, whole_w))
    shape = (1, SEQS, 2, BLK, width + 128)
    queries = gather_ctx(after(jnp.concatenate([q, q_ext], axis=2).reshape(shape), attn_own))
    rows_two = after(rows_two, queries)

    act, grad_gu = mlp(rows_two, dy_rows, gate_w, up_w, down_w)
    ff = gate_w.shape[1]
    part_two = (nt(grad_gu[:, :ff], gate_w) + nt(grad_gu[:, ff:], up_w)).astype(BF16)
    grad_two = sum_rows(part_two)
    act, rows_two, dy_rows, grad_gu = after((act, rows_two, dy_rows, grad_gu), part_two)
    extra = 2 * int(math.log2(n_ctx)) - 6
    gu = begin(rows_two, grad_gu, True)
    down = nn(act, down_w).astype(BF16)
    held = advance(gu)
    dw = begin(act, after(dy_rows, held), False)
    held = advance(dw), advance(gu)
    grad_two = after(grad_two, held, down)

    norm_two, grad_gain_two, grad_shift_two = layer_back(grad_two, unit_two, inverse_two, gain_two)
    grad_mixed = cotangent.astype(F32) + norm_two
    branch_own = grad_mixed.astype(BF16)
    grad_attn = nt(branch_own, whole_w).astype(BF16)
    grad_attn = lax.all_to_all(grad_attn, "tp", split_axis=1, concat_axis=0, tiled=True)
    branch = all_rows(after(branch_own, grad_attn))
    out_tokens = (mixed + sum_rows(after(down, branch))).astype(BF16)
    lane = jnp.arange(128)[None, :]
    ind = ((jnp.arange(width) // HEAD_DIM)[:, None] == lane // 3).astype(F32)
    delta = lax.dot_general(grad_attn.astype(F32) * attn_rows.astype(F32), ind, (((1,), (0,)), ((), ())),
                            precision=lax.Precision.HIGHEST, preferred_element_type=F32)
    do_ext = terms(-delta, lane).astype(BF16)
    held = advance(gu), advance(dw)
    grads = gather_ctx(jnp.concatenate([grad_attn, do_ext], axis=1).reshape(shape))
    grad_attn = after(grad_attn, held)
    grad_q = query_grad(place, own, q, grad_attn.reshape(q.shape), q_ext, do_ext.reshape(q_ext.shape), tabs, keys, values)
    grad_q = grad_q.reshape(-1, width)
    q_part = nt(grad_q, query_w)
    grads = after(grads, q_part)
    held = [advance(gu, grads) for _ in range(1 + extra)] + [advance(dw, grads)]
    grad_k, grad_v = key_value_grad(place, own, kv, tabs, [(x, 0) for x in queries], [(x, 0) for x in after(grads, held)])
    grad_k, grad_v = (g.reshape(-1, width) for g in (grad_k, grad_v))
    part_one = q_part + nt(grad_k, key_w) + nt(grad_v, value_w)
    part_sent = part_one.astype(BF16)
    grad_one = sum_rows(part_sent)

    rows_one, branch, grad_q, grad_k, grad_v = after((rows_one, branch, grad_q, grad_k, grad_v), part_sent)
    unit_rows = (rows_one.astype(F32) - shift_one) / gain_one
    grad_qkv = jnp.concatenate([grad_q, grad_k, grad_v], axis=1)
    bias_grad = jnp.sum(grad_qkv.astype(F32), axis=0)
    tp_row = (jnp.arange(n_tp) == lax.axis_index("tp"))[:, None]
    small = jnp.concatenate([
        jnp.sum(part_one * unit_rows, axis=0), jnp.sum(part_one, axis=0), grad_gain_two, grad_shift_two,
        jnp.where(tp_row, bias_grad[None, :], 0.0).reshape(-1)])
    qkv = begin(rows_one, grad_qkv, True)
    for _ in range(1 + extra):
        advance(dw, part_sent)
    out = begin(attn_rows, branch, False)
    held = advance(qkv)
    advance(gu, held)
    held = advance(out, held)
    small = lax.psum(after(small, held), ("ctx", "tp"))
    depth = x.shape[1]
    norms = small[:4 * depth].reshape(4, depth)
    bias_sum = jnp.sum(jnp.where(tp_row, small[4 * depth:].reshape(n_tp, -1), 0.0), axis=0)
    advance(qkv, small)
    advance(dw, small)
    grad_gate_w, grad_up_w = unpack_rows(*finish(gu), 2)
    held = advance(out), advance(qkv, (grad_gate_w, grad_up_w))
    grad_down_w = unpack_cols(*finish(dw, held))
    for _ in range(1 + extra):
        advance(out)
        advance(qkv, grad_down_w)
    advance(qkv)
    for _ in range(2):
        advance(out)
    grad_output_w = unpack_cols(*finish(out))
    grad_query_w, grad_key_w, grad_value_w = unpack_rows(*finish(qkv), 3)
    norm_one, _, _ = layer_back(grad_one, unit_one, inverse_one, gain_one)
    grad_tokens = (grad_mixed + norm_one).astype(BF16)
    return (
        out_tokens, grad_tokens, norms[0], norms[1], grad_query_w, grad_key_w, grad_value_w,
        bias_sum[:width], bias_sum[width:2 * width].reshape(heads, HEAD_DIM)[:, :ROT], bias_sum[2 * width:],
        grad_output_w, norms[2], norms[3], grad_gate_w, grad_up_w, grad_down_w,
    )


def solution(mesh):
    rows, cols, depth, flat = P(("ctx", "tp"), None), P(None, "tp"), P("tp", None), P("tp")
    in_specs = (rows, rows, P(), P(), P(), cols, cols, cols, flat, depth, flat, depth, P(), P(), cols, cols, depth)
    out_specs = (rows, rows, P(), P(), cols, cols, cols, flat, depth, flat, depth, P(), P(), cols, cols, depth)
    return jax.shard_map(local, mesh=mesh, in_specs=in_specs, out_specs=out_specs, check_vma=False)
```

```python
import functools
import jax, jax.numpy as jnp
from jax import lax
from jax.experimental import pallas as pl
from jax.experimental.pallas import tpu as pltpu

BLK = 128
CB = 4
CH = BLK * CB
NEG = -1e30
SCALE = 0.125


def nt(a, b):
    return lax.dot_general(a, b, (((1,), (1,)), ((), ())), preferred_element_type=jnp.float32)


def nn(a, b):
    return lax.dot_general(a, b, (((1,), (0,)), ((), ())), preferred_element_type=jnp.float32)


def lane_of(shape):
    return lax.broadcasted_iota(jnp.int32, shape, 1)


def row_of(shape):
    return lax.broadcasted_iota(jnp.int32, shape, 0)


def split_heads(x):
    low = lane_of(x.shape) < 64
    zero = jnp.zeros_like(x)
    return jnp.concatenate([jnp.where(low, x, zero), jnp.where(low, zero, x)], axis=0)


def join_heads(x):
    low = lane_of((BLK, 128)) < 64
    return jnp.where(low, x[:BLK], x[BLK:])


def own_lanes(pair):
    shape = (2 * BLK, 128)
    return lane_of(shape) // 3 == 2 * pair + row_of(shape) // BLK


def terms(x, lane):
    first = x.astype(jnp.bfloat16).astype(jnp.float32)
    second = (x - first).astype(jnp.bfloat16).astype(jnp.float32)
    return jnp.where(lane % 3 == 0, first, jnp.where(lane % 3 == 1, second, x - first - second))


def place_rows(place_ref, s, refs, dst_ref, lane=0):
    at = 0
    for ref in refs:
        for j in range(ref.shape[0]):
            for w in range(2):
                row = pl.multiple_of(place_ref[s, at] * BLK, BLK)
                dst_ref[pl.ds(row, BLK), lane:lane + 128] = ref[j, 0, w]
                at += 1


def fwd_kernel(place_ref, own_ref, q_ref, *refs, blocks, n):
    k_refs, v_refs, (o_ref, ext_ref, ks, vs, scr, acc) = refs[:n], refs[n:2 * n], refs[2 * n:]
    s, pair = pl.program_id(0), pl.program_id(1)

    @pl.when((s == 0) & (pair == 0))
    def _():
        vs[:, 128:256] = jnp.ones((blocks * BLK, 128), jnp.bfloat16)

    @pl.when(pair == 0)
    def _():
        ext_ref[...] = jnp.zeros_like(ext_ref)

    place_rows(place_ref, s, k_refs, ks)
    place_rows(place_ref, s, v_refs, vs)
    for w in range(2):
        rows = slice(w * BLK, (w + 1) * BLK)
        pos = own_ref[s, w]
        last = pos // CB
        qs = split_heads(q_ref[0, rows, :] * jnp.bfloat16(SCALE))

        def tiles_max(run, sc):
            for t in range(CB):
                run = jnp.maximum(run, sc[:, t * 128:(t + 1) * 128])
            return run

        def score(c, run):
            at = pl.multiple_of(c * CH, CH)
            sc = nt(qs, ks[pl.ds(at, CH), :])
            scr[c] = sc
            return tiles_max(run, sc)

        run = lax.fori_loop(0, last, score, jnp.full((2 * BLK, 128), NEG, jnp.float32))
        at = pl.multiple_of(last * CH, CH)
        sc = nt(qs, ks[pl.ds(at, CH), :])
        qpos = pos * BLK + row_of((2 * BLK, CH)) % BLK
        kpos = last * CH + lane_of((2 * BLK, CH))
        sc = jnp.where(kpos <= qpos, sc, NEG)
        scr[last] = sc
        run = tiles_max(run, sc)
        top = jnp.broadcast_to(jnp.max(run, axis=1, keepdims=True), (2 * BLK, 128))
        topc = jnp.concatenate([top] * CB, axis=1)
        acc[...] = jnp.zeros_like(acc)

        def weigh(c, carry):
            at = pl.multiple_of(c * CH, CH)
            p = jnp.exp(scr[c] - topc).astype(jnp.bfloat16)
            acc[...] += nn(p, vs[pl.ds(at, CH), :])
            return carry

        lax.fori_loop(0, last + 1, weigh, 0)
        total = acc[:, 128:256]
        o_ref[0, rows, :] = join_heads(acc[:, 0:128] / total).astype(jnp.bfloat16)
        lane = lane_of((2 * BLK, 128))
        mine = jnp.where(own_lanes(pair), terms(-(top + jnp.log(total)), lane), 0.0)
        ext_ref[0, rows, :] = (ext_ref[0, rows, :].astype(jnp.float32) + mine[:BLK] + mine[BLK:]).astype(jnp.bfloat16)


def dq_kernel(place_ref, own_ref, q_ref, do_ref, qx_ref, dox_ref, c_ref, a_ref, b_ref, *refs, blocks, n):
    k_refs, v_refs, (dq_ref, ks, vs, acc) = refs[:n], refs[n:2 * n], refs[2 * n:]
    s, pair = pl.program_id(0), pl.program_id(1)

    @pl.when((s == 0) & (pair == 0))
    def _():
        ks[:, 128:256] = jnp.ones((blocks * BLK, 128), jnp.bfloat16)
        vs[:, 128:256] = jnp.ones((blocks * BLK, 128), jnp.bfloat16)

    place_rows(place_ref, s, k_refs, ks)
    place_rows(place_ref, s, v_refs, vs)
    mine = own_lanes(pair)
    for w in range(2):
        rows = slice(w * BLK, (w + 1) * BLK)
        pos = own_ref[s, w]
        last = pos // CB

        def extend(tile, ext):
            both = jnp.concatenate([ext, ext], axis=0)
            return jnp.concatenate([split_heads(tile), jnp.where(mine, both, jnp.zeros_like(both))], axis=1)

        qs = extend(q_ref[0, rows, :] * jnp.bfloat16(SCALE), qx_ref[0, rows, :])
        dos = extend(do_ref[0, rows, :], dox_ref[0, rows, :])
        acc[...] = jnp.zeros_like(acc)

        def step(c, mask):
            at = pl.multiple_of(c * CH, CH)
            p = jnp.exp(nt(qs, ks[pl.ds(at, CH), :]))
            if mask is not None:
                p = jnp.where(mask, p, 0.0)
            ds = (p * nt(dos, vs[pl.ds(at, CH), :])).astype(jnp.bfloat16)
            acc[...] += nn(ds, ks[pl.ds(at, CH), 0:128])

        def body(c, carry):
            step(c, None)
            return carry

        lax.fori_loop(0, last, body, 0)
        qpos = pos * BLK + row_of((2 * BLK, CH)) % BLK
        kpos = last * CH + lane_of((2 * BLK, CH))
        step(last, kpos <= qpos)
        grad = join_heads(acc[...]) * SCALE
        dq_ref[0, rows, :] = turn(grad, c_ref[rows], a_ref[rows], b_ref[rows], -1.0).astype(jnp.bfloat16)


def dkv_kernel(place_ref, own_ref, k_ref, v_ref, c_ref, a_ref, b_ref, *refs, blocks, n, lead):
    q_refs, do_refs, qx_refs, dox_refs = (refs[i * n:(i + 1) * n] for i in range(4))
    dk_ref, dv_ref, qs, dos, acck, accv = refs[4 * n:]
    s, pair = pl.program_id(0) + lead, pl.program_id(1)
    place_rows(place_ref, s, q_refs, qs)
    place_rows(place_ref, s, do_refs, dos)

    @pl.when(pair == 0)
    def _():
        place_rows(place_ref, s, qx_refs, qs, 128)
        place_rows(place_ref, s, dox_refs, dos, 128)

    ones = own_lanes(pair).astype(jnp.bfloat16)
    for w in range(2):
        rows = slice(w * BLK, (w + 1) * BLK)
        pos = own_ref[s, w]
        first = pos // CB
        kw = jnp.concatenate([split_heads(k_ref[0, 0, rows, :] * jnp.bfloat16(SCALE)), ones], axis=1)
        vw = jnp.concatenate([split_heads(v_ref[0, 0, rows, :]), ones], axis=1)
        acck[...] = jnp.zeros_like(acck)
        accv[...] = jnp.zeros_like(accv)

        def step(c, mask):
            at = pl.multiple_of(c * CH, CH)
            p = jnp.exp(nt(kw, qs[pl.ds(at, CH), :]))
            if mask is not None:
                p = jnp.where(mask, p, 0.0)
            accv[...] += nn(p.astype(jnp.bfloat16), dos[pl.ds(at, CH), 0:128])
            ds = (p * nt(vw, dos[pl.ds(at, CH), :])).astype(jnp.bfloat16)
            acck[...] += nn(ds, qs[pl.ds(at, CH), 0:128])

        def body(c, carry):
            step(c, None)
            return carry

        kpos = pos * BLK + row_of((2 * BLK, CH)) % BLK
        qpos = first * CH + lane_of((2 * BLK, CH))
        step(first, kpos <= qpos)
        lax.fori_loop(first + 1, blocks // CB, body, 0)
        grad = join_heads(acck[...]) * SCALE
        dk_ref[0, rows, :] = turn(grad, c_ref[rows], a_ref[rows], b_ref[rows], -1.0).astype(jnp.bfloat16)
        dv_ref[0, rows, :] = join_heads(accv[...]).astype(jnp.bfloat16)


OWN = pl.BlockSpec((1, 2 * BLK, 128), lambda s, h, *_: (s, 0, h))
EXT = pl.BlockSpec((1, 2 * BLK, 128), lambda s, h, *_: (s, 0, 0))


def table(lead=0):
    return pl.BlockSpec((2 * BLK, 128), lambda s, h, *_: (s + lead, 0))


def piece(x, first=0, lane=None, lead=0):
    return pl.BlockSpec((1, 1, 2, BLK, 128), lambda s, h, *_: (first, s + lead, 0, 0, h if lane is None else lane))


def attention_call(kernel, name, mats, seqs, pairs, blocks, in_specs, out_specs, out_shape, scratch, args):
    work = seqs * pairs * 2 * 2 * BLK * blocks * BLK // 2
    return pl.pallas_call(
        kernel,
        grid_spec=pltpu.PrefetchScalarGridSpec(
            num_scalar_prefetch=2, grid=(seqs, pairs), in_specs=in_specs, out_specs=out_specs, scratch_shapes=scratch),
        out_shape=out_shape,
        compiler_params=pltpu.CompilerParams(vmem_limit_bytes=40 * 2**20),
        cost_estimate=pl.CostEstimate(flops=work * 512 * mats, bytes_accessed=4 * seqs * pairs * blocks * BLK * 128, transcendentals=work),
        name=name,
    )(*args)


def rows_of(blocks, lanes):
    return pltpu.VMEM((blocks * BLK, lanes), jnp.bfloat16)


def acc_of(lanes):
    return pltpu.VMEM((2 * BLK, lanes), jnp.float32)


def attend(place, own, q, keys, values):
    seqs, pairs, blocks = q.shape[0], q.shape[2] // 128, place.shape[1]
    return attention_call(
        functools.partial(fwd_kernel, blocks=blocks, n=len(keys)), "attend", 2, seqs, pairs, blocks,
        [OWN] + [piece(*e) for e in keys + values], [OWN, EXT],
        [jax.ShapeDtypeStruct(q.shape, jnp.bfloat16), jax.ShapeDtypeStruct(q.shape[:2] + (128,), jnp.bfloat16)],
        [rows_of(blocks, 128), rows_of(blocks, 256), pltpu.VMEM((blocks // CB, 2 * BLK, CH), jnp.float32), acc_of(256)],
        [place, own, q] + [e[0] for e in keys + values])


def query_grad(place, own, q, do, q_ext, do_ext, tabs, keys, values):
    seqs, pairs, blocks = q.shape[0], q.shape[2] // 128, place.shape[1]
    return attention_call(
        functools.partial(dq_kernel, blocks=blocks, n=len(keys)), "query_grad", 3, seqs, pairs, blocks,
        [OWN, OWN, EXT, EXT] + [table()] * 3 + [piece(*e) for e in keys + values], OWN,
        jax.ShapeDtypeStruct(q.shape, jnp.bfloat16),
        [rows_of(blocks, 256), rows_of(blocks, 256), acc_of(128)],
        [place, own, q, do, q_ext, do_ext, *tabs] + [e[0] for e in keys + values])


def key_value_grad(place, own, kv, tabs, queries, grads, lead, count):
    pairs, blocks = kv.shape[3] // 128, place.shape[1]
    shape = (count,) + kv.shape[2:]
    both = queries + grads

    def own_part(i):
        return pl.BlockSpec((1, 1, 2 * BLK, 128), lambda s, h, *_: (i, s + lead, 0, h))

    return attention_call(
        functools.partial(dkv_kernel, blocks=blocks, n=len(queries), lead=lead), "key_value_grad", 4, count, pairs, blocks,
        [own_part(0), own_part(1)] + [table(lead)] * 3 + [piece(x, lead=lead) for x in both]
        + [piece(x, lane=pairs, lead=lead) for x in both], [OWN, OWN],
        [jax.ShapeDtypeStruct(shape, jnp.bfloat16)] * 2,
        [rows_of(blocks, 256), rows_of(blocks, 256), acc_of(128), acc_of(128)],
        [place, own, kv, kv, *tabs] + both * 2)


import math
from jax.sharding import PartitionSpec as P

HEAD_DIM = 64
ROT = 16
SEQS = 4
EPS = 1e-05
F32 = jnp.float32
BF16 = jnp.bfloat16


def rc(left, right):
    return lax.dot_general(left, right, (((0,), (0,)), ((), ())), preferred_element_type=F32)


def layer_stats(values, gain, shift):
    mean = jnp.mean(values, axis=-1, keepdims=True)
    centred = values - mean
    inverse = lax.rsqrt(jnp.mean(centred * centred, axis=-1, keepdims=True) + EPS)
    unit = centred * inverse
    return unit * gain + shift, unit, inverse


def layer_back(grad, unit, inverse, gain):
    scaled = grad * gain
    grad_in = inverse * (
        scaled
        - jnp.mean(scaled, axis=-1, keepdims=True)
        - unit * jnp.mean(scaled * unit, axis=-1, keepdims=True)
    )
    return grad_in, jnp.sum(grad * unit, axis=0), jnp.sum(grad, axis=0)


def rotary_tables(positions):
    half = ROT // 2
    freq = 10000.0 ** (-2.0 * jnp.arange(half, dtype=F32) / ROT)
    angles = positions.astype(F32)[:, None] * freq[None, :]
    cos, sin = jnp.cos(angles), jnp.sin(angles)
    rows = positions.shape[0]
    one, none = jnp.ones((rows, HEAD_DIM - ROT), F32), jnp.zeros((rows, HEAD_DIM - ROT), F32)
    zero = jnp.zeros_like(sin)
    ctab = jnp.concatenate([cos, cos, one] * 2, axis=1)
    above = jnp.concatenate([sin, zero, none] * 2, axis=1)
    below = jnp.concatenate([zero, sin, none] * 2, axis=1)
    return ctab, above, below


def turn(x, ctab, above, below, sign):
    up = pltpu.roll(x, 128 - ROT // 2, axis=1)
    down = pltpu.roll(x, ROT // 2, axis=1)
    return x * ctab + sign * (down * below - up * above)


def project_kernel(h_ref, wq_ref, wk_ref, wv_ref, bias_ref, c_ref, a_ref, b_ref, q_ref, kv_ref):
    h = h_ref[...]
    width = wq_ref.shape[1]
    tabs = c_ref[...], a_ref[...], b_ref[...]
    for at, (w_ref, out) in enumerate(((wq_ref, q_ref.at[0]), (wk_ref, kv_ref.at[0, 0]), (wv_ref, kv_ref.at[1, 0]))):
        lin = nn(h, w_ref[...]) + bias_ref[at:at + 1, :]
        for p in range(width // 128):
            part = lin[:, p * 128:(p + 1) * 128]
            if at < 2:
                part = turn(part, *tabs, 1.0)
            out[:, p * 128:(p + 1) * 128] = part.astype(BF16)


def project(rows, wq, wk, wv, bias, tabs):
    total, depth = rows.shape
    width = wq.shape[1]
    step = total // SEQS
    weight = pl.BlockSpec((depth, width), lambda i: (0, 0))
    table = pl.BlockSpec((step, 128), lambda i: (i, 0))
    return pl.pallas_call(
        project_kernel,
        grid=(SEQS,),
        in_specs=[pl.BlockSpec((step, depth), lambda i: (i, 0)), weight, weight, weight,
                  pl.BlockSpec((3, width), lambda i: (0, 0)), table, table, table],
        out_specs=[pl.BlockSpec((1, step, width), lambda i: (i, 0, 0)),
                   pl.BlockSpec((2, 1, step, width), lambda i: (0, i, 0, 0))],
        out_shape=[jax.ShapeDtypeStruct((SEQS, step, width), BF16), jax.ShapeDtypeStruct((2, SEQS, step, width), BF16)],
        compiler_params=pltpu.CompilerParams(vmem_limit_bytes=48 * 2**20),
        cost_estimate=pl.CostEstimate(flops=6 * total * depth * width, bytes_accessed=6 * depth * width, transcendentals=0),
        name="project",
    )(rows, wq, wk, wv, bias, *tabs)


def mlp_kernel(h_ref, dy_ref, gate_ref, up_ref, down_ref, act_ref, *grad_refs):
    width = gate_ref.shape[1]
    gate = nn(h_ref[...], gate_ref[...])
    up = nn(h_ref[...], up_ref[...])
    grad = nt(dy_ref[...], down_ref[...])
    sig = 1.0 / (1.0 + jnp.exp(-gate))
    silu = gate * sig
    act_ref[...] = (silu * up).astype(BF16)
    outs = grad_refs if len(grad_refs) == 2 else (grad_refs[0].at[:, :width], grad_refs[0].at[:, width:])
    outs[0][...] = (grad * up * (sig + silu * (1.0 - sig))).astype(BF16)
    outs[1][...] = (grad * silu).astype(BF16)


def mlp(rows, dy, gate_w, up_w, down_w, step=256):
    total, depth = rows.shape
    width = gate_w.shape[1]
    joined = width % 128 == 0
    block = pl.BlockSpec((step, depth), lambda i: (i, 0))

    def whole(x):
        return pl.BlockSpec(x.shape, lambda i: (0, 0), pipeline_mode=pl.Buffered(1))

    def out(n):
        return pl.BlockSpec((step, n), lambda i: (i, 0)), jax.ShapeDtypeStruct((total, n), BF16)

    outs = [out(width), out(2 * width)] if joined else [out(width)] * 3
    act, *grads = pl.pallas_call(
        mlp_kernel,
        grid=(total // step,),
        in_specs=[block, block, whole(gate_w), whole(up_w), whole(down_w)],
        out_specs=[o[0] for o in outs],
        out_shape=[o[1] for o in outs],
        compiler_params=pltpu.CompilerParams(vmem_limit_bytes=56 * 2**20),
        cost_estimate=pl.CostEstimate(flops=6 * total * depth * width, bytes_accessed=6 * depth * width + 10 * total * depth,
                                      transcendentals=total * width),
        name="mlp",
    )(rows, dy, gate_w, up_w, down_w)
    return act, grads[0] if joined else jnp.concatenate(grads, axis=1)


def ctx_swap(x, mask):
    n = lax.axis_size("ctx")
    return lax.ppermute(x, "ctx", [(i, i ^ mask) for i in range(n)])


def add16(a, b):
    return (a.astype(F32) + b.astype(F32)).astype(BF16)


def after(x, *deps):
    return lax.optimization_barrier((x, deps))[0]


def half_of(x, bit, mine):
    side = (lax.axis_index("ctx") >> bit) & 1
    r = x.shape[0] // 2
    return lax.dynamic_slice_in_dim(x, (side if mine else 1 - side) * r, r, 0)


def weight_grad(part):
    core = lax.axis_index("ctx") & 1
    got = ctx_swap(part(1 - core).astype(BF16), 1)
    gate = yield
    half = (part(core) + after(got, gate).astype(F32)).astype(BF16)
    bits = list(range(1, int(math.log2(lax.axis_size("ctx")))))
    orders = [bits, bits[::-1]]
    r = half.shape[0] // 2
    streams = [half[:r], half[r:]]
    gate = yield streams
    for i in range(len(bits)):
        streams = after(streams, gate)
        got = [ctx_swap(half_of(x, o[i], False), 1 << o[i]) for x, o in zip(streams, orders)]
        gate = yield
        streams, got = after((streams, got), gate)
        streams = [add16(half_of(x, o[i], True), g) for x, o, g in zip(streams, orders, got)]
        gate = yield streams
    for i in reversed(range(len(bits))):
        streams = after(streams, gate)
        got = [ctx_swap(x, 1 << o[i]) for x, o in zip(streams, orders)]
        gate = yield
        streams, got = after((streams, got), gate)
        streams = [
            jnp.where(((lax.axis_index("ctx") >> o[i]) & 1) == 0, jnp.concatenate([x, g]), jnp.concatenate([g, x]))
            for x, o, g in zip(streams, orders, got)
        ]
        if i == 0:
            streams = jnp.concatenate(streams)
        gate = yield streams
    streams = after(streams, gate)
    other = ctx_swap(streams, 1)
    gate = yield
    yield after((streams, other), gate)


def begin(*args):
    chain = weight_grad(*args)
    next(chain)
    return chain


def take(chain, gate=None):
    return chain.send(gate)


def go(chain, gate=None):
    chain.send(gate)


def take_extra(chain):
    for _ in range(2 * int(math.log2(lax.axis_size("ctx"))) - 6):
        go(chain)
        take(chain)


def unpack_rows_kernel(core_ref, half_ref, other_ref, *out_refs):
    def put(src):
        at = 0
        for out in out_refs:
            out[...] = src[:, at:at + out.shape[1]].astype(F32)
            at += out.shape[1]

    @pl.when(pl.program_id(0) == core_ref[0])
    def _():
        put(half_ref)

    @pl.when(pl.program_id(0) != core_ref[0])
    def _():
        put(other_ref)


def unpack_rows(half, other, parts):
    r, c = half.shape
    step = math.gcd(r, 256)
    blocks = r // step
    core = lax.axis_index("ctx") & 1

    def mine(i, j, core_ref):
        return jnp.where(i == core_ref[0], j, jnp.where(core_ref[0] == 0, blocks - 1, 0)), 0

    def theirs(i, j, core_ref):
        return jnp.where(i != core_ref[0], j, jnp.where(core_ref[0] == 1, blocks - 1, 0)), 0

    return pl.pallas_call(
        unpack_rows_kernel,
        grid_spec=pltpu.PrefetchScalarGridSpec(
            num_scalar_prefetch=1, grid=(2, blocks),
            in_specs=[pl.BlockSpec((step, c), mine), pl.BlockSpec((step, c), theirs)],
            out_specs=[pl.BlockSpec((step, c // parts), lambda i, j, _: (i * blocks + j, 0))] * parts),
        out_shape=[jax.ShapeDtypeStruct((2 * r, c // parts), F32)] * parts,
        compiler_params=pltpu.CompilerParams(vmem_limit_bytes=40 * 2**20),
        cost_estimate=pl.CostEstimate(flops=0, bytes_accessed=12 * r * c, transcendentals=0),
        name="unpack_rows",
    )(core[None], half, other)


def columns(x, which):
    w = x.shape[1] // 2
    return lax.dynamic_slice_in_dim(x, which * w, w, 1)


def unpack_cols_kernel(core_ref, half_ref, other_ref, out_ref):
    c = half_ref.shape[1]
    core = core_ref[0]
    out_ref[:, pl.ds(pl.multiple_of(core * c, 128), c)] = half_ref[...].astype(F32)
    out_ref[:, pl.ds(pl.multiple_of((1 - core) * c, 128), c)] = other_ref[...].astype(F32)


def unpack_cols(half, other, r):
    c = half.shape[1]
    step = math.gcd(r, 256)
    block = pl.BlockSpec((step, c), lambda i, _: (i, 0))
    return pl.pallas_call(
        unpack_cols_kernel,
        grid_spec=pltpu.PrefetchScalarGridSpec(
            num_scalar_prefetch=1, grid=(r // step,), in_specs=[block, block],
            out_specs=pl.BlockSpec((step, 2 * c), lambda i, _: (i, 0))),
        out_shape=jax.ShapeDtypeStruct((r, 2 * c), F32),
        compiler_params=pltpu.CompilerParams(vmem_limit_bytes=40 * 2**20),
        cost_estimate=pl.CostEstimate(flops=0, bytes_accessed=12 * r * c, transcendentals=0),
        name="unpack_cols",
    )((lax.axis_index("ctx") & 1)[None], half, other)


def unpack_turned_kernel(core_ref, half_ref, other_ref, out_ref):
    @pl.when(pl.program_id(0) == core_ref[0])
    def _():
        out_ref[...] = half_ref[...].astype(F32).T

    @pl.when(pl.program_id(0) != core_ref[0])
    def _():
        out_ref[...] = other_ref[...].astype(F32).T


def unpack_turned(half, other, r):
    c = half.shape[1]
    step = 256
    blocks = c // step
    block = pl.BlockSpec((r, step), lambda i, j, _: (1, j))
    return pl.pallas_call(
        unpack_turned_kernel,
        grid_spec=pltpu.PrefetchScalarGridSpec(
            num_scalar_prefetch=1, grid=(2, blocks), in_specs=[block, block],
            out_specs=pl.BlockSpec((step, r), lambda i, j, _: (i * blocks + j, 0))),
        out_shape=jax.ShapeDtypeStruct((2 * c, r), F32),
        compiler_params=pltpu.CompilerParams(vmem_limit_bytes=40 * 2**20),
        cost_estimate=pl.CostEstimate(flops=0, bytes_accessed=12 * r * c, transcendentals=0),
        name="unpack_turned",
    )((lax.axis_index("ctx") & 1)[None], half, other)


def all_rows(x):
    return lax.all_gather(x, "tp", axis=0, tiled=True)


def sum_rows(x):
    return lax.psum_scatter(x, "tp", scatter_dimension=0, tiled=True).astype(F32)


def gather_pair(kv):
    n = lax.axis_size("ctx")
    held = {0: ((kv, 0), (kv, 1))}
    for bit in range(1, int(math.log2(n))):
        mask = 1 << bit
        for j in list(held):
            if j == 0:
                got = ctx_swap(kv, mask)
                held[mask] = (got, 0), (got, 1)
            elif mask == 4 and j == 2:
                held[6] = (ctx_swap(held[2][0][0][0:1], 4), 0), (ctx_swap(held[4][1][0][1:2], 2), 0)
            else:
                (k, i), (v, t) = held[j]
                if k is v:
                    got = ctx_swap(k, mask)
                    held[j | mask] = (got, i), (got, t)
                else:
                    held[j | mask] = (ctx_swap(k, mask), i), (ctx_swap(v, mask), t)
    for j in list(held):
        (k, i), (v, t) = held[j]
        got = ctx_swap(k, 1)
        held[j | 1] = (got, i), (got if k is v else ctx_swap(v, 1), t)
    return [held[j][0] for j in range(n)], [held[j][1] for j in range(n)]


def gather_other(x):
    held = {0: x, 1: ctx_swap(x, 1)}
    for j in range(2, lax.axis_size("ctx"), 2):
        held[j] = ctx_swap(x, j)
    return held


def gather_cores(held, gate=None):
    n = lax.axis_size("ctx")
    for j in range(2, n, 2):
        held[j + 1] = ctx_swap(after(held[j], gate), 1)
    return [held[j] for j in range(n)]


def sum_over_all(x):
    for axis in ("ctx", "tp"):
        n = lax.axis_size(axis)
        for bit in range(int(math.log2(n))):
            x = x + lax.ppermute(x, axis, [(i, i ^ (1 << bit)) for i in range(n)])
    return x


def local(tokens, cotangent, block_order, gain_one, shift_one, query_w, key_w, value_w, query_b, key_b, value_b,
          output_w, gain_two, shift_two, gate_w, up_w, down_w):
    heads = key_b.shape[0]
    width = heads * HEAD_DIM
    n_ctx, n_tp = lax.axis_size("ctx"), lax.axis_size("tp")
    ctx = lax.axis_index("ctx")
    own = lax.dynamic_slice_in_dim(block_order, 2 * ctx, 2, 1)
    picked = (jnp.arange(n_ctx, dtype=jnp.int32) ^ ctx)[:, None] == jnp.arange(n_ctx, dtype=jnp.int32)[None, :]
    by_ctx = block_order.reshape(SEQS, 1, n_ctx, 2)
    place = jnp.sum(jnp.where(picked[None, :, :, None], by_ctx, 0), axis=2).astype(jnp.int32).reshape(SEQS, 2 * n_ctx)
    positions = (own[:, :, None] * BLK + jnp.arange(BLK, dtype=jnp.int32)).reshape(-1)
    tabs = rotary_tables(positions)

    x = tokens.astype(F32)
    normed_one, unit_one, inverse_one = layer_stats(x, gain_one, shift_one)
    rows_one = all_rows(normed_one.astype(BF16))
    key_bias = jnp.concatenate([key_b, jnp.zeros((heads, HEAD_DIM - ROT), F32)], axis=1).reshape(-1)
    bias = jnp.stack([query_b, key_bias, value_b])
    q, kv = project(rows_one, query_w, key_w, value_w, bias, tabs)
    keys, values = gather_pair(kv.reshape(2, SEQS, 2, BLK, width))
    arrived = [e[0] for e in keys + values]

    rows_w = output_w.shape[0] // n_ctx
    part = lax.dynamic_slice_in_dim(output_w, ctx * rows_w, rows_w, 0)
    part = lax.all_gather(after(part, rows_one), "tp", axis=0)
    dy_rows = all_rows(after(cotangent, rows_one))
    whole_w = lax.all_gather(after(part, arrived), "ctx", axis=1).reshape(n_tp * output_w.shape[0], -1)

    attn, q_ext = attend(place, own, q, keys, values)
    attn_rows = attn.reshape(-1, width)
    attn_own = lax.all_to_all(attn_rows, "tp", split_axis=0, concat_axis=1, tiled=True)
    mixed = x + nn(attn_own, whole_w)
    normed_two, unit_two, inverse_two = layer_stats(mixed, gain_two, shift_two)
    rows_two = all_rows(after(normed_two.astype(BF16), dy_rows, whole_w))
    shape = (1, SEQS, 2, BLK, width + 128)
    queries = gather_cores(gather_other(after(jnp.concatenate([q, q_ext], axis=2).reshape(shape), attn_own)))
    rows_two = after(rows_two, queries)

    act, grad_gu = mlp(rows_two, dy_rows, gate_w, up_w, down_w)
    ff = gate_w.shape[1]
    part_two = (nt(grad_gu[:, :ff], gate_w) + nt(grad_gu[:, ff:], up_w)).astype(BF16)
    grad_two = sum_rows(part_two)
    act, rows_two, dy_rows, grad_gu = after((act, rows_two, dy_rows, grad_gu), part_two)
    gu = begin(lambda core: rc(columns(rows_two, core), grad_gu))
    down = nn(act, down_w).astype(BF16)
    held = take(gu)
    go(gu)
    dy_late = after(dy_rows, held)
    dw = begin(lambda core: rc(act, columns(dy_late, core)))
    take(gu)
    go(gu)
    grad_two = after(grad_two, take(gu), take(dw), down)
    go(gu)
    go(dw)

    norm_two, grad_gain_two, grad_shift_two = layer_back(grad_two, unit_two, inverse_two, gain_two)
    grad_mixed = cotangent.astype(F32) + norm_two
    branch_own = grad_mixed.astype(BF16)
    grad_attn = nt(branch_own, whole_w).astype(BF16)
    grad_attn = lax.all_to_all(grad_attn, "tp", split_axis=1, concat_axis=0, tiled=True)
    branch = all_rows(after(branch_own, grad_attn))
    out_tokens = (mixed + sum_rows(after(down, grad_attn))).astype(BF16)
    lane = jnp.arange(128)[None, :]
    ind = ((jnp.arange(width) // HEAD_DIM)[:, None] == lane // 3).astype(F32)
    delta = lax.dot_general(grad_attn.astype(F32) * attn_rows.astype(F32), ind, (((1,), (0,)), ((), ())),
                            precision=lax.Precision.HIGHEST, preferred_element_type=F32)
    do_ext = terms(-delta, lane).astype(BF16)
    do_sent = jnp.concatenate([grad_attn, do_ext], axis=1).reshape(shape)
    grads = gather_other(after(do_sent, take(gu), take(dw)))
    grad_q = query_grad(place, own, q, grad_attn.reshape(q.shape), q_ext, do_ext.reshape(q_ext.shape), tabs, keys, values)
    grad_q = grad_q.reshape(-1, width)
    q_part = nt(grad_q, query_w)
    grads = gather_cores(grads, q_part)
    go(gu, grads)
    go(dw, grads)
    rows_q, branch = after((rows_one, branch), grads)
    oq = begin(lambda core: jnp.concatenate([rc(attn_rows, columns(branch, core)), rc(grad_q, columns(rows_q, core))]))
    first = key_value_grad(place, own, kv, tabs, queries, grads, 0, SEQS // 2)
    grads = after(grads, take(gu, first), take(dw, first), take(oq, first))
    take_extra(gu)
    go(gu)
    go(dw)
    go(oq)
    second = key_value_grad(place, own, kv, tabs, queries, grads, SEQS // 2, SEQS // 2)
    grad_k, grad_v = (jnp.concatenate(pair).reshape(-1, width) for pair in zip(first, second))
    part_one = q_part + nt(grad_k, key_w) + nt(grad_v, value_w)
    part_sent = part_one.astype(BF16)
    grad_one = sum_rows(part_sent)

    rows_one, grad_q, grad_k, grad_v = after((rows_one, grad_q, grad_k, grad_v), part_sent)
    grad_kv = jnp.concatenate([grad_k, grad_v], axis=1)
    dkv = begin(lambda core: rc(columns(rows_one, core), grad_kv))
    take(dw, part_sent)
    go(dw)
    take(oq, part_sent)
    go(oq)
    unit_rows = (rows_one.astype(F32) - shift_one) / gain_one
    bias_grad = jnp.concatenate([jnp.sum(g.astype(F32), axis=0) for g in (grad_q, grad_kv)])
    tp_row = (jnp.arange(n_tp) == lax.axis_index("tp"))[:, None]
    small = jnp.concatenate([
        jnp.sum(part_one * unit_rows, axis=0), jnp.sum(part_one, axis=0), grad_gain_two, grad_shift_two,
        jnp.where(tp_row, bias_grad[None, :], 0.0).reshape(-1)])
    held = take(dkv)
    go(dkv)
    small = sum_over_all(after(small, held).reshape(-1, 1024)).reshape(-1)
    depth = x.shape[1]
    norms = small[:4 * depth].reshape(4, depth)
    bias_sum = jnp.sum(jnp.where(tp_row, small[4 * depth:].reshape(n_tp, -1), 0.0), axis=0)
    grad_gate_w, grad_up_w = unpack_rows(*take(gu, held), 2)
    held = take(dkv), take(oq), take(dw)
    go(dkv)
    go(oq)
    take_extra(dw)
    go(dw)
    held = take(dkv, (held, grad_gate_w)), take(oq, held)
    go(dkv)
    go(oq)
    grad_down_w = unpack_cols(*take(dw, held), act.shape[1])
    held = take(dkv, grad_down_w), take(oq, grad_down_w)
    take_extra(oq)
    take_extra(dkv)
    go(dkv)
    go(oq)
    halves = take(oq, held)
    grad_output_w, grad_query_w = unpack_cols(*halves, width), unpack_turned(*halves, width)
    take(dkv, held)
    go(dkv)
    grad_key_w, grad_value_w = unpack_rows(*take(dkv), 2)
    norm_one, _, _ = layer_back(grad_one, unit_one, inverse_one, gain_one)
    grad_tokens = (grad_mixed + norm_one).astype(BF16)
    return (
        out_tokens, grad_tokens, norms[0], norms[1], grad_query_w, grad_key_w, grad_value_w,
        bias_sum[:width], bias_sum[width:2 * width].reshape(heads, HEAD_DIM)[:, :ROT], bias_sum[2 * width:],
        grad_output_w, norms[2], norms[3], grad_gate_w, grad_up_w, grad_down_w,
    )


def solution(mesh):
    rows, cols, depth, flat = P(("ctx", "tp"), None), P(None, "tp"), P("tp", None), P("tp")
    in_specs = (rows, rows, P(), P(), P(), cols, cols, cols, flat, depth, flat, depth, P(), P(), cols, cols, depth)
    out_specs = (rows, rows, P(), P(), cols, cols, cols, flat, depth, flat, depth, P(), P(), cols, cols, depth)
    return jax.shard_map(local, mesh=mesh, in_specs=in_specs, out_specs=out_specs, check_vma=False)
```

```python
import functools
import jax, jax.numpy as jnp
from jax import lax
from jax.experimental import pallas as pl
from jax.experimental.pallas import tpu as pltpu

BLK = 128
CB = 4
CH = BLK * CB
NEG = -1e30
SCALE = 0.125


def nt(a, b):
    return lax.dot_general(a, b, (((1,), (1,)), ((), ())), preferred_element_type=jnp.float32)


def nn(a, b):
    return lax.dot_general(a, b, (((1,), (0,)), ((), ())), preferred_element_type=jnp.float32)


def lane_of(shape):
    return lax.broadcasted_iota(jnp.int32, shape, 1)


def row_of(shape):
    return lax.broadcasted_iota(jnp.int32, shape, 0)


def split_heads(x):
    low = lane_of(x.shape) < 64
    zero = jnp.zeros_like(x)
    return jnp.concatenate([jnp.where(low, x, zero), jnp.where(low, zero, x)], axis=0)


def join_heads(x):
    low = lane_of((BLK, 128)) < 64
    return jnp.where(low, x[:BLK], x[BLK:])


def own_lanes(pair):
    shape = (2 * BLK, 128)
    return lane_of(shape) // 3 == 2 * pair + row_of(shape) // BLK


def terms(x, lane):
    first = x.astype(jnp.bfloat16).astype(jnp.float32)
    second = (x - first).astype(jnp.bfloat16).astype(jnp.float32)
    return jnp.where(lane % 3 == 0, first, jnp.where(lane % 3 == 1, second, x - first - second))


def place_rows(place_ref, s, refs, dst_ref, lane=0):
    at = 0
    for ref in refs:
        for j in range(ref.shape[0]):
            for w in range(2):
                row = pl.multiple_of(place_ref[s, at] * BLK, BLK)
                dst_ref[pl.ds(row, BLK), lane:lane + 128] = ref[j, 0, w]
                at += 1


def fwd_kernel(place_ref, own_ref, q_ref, *refs, blocks, n):
    k_refs, v_refs, (o_ref, ext_ref, ks, vs, scr, acc) = refs[:n], refs[n:2 * n], refs[2 * n:]
    s, pair = pl.program_id(0), pl.program_id(1)

    @pl.when((s == 0) & (pair == 0))
    def _():
        vs[:, 128:256] = jnp.ones((blocks * BLK, 128), jnp.bfloat16)

    @pl.when(pair == 0)
    def _():
        ext_ref[...] = jnp.zeros_like(ext_ref)

    place_rows(place_ref, s, k_refs, ks)
    place_rows(place_ref, s, v_refs, vs)
    for w in range(2):
        rows = slice(w * BLK, (w + 1) * BLK)
        pos = own_ref[s, w]
        last = pos // CB
        qs = split_heads(q_ref[0, rows, :] * jnp.bfloat16(SCALE))

        def tiles_max(run, sc):
            for t in range(CB):
                run = jnp.maximum(run, sc[:, t * 128:(t + 1) * 128])
            return run

        def score(c, run):
            at = pl.multiple_of(c * CH, CH)
            sc = nt(qs, ks[pl.ds(at, CH), :])
            scr[c] = sc
            return tiles_max(run, sc)

        run = lax.fori_loop(0, last, score, jnp.full((2 * BLK, 128), NEG, jnp.float32))
        at = pl.multiple_of(last * CH, CH)
        sc = nt(qs, ks[pl.ds(at, CH), :])
        qpos = pos * BLK + row_of((2 * BLK, CH)) % BLK
        kpos = last * CH + lane_of((2 * BLK, CH))
        sc = jnp.where(kpos <= qpos, sc, NEG)
        scr[last] = sc
        run = tiles_max(run, sc)
        top = jnp.broadcast_to(jnp.max(run, axis=1, keepdims=True), (2 * BLK, 128))
        topc = jnp.concatenate([top] * CB, axis=1)
        acc[...] = jnp.zeros_like(acc)

        def weigh(c, carry):
            at = pl.multiple_of(c * CH, CH)
            p = jnp.exp(scr[c] - topc).astype(jnp.bfloat16)
            acc[...] += nn(p, vs[pl.ds(at, CH), :])
            return carry

        lax.fori_loop(0, last + 1, weigh, 0)
        total = acc[:, 128:256]
        o_ref[0, rows, :] = join_heads(acc[:, 0:128] / total).astype(jnp.bfloat16)
        lane = lane_of((2 * BLK, 128))
        mine = jnp.where(own_lanes(pair), terms(-(top + jnp.log(total)), lane), 0.0)
        ext_ref[0, rows, :] = (ext_ref[0, rows, :].astype(jnp.float32) + mine[:BLK] + mine[BLK:]).astype(jnp.bfloat16)


def dq_kernel(place_ref, own_ref, q_ref, do_ref, qx_ref, dox_ref, c_ref, a_ref, b_ref, *refs, blocks, n):
    k_refs, v_refs, (dq_ref, ks, vs, acc) = refs[:n], refs[n:2 * n], refs[2 * n:]
    s, pair = pl.program_id(0), pl.program_id(1)

    @pl.when((s == 0) & (pair == 0))
    def _():
        ks[:, 128:256] = jnp.ones((blocks * BLK, 128), jnp.bfloat16)
        vs[:, 128:256] = jnp.ones((blocks * BLK, 128), jnp.bfloat16)

    place_rows(place_ref, s, k_refs, ks)
    place_rows(place_ref, s, v_refs, vs)
    mine = own_lanes(pair)
    for w in range(2):
        rows = slice(w * BLK, (w + 1) * BLK)
        pos = own_ref[s, w]
        last = pos // CB

        def extend(tile, ext):
            both = jnp.concatenate([ext, ext], axis=0)
            return jnp.concatenate([split_heads(tile), jnp.where(mine, both, jnp.zeros_like(both))], axis=1)

        qs = extend(q_ref[0, rows, :] * jnp.bfloat16(SCALE), qx_ref[0, rows, :])
        dos = extend(do_ref[0, rows, :], dox_ref[0, rows, :])
        acc[...] = jnp.zeros_like(acc)

        def step(c, mask):
            at = pl.multiple_of(c * CH, CH)
            p = jnp.exp(nt(qs, ks[pl.ds(at, CH), :]))
            if mask is not None:
                p = jnp.where(mask, p, 0.0)
            ds = (p * nt(dos, vs[pl.ds(at, CH), :])).astype(jnp.bfloat16)
            acc[...] += nn(ds, ks[pl.ds(at, CH), 0:128])

        def body(c, carry):
            step(c, None)
            return carry

        lax.fori_loop(0, last, body, 0)
        qpos = pos * BLK + row_of((2 * BLK, CH)) % BLK
        kpos = last * CH + lane_of((2 * BLK, CH))
        step(last, kpos <= qpos)
        grad = join_heads(acc[...]) * SCALE
        dq_ref[0, rows, :] = turn(grad, c_ref[rows], a_ref[rows], b_ref[rows], -1.0).astype(jnp.bfloat16)


def dkv_kernel(place_ref, own_ref, k_ref, v_ref, c_ref, a_ref, b_ref, *refs, blocks, n, lead):
    q_refs, do_refs, qx_refs, dox_refs = (refs[i * n:(i + 1) * n] for i in range(4))
    dk_ref, dv_ref, qs, dos, acck, accv = refs[4 * n:]
    s, pair = pl.program_id(0) + lead, pl.program_id(1)
    place_rows(place_ref, s, q_refs, qs)
    place_rows(place_ref, s, do_refs, dos)

    @pl.when(pair == 0)
    def _():
        place_rows(place_ref, s, qx_refs, qs, 128)
        place_rows(place_ref, s, dox_refs, dos, 128)

    ones = own_lanes(pair).astype(jnp.bfloat16)
    for w in range(2):
        rows = slice(w * BLK, (w + 1) * BLK)
        pos = own_ref[s, w]
        first = pos // CB
        kw = jnp.concatenate([split_heads(k_ref[0, 0, rows, :] * jnp.bfloat16(SCALE)), ones], axis=1)
        vw = jnp.concatenate([split_heads(v_ref[0, 0, rows, :]), ones], axis=1)
        acck[...] = jnp.zeros_like(acck)
        accv[...] = jnp.zeros_like(accv)

        def step(c, mask):
            at = pl.multiple_of(c * CH, CH)
            p = jnp.exp(nt(kw, qs[pl.ds(at, CH), :]))
            if mask is not None:
                p = jnp.where(mask, p, 0.0)
            accv[...] += nn(p.astype(jnp.bfloat16), dos[pl.ds(at, CH), 0:128])
            ds = (p * nt(vw, dos[pl.ds(at, CH), :])).astype(jnp.bfloat16)
            acck[...] += nn(ds, qs[pl.ds(at, CH), 0:128])

        def body(c, carry):
            step(c, None)
            return carry

        kpos = pos * BLK + row_of((2 * BLK, CH)) % BLK
        qpos = first * CH + lane_of((2 * BLK, CH))
        step(first, kpos <= qpos)
        lax.fori_loop(first + 1, blocks // CB, body, 0)
        grad = join_heads(acck[...]) * SCALE
        dk_ref[0, rows, :] = turn(grad, c_ref[rows], a_ref[rows], b_ref[rows], -1.0).astype(jnp.bfloat16)
        dv_ref[0, rows, :] = join_heads(accv[...]).astype(jnp.bfloat16)


OWN = pl.BlockSpec((1, 2 * BLK, 128), lambda s, h, *_: (s, 0, h))
EXT = pl.BlockSpec((1, 2 * BLK, 128), lambda s, h, *_: (s, 0, 0))


def table(lead=0):
    return pl.BlockSpec((2 * BLK, 128), lambda s, h, *_: (s + lead, 0))


def piece(x, first=0, lane=None, lead=0):
    return pl.BlockSpec((1, 1, 2, BLK, 128), lambda s, h, *_: (first, s + lead, 0, 0, h if lane is None else lane))


def attention_call(kernel, name, mats, seqs, pairs, blocks, in_specs, out_specs, out_shape, scratch, args):
    work = seqs * pairs * 2 * 2 * BLK * blocks * BLK // 2
    return pl.pallas_call(
        kernel,
        grid_spec=pltpu.PrefetchScalarGridSpec(
            num_scalar_prefetch=2, grid=(seqs, pairs), in_specs=in_specs, out_specs=out_specs, scratch_shapes=scratch),
        out_shape=out_shape,
        compiler_params=pltpu.CompilerParams(vmem_limit_bytes=40 * 2**20),
        cost_estimate=pl.CostEstimate(flops=work * 512 * mats, bytes_accessed=4 * seqs * pairs * blocks * BLK * 128, transcendentals=work),
        name=name,
    )(*args)


def rows_of(blocks, lanes):
    return pltpu.VMEM((blocks * BLK, lanes), jnp.bfloat16)


def acc_of(lanes):
    return pltpu.VMEM((2 * BLK, lanes), jnp.float32)


def attend(place, own, q, keys, values):
    seqs, pairs, blocks = q.shape[0], q.shape[2] // 128, place.shape[1]
    return attention_call(
        functools.partial(fwd_kernel, blocks=blocks, n=len(keys)), "attend", 2, seqs, pairs, blocks,
        [OWN] + [piece(*e) for e in keys + values], [OWN, EXT],
        [jax.ShapeDtypeStruct(q.shape, jnp.bfloat16), jax.ShapeDtypeStruct(q.shape[:2] + (128,), jnp.bfloat16)],
        [rows_of(blocks, 128), rows_of(blocks, 256), pltpu.VMEM((blocks // CB, 2 * BLK, CH), jnp.float32), acc_of(256)],
        [place, own, q] + [e[0] for e in keys + values])


def query_grad(place, own, q, do, q_ext, do_ext, tabs, keys, values):
    seqs, pairs, blocks = q.shape[0], q.shape[2] // 128, place.shape[1]
    return attention_call(
        functools.partial(dq_kernel, blocks=blocks, n=len(keys)), "query_grad", 3, seqs, pairs, blocks,
        [OWN, OWN, EXT, EXT] + [table()] * 3 + [piece(*e) for e in keys + values], OWN,
        jax.ShapeDtypeStruct(q.shape, jnp.bfloat16),
        [rows_of(blocks, 256), rows_of(blocks, 256), acc_of(128)],
        [place, own, q, do, q_ext, do_ext, *tabs] + [e[0] for e in keys + values])


def key_value_grad(place, own, kv, tabs, queries, grads, lead, count):
    pairs, blocks = kv.shape[3] // 128, place.shape[1]
    shape = (count,) + kv.shape[2:]
    both = queries + grads

    def own_part(i):
        return pl.BlockSpec((1, 1, 2 * BLK, 128), lambda s, h, *_: (i, s + lead, 0, h))

    return attention_call(
        functools.partial(dkv_kernel, blocks=blocks, n=len(queries), lead=lead), "key_value_grad", 4, count, pairs, blocks,
        [own_part(0), own_part(1)] + [table(lead)] * 3 + [piece(x, lead=lead) for x in both]
        + [piece(x, lane=pairs, lead=lead) for x in both], [OWN, OWN],
        [jax.ShapeDtypeStruct(shape, jnp.bfloat16)] * 2,
        [rows_of(blocks, 256), rows_of(blocks, 256), acc_of(128), acc_of(128)],
        [place, own, kv, kv, *tabs] + both * 2)


import math
from jax.sharding import PartitionSpec as P

HEAD_DIM = 64
ROT = 16
SEQS = 4
EPS = 1e-05
F32 = jnp.float32
BF16 = jnp.bfloat16


def rc(left, right):
    return lax.dot_general(left, right, (((0,), (0,)), ((), ())), preferred_element_type=F32)


def layer_stats(values, gain, shift):
    mean = jnp.mean(values, axis=-1, keepdims=True)
    centred = values - mean
    inverse = lax.rsqrt(jnp.mean(centred * centred, axis=-1, keepdims=True) + EPS)
    unit = centred * inverse
    return unit * gain + shift, unit, inverse


def layer_back(grad, unit, inverse, gain):
    scaled = grad * gain
    grad_in = inverse * (
        scaled
        - jnp.mean(scaled, axis=-1, keepdims=True)
        - unit * jnp.mean(scaled * unit, axis=-1, keepdims=True)
    )
    return grad_in, jnp.sum(grad * unit, axis=0), jnp.sum(grad, axis=0)


def rotary_tables(positions):
    half = ROT // 2
    freq = 10000.0 ** (-2.0 * jnp.arange(half, dtype=F32) / ROT)
    angles = positions.astype(F32)[:, None] * freq[None, :]
    cos, sin = jnp.cos(angles), jnp.sin(angles)
    rows = positions.shape[0]
    one, none = jnp.ones((rows, HEAD_DIM - ROT), F32), jnp.zeros((rows, HEAD_DIM - ROT), F32)
    zero = jnp.zeros_like(sin)
    ctab = jnp.concatenate([cos, cos, one] * 2, axis=1)
    above = jnp.concatenate([sin, zero, none] * 2, axis=1)
    below = jnp.concatenate([zero, sin, none] * 2, axis=1)
    return ctab, above, below


def turn(x, ctab, above, below, sign):
    up = pltpu.roll(x, 128 - ROT // 2, axis=1)
    down = pltpu.roll(x, ROT // 2, axis=1)
    return x * ctab + sign * (down * below - up * above)


def project_kernel(h_ref, wq_ref, wk_ref, wv_ref, bias_ref, c_ref, a_ref, b_ref, q_ref, kv_ref):
    h = h_ref[...]
    width = wq_ref.shape[1]
    tabs = c_ref[...], a_ref[...], b_ref[...]
    for at, (w_ref, out) in enumerate(((wq_ref, q_ref.at[0]), (wk_ref, kv_ref.at[0, 0]), (wv_ref, kv_ref.at[1, 0]))):
        lin = nn(h, w_ref[...]) + bias_ref[at:at + 1, :]
        for p in range(width // 128):
            part = lin[:, p * 128:(p + 1) * 128]
            if at < 2:
                part = turn(part, *tabs, 1.0)
            out[:, p * 128:(p + 1) * 128] = part.astype(BF16)


def project(rows, wq, wk, wv, bias, tabs):
    total, depth = rows.shape
    width = wq.shape[1]
    step = total // SEQS
    weight = pl.BlockSpec((depth, width), lambda i: (0, 0))
    table = pl.BlockSpec((step, 128), lambda i: (i, 0))
    return pl.pallas_call(
        project_kernel,
        grid=(SEQS,),
        in_specs=[pl.BlockSpec((step, depth), lambda i: (i, 0)), weight, weight, weight,
                  pl.BlockSpec((3, width), lambda i: (0, 0)), table, table, table],
        out_specs=[pl.BlockSpec((1, step, width), lambda i: (i, 0, 0)),
                   pl.BlockSpec((2, 1, step, width), lambda i: (0, i, 0, 0))],
        out_shape=[jax.ShapeDtypeStruct((SEQS, step, width), BF16), jax.ShapeDtypeStruct((2, SEQS, step, width), BF16)],
        compiler_params=pltpu.CompilerParams(vmem_limit_bytes=48 * 2**20),
        cost_estimate=pl.CostEstimate(flops=6 * total * depth * width, bytes_accessed=6 * depth * width, transcendentals=0),
        name="project",
    )(rows, wq, wk, wv, bias, *tabs)


def mlp_kernel(h_ref, dy_ref, gate_ref, up_ref, down_ref, act_ref, *grad_refs):
    width = gate_ref.shape[1]
    gate = nn(h_ref[...], gate_ref[...])
    up = nn(h_ref[...], up_ref[...])
    grad = nt(dy_ref[...], down_ref[...])
    sig = 1.0 / (1.0 + jnp.exp(-gate))
    silu = gate * sig
    act_ref[...] = (silu * up).astype(BF16)
    outs = grad_refs if len(grad_refs) == 2 else (grad_refs[0].at[:, :width], grad_refs[0].at[:, width:])
    outs[0][...] = (grad * up * (sig + silu * (1.0 - sig))).astype(BF16)
    outs[1][...] = (grad * silu).astype(BF16)


def mlp(rows, dy, gate_w, up_w, down_w, step=256):
    total, depth = rows.shape
    width = gate_w.shape[1]
    joined = width % 128 == 0
    block = pl.BlockSpec((step, depth), lambda i: (i, 0))

    def whole(x):
        return pl.BlockSpec(x.shape, lambda i: (0, 0), pipeline_mode=pl.Buffered(1))

    def out(n):
        return pl.BlockSpec((step, n), lambda i: (i, 0)), jax.ShapeDtypeStruct((total, n), BF16)

    outs = [out(width), out(2 * width)] if joined else [out(width)] * 3
    act, *grads = pl.pallas_call(
        mlp_kernel,
        grid=(total // step,),
        in_specs=[block, block, whole(gate_w), whole(up_w), whole(down_w)],
        out_specs=[o[0] for o in outs],
        out_shape=[o[1] for o in outs],
        compiler_params=pltpu.CompilerParams(vmem_limit_bytes=56 * 2**20),
        cost_estimate=pl.CostEstimate(flops=6 * total * depth * width, bytes_accessed=6 * depth * width + 10 * total * depth,
                                      transcendentals=total * width),
        name="mlp",
    )(rows, dy, gate_w, up_w, down_w)
    return act, grads[0] if joined else jnp.concatenate(grads, axis=1)


def ctx_swap(x, mask):
    n = lax.axis_size("ctx")
    return lax.ppermute(x, "ctx", [(i, i ^ mask) for i in range(n)])


def add16(a, b):
    return (a.astype(F32) + b.astype(F32)).astype(BF16)


def after(x, *deps):
    if not jax.tree.leaves(deps):
        return x
    return lax.optimization_barrier((x, deps))[0]


def half_of(x, bit, mine):
    side = (lax.axis_index("ctx") >> bit) & 1
    r = x.shape[0] // 2
    return lax.dynamic_slice_in_dim(x, (side if mine else 1 - side) * r, r, 0)


def weight_grad(part):
    core = lax.axis_index("ctx") & 1
    got = ctx_swap(part(1 - core).astype(BF16), 1)
    gate = yield
    half = (part(core) + after(got, gate).astype(F32)).astype(BF16)
    bits = list(range(1, int(math.log2(lax.axis_size("ctx")))))
    orders = [bits, bits[::-1]]
    r = half.shape[0] // 2
    streams = [half[:r], half[r:]]
    gate = yield streams
    for i in range(len(bits)):
        streams = after(streams, gate)
        got = [ctx_swap(half_of(x, o[i], False), 1 << o[i]) for x, o in zip(streams, orders)]
        gate = yield
        streams, got = after((streams, got), gate)
        streams = [add16(half_of(x, o[i], True), g) for x, o, g in zip(streams, orders, got)]
        gate = yield streams
    for i in reversed(range(len(bits))):
        streams = after(streams, gate)
        got = [ctx_swap(x, 1 << o[i]) for x, o in zip(streams, orders)]
        gate = yield
        streams, got = after((streams, got), gate)
        streams = [
            jnp.where(((lax.axis_index("ctx") >> o[i]) & 1) == 0, jnp.concatenate([x, g]), jnp.concatenate([g, x]))
            for x, o, g in zip(streams, orders, got)
        ]
        if i == 0:
            streams = jnp.concatenate(streams)
        gate = yield streams
    streams = after(streams, gate)
    other = ctx_swap(streams, 1)
    gate = yield
    yield after((streams, other), gate)


def begin(*args):
    chain = weight_grad(*args)
    next(chain)
    return chain


def take(chain, gate=None):
    return chain.send(gate)


def go(chain, gate=None):
    chain.send(gate)


def take_extra(chain):
    for _ in range(2 * int(math.log2(lax.axis_size("ctx"))) - 6):
        go(chain)
        take(chain)


def unpack_rows_kernel(core_ref, half_ref, other_ref, *out_refs):
    def put(src):
        at = 0
        for out in out_refs:
            out[...] = src[:, at:at + out.shape[1]].astype(F32)
            at += out.shape[1]

    @pl.when(pl.program_id(0) == core_ref[0])
    def _():
        put(half_ref)

    @pl.when(pl.program_id(0) != core_ref[0])
    def _():
        put(other_ref)


def unpack_rows(half, other, parts):
    r, c = half.shape
    step = math.gcd(r, 256)
    blocks = r // step
    core = lax.axis_index("ctx") & 1

    def mine(i, j, core_ref):
        return jnp.where(i == core_ref[0], j, jnp.where(core_ref[0] == 0, blocks - 1, 0)), 0

    def theirs(i, j, core_ref):
        return jnp.where(i != core_ref[0], j, jnp.where(core_ref[0] == 1, blocks - 1, 0)), 0

    return pl.pallas_call(
        unpack_rows_kernel,
        grid_spec=pltpu.PrefetchScalarGridSpec(
            num_scalar_prefetch=1, grid=(2, blocks),
            in_specs=[pl.BlockSpec((step, c), mine), pl.BlockSpec((step, c), theirs)],
            out_specs=[pl.BlockSpec((step, c // parts), lambda i, j, _: (i * blocks + j, 0))] * parts),
        out_shape=[jax.ShapeDtypeStruct((2 * r, c // parts), F32)] * parts,
        compiler_params=pltpu.CompilerParams(vmem_limit_bytes=40 * 2**20),
        cost_estimate=pl.CostEstimate(flops=0, bytes_accessed=12 * r * c, transcendentals=0),
        name="unpack_rows",
    )(core[None], half, other)


def columns(x, which):
    w = x.shape[1] // 2
    return lax.dynamic_slice_in_dim(x, which * w, w, 1)


def unpack_cols_kernel(core_ref, half_ref, other_ref, out_ref):
    c = half_ref.shape[1]
    core = core_ref[0]
    out_ref[:, pl.ds(pl.multiple_of(core * c, 128), c)] = half_ref[...].astype(F32)
    out_ref[:, pl.ds(pl.multiple_of((1 - core) * c, 128), c)] = other_ref[...].astype(F32)


def unpack_cols(half, other, r):
    c = half.shape[1]
    step = math.gcd(r, 256)
    block = pl.BlockSpec((step, c), lambda i, _: (i, 0))
    return pl.pallas_call(
        unpack_cols_kernel,
        grid_spec=pltpu.PrefetchScalarGridSpec(
            num_scalar_prefetch=1, grid=(r // step,), in_specs=[block, block],
            out_specs=pl.BlockSpec((step, 2 * c), lambda i, _: (i, 0))),
        out_shape=jax.ShapeDtypeStruct((r, 2 * c), F32),
        compiler_params=pltpu.CompilerParams(vmem_limit_bytes=40 * 2**20),
        cost_estimate=pl.CostEstimate(flops=0, bytes_accessed=12 * r * c, transcendentals=0),
        name="unpack_cols",
    )((lax.axis_index("ctx") & 1)[None], half, other)


def unpack_turned_kernel(core_ref, half_ref, other_ref, out_ref):
    @pl.when(pl.program_id(0) == core_ref[0])
    def _():
        out_ref[...] = half_ref[...].astype(F32).T

    @pl.when(pl.program_id(0) != core_ref[0])
    def _():
        out_ref[...] = other_ref[...].astype(F32).T


def unpack_turned(half, other, r):
    c = half.shape[1]
    step = 256
    blocks = c // step
    block = pl.BlockSpec((r, step), lambda i, j, _: (1, j))
    return pl.pallas_call(
        unpack_turned_kernel,
        grid_spec=pltpu.PrefetchScalarGridSpec(
            num_scalar_prefetch=1, grid=(2, blocks), in_specs=[block, block],
            out_specs=pl.BlockSpec((step, r), lambda i, j, _: (i * blocks + j, 0))),
        out_shape=jax.ShapeDtypeStruct((2 * c, r), F32),
        compiler_params=pltpu.CompilerParams(vmem_limit_bytes=40 * 2**20),
        cost_estimate=pl.CostEstimate(flops=0, bytes_accessed=12 * r * c, transcendentals=0),
        name="unpack_turned",
    )((lax.axis_index("ctx") & 1)[None], half, other)


def all_rows(x):
    return lax.all_gather(x, "tp", axis=0, tiled=True)


def sum_rows(x):
    return lax.psum_scatter(x, "tp", scatter_dimension=0, tiled=True).astype(F32)


def gather_pair(kv):
    n = lax.axis_size("ctx")
    held = {0: ((kv, 0), (kv, 1))}
    for bit in range(1, int(math.log2(n))):
        mask = 1 << bit
        for j in list(held):
            if j == 0:
                got = ctx_swap(kv, mask)
                held[mask] = (got, 0), (got, 1)
            elif mask == 4 and j == 2:
                held[6] = (ctx_swap(held[2][0][0][0:1], 4), 0), (ctx_swap(held[4][1][0][1:2], 2), 0)
            else:
                (k, i), (v, t) = held[j]
                if k is v:
                    got = ctx_swap(k, mask)
                    held[j | mask] = (got, i), (got, t)
                else:
                    held[j | mask] = (ctx_swap(k, mask), i), (ctx_swap(v, mask), t)
    for j in list(held):
        (k, i), (v, t) = held[j]
        got = ctx_swap(k, 1)
        held[j | 1] = (got, i), (got if k is v else ctx_swap(v, 1), t)
    return [held[j][0] for j in range(n)], [held[j][1] for j in range(n)]


def gather_other(x):
    held = {0: x, 1: ctx_swap(x, 1)}
    for j in range(2, lax.axis_size("ctx"), 2):
        held[j] = ctx_swap(x, j)
    return held


def gather_cores(held, gate=None):
    n = lax.axis_size("ctx")
    for j in range(2, n, 2):
        held[j + 1] = ctx_swap(after(held[j], gate), 1)
    return [held[j] for j in range(n)]


def sum_over_all(x):
    for axis in ("ctx", "tp"):
        n = lax.axis_size(axis)
        for bit in range(int(math.log2(n))):
            x = x + lax.ppermute(x, axis, [(i, i ^ (1 << bit)) for i in range(n)])
            yield x
    while True:
        yield x


def gather_tp(x):
    n, me = lax.axis_size("tp"), lax.axis_index("tp")
    out = jnp.zeros((n,) + x.shape, x.dtype)
    for d in range(n):
        got = lax.ppermute(x, "tp", [(i, (i + d) % n) for i in range(n)]) if d else x
        out = lax.dynamic_update_index_in_dim(out, got, (me + n - d) % n, 0)
    return out


def local(tokens, cotangent, block_order, gain_one, shift_one, query_w, key_w, value_w, query_b, key_b, value_b,
          output_w, gain_two, shift_two, gate_w, up_w, down_w):
    heads = key_b.shape[0]
    width = heads * HEAD_DIM
    n_ctx, n_tp = lax.axis_size("ctx"), lax.axis_size("tp")
    ctx = lax.axis_index("ctx")
    own = lax.dynamic_slice_in_dim(block_order, 2 * ctx, 2, 1)
    picked = (jnp.arange(n_ctx, dtype=jnp.int32) ^ ctx)[:, None] == jnp.arange(n_ctx, dtype=jnp.int32)[None, :]
    by_ctx = block_order.reshape(SEQS, 1, n_ctx, 2)
    place = jnp.sum(jnp.where(picked[None, :, :, None], by_ctx, 0), axis=2).astype(jnp.int32).reshape(SEQS, 2 * n_ctx)
    positions = (own[:, :, None] * BLK + jnp.arange(BLK, dtype=jnp.int32)).reshape(-1)
    tabs = rotary_tables(positions)

    x = tokens.astype(F32)
    normed_one, unit_one, inverse_one = layer_stats(x, gain_one, shift_one)
    rows_one = all_rows(normed_one.astype(BF16))
    key_bias = jnp.concatenate([key_b, jnp.zeros((heads, HEAD_DIM - ROT), F32)], axis=1).reshape(-1)
    bias = jnp.stack([query_b, key_bias, value_b])
    q, kv = project(rows_one, query_w, key_w, value_w, bias, tabs)
    keys, values = gather_pair(kv.reshape(2, SEQS, 2, BLK, width))
    arrived = [e[0] for e in keys + values]

    rows_w = output_w.shape[0] // n_ctx
    part = lax.dynamic_slice_in_dim(output_w, ctx * rows_w, rows_w, 0)
    part = gather_tp(after(part, kv))
    dy_rows = all_rows(after(cotangent, rows_one))
    whole_w = lax.all_gather(after(part, arrived, dy_rows), "ctx", axis=1).reshape(n_tp * output_w.shape[0], -1)

    attn, q_ext = attend(place, own, q, keys, values)
    attn_rows = attn.reshape(-1, width)
    attn_own = lax.all_to_all(attn_rows, "tp", split_axis=0, concat_axis=1, tiled=True)
    mixed = x + nn(attn_own, whole_w)
    normed_two, unit_two, inverse_two = layer_stats(mixed, gain_two, shift_two)
    rows_two = all_rows(after(normed_two.astype(BF16), dy_rows, whole_w))
    shape = (1, SEQS, 2, BLK, width + 128)
    queries = gather_cores(gather_other(after(jnp.concatenate([q, q_ext], axis=2).reshape(shape), attn_own)))
    rows_two = after(rows_two, queries)

    act, grad_gu = mlp(rows_two, dy_rows, gate_w, up_w, down_w)
    ff = gate_w.shape[1]
    part_two = (nt(grad_gu[:, :ff], gate_w) + nt(grad_gu[:, ff:], up_w)).astype(BF16)
    grad_two = sum_rows(part_two)
    act, rows_two, dy_rows, grad_gu = after((act, rows_two, dy_rows, grad_gu), part_two)
    gu = begin(lambda core: rc(columns(rows_two, core), grad_gu))
    held = take(gu)
    go(gu)
    dw = begin(lambda core: rc(act, columns(dy_rows, core)))
    act_late = after(act, held)
    down = nn(act_late, down_w).astype(BF16)
    held = take(dw), take(gu, down)
    go(gu)
    go(dw, held)
    grad_two = after(grad_two, take(gu, held))
    go(gu)

    norm_two, grad_gain_two, grad_shift_two = layer_back(grad_two, unit_two, inverse_two, gain_two)
    grad_mixed = cotangent.astype(F32) + norm_two
    branch_own = grad_mixed.astype(BF16)
    grad_attn = nt(branch_own, whole_w).astype(BF16)
    grad_attn = after(grad_attn, take(gu), take(dw))
    go(gu)
    go(dw)
    grad_attn = lax.all_to_all(grad_attn, "tp", split_axis=1, concat_axis=0, tiled=True)
    branch = all_rows(after(branch_own, grad_attn))
    out_tokens = (mixed + sum_rows(after(down, grad_attn))).astype(BF16)
    lane = jnp.arange(128)[None, :]
    ind = ((jnp.arange(width) // HEAD_DIM)[:, None] == lane // 3).astype(F32)
    delta = lax.dot_general(grad_attn.astype(F32) * attn_rows.astype(F32), ind, (((1,), (0,)), ((), ())),
                            precision=lax.Precision.HIGHEST, preferred_element_type=F32)
    do_ext = terms(-delta, lane).astype(BF16)
    do_sent = jnp.concatenate([grad_attn, do_ext], axis=1).reshape(shape)
    grads = gather_other(after(do_sent, take(gu, grad_attn), take(dw, grad_attn)))
    take_extra(gu)
    go(gu)
    grad_q = query_grad(place, own, q, grad_attn.reshape(q.shape), q_ext, do_ext.reshape(q_ext.shape), tabs, keys, values)
    grad_q = grad_q.reshape(-1, width)
    q_part = nt(grad_q, query_w)
    go(dw, q_part)
    grads = gather_cores(grads, q_part)
    grad_gate_w, grad_up_w = unpack_rows(*take(gu, q_part), 2)
    rows_q, branch = after((rows_one, branch), grads)
    oq = begin(lambda core: jnp.concatenate([rc(attn_rows, columns(branch, core)), rc(grad_q, columns(rows_q, core))]))
    held = take(dw, grads)
    go(dw)
    first = key_value_grad(place, own, kv, tabs, queries, after(grads, held, grad_gate_w), 0, SEQS // 2)
    grads = after(grads, take(dw, first), take(oq, first))
    take_extra(dw)
    go(dw)
    go(oq)
    second = key_value_grad(place, own, kv, tabs, queries, grads, SEQS // 2, SEQS // 2)
    grad_k, grad_v = (jnp.concatenate(pair).reshape(-1, width) for pair in zip(first, second))
    part_one = q_part + nt(grad_k, key_w) + nt(grad_v, value_w)
    part_sent = part_one.astype(BF16)
    grad_one = sum_rows(part_sent)

    rows_one, grad_q, grad_k, grad_v = after((rows_one, grad_q, grad_k, grad_v), part_sent)
    grad_kv = jnp.concatenate([grad_k, grad_v], axis=1)
    dkv = begin(lambda core: rc(columns(rows_one, core), grad_kv))
    unit_rows = (rows_one.astype(F32) - shift_one) / gain_one
    bias_grad = jnp.concatenate([jnp.sum(g.astype(F32), axis=0) for g in (grad_q, grad_kv)])
    tp_row = (jnp.arange(n_tp) == lax.axis_index("tp"))[:, None]
    small = jnp.concatenate([
        jnp.sum(part_one * unit_rows, axis=0), jnp.sum(part_one, axis=0), grad_gain_two, grad_shift_two,
        jnp.where(tp_row, bias_grad[None, :], 0.0).reshape(-1)])
    held = take(dkv)
    go(dkv)
    sums = sum_over_all(after(small, held).reshape(-1, 1024))
    small = next(sums), next(sums)
    take(oq, held)
    held = take(dkv, small)
    go(oq)
    go(dkv)
    grad_down_w = unpack_cols(*take(dw, held), act.shape[1])
    small = next(sums), grad_down_w
    take(oq, held)
    held = take(dkv, small)
    go(oq)
    go(dkv)
    small = next(sums)
    take(oq, held)
    held = take(dkv, small)
    go(oq)
    go(dkv)
    for _ in range(4):
        small = next(sums)
    take(oq, held)
    take(dkv)
    take_extra(oq)
    take_extra(dkv)
    go(oq)
    go(dkv)
    depth = x.shape[1]
    small = small.reshape(-1)
    norms = small[:4 * depth].reshape(4, depth)
    bias_sum = jnp.sum(jnp.where(tp_row, small[4 * depth:].reshape(n_tp, -1), 0.0), axis=0)
    halves = take(oq)
    grad_output_w, grad_query_w = unpack_cols(*halves, width), unpack_turned(*halves, width)
    grad_key_w, grad_value_w = unpack_rows(*take(dkv), 2)
    norm_one, _, _ = layer_back(grad_one, unit_one, inverse_one, gain_one)
    grad_tokens = (grad_mixed + norm_one).astype(BF16)
    return (
        out_tokens, grad_tokens, norms[0], norms[1], grad_query_w, grad_key_w, grad_value_w,
        bias_sum[:width], bias_sum[width:2 * width].reshape(heads, HEAD_DIM)[:, :ROT], bias_sum[2 * width:],
        grad_output_w, norms[2], norms[3], grad_gate_w, grad_up_w, grad_down_w,
    )


def solution(mesh):
    rows, cols, depth, flat = P(("ctx", "tp"), None), P(None, "tp"), P("tp", None), P("tp")
    in_specs = (rows, rows, P(), P(), P(), cols, cols, cols, flat, depth, flat, depth, P(), P(), cols, cols, depth)
    out_specs = (rows, rows, P(), P(), cols, cols, cols, flat, depth, flat, depth, P(), P(), cols, cols, depth)
    return jax.shard_map(local, mesh=mesh, in_specs=in_specs, out_specs=out_specs, check_vma=False)
```

```python
import functools
import jax, jax.numpy as jnp
from jax import lax
from jax.experimental import pallas as pl
from jax.experimental.pallas import tpu as pltpu

BLK = 128
CB = 4
CH = BLK * CB
NEG = -1e30
SCALE = 0.125


def nt(a, b):
    return lax.dot_general(a, b, (((1,), (1,)), ((), ())), preferred_element_type=jnp.float32)


def nn(a, b):
    return lax.dot_general(a, b, (((1,), (0,)), ((), ())), preferred_element_type=jnp.float32)


def lane_of(shape):
    return lax.broadcasted_iota(jnp.int32, shape, 1)


def row_of(shape):
    return lax.broadcasted_iota(jnp.int32, shape, 0)


def split_heads(x):
    low = lane_of(x.shape) < 64
    zero = jnp.zeros_like(x)
    return jnp.concatenate([jnp.where(low, x, zero), jnp.where(low, zero, x)], axis=0)


def join_heads(x):
    low = lane_of((BLK, 128)) < 64
    return jnp.where(low, x[:BLK], x[BLK:])


def own_lanes(pair):
    shape = (2 * BLK, 128)
    return lane_of(shape) // 3 == 2 * pair + row_of(shape) // BLK


def terms(x, lane):
    first = x.astype(jnp.bfloat16).astype(jnp.float32)
    second = (x - first).astype(jnp.bfloat16).astype(jnp.float32)
    return jnp.where(lane % 3 == 0, first, jnp.where(lane % 3 == 1, second, x - first - second))


def place_rows(place_ref, s, refs, dst_ref, lane=0):
    at = 0
    for ref in refs:
        for j in range(ref.shape[0]):
            for w in range(2):
                row = pl.multiple_of(place_ref[s, at] * BLK, BLK)
                dst_ref[pl.ds(row, BLK), lane:lane + 128] = ref[j, 0, w]
                at += 1


def fwd_kernel(place_ref, own_ref, q_ref, *refs, blocks, n):
    k_refs, v_refs, (o_ref, ext_ref, ks, vs, scr, acc) = refs[:n], refs[n:2 * n], refs[2 * n:]
    s, pair = pl.program_id(0), pl.program_id(1)

    @pl.when((s == 0) & (pair == 0))
    def _():
        vs[:, 128:256] = jnp.ones((blocks * BLK, 128), jnp.bfloat16)

    @pl.when(pair == 0)
    def _():
        ext_ref[...] = jnp.zeros_like(ext_ref)

    place_rows(place_ref, s, k_refs, ks)
    place_rows(place_ref, s, v_refs, vs)
    for w in range(2):
        rows = slice(w * BLK, (w + 1) * BLK)
        pos = own_ref[s, w]
        last = pos // CB
        qs = split_heads(q_ref[0, rows, :] * jnp.bfloat16(SCALE))

        def tiles_max(run, sc):
            for t in range(CB):
                run = jnp.maximum(run, sc[:, t * 128:(t + 1) * 128])
            return run

        def score(c, run):
            at = pl.multiple_of(c * CH, CH)
            sc = nt(qs, ks[pl.ds(at, CH), :])
            scr[c] = sc
            return tiles_max(run, sc)

        run = lax.fori_loop(0, last, score, jnp.full((2 * BLK, 128), NEG, jnp.float32))
        at = pl.multiple_of(last * CH, CH)
        sc = nt(qs, ks[pl.ds(at, CH), :])
        qpos = pos * BLK + row_of((2 * BLK, CH)) % BLK
        kpos = last * CH + lane_of((2 * BLK, CH))
        sc = jnp.where(kpos <= qpos, sc, NEG)
        scr[last] = sc
        run = tiles_max(run, sc)
        top = jnp.broadcast_to(jnp.max(run, axis=1, keepdims=True), (2 * BLK, 128))
        topc = jnp.concatenate([top] * CB, axis=1)
        acc[...] = jnp.zeros_like(acc)

        def weigh(c, carry):
            at = pl.multiple_of(c * CH, CH)
            p = jnp.exp(scr[c] - topc).astype(jnp.bfloat16)
            acc[...] += nn(p, vs[pl.ds(at, CH), :])
            return carry

        lax.fori_loop(0, last + 1, weigh, 0)
        total = acc[:, 128:256]
        o_ref[0, rows, :] = join_heads(acc[:, 0:128] / total).astype(jnp.bfloat16)
        lane = lane_of((2 * BLK, 128))
        mine = jnp.where(own_lanes(pair), terms(-(top + jnp.log(total)), lane), 0.0)
        ext_ref[0, rows, :] = (ext_ref[0, rows, :].astype(jnp.float32) + mine[:BLK] + mine[BLK:]).astype(jnp.bfloat16)


def dq_kernel(place_ref, own_ref, q_ref, do_ref, qx_ref, dox_ref, c_ref, a_ref, b_ref, *refs, blocks, n):
    k_refs, v_refs, (dq_ref, ks, vs, acc) = refs[:n], refs[n:2 * n], refs[2 * n:]
    s, pair = pl.program_id(0), pl.program_id(1)

    @pl.when((s == 0) & (pair == 0))
    def _():
        ks[:, 128:256] = jnp.ones((blocks * BLK, 128), jnp.bfloat16)
        vs[:, 128:256] = jnp.ones((blocks * BLK, 128), jnp.bfloat16)

    place_rows(place_ref, s, k_refs, ks)
    place_rows(place_ref, s, v_refs, vs)
    mine = own_lanes(pair)
    for w in range(2):
        rows = slice(w * BLK, (w + 1) * BLK)
        pos = own_ref[s, w]
        last = pos // CB

        def extend(tile, ext):
            both = jnp.concatenate([ext, ext], axis=0)
            return jnp.concatenate([split_heads(tile), jnp.where(mine, both, jnp.zeros_like(both))], axis=1)

        qs = extend(q_ref[0, rows, :] * jnp.bfloat16(SCALE), qx_ref[0, rows, :])
        dos = extend(do_ref[0, rows, :], dox_ref[0, rows, :])
        acc[...] = jnp.zeros_like(acc)

        def step(c, mask):
            at = pl.multiple_of(c * CH, CH)
            p = jnp.exp(nt(qs, ks[pl.ds(at, CH), :]))
            if mask is not None:
                p = jnp.where(mask, p, 0.0)
            ds = (p * nt(dos, vs[pl.ds(at, CH), :])).astype(jnp.bfloat16)
            acc[...] += nn(ds, ks[pl.ds(at, CH), 0:128])

        def body(c, carry):
            step(c, None)
            return carry

        lax.fori_loop(0, last, body, 0)
        qpos = pos * BLK + row_of((2 * BLK, CH)) % BLK
        kpos = last * CH + lane_of((2 * BLK, CH))
        step(last, kpos <= qpos)
        grad = join_heads(acc[...]) * SCALE
        dq_ref[0, rows, :] = turn(grad, c_ref[rows], a_ref[rows], b_ref[rows], -1.0).astype(jnp.bfloat16)


def dkv_kernel(place_ref, own_ref, k_ref, v_ref, c_ref, a_ref, b_ref, *refs, blocks, n, lead):
    q_refs, do_refs, qx_refs, dox_refs = (refs[i * n:(i + 1) * n] for i in range(4))
    dk_ref, dv_ref, qs, dos, acck, accv = refs[4 * n:]
    s, pair = pl.program_id(0) + lead, pl.program_id(1)
    place_rows(place_ref, s, q_refs, qs)
    place_rows(place_ref, s, do_refs, dos)

    @pl.when(pair == 0)
    def _():
        place_rows(place_ref, s, qx_refs, qs, 128)
        place_rows(place_ref, s, dox_refs, dos, 128)

    ones = own_lanes(pair).astype(jnp.bfloat16)
    for w in range(2):
        rows = slice(w * BLK, (w + 1) * BLK)
        pos = own_ref[s, w]
        first = pos // CB
        kw = jnp.concatenate([split_heads(k_ref[0, 0, rows, :] * jnp.bfloat16(SCALE)), ones], axis=1)
        vw = jnp.concatenate([split_heads(v_ref[0, 0, rows, :]), ones], axis=1)
        acck[...] = jnp.zeros_like(acck)
        accv[...] = jnp.zeros_like(accv)

        def step(c, mask):
            at = pl.multiple_of(c * CH, CH)
            p = jnp.exp(nt(kw, qs[pl.ds(at, CH), :]))
            if mask is not None:
                p = jnp.where(mask, p, 0.0)
            accv[...] += nn(p.astype(jnp.bfloat16), dos[pl.ds(at, CH), 0:128])
            ds = (p * nt(vw, dos[pl.ds(at, CH), :])).astype(jnp.bfloat16)
            acck[...] += nn(ds, qs[pl.ds(at, CH), 0:128])

        def body(c, carry):
            step(c, None)
            return carry

        kpos = pos * BLK + row_of((2 * BLK, CH)) % BLK
        qpos = first * CH + lane_of((2 * BLK, CH))
        step(first, kpos <= qpos)
        lax.fori_loop(first + 1, blocks // CB, body, 0)
        grad = join_heads(acck[...]) * SCALE
        dk_ref[0, rows, :] = turn(grad, c_ref[rows], a_ref[rows], b_ref[rows], -1.0).astype(jnp.bfloat16)
        dv_ref[0, rows, :] = join_heads(accv[...]).astype(jnp.bfloat16)


OWN = pl.BlockSpec((1, 2 * BLK, 128), lambda s, h, *_: (s, 0, h))
EXT = pl.BlockSpec((1, 2 * BLK, 128), lambda s, h, *_: (s, 0, 0))


def table(lead=0):
    return pl.BlockSpec((2 * BLK, 128), lambda s, h, *_: (s + lead, 0))


def piece(x, first=0, lane=None, lead=0):
    return pl.BlockSpec((1, 1, 2, BLK, 128), lambda s, h, *_: (first, s + lead, 0, 0, h if lane is None else lane))


def attention_call(kernel, name, mats, seqs, pairs, blocks, in_specs, out_specs, out_shape, scratch, args):
    work = seqs * pairs * 2 * 2 * BLK * blocks * BLK // 2
    return pl.pallas_call(
        kernel,
        grid_spec=pltpu.PrefetchScalarGridSpec(
            num_scalar_prefetch=2, grid=(seqs, pairs), in_specs=in_specs, out_specs=out_specs, scratch_shapes=scratch),
        out_shape=out_shape,
        compiler_params=pltpu.CompilerParams(vmem_limit_bytes=40 * 2**20),
        cost_estimate=pl.CostEstimate(flops=work * 512 * mats, bytes_accessed=4 * seqs * pairs * blocks * BLK * 128, transcendentals=work),
        name=name,
    )(*args)


def rows_of(blocks, lanes):
    return pltpu.VMEM((blocks * BLK, lanes), jnp.bfloat16)


def acc_of(lanes):
    return pltpu.VMEM((2 * BLK, lanes), jnp.float32)


def attend(place, own, q, keys, values):
    seqs, pairs, blocks = q.shape[0], q.shape[2] // 128, place.shape[1]
    return attention_call(
        functools.partial(fwd_kernel, blocks=blocks, n=len(keys)), "attend", 2, seqs, pairs, blocks,
        [OWN] + [piece(*e) for e in keys + values], [OWN, EXT],
        [jax.ShapeDtypeStruct(q.shape, jnp.bfloat16), jax.ShapeDtypeStruct(q.shape[:2] + (128,), jnp.bfloat16)],
        [rows_of(blocks, 128), rows_of(blocks, 256), pltpu.VMEM((blocks // CB, 2 * BLK, CH), jnp.float32), acc_of(256)],
        [place, own, q] + [e[0] for e in keys + values])


def query_grad(place, own, q, do, q_ext, do_ext, tabs, keys, values):
    seqs, pairs, blocks = q.shape[0], q.shape[2] // 128, place.shape[1]
    return attention_call(
        functools.partial(dq_kernel, blocks=blocks, n=len(keys)), "query_grad", 3, seqs, pairs, blocks,
        [OWN, OWN, EXT, EXT] + [table()] * 3 + [piece(*e) for e in keys + values], OWN,
        jax.ShapeDtypeStruct(q.shape, jnp.bfloat16),
        [rows_of(blocks, 256), rows_of(blocks, 256), acc_of(128)],
        [place, own, q, do, q_ext, do_ext, *tabs] + [e[0] for e in keys + values])


def key_value_grad(place, own, kv, tabs, queries, grads, lead, count):
    pairs, blocks = kv.shape[3] // 128, place.shape[1]
    shape = (count,) + kv.shape[2:]
    both = queries + grads

    def own_part(i):
        return pl.BlockSpec((1, 1, 2 * BLK, 128), lambda s, h, *_: (i, s + lead, 0, h))

    return attention_call(
        functools.partial(dkv_kernel, blocks=blocks, n=len(queries), lead=lead), "key_value_grad", 4, count, pairs, blocks,
        [own_part(0), own_part(1)] + [table(lead)] * 3 + [piece(x, lead=lead) for x in both]
        + [piece(x, lane=pairs, lead=lead) for x in both], [OWN, OWN],
        [jax.ShapeDtypeStruct(shape, jnp.bfloat16)] * 2,
        [rows_of(blocks, 256), rows_of(blocks, 256), acc_of(128), acc_of(128)],
        [place, own, kv, kv, *tabs] + both * 2)


import math
from jax.sharding import PartitionSpec as P

HEAD_DIM = 64
ROT = 16
SEQS = 4
EPS = 1e-05
F32 = jnp.float32
BF16 = jnp.bfloat16


def rc(left, right):
    return lax.dot_general(left, right, (((0,), (0,)), ((), ())), preferred_element_type=F32)


def layer_stats(values, gain, shift):
    mean = jnp.mean(values, axis=-1, keepdims=True)
    centred = values - mean
    inverse = lax.rsqrt(jnp.mean(centred * centred, axis=-1, keepdims=True) + EPS)
    unit = centred * inverse
    return unit * gain + shift, unit, inverse


def layer_back(grad, unit, inverse, gain):
    scaled = grad * gain
    grad_in = inverse * (
        scaled
        - jnp.mean(scaled, axis=-1, keepdims=True)
        - unit * jnp.mean(scaled * unit, axis=-1, keepdims=True)
    )
    return grad_in, jnp.sum(grad * unit, axis=0), jnp.sum(grad, axis=0)


def rotary_tables(positions):
    half = ROT // 2
    dim = jnp.arange(2 * HEAD_DIM) % HEAD_DIM
    freq = jnp.where(dim < ROT, 10000.0 ** (-2.0 * (dim % half).astype(F32) / ROT), 0.0)
    angles = positions.astype(F32)[:, None] * freq[None, :]
    sin = jnp.sin(angles)
    return jnp.cos(angles), jnp.where(dim < half, sin, 0.0), jnp.where(dim < half, 0.0, sin)


def turn(x, ctab, above, below, sign):
    up = pltpu.roll(x, 128 - ROT // 2, axis=1)
    down = pltpu.roll(x, ROT // 2, axis=1)
    return x * ctab + sign * (down * below - up * above)


def project_kernel(h_ref, wq_ref, wk_ref, wv_ref, bias_ref, c_ref, a_ref, b_ref, q_ref, kv_ref):
    h = h_ref[...]
    width = wq_ref.shape[1]
    tabs = c_ref[...], a_ref[...], b_ref[...]
    for at, (w_ref, out) in enumerate(((wq_ref, q_ref.at[0]), (wk_ref, kv_ref.at[0, 0]), (wv_ref, kv_ref.at[1, 0]))):
        lin = nn(h, w_ref[...]) + bias_ref[at:at + 1, :]
        for p in range(width // 128):
            part = lin[:, p * 128:(p + 1) * 128]
            if at < 2:
                part = turn(part, *tabs, 1.0)
            out[:, p * 128:(p + 1) * 128] = part.astype(BF16)


def project(rows, wq, wk, wv, bias, tabs):
    total, depth = rows.shape
    width = wq.shape[1]
    step = total // SEQS
    weight = pl.BlockSpec((depth, width), lambda i: (0, 0))
    table = pl.BlockSpec((step, 128), lambda i: (i, 0))
    return pl.pallas_call(
        project_kernel,
        grid=(SEQS,),
        in_specs=[pl.BlockSpec((step, depth), lambda i: (i, 0)), weight, weight, weight,
                  pl.BlockSpec((3, width), lambda i: (0, 0)), table, table, table],
        out_specs=[pl.BlockSpec((1, step, width), lambda i: (i, 0, 0)),
                   pl.BlockSpec((2, 1, step, width), lambda i: (0, i, 0, 0))],
        out_shape=[jax.ShapeDtypeStruct((SEQS, step, width), BF16), jax.ShapeDtypeStruct((2, SEQS, step, width), BF16)],
        compiler_params=pltpu.CompilerParams(vmem_limit_bytes=48 * 2**20),
        cost_estimate=pl.CostEstimate(flops=6 * total * depth * width, bytes_accessed=6 * depth * width, transcendentals=0),
        name="project",
    )(rows, wq, wk, wv, bias, *tabs)


def mlp_kernel(h_ref, dy_ref, gate_ref, up_ref, down_ref, act_ref, *grad_refs):
    width = gate_ref.shape[1]
    gate = nn(h_ref[...], gate_ref[...])
    up = nn(h_ref[...], up_ref[...])
    grad = nt(dy_ref[...], down_ref[...])
    sig = 1.0 / (1.0 + jnp.exp(-gate))
    silu = gate * sig
    act_ref[...] = (silu * up).astype(BF16)
    outs = grad_refs if len(grad_refs) == 2 else (grad_refs[0].at[:, :width], grad_refs[0].at[:, width:])
    outs[0][...] = (grad * up * (sig + silu * (1.0 - sig))).astype(BF16)
    outs[1][...] = (grad * silu).astype(BF16)


def mlp(rows, dy, gate_w, up_w, down_w, step=256):
    total, depth = rows.shape
    width = gate_w.shape[1]
    joined = width % 128 == 0
    block = pl.BlockSpec((step, depth), lambda i: (i, 0))

    def whole(x):
        return pl.BlockSpec(x.shape, lambda i: (0, 0), pipeline_mode=pl.Buffered(1))

    def out(n):
        return pl.BlockSpec((step, n), lambda i: (i, 0)), jax.ShapeDtypeStruct((total, n), BF16)

    outs = [out(width), out(2 * width)] if joined else [out(width)] * 3
    act, *grads = pl.pallas_call(
        mlp_kernel,
        grid=(total // step,),
        in_specs=[block, block, whole(gate_w), whole(up_w), whole(down_w)],
        out_specs=[o[0] for o in outs],
        out_shape=[o[1] for o in outs],
        compiler_params=pltpu.CompilerParams(vmem_limit_bytes=56 * 2**20),
        cost_estimate=pl.CostEstimate(flops=6 * total * depth * width, bytes_accessed=6 * depth * width + 10 * total * depth,
                                      transcendentals=total * width),
        name="mlp",
    )(rows, dy, gate_w, up_w, down_w)
    return act, grads[0] if joined else jnp.concatenate(grads, axis=1)


def ctx_swap(x, mask):
    n = lax.axis_size("ctx")
    return lax.ppermute(x, "ctx", [(i, i ^ mask) for i in range(n)])


def add16(a, b):
    return (a.astype(F32) + b.astype(F32)).astype(BF16)


def after(x, *deps):
    if not jax.tree.leaves(deps):
        return x
    return lax.optimization_barrier((x, deps))[0]


def half_of(x, bit, mine):
    side = (lax.axis_index("ctx") >> bit) & 1
    r = x.shape[0] // 2
    return lax.dynamic_slice_in_dim(x, (side if mine else 1 - side) * r, r, 0)


def weight_grad(part):
    core = lax.axis_index("ctx") & 1
    got = ctx_swap(part(1 - core).astype(BF16), 1)
    gate = yield
    half = (part(core) + after(got, gate).astype(F32)).astype(BF16)
    bits = list(range(1, int(math.log2(lax.axis_size("ctx")))))
    orders = [bits, bits[::-1]]
    r = half.shape[0] // 2
    streams = [half[:r], half[r:]]
    gate = yield streams
    for i in range(len(bits)):
        streams = after(streams, gate)
        got = [ctx_swap(half_of(x, o[i], False), 1 << o[i]) for x, o in zip(streams, orders)]
        gate = yield
        streams, got = after((streams, got), gate)
        streams = [add16(half_of(x, o[i], True), g) for x, o, g in zip(streams, orders, got)]
        gate = yield streams
    for i in reversed(range(len(bits))):
        streams = after(streams, gate)
        got = [ctx_swap(x, 1 << o[i]) for x, o in zip(streams, orders)]
        gate = yield
        streams, got = after((streams, got), gate)
        streams = [
            jnp.where(((lax.axis_index("ctx") >> o[i]) & 1) == 0, jnp.concatenate([x, g]), jnp.concatenate([g, x]))
            for x, o, g in zip(streams, orders, got)
        ]
        if i == 0:
            streams = jnp.concatenate(streams)
        gate = yield streams
    streams = after(streams, gate)
    other = ctx_swap(streams, 1)
    gate = yield
    yield after((streams, other), gate)


def begin(*args):
    chain = weight_grad(*args)
    next(chain)
    return chain


def take(chain, gate=None):
    return chain.send(gate)


def go(chain, gate=None):
    chain.send(gate)


def take_extra(chain):
    for _ in range(2 * int(math.log2(lax.axis_size("ctx"))) - 6):
        go(chain)
        take(chain)


def unpack_rows_kernel(core_ref, half_ref, other_ref, *out_refs):
    def put(src):
        at = 0
        for out in out_refs:
            out[...] = src[:, at:at + out.shape[1]].astype(F32)
            at += out.shape[1]

    @pl.when(pl.program_id(0) == core_ref[0])
    def _():
        put(half_ref)

    @pl.when(pl.program_id(0) != core_ref[0])
    def _():
        put(other_ref)


def unpack_rows(half, other, parts):
    r, c = half.shape
    step = math.gcd(r, 256)
    blocks = r // step
    core = lax.axis_index("ctx") & 1

    def mine(i, j, core_ref):
        return jnp.where(i == core_ref[0], j, jnp.where(core_ref[0] == 0, blocks - 1, 0)), 0

    def theirs(i, j, core_ref):
        return jnp.where(i != core_ref[0], j, jnp.where(core_ref[0] == 1, blocks - 1, 0)), 0

    return pl.pallas_call(
        unpack_rows_kernel,
        grid_spec=pltpu.PrefetchScalarGridSpec(
            num_scalar_prefetch=1, grid=(2, blocks),
            in_specs=[pl.BlockSpec((step, c), mine), pl.BlockSpec((step, c), theirs)],
            out_specs=[pl.BlockSpec((step, c // parts), lambda i, j, _: (i * blocks + j, 0))] * parts),
        out_shape=[jax.ShapeDtypeStruct((2 * r, c // parts), F32)] * parts,
        compiler_params=pltpu.CompilerParams(vmem_limit_bytes=40 * 2**20),
        cost_estimate=pl.CostEstimate(flops=0, bytes_accessed=12 * r * c, transcendentals=0),
        name="unpack_rows",
    )(core[None], half, other)


def columns(x, which):
    w = x.shape[1] // 2
    return lax.dynamic_slice_in_dim(x, which * w, w, 1)


def all_rows(x):
    return lax.all_gather(x, "tp", axis=0, tiled=True)


def tp_shift(x, d):
    n = lax.axis_size("tp")
    return lax.ppermute(x, "tp", [(i, (i + d) % n) for i in range(n)])


def part_of(x, d, axis):
    n = lax.axis_size("tp")
    w = x.shape[axis] // n
    return lax.dynamic_slice_in_dim(x, (lax.axis_index("tp") + d) % n * w, w, axis)


def exchange(x, split, join):
    n, me = lax.axis_size("tp"), lax.axis_index("tp")
    w = x.shape[join]
    shape = list(x.shape)
    shape[split] //= n
    shape[join] *= n
    out = jnp.zeros(shape, x.dtype)
    for d in range(n):
        got = tp_shift(part_of(x, d, split), d) if d else part_of(x, 0, split)
        out = lax.dynamic_update_slice_in_dim(out, got, (me + n - d) % n * w, join)
    return out


def sum_rows(x):
    return lax.psum_scatter(x, "tp", scatter_dimension=0, tiled=True)


def gather_pair(kv):
    n = lax.axis_size("ctx")
    held = {0: ((kv, 0), (kv, 1))}
    for bit in range(1, int(math.log2(n))):
        mask = 1 << bit
        for j in list(held):
            if j == 0:
                got = ctx_swap(kv, mask)
                held[mask] = (got, 0), (got, 1)
            elif mask == 4 and j == 2:
                held[6] = (ctx_swap(held[2][0][0][0:1], 4), 0), (ctx_swap(held[4][1][0][1:2], 2), 0)
            else:
                (k, i), (v, t) = held[j]
                if k is v:
                    got = ctx_swap(k, mask)
                    held[j | mask] = (got, i), (got, t)
                else:
                    held[j | mask] = (ctx_swap(k, mask), i), (ctx_swap(v, mask), t)
    for j in list(held):
        (k, i), (v, t) = held[j]
        got = ctx_swap(k, 1)
        held[j | 1] = (got, i), (got if k is v else ctx_swap(v, 1), t)
    return [held[j][0] for j in range(n)], [held[j][1] for j in range(n)]


def gather_other(x):
    held = {0: x, 1: ctx_swap(x, 1)}
    for j in range(2, lax.axis_size("ctx"), 2):
        held[j] = ctx_swap(x, j)
    return held


def gather_cores(held, gate=None):
    n = lax.axis_size("ctx")
    for j in range(2, n, 2):
        held[j + 1] = ctx_swap(after(held[j], gate), 1)
    return [held[j] for j in range(n)]


def sum_over_all(x):
    for axis in ("ctx", "tp"):
        n = lax.axis_size(axis)
        for bit in range(int(math.log2(n))):
            x = x + lax.ppermute(x, axis, [(i, i ^ (1 << bit)) for i in range(n)])
            yield x
    while True:
        yield x


def gather_tp(x):
    n, me = lax.axis_size("tp"), lax.axis_index("tp")
    out = jnp.zeros((n,) + x.shape, x.dtype)
    for d in range(n):
        got = lax.ppermute(x, "tp", [(i, (i + d) % n) for i in range(n)]) if d else x
        out = lax.dynamic_update_index_in_dim(out, got, (me + n - d) % n, 0)
    return out


def local(tokens, cotangent, block_order, gain_one, shift_one, query_w, key_w, value_w, query_b, key_b, value_b,
          output_w, gain_two, shift_two, gate_w, up_w, down_w):
    heads = key_b.shape[0]
    width = heads * HEAD_DIM
    n_ctx, n_tp = lax.axis_size("ctx"), lax.axis_size("tp")
    ctx = lax.axis_index("ctx")
    own = lax.dynamic_slice_in_dim(block_order, 2 * ctx, 2, 1)
    picked = (jnp.arange(n_ctx, dtype=jnp.int32) ^ ctx)[:, None] == jnp.arange(n_ctx, dtype=jnp.int32)[None, :]
    by_ctx = block_order.reshape(SEQS, 1, n_ctx, 2)
    place = jnp.sum(jnp.where(picked[None, :, :, None], by_ctx, 0), axis=2).astype(jnp.int32).reshape(SEQS, 2 * n_ctx)
    positions = (own[:, :, None] * BLK + jnp.arange(BLK, dtype=jnp.int32)).reshape(-1)
    tabs = rotary_tables(positions)

    x = tokens.astype(F32)
    normed_one, unit_one, inverse_one = layer_stats(x, gain_one, shift_one)
    rows_one = all_rows(normed_one.astype(BF16))
    key_bias = jnp.concatenate([key_b, jnp.zeros((heads, HEAD_DIM - ROT), F32)], axis=1).reshape(-1)
    bias = jnp.stack([query_b, key_bias, value_b])
    q, kv = project(rows_one, query_w, key_w, value_w, bias, tabs)
    keys, values = gather_pair(kv.reshape(2, SEQS, 2, BLK, width))
    arrived = [e[0] for e in keys + values]

    rows_w = output_w.shape[0] // n_ctx
    part = lax.dynamic_slice_in_dim(output_w, ctx * rows_w, rows_w, 0)
    part = gather_tp(after(part, kv))
    dy_rows = all_rows(after(cotangent, rows_one))
    whole_w = lax.all_gather(after(part, arrived, dy_rows), "ctx", axis=1).reshape(n_tp * output_w.shape[0], -1)

    attn, q_ext = attend(place, own, q, keys, values)
    attn_rows = attn.reshape(-1, width)
    attn_own = exchange(attn_rows, 0, 1)
    mixed = x + nn(attn_own, whole_w)
    normed_two, unit_two, inverse_two = layer_stats(mixed, gain_two, shift_two)
    rows_two = all_rows(after(normed_two.astype(BF16), dy_rows, whole_w))
    shape = (1, SEQS, 2, BLK, width + 128)
    queries = gather_cores(gather_other(after(jnp.concatenate([q, q_ext], axis=2).reshape(shape), attn_own)))
    rows_two = after(rows_two, queries)

    act, grad_gu = mlp(rows_two, dy_rows, gate_w, up_w, down_w)
    ff = gate_w.shape[1]
    part_two = (nt(grad_gu[:, :ff], gate_w) + nt(grad_gu[:, ff:], up_w)).astype(BF16)
    grad_two = sum_rows(part_two)
    act, rows_two, dy_rows, grad_gu = after((act, rows_two, dy_rows, grad_gu), part_two)
    gu = begin(lambda core: rc(columns(rows_two, core), grad_gu))
    grad_down_w = rc(act, dy_rows).astype(BF16)
    held = take(gu)
    go(gu)
    down = nn(after(act, held), down_w).astype(BF16)
    held = take(gu, down)
    grad_two, grad_down_w = after((grad_two, grad_down_w), held, down)
    go(gu)
    grad_down_w = lax.psum(grad_down_w, "ctx")

    norm_two, grad_gain_two, grad_shift_two = layer_back(grad_two.astype(F32), unit_two, inverse_two, gain_two)
    grad_mixed = cotangent.astype(F32) + norm_two
    branch_own = grad_mixed.astype(BF16)
    grad_attn = nt(branch_own, whole_w).astype(BF16)
    grad_attn = after(grad_attn, take(gu))
    go(gu)
    grad_attn = exchange(grad_attn, 1, 0)
    branch = all_rows(after(branch_own, grad_attn))
    out_tokens = (mixed + sum_rows(after(down, grad_attn)).astype(F32)).astype(BF16)
    lane = jnp.arange(128)[None, :]
    ind = ((jnp.arange(width) // HEAD_DIM)[:, None] == lane // 3).astype(F32)
    delta = lax.dot_general(grad_attn.astype(F32) * attn_rows.astype(F32), ind, (((1,), (0,)), ((), ())),
                            precision=lax.Precision.HIGHEST, preferred_element_type=F32)
    do_ext = terms(-delta, lane).astype(BF16)
    do_sent = jnp.concatenate([grad_attn, do_ext], axis=1).reshape(shape)
    grads = gather_other(after(do_sent, take(gu, grad_attn)))
    grad_q = query_grad(place, own, q, grad_attn.reshape(q.shape), q_ext, do_ext.reshape(q_ext.shape), tabs, keys, values)
    grad_q = grad_q.reshape(-1, width)
    q_part = nt(grad_q, query_w)
    grads = gather_cores(grads, q_part)
    go(gu, grads)
    first = key_value_grad(place, own, kv, tabs, queries, grads, 0, SEQS // 2)
    grads = after(grads, take(gu, first))
    take_extra(gu)
    go(gu)
    second = key_value_grad(place, own, kv, tabs, queries, grads, SEQS // 2, SEQS // 2)
    grad_k, grad_v = (jnp.concatenate(pair).reshape(-1, width) for pair in zip(first, second))
    part_one = q_part + nt(grad_k, key_w) + nt(grad_v, value_w)
    part_sent = part_one.astype(BF16)
    grad_one = sum_rows(part_sent)

    rows_one, branch, grad_q, grad_k, grad_v = after((rows_one, branch, grad_q, grad_k, grad_v), part_sent)
    grad_qkv = jnp.concatenate([grad_q, grad_k, grad_v], axis=1)
    chain = begin(lambda core: rc(columns(rows_one, core), grad_qkv))
    unit_rows = (rows_one.astype(F32) - shift_one) / gain_one
    bias_grad = jnp.sum(grad_qkv.astype(F32), axis=0)
    tp_row = (jnp.arange(n_tp) == lax.axis_index("tp"))[:, None]
    small = jnp.concatenate([
        jnp.sum(part_one * unit_rows, axis=0), jnp.sum(part_one, axis=0), grad_gain_two, grad_shift_two,
        jnp.where(tp_row, bias_grad[None, :], 0.0).reshape(-1)])
    held = take(chain)
    go(chain)
    grad_output_w = lax.psum(after(rc(attn_rows, after(branch, held)).astype(BF16), grad_down_w), "ctx")
    grad_gate_w, grad_up_w = unpack_rows(*take(gu, held), 2)
    sums = sum_over_all(after(small, held).reshape(-1, 1024))
    small = next(sums), grad_gate_w
    held = take(chain, small)
    go(chain)
    small = next(sums), next(sums)
    held = take(chain, small)
    go(chain)
    grad_down_w = after(grad_down_w, held).astype(F32)
    small = next(sums), grad_down_w
    held = take(chain, small)
    go(chain)
    for _ in range(4):
        small = next(sums)
    take(chain)
    take_extra(chain)
    go(chain)
    depth = x.shape[1]
    small = small.reshape(-1)
    norms = small[:4 * depth].reshape(4, depth)
    bias_sum = jnp.sum(jnp.where(tp_row, small[4 * depth:].reshape(n_tp, -1), 0.0), axis=0)
    grad_query_w, grad_key_w, grad_value_w = unpack_rows(*take(chain), 3)
    grad_output_w = grad_output_w.astype(F32)
    norm_one, _, _ = layer_back(grad_one.astype(F32), unit_one, inverse_one, gain_one)
    grad_tokens = (grad_mixed + norm_one).astype(BF16)
    return (
        out_tokens, grad_tokens, norms[0], norms[1], grad_query_w, grad_key_w, grad_value_w,
        bias_sum[:width], bias_sum[width:2 * width].reshape(heads, HEAD_DIM)[:, :ROT], bias_sum[2 * width:],
        grad_output_w, norms[2], norms[3], grad_gate_w, grad_up_w, grad_down_w,
    )


def solution(mesh):
    rows, cols, depth, flat = P(("ctx", "tp"), None), P(None, "tp"), P("tp", None), P("tp")
    in_specs = (rows, rows, P(), P(), P(), cols, cols, cols, flat, depth, flat, depth, P(), P(), cols, cols, depth)
    out_specs = (rows, rows, P(), P(), cols, cols, cols, flat, depth, flat, depth, P(), P(), cols, cols, depth)
    return jax.shard_map(local, mesh=mesh, in_specs=in_specs, out_specs=out_specs, check_vma=False)
```

```python
import functools
import jax, jax.numpy as jnp
from jax import lax
from jax.experimental import pallas as pl
from jax.experimental.pallas import tpu as pltpu

BLK = 128
CB = 4
CH = BLK * CB
NEG = -1e30
SCALE = 0.125


def nt(a, b):
    return lax.dot_general(a, b, (((1,), (1,)), ((), ())), preferred_element_type=jnp.float32)


def nn(a, b):
    return lax.dot_general(a, b, (((1,), (0,)), ((), ())), preferred_element_type=jnp.float32)


def lane_of(shape):
    return lax.broadcasted_iota(jnp.int32, shape, 1)


def row_of(shape):
    return lax.broadcasted_iota(jnp.int32, shape, 0)


def split_heads(x):
    low = lane_of(x.shape) < 64
    zero = jnp.zeros_like(x)
    return jnp.concatenate([jnp.where(low, x, zero), jnp.where(low, zero, x)], axis=0)


def join_heads(x):
    low = lane_of((BLK, 128)) < 64
    return jnp.where(low, x[:BLK], x[BLK:])


def own_lanes(pair):
    shape = (2 * BLK, 128)
    return lane_of(shape) // 3 == 2 * pair + row_of(shape) // BLK


def terms(x, lane):
    first = x.astype(jnp.bfloat16).astype(jnp.float32)
    second = (x - first).astype(jnp.bfloat16).astype(jnp.float32)
    return jnp.where(lane % 3 == 0, first, jnp.where(lane % 3 == 1, second, x - first - second))


def place_rows(place_ref, s, refs, dst_ref, lane=0):
    at = 0
    for ref in refs:
        for j in range(ref.shape[0]):
            for w in range(2):
                row = pl.multiple_of(place_ref[s, at] * BLK, BLK)
                dst_ref[pl.ds(row, BLK), lane:lane + 128] = ref[j, 0, w]
                at += 1


def fwd_kernel(place_ref, own_ref, q_ref, *refs, blocks, n):
    k_refs, v_refs, (o_ref, ext_ref, ks, vs, scr, acc) = refs[:n], refs[n:2 * n], refs[2 * n:]
    s, pair = pl.program_id(0), pl.program_id(1)

    @pl.when((s == 0) & (pair == 0))
    def _():
        vs[:, 128:256] = jnp.ones((blocks * BLK, 128), jnp.bfloat16)

    @pl.when(pair == 0)
    def _():
        ext_ref[...] = jnp.zeros_like(ext_ref)

    place_rows(place_ref, s, k_refs, ks)
    place_rows(place_ref, s, v_refs, vs)
    for w in range(2):
        rows = slice(w * BLK, (w + 1) * BLK)
        pos = own_ref[s, w]
        last = pos // CB
        qs = split_heads(q_ref[0, rows, :] * jnp.bfloat16(SCALE))

        def tiles_max(run, sc):
            for t in range(CB):
                run = jnp.maximum(run, sc[:, t * 128:(t + 1) * 128])
            return run

        def score(c, run):
            at = pl.multiple_of(c * CH, CH)
            sc = nt(qs, ks[pl.ds(at, CH), :])
            scr[c] = sc
            return tiles_max(run, sc)

        run = lax.fori_loop(0, last, score, jnp.full((2 * BLK, 128), NEG, jnp.float32))
        at = pl.multiple_of(last * CH, CH)
        sc = nt(qs, ks[pl.ds(at, CH), :])
        qpos = pos * BLK + row_of((2 * BLK, CH)) % BLK
        kpos = last * CH + lane_of((2 * BLK, CH))
        sc = jnp.where(kpos <= qpos, sc, NEG)
        scr[last] = sc
        run = tiles_max(run, sc)
        top = jnp.broadcast_to(jnp.max(run, axis=1, keepdims=True), (2 * BLK, 128))
        topc = jnp.concatenate([top] * CB, axis=1)
        acc[...] = jnp.zeros_like(acc)

        def weigh(c, carry):
            at = pl.multiple_of(c * CH, CH)
            p = jnp.exp(scr[c] - topc).astype(jnp.bfloat16)
            acc[...] += nn(p, vs[pl.ds(at, CH), :])
            return carry

        lax.fori_loop(0, last + 1, weigh, 0)
        total = acc[:, 128:256]
        o_ref[0, rows, :] = join_heads(acc[:, 0:128] / total).astype(jnp.bfloat16)
        lane = lane_of((2 * BLK, 128))
        mine = jnp.where(own_lanes(pair), terms(-(top + jnp.log(total)), lane), 0.0)
        ext_ref[0, rows, :] = (ext_ref[0, rows, :].astype(jnp.float32) + mine[:BLK] + mine[BLK:]).astype(jnp.bfloat16)


def dq_kernel(place_ref, own_ref, q_ref, do_ref, qx_ref, dox_ref, c_ref, a_ref, b_ref, *refs, blocks, n):
    k_refs, v_refs, (dq_ref, ks, vs, acc) = refs[:n], refs[n:2 * n], refs[2 * n:]
    s, pair = pl.program_id(0), pl.program_id(1)

    @pl.when((s == 0) & (pair == 0))
    def _():
        ks[:, 128:256] = jnp.ones((blocks * BLK, 128), jnp.bfloat16)
        vs[:, 128:256] = jnp.ones((blocks * BLK, 128), jnp.bfloat16)

    place_rows(place_ref, s, k_refs, ks)
    place_rows(place_ref, s, v_refs, vs)
    mine = own_lanes(pair)
    for w in range(2):
        rows = slice(w * BLK, (w + 1) * BLK)
        pos = own_ref[s, w]
        last = pos // CB

        def extend(tile, ext):
            both = jnp.concatenate([ext, ext], axis=0)
            return jnp.concatenate([split_heads(tile), jnp.where(mine, both, jnp.zeros_like(both))], axis=1)

        qs = extend(q_ref[0, rows, :] * jnp.bfloat16(SCALE), qx_ref[0, rows, :])
        dos = extend(do_ref[0, rows, :], dox_ref[0, rows, :])
        acc[...] = jnp.zeros_like(acc)

        def step(c, mask):
            at = pl.multiple_of(c * CH, CH)
            p = jnp.exp(nt(qs, ks[pl.ds(at, CH), :]))
            if mask is not None:
                p = jnp.where(mask, p, 0.0)
            ds = (p * nt(dos, vs[pl.ds(at, CH), :])).astype(jnp.bfloat16)
            acc[...] += nn(ds, ks[pl.ds(at, CH), 0:128])

        def body(c, carry):
            step(c, None)
            return carry

        lax.fori_loop(0, last, body, 0)
        qpos = pos * BLK + row_of((2 * BLK, CH)) % BLK
        kpos = last * CH + lane_of((2 * BLK, CH))
        step(last, kpos <= qpos)
        grad = join_heads(acc[...]) * SCALE
        dq_ref[0, rows, :] = turn(grad, c_ref[rows], a_ref[rows], b_ref[rows], -1.0).astype(jnp.bfloat16)


def dkv_kernel(place_ref, own_ref, k_ref, v_ref, c_ref, a_ref, b_ref, *refs, blocks, n, lead):
    q_refs, do_refs, qx_refs, dox_refs = (refs[i * n:(i + 1) * n] for i in range(4))
    dk_ref, dv_ref, qs, dos, acck, accv = refs[4 * n:]
    s, pair = pl.program_id(0) + lead, pl.program_id(1)
    place_rows(place_ref, s, q_refs, qs)
    place_rows(place_ref, s, do_refs, dos)

    @pl.when(pair == 0)
    def _():
        place_rows(place_ref, s, qx_refs, qs, 128)
        place_rows(place_ref, s, dox_refs, dos, 128)

    ones = own_lanes(pair).astype(jnp.bfloat16)
    for w in range(2):
        rows = slice(w * BLK, (w + 1) * BLK)
        pos = own_ref[s, w]
        first = pos // CB
        kw = jnp.concatenate([split_heads(k_ref[0, 0, rows, :] * jnp.bfloat16(SCALE)), ones], axis=1)
        vw = jnp.concatenate([split_heads(v_ref[0, 0, rows, :]), ones], axis=1)
        acck[...] = jnp.zeros_like(acck)
        accv[...] = jnp.zeros_like(accv)

        def step(c, mask):
            at = pl.multiple_of(c * CH, CH)
            p = jnp.exp(nt(kw, qs[pl.ds(at, CH), :]))
            if mask is not None:
                p = jnp.where(mask, p, 0.0)
            accv[...] += nn(p.astype(jnp.bfloat16), dos[pl.ds(at, CH), 0:128])
            ds = (p * nt(vw, dos[pl.ds(at, CH), :])).astype(jnp.bfloat16)
            acck[...] += nn(ds, qs[pl.ds(at, CH), 0:128])

        def body(c, carry):
            step(c, None)
            return carry

        kpos = pos * BLK + row_of((2 * BLK, CH)) % BLK
        qpos = first * CH + lane_of((2 * BLK, CH))
        step(first, kpos <= qpos)
        lax.fori_loop(first + 1, blocks // CB, body, 0)
        grad = join_heads(acck[...]) * SCALE
        dk_ref[0, rows, :] = turn(grad, c_ref[rows], a_ref[rows], b_ref[rows], -1.0).astype(jnp.bfloat16)
        dv_ref[0, rows, :] = join_heads(accv[...]).astype(jnp.bfloat16)


OWN = pl.BlockSpec((1, 2 * BLK, 128), lambda s, h, *_: (s, 0, h))
EXT = pl.BlockSpec((1, 2 * BLK, 128), lambda s, h, *_: (s, 0, 0))


def table(lead=0):
    return pl.BlockSpec((2 * BLK, 128), lambda s, h, *_: (s + lead, 0))


def piece(x, first=0, lane=None, lead=0):
    return pl.BlockSpec((1, 1, 2, BLK, 128), lambda s, h, *_: (first, s + lead, 0, 0, h if lane is None else lane))


def attention_call(kernel, name, mats, seqs, pairs, blocks, in_specs, out_specs, out_shape, scratch, args):
    work = seqs * pairs * 2 * 2 * BLK * blocks * BLK // 2
    return pl.pallas_call(
        kernel,
        grid_spec=pltpu.PrefetchScalarGridSpec(
            num_scalar_prefetch=2, grid=(seqs, pairs), in_specs=in_specs, out_specs=out_specs, scratch_shapes=scratch),
        out_shape=out_shape,
        compiler_params=pltpu.CompilerParams(vmem_limit_bytes=40 * 2**20),
        cost_estimate=pl.CostEstimate(flops=work * 512 * mats, bytes_accessed=4 * seqs * pairs * blocks * BLK * 128, transcendentals=work),
        name=name,
    )(*args)


def rows_of(blocks, lanes):
    return pltpu.VMEM((blocks * BLK, lanes), jnp.bfloat16)


def acc_of(lanes):
    return pltpu.VMEM((2 * BLK, lanes), jnp.float32)


def attend(place, own, q, keys, values):
    seqs, pairs, blocks = q.shape[0], q.shape[2] // 128, place.shape[1]
    return attention_call(
        functools.partial(fwd_kernel, blocks=blocks, n=len(keys)), "attend", 2, seqs, pairs, blocks,
        [OWN] + [piece(*e) for e in keys + values], [OWN, EXT],
        [jax.ShapeDtypeStruct(q.shape, jnp.bfloat16), jax.ShapeDtypeStruct(q.shape[:2] + (128,), jnp.bfloat16)],
        [rows_of(blocks, 128), rows_of(blocks, 256), pltpu.VMEM((blocks // CB, 2 * BLK, CH), jnp.float32), acc_of(256)],
        [place, own, q] + [e[0] for e in keys + values])


def query_grad(place, own, q, do, q_ext, do_ext, tabs, keys, values):
    seqs, pairs, blocks = q.shape[0], q.shape[2] // 128, place.shape[1]
    return attention_call(
        functools.partial(dq_kernel, blocks=blocks, n=len(keys)), "query_grad", 3, seqs, pairs, blocks,
        [OWN, OWN, EXT, EXT] + [table()] * 3 + [piece(*e) for e in keys + values], OWN,
        jax.ShapeDtypeStruct(q.shape, jnp.bfloat16),
        [rows_of(blocks, 256), rows_of(blocks, 256), acc_of(128)],
        [place, own, q, do, q_ext, do_ext, *tabs] + [e[0] for e in keys + values])


def key_value_grad(place, own, kv, tabs, queries, grads, lead, count):
    pairs, blocks = kv.shape[3] // 128, place.shape[1]
    shape = (count,) + kv.shape[2:]
    both = queries + grads

    def own_part(i):
        return pl.BlockSpec((1, 1, 2 * BLK, 128), lambda s, h, *_: (i, s + lead, 0, h))

    return attention_call(
        functools.partial(dkv_kernel, blocks=blocks, n=len(queries), lead=lead), "key_value_grad", 4, count, pairs, blocks,
        [own_part(0), own_part(1)] + [table(lead)] * 3 + [piece(x, lead=lead) for x in both]
        + [piece(x, lane=pairs, lead=lead) for x in both], [OWN, OWN],
        [jax.ShapeDtypeStruct(shape, jnp.bfloat16)] * 2,
        [rows_of(blocks, 256), rows_of(blocks, 256), acc_of(128), acc_of(128)],
        [place, own, kv, kv, *tabs] + both * 2)


import math
from jax.sharding import PartitionSpec as P

HEAD_DIM = 64
ROT = 16
SEQS = 4
EPS = 1e-05
F32 = jnp.float32
BF16 = jnp.bfloat16


def rc(left, right):
    return lax.dot_general(left, right, (((0,), (0,)), ((), ())), preferred_element_type=F32)


def layer_stats(values, gain, shift):
    mean = jnp.mean(values, axis=-1, keepdims=True)
    centred = values - mean
    inverse = lax.rsqrt(jnp.mean(centred * centred, axis=-1, keepdims=True) + EPS)
    unit = centred * inverse
    return unit * gain + shift, unit, inverse


def layer_back(grad, unit, inverse, gain):
    scaled = grad * gain
    grad_in = inverse * (
        scaled
        - jnp.mean(scaled, axis=-1, keepdims=True)
        - unit * jnp.mean(scaled * unit, axis=-1, keepdims=True)
    )
    return grad_in, jnp.sum(grad * unit, axis=0), jnp.sum(grad, axis=0)


def rotary_tables(positions):
    half = ROT // 2
    dim = jnp.arange(2 * HEAD_DIM) % HEAD_DIM
    freq = jnp.where(dim < ROT, 10000.0 ** (-2.0 * (dim % half).astype(F32) / ROT), 0.0)
    angles = positions.astype(F32)[:, None] * freq[None, :]
    sin = jnp.sin(angles)
    return jnp.cos(angles), jnp.where(dim < half, sin, 0.0), jnp.where(dim < half, 0.0, sin)


def turn(x, ctab, above, below, sign):
    up = pltpu.roll(x, 128 - ROT // 2, axis=1)
    down = pltpu.roll(x, ROT // 2, axis=1)
    return x * ctab + sign * (down * below - up * above)


def project_kernel(h_ref, wq_ref, wk_ref, wv_ref, bias_ref, c_ref, a_ref, b_ref, q_ref, kv_ref):
    h = h_ref[...]
    width = wq_ref.shape[1]
    tabs = c_ref[...], a_ref[...], b_ref[...]
    for at, (w_ref, out) in enumerate(((wq_ref, q_ref.at[0]), (wk_ref, kv_ref.at[0, 0]), (wv_ref, kv_ref.at[1, 0]))):
        lin = nn(h, w_ref[...]) + bias_ref[at:at + 1, :]
        for p in range(width // 128):
            part = lin[:, p * 128:(p + 1) * 128]
            if at < 2:
                part = turn(part, *tabs, 1.0)
            out[:, p * 128:(p + 1) * 128] = part.astype(BF16)


def project(rows, wq, wk, wv, bias, tabs):
    total, depth = rows.shape
    width = wq.shape[1]
    step = total // SEQS
    weight = pl.BlockSpec((depth, width), lambda i: (0, 0))
    table = pl.BlockSpec((step, 128), lambda i: (i, 0))
    return pl.pallas_call(
        project_kernel,
        grid=(SEQS,),
        in_specs=[pl.BlockSpec((step, depth), lambda i: (i, 0)), weight, weight, weight,
                  pl.BlockSpec((3, width), lambda i: (0, 0)), table, table, table],
        out_specs=[pl.BlockSpec((1, step, width), lambda i: (i, 0, 0)),
                   pl.BlockSpec((2, 1, step, width), lambda i: (0, i, 0, 0))],
        out_shape=[jax.ShapeDtypeStruct((SEQS, step, width), BF16), jax.ShapeDtypeStruct((2, SEQS, step, width), BF16)],
        compiler_params=pltpu.CompilerParams(vmem_limit_bytes=48 * 2**20),
        cost_estimate=pl.CostEstimate(flops=6 * total * depth * width, bytes_accessed=6 * depth * width, transcendentals=0),
        name="project",
    )(rows, wq, wk, wv, bias, *tabs)


def mlp_kernel(h_ref, dy_ref, gate_ref, up_ref, down_ref, act_ref, *grad_refs):
    width = gate_ref.shape[1]
    gate = nn(h_ref[...], gate_ref[...])
    up = nn(h_ref[...], up_ref[...])
    grad = nt(dy_ref[...], down_ref[...])
    sig = 1.0 / (1.0 + jnp.exp(-gate))
    silu = gate * sig
    act_ref[...] = (silu * up).astype(BF16)
    outs = grad_refs if len(grad_refs) == 2 else (grad_refs[0].at[:, :width], grad_refs[0].at[:, width:])
    outs[0][...] = (grad * up * (sig + silu * (1.0 - sig))).astype(BF16)
    outs[1][...] = (grad * silu).astype(BF16)


def mlp(rows, dy, gate_w, up_w, down_w, step=256):
    total, depth = rows.shape
    width = gate_w.shape[1]
    joined = width % 128 == 0
    block = pl.BlockSpec((step, depth), lambda i: (i, 0))

    def whole(x):
        return pl.BlockSpec(x.shape, lambda i: (0, 0), pipeline_mode=pl.Buffered(1))

    def out(n):
        return pl.BlockSpec((step, n), lambda i: (i, 0)), jax.ShapeDtypeStruct((total, n), BF16)

    outs = [out(width), out(2 * width)] if joined else [out(width)] * 3
    act, *grads = pl.pallas_call(
        mlp_kernel,
        grid=(total // step,),
        in_specs=[block, block, whole(gate_w), whole(up_w), whole(down_w)],
        out_specs=[o[0] for o in outs],
        out_shape=[o[1] for o in outs],
        compiler_params=pltpu.CompilerParams(vmem_limit_bytes=56 * 2**20),
        cost_estimate=pl.CostEstimate(flops=6 * total * depth * width, bytes_accessed=6 * depth * width + 10 * total * depth,
                                      transcendentals=total * width),
        name="mlp",
    )(rows, dy, gate_w, up_w, down_w)
    return act, grads[0] if joined else jnp.concatenate(grads, axis=1)


def ctx_swap(x, mask):
    n = lax.axis_size("ctx")
    return lax.ppermute(x, "ctx", [(i, i ^ mask) for i in range(n)])


def add16(a, b):
    return (a.astype(F32) + b.astype(F32)).astype(BF16)


def after(x, *deps):
    if not jax.tree.leaves(deps):
        return x
    return lax.optimization_barrier((x, deps))[0]


def half_of(x, bit, mine):
    side = (lax.axis_index("ctx") >> bit) & 1
    r = x.shape[0] // 2
    return lax.dynamic_slice_in_dim(x, (side if mine else 1 - side) * r, r, 0)


def weight_grad(part):
    core = lax.axis_index("ctx") & 1
    got = ctx_swap(part(1 - core).astype(BF16), 1)
    gate = yield
    half = (part(core) + after(got, gate).astype(F32)).astype(BF16)
    bits = list(range(1, int(math.log2(lax.axis_size("ctx")))))
    orders = [bits, bits[::-1]]
    r = half.shape[0] // 2
    streams = [half[:r], half[r:]]
    gate = yield streams
    for i in range(len(bits)):
        streams = after(streams, gate)
        got = [ctx_swap(half_of(x, o[i], False), 1 << o[i]) for x, o in zip(streams, orders)]
        gate = yield
        streams, got = after((streams, got), gate)
        streams = [add16(half_of(x, o[i], True), g) for x, o, g in zip(streams, orders, got)]
        gate = yield streams
    for i in reversed(range(len(bits))):
        streams = after(streams, gate)
        got = [ctx_swap(x, 1 << o[i]) for x, o in zip(streams, orders)]
        gate = yield
        streams, got = after((streams, got), gate)
        streams = [
            jnp.where(((lax.axis_index("ctx") >> o[i]) & 1) == 0, jnp.concatenate([x, g]), jnp.concatenate([g, x]))
            for x, o, g in zip(streams, orders, got)
        ]
        if i == 0:
            streams = jnp.concatenate(streams)
        gate = yield streams
    streams = after(streams, gate)
    other = ctx_swap(streams, 1)
    gate = yield
    yield after((streams, other), gate)


def begin(*args):
    chain = weight_grad(*args)
    next(chain)
    return chain


def take(chain, gate=None):
    return chain.send(gate)


def go(chain, gate=None):
    chain.send(gate)


def take_extra(chain):
    for _ in range(2 * int(math.log2(lax.axis_size("ctx"))) - 6):
        go(chain)
        take(chain)


def unpack_rows_kernel(core_ref, half_ref, other_ref, *out_refs):
    def put(src):
        at = 0
        for out in out_refs:
            out[...] = src[:, at:at + out.shape[1]].astype(F32)
            at += out.shape[1]

    @pl.when(pl.program_id(0) == core_ref[0])
    def _():
        put(half_ref)

    @pl.when(pl.program_id(0) != core_ref[0])
    def _():
        put(other_ref)


def unpack_rows(half, other, parts):
    r, c = half.shape
    step = math.gcd(r, 256)
    blocks = r // step
    core = lax.axis_index("ctx") & 1

    def mine(i, j, core_ref):
        return jnp.where(i == core_ref[0], j, jnp.where(core_ref[0] == 0, blocks - 1, 0)), 0

    def theirs(i, j, core_ref):
        return jnp.where(i != core_ref[0], j, jnp.where(core_ref[0] == 1, blocks - 1, 0)), 0

    return pl.pallas_call(
        unpack_rows_kernel,
        grid_spec=pltpu.PrefetchScalarGridSpec(
            num_scalar_prefetch=1, grid=(2, blocks),
            in_specs=[pl.BlockSpec((step, c), mine), pl.BlockSpec((step, c), theirs)],
            out_specs=[pl.BlockSpec((step, c // parts), lambda i, j, _: (i * blocks + j, 0))] * parts),
        out_shape=[jax.ShapeDtypeStruct((2 * r, c // parts), F32)] * parts,
        compiler_params=pltpu.CompilerParams(vmem_limit_bytes=40 * 2**20),
        cost_estimate=pl.CostEstimate(flops=0, bytes_accessed=12 * r * c, transcendentals=0),
        name="unpack_rows",
    )(core[None], half, other)


def columns(x, which):
    w = x.shape[1] // 2
    return lax.dynamic_slice_in_dim(x, which * w, w, 1)


def unpack_cols_kernel(core_ref, half_ref, other_ref, out_ref):
    c = half_ref.shape[1]
    core = core_ref[0]
    out_ref[:, pl.ds(pl.multiple_of(core * c, 128), c)] = half_ref[...].astype(F32)
    out_ref[:, pl.ds(pl.multiple_of((1 - core) * c, 128), c)] = other_ref[...].astype(F32)


def unpack_cols(half, other):
    r, c = half.shape
    step = math.gcd(r, 256)
    block = pl.BlockSpec((step, c), lambda i, _: (i, 0))
    return pl.pallas_call(
        unpack_cols_kernel,
        grid_spec=pltpu.PrefetchScalarGridSpec(
            num_scalar_prefetch=1, grid=(r // step,), in_specs=[block, block],
            out_specs=pl.BlockSpec((step, 2 * c), lambda i, _: (i, 0))),
        out_shape=jax.ShapeDtypeStruct((r, 2 * c), F32),
        compiler_params=pltpu.CompilerParams(vmem_limit_bytes=40 * 2**20),
        cost_estimate=pl.CostEstimate(flops=0, bytes_accessed=12 * r * c, transcendentals=0),
        name="unpack_cols",
    )((lax.axis_index("ctx") & 1)[None], half, other)


def all_rows(x):
    return lax.all_gather(x, "tp", axis=0, tiled=True)


def tp_shift(x, d):
    n = lax.axis_size("tp")
    return lax.ppermute(x, "tp", [(i, (i + d) % n) for i in range(n)])


def part_of(x, d, axis):
    n = lax.axis_size("tp")
    w = x.shape[axis] // n
    return lax.dynamic_slice_in_dim(x, (lax.axis_index("tp") + d) % n * w, w, axis)


def exchange(x, split, join):
    n, me = lax.axis_size("tp"), lax.axis_index("tp")
    w = x.shape[join]
    shape = list(x.shape)
    shape[split] //= n
    shape[join] *= n
    out = jnp.zeros(shape, x.dtype)
    for d in range(n):
        got = tp_shift(part_of(x, d, split), d) if d else part_of(x, 0, split)
        out = lax.dynamic_update_slice_in_dim(out, got, (me + n - d) % n * w, join)
    return out


def sum_rows(x):
    return lax.psum_scatter(x, "tp", scatter_dimension=0, tiled=True)


def gather_pair(kv):
    n = lax.axis_size("ctx")
    held = {0: ((kv, 0), (kv, 1))}
    for bit in range(1, int(math.log2(n))):
        mask = 1 << bit
        for j in list(held):
            if j == 0:
                got = ctx_swap(kv, mask)
                held[mask] = (got, 0), (got, 1)
            elif mask == 4 and j == 2:
                held[6] = (ctx_swap(held[2][0][0][0:1], 4), 0), (ctx_swap(held[4][1][0][1:2], 2), 0)
            else:
                (k, i), (v, t) = held[j]
                if k is v:
                    got = ctx_swap(k, mask)
                    held[j | mask] = (got, i), (got, t)
                else:
                    held[j | mask] = (ctx_swap(k, mask), i), (ctx_swap(v, mask), t)
    for j in list(held):
        (k, i), (v, t) = held[j]
        got = ctx_swap(k, 1)
        held[j | 1] = (got, i), (got if k is v else ctx_swap(v, 1), t)
    return [held[j][0] for j in range(n)], [held[j][1] for j in range(n)]


def gather_other(x):
    held = {0: x, 1: ctx_swap(x, 1)}
    for j in range(2, lax.axis_size("ctx"), 2):
        held[j] = ctx_swap(x, j)
    return held


def gather_cores(held, gate=None):
    n = lax.axis_size("ctx")
    for j in range(2, n, 2):
        held[j + 1] = ctx_swap(after(held[j], gate), 1)
    return [held[j] for j in range(n)]


def sum_over_all(x):
    for axis in ("ctx", "tp"):
        n = lax.axis_size(axis)
        for bit in range(int(math.log2(n))):
            x = x + lax.ppermute(x, axis, [(i, i ^ (1 << bit)) for i in range(n)])
            yield x
    while True:
        yield x


def gather_tp(x):
    n, me = lax.axis_size("tp"), lax.axis_index("tp")
    out = jnp.zeros((n,) + x.shape, x.dtype)
    for d in range(n):
        got = lax.ppermute(x, "tp", [(i, (i + d) % n) for i in range(n)]) if d else x
        out = lax.dynamic_update_index_in_dim(out, got, (me + n - d) % n, 0)
    return out


def local(tokens, cotangent, block_order, gain_one, shift_one, query_w, key_w, value_w, query_b, key_b, value_b,
          output_w, gain_two, shift_two, gate_w, up_w, down_w):
    heads = key_b.shape[0]
    width = heads * HEAD_DIM
    n_ctx, n_tp = lax.axis_size("ctx"), lax.axis_size("tp")
    ctx = lax.axis_index("ctx")
    own = lax.dynamic_slice_in_dim(block_order, 2 * ctx, 2, 1)
    picked = (jnp.arange(n_ctx, dtype=jnp.int32) ^ ctx)[:, None] == jnp.arange(n_ctx, dtype=jnp.int32)[None, :]
    by_ctx = block_order.reshape(SEQS, 1, n_ctx, 2)
    place = jnp.sum(jnp.where(picked[None, :, :, None], by_ctx, 0), axis=2).astype(jnp.int32).reshape(SEQS, 2 * n_ctx)
    positions = (own[:, :, None] * BLK + jnp.arange(BLK, dtype=jnp.int32)).reshape(-1)
    tabs = rotary_tables(positions)

    x = tokens.astype(F32)
    normed_one, unit_one, inverse_one = layer_stats(x, gain_one, shift_one)
    rows_one = all_rows(normed_one.astype(BF16))
    key_bias = jnp.concatenate([key_b, jnp.zeros((heads, HEAD_DIM - ROT), F32)], axis=1).reshape(-1)
    bias = jnp.stack([query_b, key_bias, value_b])
    q, kv = project(rows_one, query_w, key_w, value_w, bias, tabs)
    keys, values = gather_pair(kv.reshape(2, SEQS, 2, BLK, width))
    arrived = [e[0] for e in keys + values]

    rows_w = output_w.shape[0] // n_ctx
    part = lax.dynamic_slice_in_dim(output_w, ctx * rows_w, rows_w, 0)
    part = gather_tp(after(part, kv))
    dy_rows = all_rows(after(cotangent, rows_one))
    whole_w = lax.all_gather(after(part, arrived, dy_rows), "ctx", axis=1).reshape(n_tp * output_w.shape[0], -1)

    attn, q_ext = attend(place, own, q, keys, values)
    attn_rows = attn.reshape(-1, width)
    attn_own = exchange(attn_rows, 0, 1)
    mixed = x + nn(attn_own, whole_w)
    normed_two, unit_two, inverse_two = layer_stats(mixed, gain_two, shift_two)
    rows_two = all_rows(after(normed_two.astype(BF16), dy_rows, whole_w))
    shape = (1, SEQS, 2, BLK, width + 128)
    queries = gather_cores(gather_other(after(jnp.concatenate([q, q_ext], axis=2).reshape(shape), attn_own)))
    rows_two = after(rows_two, queries)

    act, grad_gu = mlp(rows_two, dy_rows, gate_w, up_w, down_w)
    ff = gate_w.shape[1]
    part_two = (nt(grad_gu[:, :ff], gate_w) + nt(grad_gu[:, ff:], up_w)).astype(BF16)
    grad_two = sum_rows(part_two)
    act, rows_two, dy_rows, grad_gu = after((act, rows_two, dy_rows, grad_gu), part_two)
    gu = begin(lambda core: rc(columns(rows_two, core), grad_gu))
    dw = begin(lambda core: rc(act, columns(dy_rows, core)))
    held = take(gu)
    go(gu)
    down = nn(after(act, held), down_w).astype(BF16)
    held = take(dw, held), take(gu, down)
    go(gu)
    go(dw, held)
    grad_two = after(grad_two, held)

    norm_two, grad_gain_two, grad_shift_two = layer_back(grad_two.astype(F32), unit_two, inverse_two, gain_two)
    grad_mixed = cotangent.astype(F32) + norm_two
    branch_own = grad_mixed.astype(BF16)
    grad_attn = nt(branch_own, whole_w).astype(BF16)
    grad_attn = after(grad_attn, take(gu), take(dw))
    go(gu)
    go(dw)
    grad_attn = exchange(grad_attn, 1, 0)
    branch = all_rows(after(branch_own, grad_attn))
    out_tokens = (mixed + sum_rows(after(down, grad_attn)).astype(F32)).astype(BF16)
    lane = jnp.arange(128)[None, :]
    ind = ((jnp.arange(width) // HEAD_DIM)[:, None] == lane // 3).astype(F32)
    delta = lax.dot_general(grad_attn.astype(F32) * attn_rows.astype(F32), ind, (((1,), (0,)), ((), ())),
                            precision=lax.Precision.HIGHEST, preferred_element_type=F32)
    do_ext = terms(-delta, lane).astype(BF16)
    do_sent = jnp.concatenate([grad_attn, do_ext], axis=1).reshape(shape)
    grads = gather_other(after(do_sent, take(gu, grad_attn), take(dw, grad_attn)))
    grad_q = query_grad(place, own, q, grad_attn.reshape(q.shape), q_ext, do_ext.reshape(q_ext.shape), tabs, keys, values)
    grad_q = grad_q.reshape(-1, width)
    q_part = nt(grad_q, query_w)
    grads = gather_cores(grads, q_part)
    go(gu, grads)
    go(dw, grads)
    first = key_value_grad(place, own, kv, tabs, queries, grads, 0, SEQS // 2)
    grads = after(grads, take(dw, first))
    go(dw)
    second = key_value_grad(place, own, kv, tabs, queries, grads, SEQS // 2, SEQS // 2)
    grad_k, grad_v = (jnp.concatenate(pair).reshape(-1, width) for pair in zip(first, second))
    part_one = q_part + nt(grad_k, key_w) + nt(grad_v, value_w)
    part_sent = part_one.astype(BF16)
    grad_one = sum_rows(part_sent)

    rows_one, branch, grad_q, grad_k, grad_v = after((rows_one, branch, grad_q, grad_k, grad_v), part_sent)
    grad_qkv = jnp.concatenate([grad_q, grad_k, grad_v], axis=1)
    chain = begin(lambda core: rc(columns(rows_one, core), grad_qkv))
    take(gu, part_sent)
    take_extra(gu)
    go(gu)
    unit_rows = (rows_one.astype(F32) - shift_one) / gain_one
    bias_grad = jnp.sum(grad_qkv.astype(F32), axis=0)
    tp_row = (jnp.arange(n_tp) == lax.axis_index("tp"))[:, None]
    small = jnp.concatenate([
        jnp.sum(part_one * unit_rows, axis=0), jnp.sum(part_one, axis=0), grad_gain_two, grad_shift_two,
        jnp.where(tp_row, bias_grad[None, :], 0.0).reshape(-1)])
    held = take(chain)
    go(chain)
    take(dw, held)
    take_extra(dw)
    go(dw)
    grad_output_w = rc(attn_rows, after(branch, held)).astype(BF16)
    sums = sum_over_all(after(small, held).reshape(-1, 1024))
    grad_gate_w, grad_up_w = unpack_rows(*take(gu, held), 2)
    held = take(chain, (grad_gate_w, grad_output_w))
    go(chain)
    grad_output_w = lax.psum(grad_output_w, "ctx")
    grad_down_w = unpack_cols(*take(dw, held))
    held = take(chain, grad_down_w)
    go(chain)
    held = take(chain, held)
    go(chain)
    take(chain)
    take_extra(chain)
    go(chain)
    for _ in range(9):
        small = next(sums)
    depth = x.shape[1]
    small = small.reshape(-1)
    norms = small[:4 * depth].reshape(4, depth)
    bias_sum = jnp.sum(jnp.where(tp_row, small[4 * depth:].reshape(n_tp, -1), 0.0), axis=0)
    grad_query_w, grad_key_w, grad_value_w = unpack_rows(*take(chain), 3)
    grad_output_w = grad_output_w.astype(F32)
    norm_one, _, _ = layer_back(grad_one.astype(F32), unit_one, inverse_one, gain_one)
    grad_tokens = (grad_mixed + norm_one).astype(BF16)
    return (
        out_tokens, grad_tokens, norms[0], norms[1], grad_query_w, grad_key_w, grad_value_w,
        bias_sum[:width], bias_sum[width:2 * width].reshape(heads, HEAD_DIM)[:, :ROT], bias_sum[2 * width:],
        grad_output_w, norms[2], norms[3], grad_gate_w, grad_up_w, grad_down_w,
    )


def solution(mesh):
    rows, cols, depth, flat = P(("ctx", "tp"), None), P(None, "tp"), P("tp", None), P("tp")
    in_specs = (rows, rows, P(), P(), P(), cols, cols, cols, flat, depth, flat, depth, P(), P(), cols, cols, depth)
    out_specs = (rows, rows, P(), P(), cols, cols, cols, flat, depth, flat, depth, P(), P(), cols, cols, depth)
    return jax.shard_map(local, mesh=mesh, in_specs=in_specs, out_specs=out_specs, check_vma=False)
```

```python
import functools
import jax, jax.numpy as jnp
from jax import lax
from jax.experimental import pallas as pl
from jax.experimental.pallas import tpu as pltpu

BLK = 128
CB = 4
CH = BLK * CB
NEG = -1e30
SCALE = 0.125


def nt(a, b):
    return lax.dot_general(a, b, (((1,), (1,)), ((), ())), preferred_element_type=jnp.float32)


def nn(a, b):
    return lax.dot_general(a, b, (((1,), (0,)), ((), ())), preferred_element_type=jnp.float32)


def lane_of(shape):
    return lax.broadcasted_iota(jnp.int32, shape, 1)


def row_of(shape):
    return lax.broadcasted_iota(jnp.int32, shape, 0)


def split_heads(x):
    low = lane_of(x.shape) < 64
    zero = jnp.zeros_like(x)
    return jnp.concatenate([jnp.where(low, x, zero), jnp.where(low, zero, x)], axis=0)


def join_heads(x):
    low = lane_of((BLK, 128)) < 64
    return jnp.where(low, x[:BLK], x[BLK:])


def own_lanes(pair):
    shape = (2 * BLK, 128)
    return lane_of(shape) // 3 == 2 * pair + row_of(shape) // BLK


def terms(x, lane):
    first = x.astype(jnp.bfloat16).astype(jnp.float32)
    second = (x - first).astype(jnp.bfloat16).astype(jnp.float32)
    return jnp.where(lane % 3 == 0, first, jnp.where(lane % 3 == 1, second, x - first - second))


def place_rows(place_ref, s, refs, dst_ref, lane=0):
    at = 0
    for ref in refs:
        for j in range(ref.shape[0]):
            for w in range(2):
                row = pl.multiple_of(place_ref[s, at] * BLK, BLK)
                dst_ref[pl.ds(row, BLK), lane:lane + 128] = ref[j, 0, w]
                at += 1


def fwd_kernel(place_ref, own_ref, q_ref, *refs, blocks, n):
    k_refs, v_refs, (o_ref, ext_ref, ks, vs, scr, acc) = refs[:n], refs[n:2 * n], refs[2 * n:]
    s, pair = pl.program_id(0), pl.program_id(1)

    @pl.when((s == 0) & (pair == 0))
    def _():
        vs[:, 128:256] = jnp.ones((blocks * BLK, 128), jnp.bfloat16)

    @pl.when(pair == 0)
    def _():
        ext_ref[...] = jnp.zeros_like(ext_ref)

    place_rows(place_ref, s, k_refs, ks)
    place_rows(place_ref, s, v_refs, vs)
    for w in range(2):
        rows = slice(w * BLK, (w + 1) * BLK)
        pos = own_ref[s, w]
        last = pos // CB
        qs = split_heads(q_ref[0, rows, :] * jnp.bfloat16(SCALE))

        def tiles_max(run, sc):
            for t in range(CB):
                run = jnp.maximum(run, sc[:, t * 128:(t + 1) * 128])
            return run

        def score(c, run):
            at = pl.multiple_of(c * CH, CH)
            sc = nt(qs, ks[pl.ds(at, CH), :])
            scr[c] = sc
            return tiles_max(run, sc)

        run = lax.fori_loop(0, last, score, jnp.full((2 * BLK, 128), NEG, jnp.float32))
        at = pl.multiple_of(last * CH, CH)
        sc = nt(qs, ks[pl.ds(at, CH), :])
        qpos = pos * BLK + row_of((2 * BLK, CH)) % BLK
        kpos = last * CH + lane_of((2 * BLK, CH))
        sc = jnp.where(kpos <= qpos, sc, NEG)
        scr[last] = sc
        run = tiles_max(run, sc)
        top = jnp.broadcast_to(jnp.max(run, axis=1, keepdims=True), (2 * BLK, 128))
        topc = jnp.concatenate([top] * CB, axis=1)
        acc[...] = jnp.zeros_like(acc)

        def weigh(c, carry):
            at = pl.multiple_of(c * CH, CH)
            p = jnp.exp(scr[c] - topc).astype(jnp.bfloat16)
            acc[...] += nn(p, vs[pl.ds(at, CH), :])
            return carry

        lax.fori_loop(0, last + 1, weigh, 0)
        total = acc[:, 128:256]
        o_ref[0, rows, :] = join_heads(acc[:, 0:128] / total).astype(jnp.bfloat16)
        lane = lane_of((2 * BLK, 128))
        mine = jnp.where(own_lanes(pair), terms(-(top + jnp.log(total)), lane), 0.0)
        ext_ref[0, rows, :] = (ext_ref[0, rows, :].astype(jnp.float32) + mine[:BLK] + mine[BLK:]).astype(jnp.bfloat16)


def dq_kernel(place_ref, own_ref, q_ref, do_ref, qx_ref, dox_ref, c_ref, a_ref, b_ref, *refs, blocks, n):
    k_refs, v_refs, (dq_ref, ks, vs, acc) = refs[:n], refs[n:2 * n], refs[2 * n:]
    s, pair = pl.program_id(0), pl.program_id(1)

    @pl.when((s == 0) & (pair == 0))
    def _():
        ks[:, 128:256] = jnp.ones((blocks * BLK, 128), jnp.bfloat16)
        vs[:, 128:256] = jnp.ones((blocks * BLK, 128), jnp.bfloat16)

    place_rows(place_ref, s, k_refs, ks)
    place_rows(place_ref, s, v_refs, vs)
    mine = own_lanes(pair)
    for w in range(2):
        rows = slice(w * BLK, (w + 1) * BLK)
        pos = own_ref[s, w]
        last = pos // CB

        def extend(tile, ext):
            both = jnp.concatenate([ext, ext], axis=0)
            return jnp.concatenate([split_heads(tile), jnp.where(mine, both, jnp.zeros_like(both))], axis=1)

        qs = extend(q_ref[0, rows, :] * jnp.bfloat16(SCALE), qx_ref[0, rows, :])
        dos = extend(do_ref[0, rows, :], dox_ref[0, rows, :])
        acc[...] = jnp.zeros_like(acc)

        def step(c, mask):
            at = pl.multiple_of(c * CH, CH)
            p = jnp.exp(nt(qs, ks[pl.ds(at, CH), :]))
            if mask is not None:
                p = jnp.where(mask, p, 0.0)
            ds = (p * nt(dos, vs[pl.ds(at, CH), :])).astype(jnp.bfloat16)
            acc[...] += nn(ds, ks[pl.ds(at, CH), 0:128])

        def body(c, carry):
            step(c, None)
            return carry

        lax.fori_loop(0, last, body, 0)
        qpos = pos * BLK + row_of((2 * BLK, CH)) % BLK
        kpos = last * CH + lane_of((2 * BLK, CH))
        step(last, kpos <= qpos)
        grad = join_heads(acc[...]) * SCALE
        dq_ref[0, rows, :] = turn(grad, c_ref[rows], a_ref[rows], b_ref[rows], -1.0).astype(jnp.bfloat16)


def dkv_kernel(place_ref, own_ref, slots_ref, k_ref, v_ref, c_ref, a_ref, b_ref, *refs, blocks, n, lead):
    q_refs, qx_refs, (do_ref, dox_ref, dk_ref, dv_ref, qs, dos, acck, accv) = refs[:n], refs[n:2 * n], refs[2 * n:]
    s, pair = pl.program_id(0) + lead, pl.program_id(1)
    place_rows(place_ref, s, q_refs, qs)
    place_rows(slots_ref, s, [do_ref], dos)

    @pl.when(pair == 0)
    def _():
        place_rows(place_ref, s, qx_refs, qs, 128)
        place_rows(slots_ref, s, [dox_ref], dos, 128)

    ones = own_lanes(pair).astype(jnp.bfloat16)
    for w in range(2):
        rows = slice(w * BLK, (w + 1) * BLK)
        pos = own_ref[s, w]
        first = pos // CB
        kw = jnp.concatenate([split_heads(k_ref[0, 0, rows, :] * jnp.bfloat16(SCALE)), ones], axis=1)
        vw = jnp.concatenate([split_heads(v_ref[0, 0, rows, :]), ones], axis=1)
        acck[...] = jnp.zeros_like(acck)
        accv[...] = jnp.zeros_like(accv)

        def step(c, mask):
            at = pl.multiple_of(c * CH, CH)
            p = jnp.exp(nt(kw, qs[pl.ds(at, CH), :]))
            if mask is not None:
                p = jnp.where(mask, p, 0.0)
            accv[...] += nn(p.astype(jnp.bfloat16), dos[pl.ds(at, CH), 0:128])
            ds = (p * nt(vw, dos[pl.ds(at, CH), :])).astype(jnp.bfloat16)
            acck[...] += nn(ds, qs[pl.ds(at, CH), 0:128])

        def body(c, carry):
            step(c, None)
            return carry

        kpos = pos * BLK + row_of((2 * BLK, CH)) % BLK
        qpos = first * CH + lane_of((2 * BLK, CH))
        step(first, kpos <= qpos)
        lax.fori_loop(first + 1, blocks // CB, body, 0)
        grad = join_heads(acck[...]) * SCALE
        dk_ref[0, rows, :] = turn(grad, c_ref[rows], a_ref[rows], b_ref[rows], -1.0).astype(jnp.bfloat16)
        dv_ref[0, rows, :] = join_heads(accv[...]).astype(jnp.bfloat16)


OWN = pl.BlockSpec((1, 2 * BLK, 128), lambda s, h, *_: (s, 0, h))
EXT = pl.BlockSpec((1, 2 * BLK, 128), lambda s, h, *_: (s, 0, 0))


def table(lead=0):
    return pl.BlockSpec((2 * BLK, 128), lambda s, h, *_: (s + lead, 0))


def piece(x, first=0, lane=None, lead=0, count=1):
    return pl.BlockSpec((count, 1, 2, BLK, 128), lambda s, h, *_: (first, s + lead, 0, 0, h if lane is None else lane))


def attention_call(kernel, name, mats, seqs, pairs, blocks, in_specs, out_specs, out_shape, scratch, args, prefetch=2):
    work = seqs * pairs * 2 * 2 * BLK * blocks * BLK // 2
    return pl.pallas_call(
        kernel,
        grid_spec=pltpu.PrefetchScalarGridSpec(
            num_scalar_prefetch=prefetch, grid=(seqs, pairs), in_specs=in_specs, out_specs=out_specs, scratch_shapes=scratch),
        out_shape=out_shape,
        compiler_params=pltpu.CompilerParams(vmem_limit_bytes=40 * 2**20),
        cost_estimate=pl.CostEstimate(flops=work * 512 * mats, bytes_accessed=4 * seqs * pairs * blocks * BLK * 128, transcendentals=work),
        name=name,
    )(*args)


def rows_of(blocks, lanes):
    return pltpu.VMEM((blocks * BLK, lanes), jnp.bfloat16)


def acc_of(lanes):
    return pltpu.VMEM((2 * BLK, lanes), jnp.float32)


def attend(place, own, q, keys, values):
    seqs, pairs, blocks = q.shape[0], q.shape[2] // 128, place.shape[1]
    return attention_call(
        functools.partial(fwd_kernel, blocks=blocks, n=len(keys)), "attend", 2, seqs, pairs, blocks,
        [OWN] + [piece(*e) for e in keys + values], [OWN, EXT],
        [jax.ShapeDtypeStruct(q.shape, jnp.bfloat16), jax.ShapeDtypeStruct(q.shape[:2] + (128,), jnp.bfloat16)],
        [rows_of(blocks, 128), rows_of(blocks, 256), pltpu.VMEM((blocks // CB, 2 * BLK, CH), jnp.float32), acc_of(256)],
        [place, own, q] + [e[0] for e in keys + values])


def query_grad(place, own, q, do, q_ext, do_ext, tabs, keys, values):
    seqs, pairs, blocks = q.shape[0], q.shape[2] // 128, place.shape[1]
    return attention_call(
        functools.partial(dq_kernel, blocks=blocks, n=len(keys)), "query_grad", 3, seqs, pairs, blocks,
        [OWN, OWN, EXT, EXT] + [table()] * 3 + [piece(*e) for e in keys + values], OWN,
        jax.ShapeDtypeStruct(q.shape, jnp.bfloat16),
        [rows_of(blocks, 256), rows_of(blocks, 256), acc_of(128)],
        [place, own, q, do, q_ext, do_ext, *tabs] + [e[0] for e in keys + values])


def key_value_grad(place, own, slots, kv, tabs, queries, grads, lead, count):
    pairs, blocks = kv.shape[3] // 128, place.shape[1]
    shape = (count,) + kv.shape[2:]
    n = grads.shape[0]

    def own_part(i):
        return pl.BlockSpec((1, 1, 2 * BLK, 128), lambda s, h, *_: (i, s + lead, 0, h))

    return attention_call(
        functools.partial(dkv_kernel, blocks=blocks, n=len(queries), lead=lead), "key_value_grad", 4, count, pairs, blocks,
        [own_part(0), own_part(1)] + [table(lead)] * 3 + [piece(x, lead=lead) for x in queries]
        + [piece(x, lane=pairs, lead=lead) for x in queries]
        + [piece(grads, lead=lead, count=n), piece(grads, lane=pairs, lead=lead, count=n)], [OWN, OWN],
        [jax.ShapeDtypeStruct(shape, jnp.bfloat16)] * 2,
        [rows_of(blocks, 256), rows_of(blocks, 256), acc_of(128), acc_of(128)],
        [place, own, slots, kv, kv, *tabs] + queries * 2 + [grads] * 2, prefetch=3)


import math
from jax.sharding import PartitionSpec as P

HEAD_DIM = 64
ROT = 16
SEQS = 4
EPS = 1e-05
F32 = jnp.float32
BF16 = jnp.bfloat16


def rc(left, right):
    return lax.dot_general(left, right, (((0,), (0,)), ((), ())), preferred_element_type=F32)


def layer_stats(values, gain, shift):
    mean = jnp.mean(values, axis=-1, keepdims=True)
    centred = values - mean
    inverse = lax.rsqrt(jnp.mean(centred * centred, axis=-1, keepdims=True) + EPS)
    unit = centred * inverse
    return unit * gain + shift, unit, inverse


def layer_back(grad, unit, inverse, gain):
    scaled = grad * gain
    grad_in = inverse * (
        scaled
        - jnp.mean(scaled, axis=-1, keepdims=True)
        - unit * jnp.mean(scaled * unit, axis=-1, keepdims=True)
    )
    return grad_in, jnp.sum(grad * unit, axis=0), jnp.sum(grad, axis=0)


def rotary_tables(positions):
    half = ROT // 2
    dim = jnp.arange(2 * HEAD_DIM) % HEAD_DIM
    freq = jnp.where(dim < ROT, 10000.0 ** (-2.0 * (dim % half).astype(F32) / ROT), 0.0)
    angles = positions.astype(F32)[:, None] * freq[None, :]
    sin = jnp.sin(angles)
    return jnp.cos(angles), jnp.where(dim < half, sin, 0.0), jnp.where(dim < half, 0.0, sin)


def turn(x, ctab, above, below, sign):
    up = pltpu.roll(x, 128 - ROT // 2, axis=1)
    down = pltpu.roll(x, ROT // 2, axis=1)
    return x * ctab + sign * (down * below - up * above)


def project_kernel(h_ref, wq_ref, wk_ref, wv_ref, bias_ref, c_ref, a_ref, b_ref, q_ref, kv_ref):
    h = h_ref[...]
    width = wq_ref.shape[1]
    tabs = c_ref[...], a_ref[...], b_ref[...]
    for at, (w_ref, out) in enumerate(((wq_ref, q_ref.at[0]), (wk_ref, kv_ref.at[0, 0]), (wv_ref, kv_ref.at[1, 0]))):
        lin = nn(h, w_ref[...]) + bias_ref[at:at + 1, :]
        for p in range(width // 128):
            part = lin[:, p * 128:(p + 1) * 128]
            if at < 2:
                part = turn(part, *tabs, 1.0)
            out[:, p * 128:(p + 1) * 128] = part.astype(BF16)


def project(rows, wq, wk, wv, bias, tabs):
    total, depth = rows.shape
    width = wq.shape[1]
    step = total // SEQS
    weight = pl.BlockSpec((depth, width), lambda i: (0, 0))
    table = pl.BlockSpec((step, 128), lambda i: (i, 0))
    return pl.pallas_call(
        project_kernel,
        grid=(SEQS,),
        in_specs=[pl.BlockSpec((step, depth), lambda i: (i, 0)), weight, weight, weight,
                  pl.BlockSpec((3, width), lambda i: (0, 0)), table, table, table],
        out_specs=[pl.BlockSpec((1, step, width), lambda i: (i, 0, 0)),
                   pl.BlockSpec((2, 1, step, width), lambda i: (0, i, 0, 0))],
        out_shape=[jax.ShapeDtypeStruct((SEQS, step, width), BF16), jax.ShapeDtypeStruct((2, SEQS, step, width), BF16)],
        compiler_params=pltpu.CompilerParams(vmem_limit_bytes=48 * 2**20),
        cost_estimate=pl.CostEstimate(flops=6 * total * depth * width, bytes_accessed=6 * depth * width, transcendentals=0),
        name="project",
    )(rows, wq, wk, wv, bias, *tabs)


def mlp_kernel(h_ref, dy_ref, gate_ref, up_ref, down_ref, act_ref, *grad_refs):
    width = gate_ref.shape[1]
    gate = nn(h_ref[...], gate_ref[...])
    up = nn(h_ref[...], up_ref[...])
    grad = nt(dy_ref[...], down_ref[...])
    sig = 1.0 / (1.0 + jnp.exp(-gate))
    silu = gate * sig
    act_ref[...] = (silu * up).astype(BF16)
    outs = grad_refs if len(grad_refs) == 2 else (grad_refs[0].at[:, :width], grad_refs[0].at[:, width:])
    outs[0][...] = (grad * up * (sig + silu * (1.0 - sig))).astype(BF16)
    outs[1][...] = (grad * silu).astype(BF16)


def mlp(rows, dy, gate_w, up_w, down_w, step=256):
    total, depth = rows.shape
    width = gate_w.shape[1]
    joined = width % 128 == 0
    block = pl.BlockSpec((step, depth), lambda i: (i, 0))

    def whole(x):
        return pl.BlockSpec(x.shape, lambda i: (0, 0), pipeline_mode=pl.Buffered(1))

    def out(n):
        return pl.BlockSpec((step, n), lambda i: (i, 0)), jax.ShapeDtypeStruct((total, n), BF16)

    outs = [out(width), out(2 * width)] if joined else [out(width)] * 3
    act, *grads = pl.pallas_call(
        mlp_kernel,
        grid=(total // step,),
        in_specs=[block, block, whole(gate_w), whole(up_w), whole(down_w)],
        out_specs=[o[0] for o in outs],
        out_shape=[o[1] for o in outs],
        compiler_params=pltpu.CompilerParams(vmem_limit_bytes=56 * 2**20),
        cost_estimate=pl.CostEstimate(flops=6 * total * depth * width, bytes_accessed=6 * depth * width + 10 * total * depth,
                                      transcendentals=total * width),
        name="mlp",
    )(rows, dy, gate_w, up_w, down_w)
    return act, grads[0] if joined else jnp.concatenate(grads, axis=1)


def ctx_swap(x, mask):
    n = lax.axis_size("ctx")
    return lax.ppermute(x, "ctx", [(i, i ^ mask) for i in range(n)])


def add16(a, b):
    return (a.astype(F32) + b.astype(F32)).astype(BF16)


def after(x, *deps):
    if not jax.tree.leaves(deps):
        return x
    return lax.optimization_barrier((x, deps))[0]


def half_of(x, bit, mine):
    side = (lax.axis_index("ctx") >> bit) & 1
    r = x.shape[0] // 2
    return lax.dynamic_slice_in_dim(x, (side if mine else 1 - side) * r, r, 0)


def weight_grad(part):
    core = lax.axis_index("ctx") & 1
    got = ctx_swap(part(1 - core).astype(BF16), 1)
    gate = yield
    half = (part(core) + after(got, gate).astype(F32)).astype(BF16)
    bits = list(range(1, int(math.log2(lax.axis_size("ctx")))))
    orders = [bits, bits[::-1]]
    r = half.shape[0] // 2
    streams = [half[:r], half[r:]]
    gate = yield streams
    for i in range(len(bits)):
        streams = after(streams, gate)
        got = [ctx_swap(half_of(x, o[i], False), 1 << o[i]) for x, o in zip(streams, orders)]
        gate = yield
        streams, got = after((streams, got), gate)
        streams = [add16(half_of(x, o[i], True), g) for x, o, g in zip(streams, orders, got)]
        gate = yield streams
    for i in reversed(range(len(bits))):
        streams = after(streams, gate)
        got = [ctx_swap(x, 1 << o[i]) for x, o in zip(streams, orders)]
        gate = yield
        streams, got = after((streams, got), gate)
        streams = [
            jnp.where(((lax.axis_index("ctx") >> o[i]) & 1) == 0, jnp.concatenate([x, g]), jnp.concatenate([g, x]))
            for x, o, g in zip(streams, orders, got)
        ]
        if i == 0:
            streams = jnp.concatenate(streams)
        gate = yield streams
    streams = after(streams, gate)
    other = ctx_swap(streams, 1)
    gate = yield
    yield after((streams, other), gate)


def begin(*args):
    chain = weight_grad(*args)
    next(chain)
    return chain


def take(chain, gate=None):
    return chain.send(gate)


def go(chain, gate=None):
    chain.send(gate)


def take_extra(chain):
    for _ in range(2 * int(math.log2(lax.axis_size("ctx"))) - 6):
        go(chain)
        take(chain)


def unpack_rows_kernel(core_ref, half_ref, other_ref, *out_refs, turned):
    def put(src):
        at = 0
        for i, out in enumerate(out_refs):
            if turned and i == len(out_refs) - 1:
                out[...] = src[:, at:].astype(F32).T
            else:
                out[...] = src[:, at:at + out.shape[1]].astype(F32)
                at += out.shape[1]

    @pl.when(pl.program_id(0) == core_ref[0])
    def _():
        put(half_ref)

    @pl.when(pl.program_id(0) != core_ref[0])
    def _():
        put(other_ref)


def unpack_rows(half, other, parts, turned=False):
    r, c = half.shape
    step = math.gcd(r, 256)
    blocks = r // step
    w = c // parts
    core = lax.axis_index("ctx") & 1

    def mine(i, j, core_ref):
        return jnp.where(i == core_ref[0], j, jnp.where(core_ref[0] == 0, blocks - 1, 0)), 0

    def theirs(i, j, core_ref):
        return jnp.where(i != core_ref[0], j, jnp.where(core_ref[0] == 1, blocks - 1, 0)), 0

    specs = [pl.BlockSpec((step, w), lambda i, j, _: (i * blocks + j, 0))] * parts
    shapes = [jax.ShapeDtypeStruct((2 * r, w), F32)] * parts
    if turned:
        specs[-1] = pl.BlockSpec((w, step), lambda i, j, _: (0, i * blocks + j))
        shapes[-1] = jax.ShapeDtypeStruct((w, 2 * r), F32)
    return pl.pallas_call(
        functools.partial(unpack_rows_kernel, turned=turned),
        grid_spec=pltpu.PrefetchScalarGridSpec(
            num_scalar_prefetch=1, grid=(2, blocks),
            in_specs=[pl.BlockSpec((step, c), mine), pl.BlockSpec((step, c), theirs)], out_specs=specs),
        out_shape=shapes,
        compiler_params=pltpu.CompilerParams(vmem_limit_bytes=40 * 2**20),
        cost_estimate=pl.CostEstimate(flops=0, bytes_accessed=12 * r * c, transcendentals=0),
        name="unpack_rows",
    )(core[None], half, other)


def columns(x, which):
    w = x.shape[1] // 2
    return lax.dynamic_slice_in_dim(x, which * w, w, 1)


def unpack_cols_kernel(core_ref, half_ref, other_ref, out_ref):
    c = half_ref.shape[1]
    core = core_ref[0]
    out_ref[:, pl.ds(pl.multiple_of(core * c, 128), c)] = half_ref[...].astype(F32)
    out_ref[:, pl.ds(pl.multiple_of((1 - core) * c, 128), c)] = other_ref[...].astype(F32)


def unpack_cols(half, other):
    r, c = half.shape
    step = math.gcd(r, 256)
    block = pl.BlockSpec((step, c), lambda i, _: (i, 0))
    return pl.pallas_call(
        unpack_cols_kernel,
        grid_spec=pltpu.PrefetchScalarGridSpec(
            num_scalar_prefetch=1, grid=(r // step,), in_specs=[block, block],
            out_specs=pl.BlockSpec((step, 2 * c), lambda i, _: (i, 0))),
        out_shape=jax.ShapeDtypeStruct((r, 2 * c), F32),
        compiler_params=pltpu.CompilerParams(vmem_limit_bytes=40 * 2**20),
        cost_estimate=pl.CostEstimate(flops=0, bytes_accessed=12 * r * c, transcendentals=0),
        name="unpack_cols",
    )((lax.axis_index("ctx") & 1)[None], half, other)


def all_rows(x):
    return lax.all_gather(x, "tp", axis=0, tiled=True)


def tp_shift(x, d):
    n = lax.axis_size("tp")
    return lax.ppermute(x, "tp", [(i, (i + d) % n) for i in range(n)])


def part_of(x, d, axis):
    n = lax.axis_size("tp")
    w = x.shape[axis] // n
    return lax.dynamic_slice_in_dim(x, (lax.axis_index("tp") + d) % n * w, w, axis)


def exchange(x, split, join):
    n, me = lax.axis_size("tp"), lax.axis_index("tp")
    w = x.shape[join]
    shape = list(x.shape)
    shape[split] //= n
    shape[join] *= n
    out = jnp.zeros(shape, x.dtype)
    for d in range(n):
        got = tp_shift(part_of(x, d, split), d) if d else part_of(x, 0, split)
        out = lax.dynamic_update_slice_in_dim(out, got, (me + n - d) % n * w, join)
    return out


def sum_rows(x):
    return lax.psum_scatter(x, "tp", scatter_dimension=0, tiled=True)


def gather_pair(kv):
    n = lax.axis_size("ctx")
    held = {0: ((kv, 0), (kv, 1))}
    for bit in range(1, int(math.log2(n))):
        mask = 1 << bit
        for j in list(held):
            if j == 0:
                got = ctx_swap(kv, mask)
                held[mask] = (got, 0), (got, 1)
            elif mask == 4 and j == 2:
                held[6] = (ctx_swap(held[2][0][0][0:1], 4), 0), (ctx_swap(held[4][1][0][1:2], 2), 0)
            else:
                (k, i), (v, t) = held[j]
                if k is v:
                    got = ctx_swap(k, mask)
                    held[j | mask] = (got, i), (got, t)
                else:
                    held[j | mask] = (ctx_swap(k, mask), i), (ctx_swap(v, mask), t)
    for j in list(held):
        (k, i), (v, t) = held[j]
        got = ctx_swap(k, 1)
        held[j | 1] = (got, i), (got if k is v else ctx_swap(v, 1), t)
    return [held[j][0] for j in range(n)], [held[j][1] for j in range(n)]


def gather_other(x):
    held = {0: x, 1: ctx_swap(x, 1)}
    for j in range(2, lax.axis_size("ctx"), 2):
        held[j] = ctx_swap(x, j)
    return held


def gather_cores(held, gate=None):
    n = lax.axis_size("ctx")
    for j in range(2, n, 2):
        held[j + 1] = ctx_swap(after(held[j], gate), 1)
    return [held[j] for j in range(n)]


def sum_over_all(x):
    for axis in ("ctx", "tp"):
        n = lax.axis_size(axis)
        for bit in range(int(math.log2(n))):
            x = x + lax.ppermute(x, axis, [(i, i ^ (1 << bit)) for i in range(n)])
            yield x
    while True:
        yield x


def gather_tp(x):
    n, me = lax.axis_size("tp"), lax.axis_index("tp")
    out = jnp.zeros((n,) + x.shape, x.dtype)
    for d in range(n):
        got = lax.ppermute(x, "tp", [(i, (i + d) % n) for i in range(n)]) if d else x
        out = lax.dynamic_update_index_in_dim(out, got, (me + n - d) % n, 0)
    return out


def local(tokens, cotangent, block_order, gain_one, shift_one, query_w, key_w, value_w, query_b, key_b, value_b,
          output_w, gain_two, shift_two, gate_w, up_w, down_w):
    heads = key_b.shape[0]
    width = heads * HEAD_DIM
    n_ctx, n_tp = lax.axis_size("ctx"), lax.axis_size("tp")
    ctx = lax.axis_index("ctx")
    own = lax.dynamic_slice_in_dim(block_order, 2 * ctx, 2, 1)
    picked = (jnp.arange(n_ctx, dtype=jnp.int32) ^ ctx)[:, None] == jnp.arange(n_ctx, dtype=jnp.int32)[None, :]
    by_ctx = block_order.reshape(SEQS, 1, n_ctx, 2)
    place = jnp.sum(jnp.where(picked[None, :, :, None], by_ctx, 0), axis=2).astype(jnp.int32).reshape(SEQS, 2 * n_ctx)
    positions = (own[:, :, None] * BLK + jnp.arange(BLK, dtype=jnp.int32)).reshape(-1)
    tabs = rotary_tables(positions)

    x = tokens.astype(F32)
    normed_one, unit_one, inverse_one = layer_stats(x, gain_one, shift_one)
    rows_one = all_rows(normed_one.astype(BF16))
    key_bias = jnp.concatenate([key_b, jnp.zeros((heads, HEAD_DIM - ROT), F32)], axis=1).reshape(-1)
    bias = jnp.stack([query_b, key_bias, value_b])
    q, kv = project(rows_one, query_w, key_w, value_w, bias, tabs)
    keys, values = gather_pair(kv.reshape(2, SEQS, 2, BLK, width))
    arrived = [e[0] for e in keys + values]

    rows_w = output_w.shape[0] // n_ctx
    part = lax.dynamic_slice_in_dim(output_w, ctx * rows_w, rows_w, 0)
    part = gather_tp(after(part, kv))
    dy_rows = all_rows(after(cotangent, rows_one))
    whole_w = lax.all_gather(after(part, arrived, dy_rows), "ctx", axis=1).reshape(n_tp * output_w.shape[0], -1)

    attn, q_ext = attend(place, own, q, keys, values)
    attn_rows = attn.reshape(-1, width)
    attn_own = exchange(attn_rows, 0, 1)
    mixed = x + nn(attn_own, whole_w)
    normed_two, unit_two, inverse_two = layer_stats(mixed, gain_two, shift_two)
    rows_two = all_rows(after(normed_two.astype(BF16), dy_rows, whole_w))
    shape = (1, SEQS, 2, BLK, width + 128)
    queries = gather_cores(gather_other(after(jnp.concatenate([q, q_ext], axis=2).reshape(shape), attn_own)))
    rows_two = after(rows_two, queries)

    act, grad_gu = mlp(rows_two, dy_rows, gate_w, up_w, down_w)
    ff = gate_w.shape[1]
    part_two = (nt(grad_gu[:, :ff], gate_w) + nt(grad_gu[:, ff:], up_w)).astype(BF16)
    grad_two = sum_rows(part_two)
    act, rows_two, dy_rows, grad_gu = after((act, rows_two, dy_rows, grad_gu), part_two)
    gu = begin(lambda core: rc(columns(rows_two, core), grad_gu))
    dw = begin(lambda core: rc(act, columns(dy_rows, core)))
    held = take(gu)
    go(gu)
    down = nn(after(act, held), down_w).astype(BF16)
    held = take(dw), take(gu, down)
    go(gu)
    go(dw, held)
    grad_two = after(grad_two, held)

    norm_two, grad_gain_two, grad_shift_two = layer_back(grad_two.astype(F32), unit_two, inverse_two, gain_two)
    grad_mixed = cotangent.astype(F32) + norm_two
    branch_own = grad_mixed.astype(BF16)
    grad_attn = nt(branch_own, whole_w).astype(BF16)
    grad_attn = after(grad_attn, take(gu, grad_attn), take(dw, grad_attn))
    go(gu)
    go(dw)
    grad_attn = exchange(grad_attn, 1, 0)
    lane = jnp.arange(128)[None, :]
    ind = ((jnp.arange(width) // HEAD_DIM)[:, None] == lane // 3).astype(F32)
    delta = lax.dot_general(grad_attn.astype(F32) * attn_rows.astype(F32), ind, (((1,), (0,)), ((), ())),
                            precision=lax.Precision.HIGHEST, preferred_element_type=F32)
    do_ext = terms(-delta, lane).astype(BF16)
    do_sent = jnp.concatenate([grad_attn, do_ext], axis=1).reshape(shape)
    grads = lax.all_gather(do_sent, "ctx", axis=0, tiled=True)
    grad_q = query_grad(place, own, q, grad_attn.reshape(q.shape), q_ext, do_ext.reshape(q_ext.shape), tabs, keys, values)
    grad_q = grad_q.reshape(-1, width)
    q_part = nt(grad_q, query_w)
    held = take(gu, q_part), take(dw, q_part)
    go(gu)
    go(dw)
    grads = after(grads, held)
    branch = all_rows(after(branch_own, grads))
    first = key_value_grad(place, own, block_order, kv, tabs, queries, grads, 0, SEQS // 2)
    grads = after(grads, take(dw, first))
    go(dw)
    second = key_value_grad(place, own, block_order, kv, tabs, queries, grads, SEQS // 2, SEQS // 2)
    grad_k, grad_v = (jnp.concatenate(pair).reshape(-1, width) for pair in zip(first, second))
    part_one = q_part + nt(grad_k, key_w) + nt(grad_v, value_w)
    part_sent = after(part_one.astype(BF16), branch)
    grad_one = sum_rows(part_sent)
    out_tokens = (mixed + sum_rows(after(down, grad_one)).astype(F32)).astype(BF16)

    rows_one, branch, grad_q, grad_k, grad_v = after((rows_one, branch, grad_q, grad_k, grad_v), part_sent)
    grad_qkv = jnp.concatenate([grad_q, grad_k, grad_v], axis=1)
    chain = begin(lambda core: jnp.concatenate([rc(columns(rows_one, core), grad_qkv), rc(columns(branch, core), attn_rows)], axis=1))
    take(gu, part_sent)
    take_extra(gu)
    go(gu)
    unit_rows = (rows_one.astype(F32) - shift_one) / gain_one
    bias_grad = jnp.sum(grad_qkv.astype(F32), axis=0)
    tp_row = (jnp.arange(n_tp) == lax.axis_index("tp"))[:, None]
    small = jnp.concatenate([
        jnp.sum(part_one * unit_rows, axis=0), jnp.sum(part_one, axis=0), grad_gain_two, grad_shift_two,
        jnp.where(tp_row, bias_grad[None, :], 0.0).reshape(-1)])
    sums = sum_over_all(small.reshape(-1, 1024))
    for _ in range(9):
        small = next(sums)
    held = take(chain)
    go(chain)
    take(dw, (held, small))
    take_extra(dw)
    go(dw)
    grad_gate_w, grad_up_w = unpack_rows(*take(gu, held), 2)
    held = take(chain, grad_gate_w)
    go(chain)
    grad_down_w = unpack_cols(*take(dw, held))
    held = take(chain, grad_down_w)
    go(chain)
    held = take(chain, held)
    go(chain)
    take(chain)
    take_extra(chain)
    go(chain)
    depth = x.shape[1]
    small = small.reshape(-1)
    norms = small[:4 * depth].reshape(4, depth)
    bias_sum = jnp.sum(jnp.where(tp_row, small[4 * depth:].reshape(n_tp, -1), 0.0), axis=0)
    grad_query_w, grad_key_w, grad_value_w, grad_output_w = unpack_rows(*take(chain), 4, True)
    norm_one, _, _ = layer_back(grad_one.astype(F32), unit_one, inverse_one, gain_one)
    grad_tokens = (grad_mixed + norm_one).astype(BF16)
    return (
        out_tokens, grad_tokens, norms[0], norms[1], grad_query_w, grad_key_w, grad_value_w,
        bias_sum[:width], bias_sum[width:2 * width].reshape(heads, HEAD_DIM)[:, :ROT], bias_sum[2 * width:],
        grad_output_w, norms[2], norms[3], grad_gate_w, grad_up_w, grad_down_w,
    )


def solution(mesh):
    rows, cols, depth, flat = P(("ctx", "tp"), None), P(None, "tp"), P("tp", None), P("tp")
    in_specs = (rows, rows, P(), P(), P(), cols, cols, cols, flat, depth, flat, depth, P(), P(), cols, cols, depth)
    out_specs = (rows, rows, P(), P(), cols, cols, cols, flat, depth, flat, depth, P(), P(), cols, cols, depth)
    return jax.shard_map(local, mesh=mesh, in_specs=in_specs, out_specs=out_specs, check_vma=False)
```

```python
import functools
import jax, jax.numpy as jnp
from jax import lax
from jax.experimental import pallas as pl
from jax.experimental.pallas import tpu as pltpu

BLK = 128
CB = 4
CH = BLK * CB
NEG = -1e30
SCALE = 0.125


def nt(a, b):
    return lax.dot_general(a, b, (((1,), (1,)), ((), ())), preferred_element_type=jnp.float32)


def nn(a, b):
    return lax.dot_general(a, b, (((1,), (0,)), ((), ())), preferred_element_type=jnp.float32)


def lane_of(shape):
    return lax.broadcasted_iota(jnp.int32, shape, 1)


def row_of(shape):
    return lax.broadcasted_iota(jnp.int32, shape, 0)


def split_heads(x):
    low = lane_of(x.shape) < 64
    zero = jnp.zeros_like(x)
    return jnp.concatenate([jnp.where(low, x, zero), jnp.where(low, zero, x)], axis=0)


def join_heads(x):
    low = lane_of((BLK, 128)) < 64
    return jnp.where(low, x[:BLK], x[BLK:])


def own_lanes(pair):
    shape = (2 * BLK, 128)
    return lane_of(shape) // 3 == 2 * pair + row_of(shape) // BLK


def terms(x, lane):
    first = x.astype(jnp.bfloat16).astype(jnp.float32)
    second = (x - first).astype(jnp.bfloat16).astype(jnp.float32)
    return jnp.where(lane % 3 == 0, first, jnp.where(lane % 3 == 1, second, x - first - second))


def place_rows(place_ref, s, refs, dst_ref, lane=0):
    at = 0
    for ref in refs:
        for j in range(ref.shape[0]):
            for w in range(2):
                row = pl.multiple_of(place_ref[s, at] * BLK, BLK)
                dst_ref[pl.ds(row, BLK), lane:lane + 128] = ref[j, 0, w]
                at += 1


def fwd_kernel(place_ref, own_ref, q_ref, *refs, blocks, n):
    k_refs, v_refs, (o_ref, ext_ref, ks, vs, scr, acc) = refs[:n], refs[n:2 * n], refs[2 * n:]
    s, pair = pl.program_id(0), pl.program_id(1)

    @pl.when((s == 0) & (pair == 0))
    def _():
        vs[:, 128:256] = jnp.ones((blocks * BLK, 128), jnp.bfloat16)

    @pl.when(pair == 0)
    def _():
        ext_ref[...] = jnp.zeros_like(ext_ref)

    place_rows(place_ref, s, k_refs, ks)
    place_rows(place_ref, s, v_refs, vs)
    for w in range(2):
        rows = slice(w * BLK, (w + 1) * BLK)
        pos = own_ref[s, w]
        last = pos // CB
        qs = split_heads(q_ref[0, rows, :] * jnp.bfloat16(SCALE))

        def tiles_max(run, sc):
            for t in range(CB):
                run = jnp.maximum(run, sc[:, t * 128:(t + 1) * 128])
            return run

        def score(c, run):
            at = pl.multiple_of(c * CH, CH)
            sc = nt(qs, ks[pl.ds(at, CH), :])
            scr[c] = sc
            return tiles_max(run, sc)

        run = lax.fori_loop(0, last, score, jnp.full((2 * BLK, 128), NEG, jnp.float32))
        at = pl.multiple_of(last * CH, CH)
        sc = nt(qs, ks[pl.ds(at, CH), :])
        qpos = pos * BLK + row_of((2 * BLK, CH)) % BLK
        kpos = last * CH + lane_of((2 * BLK, CH))
        sc = jnp.where(kpos <= qpos, sc, NEG)
        scr[last] = sc
        run = tiles_max(run, sc)
        top = jnp.broadcast_to(jnp.max(run, axis=1, keepdims=True), (2 * BLK, 128))
        topc = jnp.concatenate([top] * CB, axis=1)
        acc[...] = jnp.zeros_like(acc)

        def weigh(c, carry):
            at = pl.multiple_of(c * CH, CH)
            p = jnp.exp(scr[c] - topc).astype(jnp.bfloat16)
            acc[...] += nn(p, vs[pl.ds(at, CH), :])
            return carry

        lax.fori_loop(0, last + 1, weigh, 0)
        total = acc[:, 128:256]
        o_ref[0, rows, :] = join_heads(acc[:, 0:128] / total).astype(jnp.bfloat16)
        lane = lane_of((2 * BLK, 128))
        mine = jnp.where(own_lanes(pair), terms(-(top + jnp.log(total)), lane), 0.0)
        ext_ref[0, rows, :] = (ext_ref[0, rows, :].astype(jnp.float32) + mine[:BLK] + mine[BLK:]).astype(jnp.bfloat16)


def dq_kernel(place_ref, own_ref, q_ref, do_ref, qx_ref, dox_ref, c_ref, a_ref, b_ref, *refs, blocks, n):
    k_refs, v_refs, (dq_ref, ks, vs, acc) = refs[:n], refs[n:2 * n], refs[2 * n:]
    s, pair = pl.program_id(0), pl.program_id(1)

    @pl.when((s == 0) & (pair == 0))
    def _():
        ks[:, 128:256] = jnp.ones((blocks * BLK, 128), jnp.bfloat16)
        vs[:, 128:256] = jnp.ones((blocks * BLK, 128), jnp.bfloat16)

    place_rows(place_ref, s, k_refs, ks)
    place_rows(place_ref, s, v_refs, vs)
    mine = own_lanes(pair)
    for w in range(2):
        rows = slice(w * BLK, (w + 1) * BLK)
        pos = own_ref[s, w]
        last = pos // CB

        def extend(tile, ext):
            both = jnp.concatenate([ext, ext], axis=0)
            return jnp.concatenate([split_heads(tile), jnp.where(mine, both, jnp.zeros_like(both))], axis=1)

        qs = extend(q_ref[0, rows, :] * jnp.bfloat16(SCALE), qx_ref[0, rows, :])
        dos = extend(do_ref[0, rows, :], dox_ref[0, rows, :])
        acc[...] = jnp.zeros_like(acc)

        def step(c, mask):
            at = pl.multiple_of(c * CH, CH)
            p = jnp.exp(nt(qs, ks[pl.ds(at, CH), :]))
            if mask is not None:
                p = jnp.where(mask, p, 0.0)
            ds = (p * nt(dos, vs[pl.ds(at, CH), :])).astype(jnp.bfloat16)
            acc[...] += nn(ds, ks[pl.ds(at, CH), 0:128])

        def body(c, carry):
            step(c, None)
            return carry

        lax.fori_loop(0, last, body, 0)
        qpos = pos * BLK + row_of((2 * BLK, CH)) % BLK
        kpos = last * CH + lane_of((2 * BLK, CH))
        step(last, kpos <= qpos)
        grad = join_heads(acc[...]) * SCALE
        dq_ref[0, rows, :] = turn(grad, c_ref[rows], a_ref[rows], b_ref[rows], -1.0).astype(jnp.bfloat16)


def dkv_kernel(place_ref, own_ref, slots_ref, k_ref, v_ref, c_ref, a_ref, b_ref, *refs, blocks, n, lead):
    q_refs, qx_refs, (do_ref, dox_ref, dk_ref, dv_ref, qs, dos, acck, accv) = refs[:n], refs[n:2 * n], refs[2 * n:]
    s, pair = pl.program_id(0) + lead, pl.program_id(1)
    place_rows(place_ref, s, q_refs, qs)
    place_rows(slots_ref, s, [do_ref], dos)

    @pl.when(pair == 0)
    def _():
        place_rows(place_ref, s, qx_refs, qs, 128)
        place_rows(slots_ref, s, [dox_ref], dos, 128)

    ones = own_lanes(pair).astype(jnp.bfloat16)
    for w in range(2):
        rows = slice(w * BLK, (w + 1) * BLK)
        pos = own_ref[s, w]
        first = pos // CB
        kw = jnp.concatenate([split_heads(k_ref[0, 0, rows, :] * jnp.bfloat16(SCALE)), ones], axis=1)
        vw = jnp.concatenate([split_heads(v_ref[0, 0, rows, :]), ones], axis=1)
        acck[...] = jnp.zeros_like(acck)
        accv[...] = jnp.zeros_like(accv)

        def step(c, mask):
            at = pl.multiple_of(c * CH, CH)
            p = jnp.exp(nt(kw, qs[pl.ds(at, CH), :]))
            if mask is not None:
                p = jnp.where(mask, p, 0.0)
            accv[...] += nn(p.astype(jnp.bfloat16), dos[pl.ds(at, CH), 0:128])
            ds = (p * nt(vw, dos[pl.ds(at, CH), :])).astype(jnp.bfloat16)
            acck[...] += nn(ds, qs[pl.ds(at, CH), 0:128])

        def body(c, carry):
            step(c, None)
            return carry

        kpos = pos * BLK + row_of((2 * BLK, CH)) % BLK
        qpos = first * CH + lane_of((2 * BLK, CH))
        step(first, kpos <= qpos)
        lax.fori_loop(first + 1, blocks // CB, body, 0)
        grad = join_heads(acck[...]) * SCALE
        dk_ref[0, rows, :] = turn(grad, c_ref[rows], a_ref[rows], b_ref[rows], -1.0).astype(jnp.bfloat16)
        dv_ref[0, rows, :] = join_heads(accv[...]).astype(jnp.bfloat16)


OWN = pl.BlockSpec((1, 2 * BLK, 128), lambda s, h, *_: (s, 0, h))
EXT = pl.BlockSpec((1, 2 * BLK, 128), lambda s, h, *_: (s, 0, 0))


def table(lead=0):
    return pl.BlockSpec((2 * BLK, 128), lambda s, h, *_: (s + lead, 0))


def piece(x, first=0, lane=None, lead=0, count=1):
    return pl.BlockSpec((count, 1, 2, BLK, 128), lambda s, h, *_: (first, s + lead, 0, 0, h if lane is None else lane))


def attention_call(kernel, name, mats, seqs, pairs, blocks, in_specs, out_specs, out_shape, scratch, args, prefetch=2):
    work = seqs * pairs * 2 * 2 * BLK * blocks * BLK // 2
    return pl.pallas_call(
        kernel,
        grid_spec=pltpu.PrefetchScalarGridSpec(
            num_scalar_prefetch=prefetch, grid=(seqs, pairs), in_specs=in_specs, out_specs=out_specs, scratch_shapes=scratch),
        out_shape=out_shape,
        compiler_params=pltpu.CompilerParams(vmem_limit_bytes=60 * 2**20),
        cost_estimate=pl.CostEstimate(flops=work * 512 * mats, bytes_accessed=4 * seqs * pairs * blocks * BLK * 128, transcendentals=work),
        name=name,
    )(*args)


def rows_of(blocks, lanes):
    return pltpu.VMEM((blocks * BLK, lanes), jnp.bfloat16)


def acc_of(lanes):
    return pltpu.VMEM((2 * BLK, lanes), jnp.float32)


def attend(place, own, q, keys, values):
    seqs, pairs, blocks = q.shape[0], q.shape[2] // 128, place.shape[1]
    return attention_call(
        functools.partial(fwd_kernel, blocks=blocks, n=len(keys)), "attend", 2, seqs, pairs, blocks,
        [OWN] + [piece(*e) for e in keys + values], [OWN, EXT],
        [jax.ShapeDtypeStruct(q.shape, jnp.bfloat16), jax.ShapeDtypeStruct(q.shape[:2] + (128,), jnp.bfloat16)],
        [rows_of(blocks, 128), rows_of(blocks, 256), pltpu.VMEM((blocks // CB, 2 * BLK, CH), jnp.float32), acc_of(256)],
        [place, own, q] + [e[0] for e in keys + values])


def query_grad(place, own, q, do, q_ext, do_ext, tabs, keys, values):
    seqs, pairs, blocks = q.shape[0], q.shape[2] // 128, place.shape[1]
    return attention_call(
        functools.partial(dq_kernel, blocks=blocks, n=len(keys)), "query_grad", 3, seqs, pairs, blocks,
        [OWN, OWN, EXT, EXT] + [table()] * 3 + [piece(*e) for e in keys + values], OWN,
        jax.ShapeDtypeStruct(q.shape, jnp.bfloat16),
        [rows_of(blocks, 256), rows_of(blocks, 256), acc_of(128)],
        [place, own, q, do, q_ext, do_ext, *tabs] + [e[0] for e in keys + values])


def key_value_grad(place, own, slots, kv, tabs, queries, grads, lead, count):
    pairs, blocks = kv.shape[3] // 128, place.shape[1]
    shape = (count,) + kv.shape[2:]
    n = grads.shape[0]

    def own_part(i):
        return pl.BlockSpec((1, 1, 2 * BLK, 128), lambda s, h, *_: (i, s + lead, 0, h))

    return attention_call(
        functools.partial(dkv_kernel, blocks=blocks, n=len(queries), lead=lead), "key_value_grad", 4, count, pairs, blocks,
        [own_part(0), own_part(1)] + [table(lead)] * 3 + [piece(x, lead=lead) for x in queries]
        + [piece(x, lane=pairs, lead=lead) for x in queries]
        + [piece(grads, lead=lead, count=n), piece(grads, lane=pairs, lead=lead, count=n)], [OWN, OWN],
        [jax.ShapeDtypeStruct(shape, jnp.bfloat16)] * 2,
        [rows_of(blocks, 256), rows_of(blocks, 256), acc_of(128), acc_of(128)],
        [place, own, slots, kv, kv, *tabs] + queries * 2 + [grads] * 2, prefetch=3)


import math
from jax.sharding import PartitionSpec as P

HEAD_DIM = 64
ROT = 16
SEQS = 4
EPS = 1e-05
F32 = jnp.float32
BF16 = jnp.bfloat16


def rc(left, right):
    return lax.dot_general(left, right, (((0,), (0,)), ((), ())), preferred_element_type=F32)


def layer_stats(values, gain, shift):
    mean = jnp.mean(values, axis=-1, keepdims=True)
    centred = values - mean
    inverse = lax.rsqrt(jnp.mean(centred * centred, axis=-1, keepdims=True) + EPS)
    unit = centred * inverse
    return unit * gain + shift, unit, inverse


def layer_back(grad, unit, inverse, gain):
    scaled = grad * gain
    grad_in = inverse * (
        scaled
        - jnp.mean(scaled, axis=-1, keepdims=True)
        - unit * jnp.mean(scaled * unit, axis=-1, keepdims=True)
    )
    return grad_in, jnp.sum(grad * unit, axis=0), jnp.sum(grad, axis=0)


def rotary_tables(positions):
    half = ROT // 2
    dim = jnp.arange(2 * HEAD_DIM) % HEAD_DIM
    freq = jnp.where(dim < ROT, 10000.0 ** (-2.0 * (dim % half).astype(F32) / ROT), 0.0)
    angles = positions.astype(F32)[:, None] * freq[None, :]
    sin = jnp.sin(angles)
    return jnp.cos(angles), jnp.where(dim < half, sin, 0.0), jnp.where(dim < half, 0.0, sin)


def turn(x, ctab, above, below, sign):
    up = pltpu.roll(x, 128 - ROT // 2, axis=1)
    down = pltpu.roll(x, ROT // 2, axis=1)
    return x * ctab + sign * (down * below - up * above)


def project_kernel(h_ref, wq_ref, wk_ref, wv_ref, bias_ref, c_ref, a_ref, b_ref, q_ref, kv_ref):
    h = h_ref[...]
    width = wq_ref.shape[1]
    tabs = c_ref[...], a_ref[...], b_ref[...]
    for at, (w_ref, out) in enumerate(((wq_ref, q_ref.at[0]), (wk_ref, kv_ref.at[0, 0]), (wv_ref, kv_ref.at[1, 0]))):
        lin = nn(h, w_ref[...]) + bias_ref[at:at + 1, :]
        for p in range(width // 128):
            part = lin[:, p * 128:(p + 1) * 128]
            if at < 2:
                part = turn(part, *tabs, 1.0)
            out[:, p * 128:(p + 1) * 128] = part.astype(BF16)


def project(rows, wq, wk, wv, bias, tabs):
    total, depth = rows.shape
    width = wq.shape[1]
    step = total // SEQS
    weight = pl.BlockSpec((depth, width), lambda i: (0, 0))
    table = pl.BlockSpec((step, 128), lambda i: (i, 0))
    return pl.pallas_call(
        project_kernel,
        grid=(SEQS,),
        in_specs=[pl.BlockSpec((step, depth), lambda i: (i, 0)), weight, weight, weight,
                  pl.BlockSpec((3, width), lambda i: (0, 0)), table, table, table],
        out_specs=[pl.BlockSpec((1, step, width), lambda i: (i, 0, 0)),
                   pl.BlockSpec((2, 1, step, width), lambda i: (0, i, 0, 0))],
        out_shape=[jax.ShapeDtypeStruct((SEQS, step, width), BF16), jax.ShapeDtypeStruct((2, SEQS, step, width), BF16)],
        compiler_params=pltpu.CompilerParams(vmem_limit_bytes=48 * 2**20),
        cost_estimate=pl.CostEstimate(flops=6 * total * depth * width, bytes_accessed=6 * depth * width, transcendentals=0),
        name="project",
    )(rows, wq, wk, wv, bias, *tabs)


def mlp_kernel(h_ref, dy_ref, gate_ref, up_ref, down_ref, act_ref, *grad_refs):
    width = gate_ref.shape[1]
    gate = nn(h_ref[...], gate_ref[...])
    up = nn(h_ref[...], up_ref[...])
    grad = nt(dy_ref[...], down_ref[...])
    sig = 1.0 / (1.0 + jnp.exp(-gate))
    silu = gate * sig
    act_ref[...] = (silu * up).astype(BF16)
    outs = grad_refs if len(grad_refs) == 2 else (grad_refs[0].at[:, :width], grad_refs[0].at[:, width:])
    outs[0][...] = (grad * up * (sig + silu * (1.0 - sig))).astype(BF16)
    outs[1][...] = (grad * silu).astype(BF16)


def mlp(rows, dy, gate_w, up_w, down_w, step=256):
    total, depth = rows.shape
    width = gate_w.shape[1]
    joined = width % 128 == 0
    block = pl.BlockSpec((step, depth), lambda i: (i, 0))

    def whole(x):
        return pl.BlockSpec(x.shape, lambda i: (0, 0), pipeline_mode=pl.Buffered(1))

    def out(n):
        return pl.BlockSpec((step, n), lambda i: (i, 0)), jax.ShapeDtypeStruct((total, n), BF16)

    outs = [out(width), out(2 * width)] if joined else [out(width)] * 3
    act, *grads = pl.pallas_call(
        mlp_kernel,
        grid=(total // step,),
        in_specs=[block, block, whole(gate_w), whole(up_w), whole(down_w)],
        out_specs=[o[0] for o in outs],
        out_shape=[o[1] for o in outs],
        compiler_params=pltpu.CompilerParams(vmem_limit_bytes=56 * 2**20),
        cost_estimate=pl.CostEstimate(flops=6 * total * depth * width, bytes_accessed=6 * depth * width + 10 * total * depth,
                                      transcendentals=total * width),
        name="mlp",
    )(rows, dy, gate_w, up_w, down_w)
    return act, grads[0] if joined else jnp.concatenate(grads, axis=1)


def ctx_swap(x, mask):
    n = lax.axis_size("ctx")
    return lax.ppermute(x, "ctx", [(i, i ^ mask) for i in range(n)])


def add16(a, b):
    return (a.astype(F32) + b.astype(F32)).astype(BF16)


def after(x, *deps):
    if not jax.tree.leaves(deps):
        return x
    return lax.optimization_barrier((x, deps))[0]


def half_of(x, bit, mine):
    side = (lax.axis_index("ctx") >> bit) & 1
    r = x.shape[0] // 2
    return lax.dynamic_slice_in_dim(x, (side if mine else 1 - side) * r, r, 0)


def weight_grad(part):
    core = lax.axis_index("ctx") & 1
    got = ctx_swap(part(1 - core).astype(BF16), 1)
    gate = yield
    half = (part(core) + after(got, gate).astype(F32)).astype(BF16)
    bits = list(range(1, int(math.log2(lax.axis_size("ctx")))))
    orders = [bits, bits[::-1]]
    r = half.shape[0] // 2
    streams = [half[:r], half[r:]]
    gate = yield streams
    for i in range(len(bits)):
        streams = after(streams, gate)
        got = [ctx_swap(half_of(x, o[i], False), 1 << o[i]) for x, o in zip(streams, orders)]
        gate = yield
        streams, got = after((streams, got), gate)
        streams = [add16(half_of(x, o[i], True), g) for x, o, g in zip(streams, orders, got)]
        gate = yield streams
    for i in reversed(range(len(bits))):
        streams = after(streams, gate)
        got = [ctx_swap(x, 1 << o[i]) for x, o in zip(streams, orders)]
        gate = yield
        streams, got = after((streams, got), gate)
        streams = [
            jnp.where(((lax.axis_index("ctx") >> o[i]) & 1) == 0, jnp.concatenate([x, g]), jnp.concatenate([g, x]))
            for x, o, g in zip(streams, orders, got)
        ]
        if i == 0:
            streams = jnp.concatenate(streams)
        gate = yield streams
    streams = after(streams, gate)
    other = ctx_swap(streams, 1)
    gate = yield
    yield after((streams, other), gate)


def begin(*args):
    chain = weight_grad(*args)
    next(chain)
    return chain


def take(chain, gate=None):
    return chain.send(gate)


def go(chain, gate=None):
    chain.send(gate)


def take_extra(chain):
    for _ in range(2 * int(math.log2(lax.axis_size("ctx"))) - 6):
        go(chain)
        take(chain)


def unpack_rows_kernel(core_ref, half_ref, other_ref, *out_refs, turned):
    def put(src):
        at = 0
        for i, out in enumerate(out_refs):
            if turned and i == len(out_refs) - 1:
                out[...] = src[:, at:].astype(F32).T
            else:
                out[...] = src[:, at:at + out.shape[1]].astype(F32)
                at += out.shape[1]

    @pl.when(pl.program_id(0) == core_ref[0])
    def _():
        put(half_ref)

    @pl.when(pl.program_id(0) != core_ref[0])
    def _():
        put(other_ref)


def unpack_rows(half, other, parts, turned=False):
    r, c = half.shape
    step = math.gcd(r, 256)
    blocks = r // step
    w = c // parts
    core = lax.axis_index("ctx") & 1

    def mine(i, j, core_ref):
        return jnp.where(i == core_ref[0], j, jnp.where(core_ref[0] == 0, blocks - 1, 0)), 0

    def theirs(i, j, core_ref):
        return jnp.where(i != core_ref[0], j, jnp.where(core_ref[0] == 1, blocks - 1, 0)), 0

    specs = [pl.BlockSpec((step, w), lambda i, j, _: (i * blocks + j, 0))] * parts
    shapes = [jax.ShapeDtypeStruct((2 * r, w), F32)] * parts
    if turned:
        specs[-1] = pl.BlockSpec((w, step), lambda i, j, _: (0, i * blocks + j))
        shapes[-1] = jax.ShapeDtypeStruct((w, 2 * r), F32)
    return pl.pallas_call(
        functools.partial(unpack_rows_kernel, turned=turned),
        grid_spec=pltpu.PrefetchScalarGridSpec(
            num_scalar_prefetch=1, grid=(2, blocks),
            in_specs=[pl.BlockSpec((step, c), mine), pl.BlockSpec((step, c), theirs)], out_specs=specs),
        out_shape=shapes,
        compiler_params=pltpu.CompilerParams(vmem_limit_bytes=40 * 2**20),
        cost_estimate=pl.CostEstimate(flops=0, bytes_accessed=12 * r * c, transcendentals=0),
        name="unpack_rows",
    )(core[None], half, other)


def columns(x, which):
    w = x.shape[1] // 2
    return lax.dynamic_slice_in_dim(x, which * w, w, 1)


def unpack_cols_kernel(core_ref, half_ref, other_ref, out_ref):
    c = half_ref.shape[1]
    core = core_ref[0]
    out_ref[:, pl.ds(pl.multiple_of(core * c, 128), c)] = half_ref[...].astype(F32)
    out_ref[:, pl.ds(pl.multiple_of((1 - core) * c, 128), c)] = other_ref[...].astype(F32)


def unpack_cols(half, other):
    r, c = half.shape
    step = math.gcd(r, 256)
    block = pl.BlockSpec((step, c), lambda i, _: (i, 0))
    return pl.pallas_call(
        unpack_cols_kernel,
        grid_spec=pltpu.PrefetchScalarGridSpec(
            num_scalar_prefetch=1, grid=(r // step,), in_specs=[block, block],
            out_specs=pl.BlockSpec((step, 2 * c), lambda i, _: (i, 0))),
        out_shape=jax.ShapeDtypeStruct((r, 2 * c), F32),
        compiler_params=pltpu.CompilerParams(vmem_limit_bytes=40 * 2**20),
        cost_estimate=pl.CostEstimate(flops=0, bytes_accessed=12 * r * c, transcendentals=0),
        name="unpack_cols",
    )((lax.axis_index("ctx") & 1)[None], half, other)


def all_rows(x):
    return lax.all_gather(x, "tp", axis=0, tiled=True)


def tp_shift(x, d):
    n = lax.axis_size("tp")
    return lax.ppermute(x, "tp", [(i, (i + d) % n) for i in range(n)])


def part_of(x, d, axis):
    n = lax.axis_size("tp")
    w = x.shape[axis] // n
    return lax.dynamic_slice_in_dim(x, (lax.axis_index("tp") + d) % n * w, w, axis)


def exchange(x, split, join):
    n, me = lax.axis_size("tp"), lax.axis_index("tp")
    w = x.shape[join]
    shape = list(x.shape)
    shape[split] //= n
    shape[join] *= n
    out = jnp.zeros(shape, x.dtype)
    for d in range(n):
        got = tp_shift(part_of(x, d, split), d) if d else part_of(x, 0, split)
        out = lax.dynamic_update_slice_in_dim(out, got, (me + n - d) % n * w, join)
    return out


def sum_rows(x):
    return lax.psum_scatter(x, "tp", scatter_dimension=0, tiled=True)


def gather_pair(kv):
    n = lax.axis_size("ctx")
    held = {0: ((kv, 0), (kv, 1))}
    for bit in range(1, int(math.log2(n))):
        mask = 1 << bit
        for j in list(held):
            if j == 0:
                got = ctx_swap(kv, mask)
                held[mask] = (got, 0), (got, 1)
            elif mask == 4 and j == 2:
                held[6] = (ctx_swap(held[2][0][0][0:1], 4), 0), (ctx_swap(held[4][1][0][1:2], 2), 0)
            else:
                (k, i), (v, t) = held[j]
                if k is v:
                    got = ctx_swap(k, mask)
                    held[j | mask] = (got, i), (got, t)
                else:
                    held[j | mask] = (ctx_swap(k, mask), i), (ctx_swap(v, mask), t)
    for j in list(held):
        (k, i), (v, t) = held[j]
        got = ctx_swap(k, 1)
        held[j | 1] = (got, i), (got if k is v else ctx_swap(v, 1), t)
    return [held[j][0] for j in range(n)], [held[j][1] for j in range(n)]


def gather_other(x):
    held = {0: x, 1: ctx_swap(x, 1)}
    for j in range(2, lax.axis_size("ctx"), 2):
        held[j] = ctx_swap(x, j)
    return held


def gather_cores(held, gate=None):
    n = lax.axis_size("ctx")
    for j in range(2, n, 2):
        held[j + 1] = ctx_swap(after(held[j], gate), 1)
    return [held[j] for j in range(n)]


def sum_over_all(x):
    for axis in ("ctx", "tp"):
        n = lax.axis_size(axis)
        for bit in range(int(math.log2(n))):
            x = x + lax.ppermute(x, axis, [(i, i ^ (1 << bit)) for i in range(n)])
            yield x
    while True:
        yield x


def gather_tp(x):
    n, me = lax.axis_size("tp"), lax.axis_index("tp")
    out = jnp.zeros((n,) + x.shape, x.dtype)
    for d in range(n):
        got = lax.ppermute(x, "tp", [(i, (i + d) % n) for i in range(n)]) if d else x
        out = lax.dynamic_update_index_in_dim(out, got, (me + n - d) % n, 0)
    return out


def local(tokens, cotangent, block_order, gain_one, shift_one, query_w, key_w, value_w, query_b, key_b, value_b,
          output_w, gain_two, shift_two, gate_w, up_w, down_w):
    heads = key_b.shape[0]
    width = heads * HEAD_DIM
    n_ctx, n_tp = lax.axis_size("ctx"), lax.axis_size("tp")
    ctx = lax.axis_index("ctx")
    own = lax.dynamic_slice_in_dim(block_order, 2 * ctx, 2, 1)
    picked = (jnp.arange(n_ctx, dtype=jnp.int32) ^ ctx)[:, None] == jnp.arange(n_ctx, dtype=jnp.int32)[None, :]
    by_ctx = block_order.reshape(SEQS, 1, n_ctx, 2)
    place = jnp.sum(jnp.where(picked[None, :, :, None], by_ctx, 0), axis=2).astype(jnp.int32).reshape(SEQS, 2 * n_ctx)
    positions = (own[:, :, None] * BLK + jnp.arange(BLK, dtype=jnp.int32)).reshape(-1)
    tabs = rotary_tables(positions)

    x = tokens.astype(F32)
    normed_one, unit_one, inverse_one = layer_stats(x, gain_one, shift_one)
    rows_one = all_rows(normed_one.astype(BF16))
    key_bias = jnp.concatenate([key_b, jnp.zeros((heads, HEAD_DIM - ROT), F32)], axis=1).reshape(-1)
    bias = jnp.stack([query_b, key_bias, value_b])
    q, kv = project(rows_one, query_w, key_w, value_w, bias, tabs)
    keys, values = gather_pair(kv.reshape(2, SEQS, 2, BLK, width))
    arrived = [e[0] for e in keys + values]

    rows_w = output_w.shape[0] // n_ctx
    part = lax.dynamic_slice_in_dim(output_w, ctx * rows_w, rows_w, 0)
    part = gather_tp(after(part, kv))
    dy_rows = all_rows(after(cotangent, rows_one))
    whole_w = lax.all_gather(after(part, arrived, dy_rows), "ctx", axis=1).reshape(n_tp * output_w.shape[0], -1)

    attn, q_ext = attend(place, own, q, keys, values)
    attn_rows = attn.reshape(-1, width)
    attn_own = exchange(attn_rows, 0, 1)
    mixed = x + nn(attn_own, whole_w)
    normed_two, unit_two, inverse_two = layer_stats(mixed, gain_two, shift_two)
    rows_two = all_rows(after(normed_two.astype(BF16), dy_rows, whole_w))
    shape = (1, SEQS, 2, BLK, width + 128)
    queries = gather_cores(gather_other(after(jnp.concatenate([q, q_ext], axis=2).reshape(shape), attn_own)))
    rows_two = after(rows_two, queries)

    act, grad_gu = mlp(rows_two, dy_rows, gate_w, up_w, down_w)
    ff = gate_w.shape[1]
    part_two = (nt(grad_gu[:, :ff], gate_w) + nt(grad_gu[:, ff:], up_w)).astype(BF16)
    grad_two = sum_rows(part_two)
    act, rows_two, dy_rows, grad_gu = after((act, rows_two, dy_rows, grad_gu), part_two)
    gu = begin(lambda core: rc(columns(rows_two, core), grad_gu))
    dw = begin(lambda core: rc(act, columns(dy_rows, core)))
    held = take(gu)
    go(gu)
    down = nn(after(act, held), down_w).astype(BF16)
    held = take(dw), take(gu, down)
    go(gu)
    go(dw, held)
    grad_two = after(grad_two, held)
    out_sum = sum_rows(after(down, grad_two))

    norm_two, grad_gain_two, grad_shift_two = layer_back(grad_two.astype(F32), unit_two, inverse_two, gain_two)
    grad_mixed = cotangent.astype(F32) + norm_two
    branch_own = grad_mixed.astype(BF16)
    grad_attn = nt(branch_own, whole_w).astype(BF16)
    held = take(gu, grad_attn)
    go(gu)
    grad_attn = exchange(grad_attn, 1, 0)
    lane = jnp.arange(128)[None, :]
    ind = ((jnp.arange(width) // HEAD_DIM)[:, None] == lane // 3).astype(F32)
    delta = lax.dot_general(grad_attn.astype(F32) * attn_rows.astype(F32), ind, (((1,), (0,)), ((), ())),
                            precision=lax.Precision.HIGHEST, preferred_element_type=F32)
    do_ext = terms(-delta, lane).astype(BF16)
    do_sent = jnp.concatenate([grad_attn, do_ext], axis=1).reshape(shape)
    do_sent = after(do_sent, held)
    grads = lax.all_gather(do_sent, "ctx", axis=0, tiled=True)
    grad_q = query_grad(place, own, q, grad_attn.reshape(q.shape), q_ext, do_ext.reshape(q_ext.shape), tabs, keys, values)
    grad_q = grad_q.reshape(-1, width)
    q_part = nt(grad_q, query_w)
    held = take(gu, q_part), take(dw, q_part)
    go(gu)
    go(dw)
    grads = after(grads, held)
    branch = all_rows(after(branch_own, grads))
    first = key_value_grad(place, own, block_order, kv, tabs, queries, grads, 0, SEQS // 2)
    grads = after(grads, take(dw, first))
    go(dw)
    second = key_value_grad(place, own, block_order, kv, tabs, queries, grads, SEQS // 2, SEQS // 2)
    grad_k, grad_v = (jnp.concatenate(pair).reshape(-1, width) for pair in zip(first, second))
    part_one = q_part + nt(grad_k, key_w) + nt(grad_v, value_w)
    part_sent = after(part_one.astype(BF16), branch)
    grad_one = sum_rows(part_sent)
    mixed_late, out_sum = after((mixed, out_sum), part_sent)
    out_tokens = (mixed_late + out_sum.astype(F32)).astype(BF16)

    rows_one, branch, grad_q, grad_k, grad_v = after((rows_one, branch, grad_q, grad_k, grad_v), part_sent)
    grad_qkv = jnp.concatenate([grad_q, grad_k, grad_v], axis=1)
    chain = begin(lambda core: rc(columns(rows_one, core), grad_qkv))
    take(gu, part_sent)
    take_extra(gu)
    go(gu)
    held = take(chain)
    go(chain)
    grad_output_w = rc(attn_rows, after(branch, held)).astype(BF16)
    grad_output_w = lax.psum(after(grad_output_w, grad_one), "ctx")
    unit_rows = (rows_one.astype(F32) - shift_one) / gain_one
    bias_grad = jnp.sum(grad_qkv.astype(F32), axis=0)
    tp_row = (jnp.arange(n_tp) == lax.axis_index("tp"))[:, None]
    small = jnp.concatenate([
        jnp.sum(part_one * unit_rows, axis=0), jnp.sum(part_one, axis=0), grad_gain_two, grad_shift_two,
        jnp.where(tp_row, bias_grad[None, :], 0.0).reshape(-1)])
    sums = sum_over_all(after(small, held).reshape(-1, 1024))
    for _ in range(9):
        small = next(sums)
    made = take(dw, held)
    take_extra(dw)
    go(dw)
    held = take(chain, made)
    go(chain)
    held = take(chain, small)
    go(chain)
    grad_gate_w, grad_up_w = unpack_rows(*take(gu, held), 2)
    held = take(chain, grad_gate_w)
    go(chain)
    take(dw, held)
    go(dw)
    take(chain)
    take_extra(chain)
    go(chain)
    grad_down_w = unpack_cols(*take(dw))
    depth = x.shape[1]
    small = small.reshape(-1)
    norms = small[:4 * depth].reshape(4, depth)
    bias_sum = jnp.sum(jnp.where(tp_row, small[4 * depth:].reshape(n_tp, -1), 0.0), axis=0)
    grad_query_w, grad_key_w, grad_value_w = unpack_rows(*take(chain), 3)
    grad_output_w = grad_output_w.astype(F32)
    norm_one, _, _ = layer_back(grad_one.astype(F32), unit_one, inverse_one, gain_one)
    grad_tokens = (grad_mixed + norm_one).astype(BF16)
    return (
        out_tokens, grad_tokens, norms[0], norms[1], grad_query_w, grad_key_w, grad_value_w,
        bias_sum[:width], bias_sum[width:2 * width].reshape(heads, HEAD_DIM)[:, :ROT], bias_sum[2 * width:],
        grad_output_w, norms[2], norms[3], grad_gate_w, grad_up_w, grad_down_w,
    )


def solution(mesh):
    rows, cols, depth, flat = P(("ctx", "tp"), None), P(None, "tp"), P("tp", None), P("tp")
    in_specs = (rows, rows, P(), P(), P(), cols, cols, cols, flat, depth, flat, depth, P(), P(), cols, cols, depth)
    out_specs = (rows, rows, P(), P(), cols, cols, cols, flat, depth, flat, depth, P(), P(), cols, cols, depth)
    return jax.shard_map(local, mesh=mesh, in_specs=in_specs, out_specs=out_specs, check_vma=False)
```

```python
import functools
import jax, jax.numpy as jnp
from jax import lax
from jax.experimental import pallas as pl
from jax.experimental.pallas import tpu as pltpu

BLK = 128
CB = 4
CH = BLK * CB
NEG = -1e30
SCALE = 0.125


def nt(a, b):
    return lax.dot_general(a, b, (((1,), (1,)), ((), ())), preferred_element_type=jnp.float32)


def nn(a, b):
    return lax.dot_general(a, b, (((1,), (0,)), ((), ())), preferred_element_type=jnp.float32)


def lane_of(shape):
    return lax.broadcasted_iota(jnp.int32, shape, 1)


def row_of(shape):
    return lax.broadcasted_iota(jnp.int32, shape, 0)


def split_heads(x):
    low = lane_of(x.shape) < 64
    zero = jnp.zeros_like(x)
    return jnp.concatenate([jnp.where(low, x, zero), jnp.where(low, zero, x)], axis=0)


def join_heads(x):
    low = lane_of((BLK, 128)) < 64
    return jnp.where(low, x[:BLK], x[BLK:])


def own_lanes(pair):
    shape = (2 * BLK, 128)
    return lane_of(shape) // 3 == 2 * pair + row_of(shape) // BLK


def terms(x, lane):
    first = x.astype(jnp.bfloat16).astype(jnp.float32)
    second = (x - first).astype(jnp.bfloat16).astype(jnp.float32)
    return jnp.where(lane % 3 == 0, first, jnp.where(lane % 3 == 1, second, x - first - second))


def place_rows(place_ref, s, refs, dst_ref, lane=0):
    at = 0
    for ref in refs:
        for j in range(ref.shape[0]):
            for w in range(2):
                row = pl.multiple_of(place_ref[s, at] * BLK, BLK)
                dst_ref[pl.ds(row, BLK), lane:lane + 128] = ref[j, 0, w]
                at += 1


def fwd_kernel(place_ref, own_ref, q_ref, *refs, blocks, n):
    k_refs, v_refs, (o_ref, ext_ref, ks, vs, scr, acc) = refs[:n], refs[n:2 * n], refs[2 * n:]
    s, pair = pl.program_id(0), pl.program_id(1)

    @pl.when((s == 0) & (pair == 0))
    def _():
        vs[:, 128:256] = jnp.ones((blocks * BLK, 128), jnp.bfloat16)

    @pl.when(pair == 0)
    def _():
        ext_ref[...] = jnp.zeros_like(ext_ref)

    place_rows(place_ref, s, k_refs, ks)
    place_rows(place_ref, s, v_refs, vs)
    for w in range(2):
        rows = slice(w * BLK, (w + 1) * BLK)
        pos = own_ref[s, w]
        last = pos // CB
        qs = split_heads(q_ref[0, rows, :] * jnp.bfloat16(SCALE))

        def tiles_max(run, sc):
            for t in range(CB):
                run = jnp.maximum(run, sc[:, t * 128:(t + 1) * 128])
            return run

        def score(c, run):
            at = pl.multiple_of(c * CH, CH)
            sc = nt(qs, ks[pl.ds(at, CH), :])
            scr[c] = sc
            return tiles_max(run, sc)

        run = lax.fori_loop(0, last, score, jnp.full((2 * BLK, 128), NEG, jnp.float32))
        at = pl.multiple_of(last * CH, CH)
        sc = nt(qs, ks[pl.ds(at, CH), :])
        qpos = pos * BLK + row_of((2 * BLK, CH)) % BLK
        kpos = last * CH + lane_of((2 * BLK, CH))
        sc = jnp.where(kpos <= qpos, sc, NEG)
        scr[last] = sc
        run = tiles_max(run, sc)
        top = jnp.broadcast_to(jnp.max(run, axis=1, keepdims=True), (2 * BLK, 128))
        topc = jnp.concatenate([top] * CB, axis=1)
        acc[...] = jnp.zeros_like(acc)

        def weigh(c, carry):
            at = pl.multiple_of(c * CH, CH)
            p = jnp.exp(scr[c] - topc).astype(jnp.bfloat16)
            acc[...] += nn(p, vs[pl.ds(at, CH), :])
            return carry

        lax.fori_loop(0, last + 1, weigh, 0)
        total = acc[:, 128:256]
        o_ref[0, rows, :] = join_heads(acc[:, 0:128] / total).astype(jnp.bfloat16)
        lane = lane_of((2 * BLK, 128))
        mine = jnp.where(own_lanes(pair), terms(-(top + jnp.log(total)), lane), 0.0)
        ext_ref[0, rows, :] = (ext_ref[0, rows, :].astype(jnp.float32) + mine[:BLK] + mine[BLK:]).astype(jnp.bfloat16)


def dq_kernel(place_ref, own_ref, q_ref, do_ref, qx_ref, dox_ref, c_ref, a_ref, b_ref, *refs, blocks, n):
    k_refs, v_refs, (dq_ref, ks, vs, acc) = refs[:n], refs[n:2 * n], refs[2 * n:]
    s, pair = pl.program_id(0), pl.program_id(1)

    @pl.when((s == 0) & (pair == 0))
    def _():
        ks[:, 128:256] = jnp.ones((blocks * BLK, 128), jnp.bfloat16)
        vs[:, 128:256] = jnp.ones((blocks * BLK, 128), jnp.bfloat16)

    place_rows(place_ref, s, k_refs, ks)
    place_rows(place_ref, s, v_refs, vs)
    mine = own_lanes(pair)
    for w in range(2):
        rows = slice(w * BLK, (w + 1) * BLK)
        pos = own_ref[s, w]
        last = pos // CB

        def extend(tile, ext):
            both = jnp.concatenate([ext, ext], axis=0)
            return jnp.concatenate([split_heads(tile), jnp.where(mine, both, jnp.zeros_like(both))], axis=1)

        qs = extend(q_ref[0, rows, :] * jnp.bfloat16(SCALE), qx_ref[0, rows, :])
        dos = extend(do_ref[0, rows, :], dox_ref[0, rows, :])
        acc[...] = jnp.zeros_like(acc)

        def step(c, mask):
            at = pl.multiple_of(c * CH, CH)
            p = jnp.exp(nt(qs, ks[pl.ds(at, CH), :]))
            if mask is not None:
                p = jnp.where(mask, p, 0.0)
            ds = (p * nt(dos, vs[pl.ds(at, CH), :])).astype(jnp.bfloat16)
            acc[...] += nn(ds, ks[pl.ds(at, CH), 0:128])

        def body(c, carry):
            step(c, None)
            return carry

        lax.fori_loop(0, last, body, 0)
        qpos = pos * BLK + row_of((2 * BLK, CH)) % BLK
        kpos = last * CH + lane_of((2 * BLK, CH))
        step(last, kpos <= qpos)
        grad = join_heads(acc[...]) * SCALE
        dq_ref[0, rows, :] = turn(grad, c_ref[rows], a_ref[rows], b_ref[rows], -1.0).astype(jnp.bfloat16)


def dkv_kernel(place_ref, own_ref, slots_ref, k_ref, v_ref, c_ref, a_ref, b_ref, *refs, blocks, n, lead):
    q_refs, qx_refs, (do_ref, dox_ref, dk_ref, dv_ref, qs, dos, acck, accv) = refs[:n], refs[n:2 * n], refs[2 * n:]
    s, pair = pl.program_id(0) + lead, pl.program_id(1)
    place_rows(place_ref, s, q_refs, qs)
    place_rows(slots_ref, s, [do_ref], dos)

    @pl.when(pair == 0)
    def _():
        place_rows(place_ref, s, qx_refs, qs, 128)
        place_rows(slots_ref, s, [dox_ref], dos, 128)

    ones = own_lanes(pair).astype(jnp.bfloat16)
    for w in range(2):
        rows = slice(w * BLK, (w + 1) * BLK)
        pos = own_ref[s, w]
        first = pos // CB
        kw = jnp.concatenate([split_heads(k_ref[0, 0, rows, :] * jnp.bfloat16(SCALE)), ones], axis=1)
        vw = jnp.concatenate([split_heads(v_ref[0, 0, rows, :]), ones], axis=1)
        acck[...] = jnp.zeros_like(acck)
        accv[...] = jnp.zeros_like(accv)

        def step(c, mask):
            at = pl.multiple_of(c * CH, CH)
            p = jnp.exp(nt(kw, qs[pl.ds(at, CH), :]))
            if mask is not None:
                p = jnp.where(mask, p, 0.0)
            accv[...] += nn(p.astype(jnp.bfloat16), dos[pl.ds(at, CH), 0:128])
            ds = (p * nt(vw, dos[pl.ds(at, CH), :])).astype(jnp.bfloat16)
            acck[...] += nn(ds, qs[pl.ds(at, CH), 0:128])

        def body(c, carry):
            step(c, None)
            return carry

        kpos = pos * BLK + row_of((2 * BLK, CH)) % BLK
        qpos = first * CH + lane_of((2 * BLK, CH))
        step(first, kpos <= qpos)
        lax.fori_loop(first + 1, blocks // CB, body, 0)
        grad = join_heads(acck[...]) * SCALE
        dk_ref[0, rows, :] = turn(grad, c_ref[rows], a_ref[rows], b_ref[rows], -1.0).astype(jnp.bfloat16)
        dv_ref[0, rows, :] = join_heads(accv[...]).astype(jnp.bfloat16)


OWN = pl.BlockSpec((1, 2 * BLK, 128), lambda s, h, *_: (s, 0, h))
EXT = pl.BlockSpec((1, 2 * BLK, 128), lambda s, h, *_: (s, 0, 0))


def table(lead=0):
    return pl.BlockSpec((2 * BLK, 128), lambda s, h, *_: (s + lead, 0))


def piece(x, first=0, lane=None, lead=0, count=1):
    return pl.BlockSpec((count, 1, 2, BLK, 128), lambda s, h, *_: (first, s + lead, 0, 0, h if lane is None else lane))


def attention_call(kernel, name, mats, seqs, pairs, blocks, in_specs, out_specs, out_shape, scratch, args, prefetch=2):
    work = seqs * pairs * 2 * 2 * BLK * blocks * BLK // 2
    return pl.pallas_call(
        kernel,
        grid_spec=pltpu.PrefetchScalarGridSpec(
            num_scalar_prefetch=prefetch, grid=(seqs, pairs), in_specs=in_specs, out_specs=out_specs, scratch_shapes=scratch),
        out_shape=out_shape,
        compiler_params=pltpu.CompilerParams(vmem_limit_bytes=60 * 2**20),
        cost_estimate=pl.CostEstimate(flops=work * 512 * mats, bytes_accessed=4 * seqs * pairs * blocks * BLK * 128, transcendentals=work),
        name=name,
    )(*args)


def rows_of(blocks, lanes):
    return pltpu.VMEM((blocks * BLK, lanes), jnp.bfloat16)


def acc_of(lanes):
    return pltpu.VMEM((2 * BLK, lanes), jnp.float32)


def attend(place, own, q, keys, values):
    seqs, pairs, blocks = q.shape[0], q.shape[2] // 128, place.shape[1]
    return attention_call(
        functools.partial(fwd_kernel, blocks=blocks, n=len(keys)), "attend", 2, seqs, pairs, blocks,
        [OWN] + [piece(*e) for e in keys + values], [OWN, EXT],
        [jax.ShapeDtypeStruct(q.shape, jnp.bfloat16), jax.ShapeDtypeStruct(q.shape[:2] + (128,), jnp.bfloat16)],
        [rows_of(blocks, 128), rows_of(blocks, 256), pltpu.VMEM((blocks // CB, 2 * BLK, CH), jnp.float32), acc_of(256)],
        [place, own, q] + [e[0] for e in keys + values])


def query_grad(place, own, q, do, q_ext, do_ext, tabs, keys, values):
    seqs, pairs, blocks = q.shape[0], q.shape[2] // 128, place.shape[1]
    return attention_call(
        functools.partial(dq_kernel, blocks=blocks, n=len(keys)), "query_grad", 3, seqs, pairs, blocks,
        [OWN, OWN, EXT, EXT] + [table()] * 3 + [piece(*e) for e in keys + values], OWN,
        jax.ShapeDtypeStruct(q.shape, jnp.bfloat16),
        [rows_of(blocks, 256), rows_of(blocks, 256), acc_of(128)],
        [place, own, q, do, q_ext, do_ext, *tabs] + [e[0] for e in keys + values])


def key_value_grad(place, own, slots, kv, tabs, queries, grads, lead, count):
    pairs, blocks = kv.shape[3] // 128, place.shape[1]
    shape = (count,) + kv.shape[2:]
    n = grads.shape[0]

    def own_part(i):
        return pl.BlockSpec((1, 1, 2 * BLK, 128), lambda s, h, *_: (i, s + lead, 0, h))

    return attention_call(
        functools.partial(dkv_kernel, blocks=blocks, n=len(queries), lead=lead), "key_value_grad", 4, count, pairs, blocks,
        [own_part(0), own_part(1)] + [table(lead)] * 3 + [piece(x, lead=lead) for x in queries]
        + [piece(x, lane=pairs, lead=lead) for x in queries]
        + [piece(grads, lead=lead, count=n), piece(grads, lane=pairs, lead=lead, count=n)], [OWN, OWN],
        [jax.ShapeDtypeStruct(shape, jnp.bfloat16)] * 2,
        [rows_of(blocks, 256), rows_of(blocks, 256), acc_of(128), acc_of(128)],
        [place, own, slots, kv, kv, *tabs] + queries * 2 + [grads] * 2, prefetch=3)


import math
from jax.sharding import PartitionSpec as P

HEAD_DIM = 64
ROT = 16
SEQS = 4
EPS = 1e-05
F32 = jnp.float32
BF16 = jnp.bfloat16


def rc(left, right):
    return lax.dot_general(left, right, (((0,), (0,)), ((), ())), preferred_element_type=F32)


def layer_stats(values, gain, shift):
    mean = jnp.mean(values, axis=-1, keepdims=True)
    centred = values - mean
    inverse = lax.rsqrt(jnp.mean(centred * centred, axis=-1, keepdims=True) + EPS)
    unit = centred * inverse
    return unit * gain + shift, unit, inverse


def layer_back(grad, unit, inverse, gain):
    scaled = grad * gain
    grad_in = inverse * (
        scaled
        - jnp.mean(scaled, axis=-1, keepdims=True)
        - unit * jnp.mean(scaled * unit, axis=-1, keepdims=True)
    )
    return grad_in, jnp.sum(grad * unit, axis=0), jnp.sum(grad, axis=0)


def rotary_tables(positions):
    half = ROT // 2
    dim = jnp.arange(2 * HEAD_DIM) % HEAD_DIM
    freq = jnp.where(dim < ROT, 10000.0 ** (-2.0 * (dim % half).astype(F32) / ROT), 0.0)
    angles = positions.astype(F32)[:, None] * freq[None, :]
    sin = jnp.sin(angles)
    return jnp.cos(angles), jnp.where(dim < half, sin, 0.0), jnp.where(dim < half, 0.0, sin)


def turn(x, ctab, above, below, sign):
    up = pltpu.roll(x, 128 - ROT // 2, axis=1)
    down = pltpu.roll(x, ROT // 2, axis=1)
    return x * ctab + sign * (down * below - up * above)


def project_kernel(h_ref, wq_ref, wk_ref, wv_ref, bias_ref, c_ref, a_ref, b_ref, q_ref, kv_ref):
    h = h_ref[...]
    width = wq_ref.shape[1]
    tabs = c_ref[...], a_ref[...], b_ref[...]
    for at, (w_ref, out) in enumerate(((wq_ref, q_ref.at[0]), (wk_ref, kv_ref.at[0, 0]), (wv_ref, kv_ref.at[1, 0]))):
        lin = nn(h, w_ref[...]) + bias_ref[at:at + 1, :]
        for p in range(width // 128):
            part = lin[:, p * 128:(p + 1) * 128]
            if at < 2:
                part = turn(part, *tabs, 1.0)
            out[:, p * 128:(p + 1) * 128] = part.astype(BF16)


def project(rows, wq, wk, wv, bias, tabs):
    total, depth = rows.shape
    width = wq.shape[1]
    step = total // SEQS
    weight = pl.BlockSpec((depth, width), lambda i: (0, 0))
    table = pl.BlockSpec((step, 128), lambda i: (i, 0))
    return pl.pallas_call(
        project_kernel,
        grid=(SEQS,),
        in_specs=[pl.BlockSpec((step, depth), lambda i: (i, 0)), weight, weight, weight,
                  pl.BlockSpec((3, width), lambda i: (0, 0)), table, table, table],
        out_specs=[pl.BlockSpec((1, step, width), lambda i: (i, 0, 0)),
                   pl.BlockSpec((2, 1, step, width), lambda i: (0, i, 0, 0))],
        out_shape=[jax.ShapeDtypeStruct((SEQS, step, width), BF16), jax.ShapeDtypeStruct((2, SEQS, step, width), BF16)],
        compiler_params=pltpu.CompilerParams(vmem_limit_bytes=48 * 2**20),
        cost_estimate=pl.CostEstimate(flops=6 * total * depth * width, bytes_accessed=6 * depth * width, transcendentals=0),
        name="project",
    )(rows, wq, wk, wv, bias, *tabs)


def mlp_kernel(h_ref, dy_ref, gate_ref, up_ref, down_ref, act_ref, *grad_refs):
    width = gate_ref.shape[1]
    gate = nn(h_ref[...], gate_ref[...])
    up = nn(h_ref[...], up_ref[...])
    grad = nt(dy_ref[...], down_ref[...])
    sig = 1.0 / (1.0 + jnp.exp(-gate))
    silu = gate * sig
    act_ref[...] = (silu * up).astype(BF16)
    outs = grad_refs if len(grad_refs) == 2 else (grad_refs[0].at[:, :width], grad_refs[0].at[:, width:])
    outs[0][...] = (grad * up * (sig + silu * (1.0 - sig))).astype(BF16)
    outs[1][...] = (grad * silu).astype(BF16)


def mlp(rows, dy, gate_w, up_w, down_w, step=256):
    total, depth = rows.shape
    width = gate_w.shape[1]
    joined = width % 128 == 0
    block = pl.BlockSpec((step, depth), lambda i: (i, 0))

    def whole(x):
        return pl.BlockSpec(x.shape, lambda i: (0, 0), pipeline_mode=pl.Buffered(1))

    def out(n):
        return pl.BlockSpec((step, n), lambda i: (i, 0)), jax.ShapeDtypeStruct((total, n), BF16)

    outs = [out(width), out(2 * width)] if joined else [out(width)] * 3
    act, *grads = pl.pallas_call(
        mlp_kernel,
        grid=(total // step,),
        in_specs=[block, block, whole(gate_w), whole(up_w), whole(down_w)],
        out_specs=[o[0] for o in outs],
        out_shape=[o[1] for o in outs],
        compiler_params=pltpu.CompilerParams(vmem_limit_bytes=56 * 2**20),
        cost_estimate=pl.CostEstimate(flops=6 * total * depth * width, bytes_accessed=6 * depth * width + 10 * total * depth,
                                      transcendentals=total * width),
        name="mlp",
    )(rows, dy, gate_w, up_w, down_w)
    return act, grads[0] if joined else jnp.concatenate(grads, axis=1)


def ctx_swap(x, mask):
    n = lax.axis_size("ctx")
    return lax.ppermute(x, "ctx", [(i, i ^ mask) for i in range(n)])


def add16(a, b):
    return (a.astype(F32) + b.astype(F32)).astype(BF16)


def after(x, *deps):
    if not jax.tree.leaves(deps):
        return x
    return lax.optimization_barrier((x, deps))[0]


def half_of(x, bit, mine):
    side = (lax.axis_index("ctx") >> bit) & 1
    r = x.shape[0] // 2
    return lax.dynamic_slice_in_dim(x, (side if mine else 1 - side) * r, r, 0)


def weight_grad(part):
    core = lax.axis_index("ctx") & 1
    got = ctx_swap(part(1 - core).astype(BF16), 1)
    gate = yield
    half = (part(core) + after(got, gate).astype(F32)).astype(BF16)
    bits = list(range(1, int(math.log2(lax.axis_size("ctx")))))
    orders = [bits, bits[::-1]]
    r = half.shape[0] // 2
    streams = [half[:r], half[r:]]
    gate = yield streams
    for i in range(len(bits)):
        streams = after(streams, gate)
        got = [ctx_swap(half_of(x, o[i], False), 1 << o[i]) for x, o in zip(streams, orders)]
        gate = yield
        streams, got = after((streams, got), gate)
        streams = [add16(half_of(x, o[i], True), g) for x, o, g in zip(streams, orders, got)]
        gate = yield streams
    for i in reversed(range(len(bits))):
        streams = after(streams, gate)
        got = [ctx_swap(x, 1 << o[i]) for x, o in zip(streams, orders)]
        gate = yield
        streams, got = after((streams, got), gate)
        streams = [
            jnp.where(((lax.axis_index("ctx") >> o[i]) & 1) == 0, jnp.concatenate([x, g]), jnp.concatenate([g, x]))
            for x, o, g in zip(streams, orders, got)
        ]
        if i == 0:
            streams = jnp.concatenate(streams)
        gate = yield streams
    streams = after(streams, gate)
    other = ctx_swap(streams, 1)
    gate = yield
    yield after((streams, other), gate)


def begin(*args):
    chain = weight_grad(*args)
    next(chain)
    return chain


def take(chain, gate=None):
    return chain.send(gate)


def go(chain, gate=None):
    chain.send(gate)


def take_extra(chain):
    for _ in range(2 * int(math.log2(lax.axis_size("ctx"))) - 6):
        go(chain)
        take(chain)


def unpack_rows_kernel(core_ref, half_ref, other_ref, *out_refs, turned):
    def put(src):
        at = 0
        for i, out in enumerate(out_refs):
            if turned and i == len(out_refs) - 1:
                out[...] = src[:, at:].astype(F32).T
            else:
                out[...] = src[:, at:at + out.shape[1]].astype(F32)
                at += out.shape[1]

    @pl.when(pl.program_id(0) == core_ref[0])
    def _():
        put(half_ref)

    @pl.when(pl.program_id(0) != core_ref[0])
    def _():
        put(other_ref)


def unpack_rows(half, other, parts, turned=False):
    r, c = half.shape
    step = math.gcd(r, 256)
    blocks = r // step
    w = c // parts
    core = lax.axis_index("ctx") & 1

    def mine(i, j, core_ref):
        return jnp.where(i == core_ref[0], j, jnp.where(core_ref[0] == 0, blocks - 1, 0)), 0

    def theirs(i, j, core_ref):
        return jnp.where(i != core_ref[0], j, jnp.where(core_ref[0] == 1, blocks - 1, 0)), 0

    specs = [pl.BlockSpec((step, w), lambda i, j, _: (i * blocks + j, 0))] * parts
    shapes = [jax.ShapeDtypeStruct((2 * r, w), F32)] * parts
    if turned:
        specs[-1] = pl.BlockSpec((w, step), lambda i, j, _: (0, i * blocks + j))
        shapes[-1] = jax.ShapeDtypeStruct((w, 2 * r), F32)
    return pl.pallas_call(
        functools.partial(unpack_rows_kernel, turned=turned),
        grid_spec=pltpu.PrefetchScalarGridSpec(
            num_scalar_prefetch=1, grid=(2, blocks),
            in_specs=[pl.BlockSpec((step, c), mine), pl.BlockSpec((step, c), theirs)], out_specs=specs),
        out_shape=shapes,
        compiler_params=pltpu.CompilerParams(vmem_limit_bytes=40 * 2**20),
        cost_estimate=pl.CostEstimate(flops=0, bytes_accessed=12 * r * c, transcendentals=0),
        name="unpack_rows",
    )(core[None], half, other)


def columns(x, which):
    w = x.shape[1] // 2
    return lax.dynamic_slice_in_dim(x, which * w, w, 1)


def unpack_cols_kernel(core_ref, half_ref, other_ref, out_ref):
    c = half_ref.shape[1]
    core = core_ref[0]
    out_ref[:, pl.ds(pl.multiple_of(core * c, 128), c)] = half_ref[...].astype(F32)
    out_ref[:, pl.ds(pl.multiple_of((1 - core) * c, 128), c)] = other_ref[...].astype(F32)


def unpack_cols(half, other):
    r, c = half.shape
    step = math.gcd(r, 256)
    block = pl.BlockSpec((step, c), lambda i, _: (i, 0))
    return pl.pallas_call(
        unpack_cols_kernel,
        grid_spec=pltpu.PrefetchScalarGridSpec(
            num_scalar_prefetch=1, grid=(r // step,), in_specs=[block, block],
            out_specs=pl.BlockSpec((step, 2 * c), lambda i, _: (i, 0))),
        out_shape=jax.ShapeDtypeStruct((r, 2 * c), F32),
        compiler_params=pltpu.CompilerParams(vmem_limit_bytes=40 * 2**20),
        cost_estimate=pl.CostEstimate(flops=0, bytes_accessed=12 * r * c, transcendentals=0),
        name="unpack_cols",
    )((lax.axis_index("ctx") & 1)[None], half, other)


def all_rows(x):
    return lax.all_gather(x, "tp", axis=0, tiled=True)


def tp_shift(x, d):
    n = lax.axis_size("tp")
    return lax.ppermute(x, "tp", [(i, (i + d) % n) for i in range(n)])


def part_of(x, d, axis):
    n = lax.axis_size("tp")
    w = x.shape[axis] // n
    return lax.dynamic_slice_in_dim(x, (lax.axis_index("tp") + d) % n * w, w, axis)


def exchange(x, split, join):
    n, me = lax.axis_size("tp"), lax.axis_index("tp")
    w = x.shape[join]
    shape = list(x.shape)
    shape[split] //= n
    shape[join] *= n
    out = jnp.zeros(shape, x.dtype)
    for d in range(n):
        got = tp_shift(part_of(x, d, split), d) if d else part_of(x, 0, split)
        out = lax.dynamic_update_slice_in_dim(out, got, (me + n - d) % n * w, join)
    return out


def sum_rows(x):
    return lax.psum_scatter(x, "tp", scatter_dimension=0, tiled=True)


def gather_pair(kv):
    n = lax.axis_size("ctx")
    held = {0: ((kv, 0), (kv, 1))}
    for bit in range(1, int(math.log2(n))):
        mask = 1 << bit
        for j in list(held):
            if j == 0:
                got = ctx_swap(kv, mask)
                held[mask] = (got, 0), (got, 1)
            elif mask == 4 and j == 2:
                held[6] = (ctx_swap(held[2][0][0][0:1], 4), 0), (ctx_swap(held[4][1][0][1:2], 2), 0)
            else:
                (k, i), (v, t) = held[j]
                if k is v:
                    got = ctx_swap(k, mask)
                    held[j | mask] = (got, i), (got, t)
                else:
                    held[j | mask] = (ctx_swap(k, mask), i), (ctx_swap(v, mask), t)
    for j in list(held):
        (k, i), (v, t) = held[j]
        got = ctx_swap(k, 1)
        held[j | 1] = (got, i), (got if k is v else ctx_swap(v, 1), t)
    return [held[j][0] for j in range(n)], [held[j][1] for j in range(n)]


def gather_other(x):
    held = {0: x, 1: ctx_swap(x, 1)}
    for j in range(2, lax.axis_size("ctx"), 2):
        held[j] = ctx_swap(x, j)
    return held


def gather_cores(held, gate=None):
    n = lax.axis_size("ctx")
    for j in range(2, n, 2):
        held[j + 1] = ctx_swap(after(held[j], gate), 1)
    return [held[j] for j in range(n)]


def sum_over_all(x):
    steps = [(axis, bit) for axis in ("ctx", "tp") for bit in range(int(math.log2(lax.axis_size(axis))))]
    for axis, bit in sorted(steps, key=lambda step: step[0] == "ctx" and step[1] > 0):
        x = x + lax.ppermute(x, axis, [(i, i ^ (1 << bit)) for i in range(lax.axis_size(axis))])
        yield x
    while True:
        yield x


def gather_tp(x):
    n, me = lax.axis_size("tp"), lax.axis_index("tp")
    out = jnp.zeros((n,) + x.shape, x.dtype)
    for d in range(n):
        got = lax.ppermute(x, "tp", [(i, (i + d) % n) for i in range(n)]) if d else x
        out = lax.dynamic_update_index_in_dim(out, got, (me + n - d) % n, 0)
    return out


def local(tokens, cotangent, block_order, gain_one, shift_one, query_w, key_w, value_w, query_b, key_b, value_b,
          output_w, gain_two, shift_two, gate_w, up_w, down_w):
    heads = key_b.shape[0]
    width = heads * HEAD_DIM
    n_ctx, n_tp = lax.axis_size("ctx"), lax.axis_size("tp")
    ctx = lax.axis_index("ctx")
    own = lax.dynamic_slice_in_dim(block_order, 2 * ctx, 2, 1)
    picked = (jnp.arange(n_ctx, dtype=jnp.int32) ^ ctx)[:, None] == jnp.arange(n_ctx, dtype=jnp.int32)[None, :]
    by_ctx = block_order.reshape(SEQS, 1, n_ctx, 2)
    place = jnp.sum(jnp.where(picked[None, :, :, None], by_ctx, 0), axis=2).astype(jnp.int32).reshape(SEQS, 2 * n_ctx)
    positions = (own[:, :, None] * BLK + jnp.arange(BLK, dtype=jnp.int32)).reshape(-1)
    tabs = rotary_tables(positions)

    x = tokens.astype(F32)
    normed_one, unit_one, inverse_one = layer_stats(x, gain_one, shift_one)
    rows_one = all_rows(normed_one.astype(BF16))
    key_bias = jnp.concatenate([key_b, jnp.zeros((heads, HEAD_DIM - ROT), F32)], axis=1).reshape(-1)
    bias = jnp.stack([query_b, key_bias, value_b])
    q, kv = project(rows_one, query_w, key_w, value_w, bias, tabs)
    keys, values = gather_pair(kv.reshape(2, SEQS, 2, BLK, width))
    arrived = [e[0] for e in keys + values]

    rows_w = output_w.shape[0] // n_ctx
    part = lax.dynamic_slice_in_dim(output_w, ctx * rows_w, rows_w, 0)
    part = gather_tp(after(part, kv))
    dy_rows = all_rows(after(cotangent, rows_one))
    whole_w = lax.all_gather(after(part, arrived, dy_rows), "ctx", axis=1).reshape(n_tp * output_w.shape[0], -1)

    attn, q_ext = attend(place, own, q, keys, values)
    attn_rows = attn.reshape(-1, width)
    attn_own = exchange(attn_rows, 0, 1)
    mixed = x + nn(attn_own, whole_w)
    normed_two, unit_two, inverse_two = layer_stats(mixed, gain_two, shift_two)
    rows_two = all_rows(after(normed_two.astype(BF16), dy_rows, whole_w))
    shape = (1, SEQS, 2, BLK, width + 128)
    queries = gather_cores(gather_other(after(jnp.concatenate([q, q_ext], axis=2).reshape(shape), attn_own)))
    rows_two = after(rows_two, queries)

    act, grad_gu = mlp(rows_two, dy_rows, gate_w, up_w, down_w)
    ff = gate_w.shape[1]
    part_two = (nt(grad_gu[:, :ff], gate_w) + nt(grad_gu[:, ff:], up_w)).astype(BF16)
    grad_two = sum_rows(part_two)
    act, rows_two, dy_rows, grad_gu = after((act, rows_two, dy_rows, grad_gu), part_two)
    gu = begin(lambda core: rc(columns(rows_two, core), grad_gu))
    dw = begin(lambda core: rc(act, columns(dy_rows, core)))
    held = take(gu)
    go(gu)
    down = nn(after(act, held), down_w).astype(BF16)
    held = take(dw), take(gu, down)
    go(gu)
    go(dw, held)
    grad_two = after(grad_two, held)

    norm_two, grad_gain_two, grad_shift_two = layer_back(grad_two.astype(F32), unit_two, inverse_two, gain_two)
    grad_mixed = cotangent.astype(F32) + norm_two
    branch_own = grad_mixed.astype(BF16)
    grad_attn = nt(branch_own, whole_w).astype(BF16)
    held = take(gu, grad_attn)
    go(gu)
    grad_attn = exchange(grad_attn, 1, 0)
    lane = jnp.arange(128)[None, :]
    ind = ((jnp.arange(width) // HEAD_DIM)[:, None] == lane // 3).astype(F32)
    delta = lax.dot_general(grad_attn.astype(F32) * attn_rows.astype(F32), ind, (((1,), (0,)), ((), ())),
                            precision=lax.Precision.HIGHEST, preferred_element_type=F32)
    do_ext = terms(-delta, lane).astype(BF16)
    do_sent = jnp.concatenate([grad_attn, do_ext], axis=1).reshape(shape)
    do_sent = after(do_sent, held)
    grads = lax.all_gather(do_sent, "ctx", axis=0, tiled=True)
    grad_q = query_grad(place, own, q, grad_attn.reshape(q.shape), q_ext, do_ext.reshape(q_ext.shape), tabs, keys, values)
    grad_q = grad_q.reshape(-1, width)
    q_part = nt(grad_q, query_w)
    held = take(gu, q_part), take(dw, q_part)
    go(gu)
    go(dw)
    grads = after(grads, held)
    branch = all_rows(after(branch_own, grads))
    first = key_value_grad(place, own, block_order, kv, tabs, queries, grads, 0, SEQS // 2)
    grads = after(grads, take(dw, first))
    go(dw)
    second = key_value_grad(place, own, block_order, kv, tabs, queries, grads, SEQS // 2, SEQS // 2)
    grad_k, grad_v = (jnp.concatenate(pair).reshape(-1, width) for pair in zip(first, second))
    part_one = q_part + nt(grad_k, key_w) + nt(grad_v, value_w)
    part_sent = after(part_one.astype(BF16), branch)
    grad_one = sum_rows(part_sent)
    out_tokens = (mixed + sum_rows(after(down, grad_one)).astype(F32)).astype(BF16)

    rows_one, branch, grad_q, grad_k, grad_v = after((rows_one, branch, grad_q, grad_k, grad_v), part_sent)
    grad_qkv = jnp.concatenate([grad_q, grad_k, grad_v], axis=1)
    chain = begin(lambda core: jnp.concatenate([rc(columns(rows_one, core), grad_qkv), rc(columns(branch, core), attn_rows)], axis=1))
    take(gu, part_sent)
    take_extra(gu)
    go(gu)
    held = take(chain)
    go(chain)
    unit_rows = (rows_one.astype(F32) - shift_one) / gain_one
    bias_grad = jnp.sum(grad_qkv.astype(F32), axis=0)
    tp_row = (jnp.arange(n_tp) == lax.axis_index("tp"))[:, None]
    small = jnp.concatenate([
        jnp.sum(part_one * unit_rows, axis=0), jnp.sum(part_one, axis=0), grad_gain_two, grad_shift_two,
        jnp.where(tp_row, bias_grad[None, :], 0.0).reshape(-1)])
    sums = sum_over_all(after(small, held).reshape(-1, 1024))
    small = [next(sums) for _ in range(1 + int(math.log2(n_tp)))]
    made = take(dw, held)
    take_extra(dw)
    go(dw)
    held = take(chain, (made, small))
    go(chain)
    small = next(sums)
    take(dw, held)
    go(dw)
    held = take(chain, small)
    go(chain)
    grad_gate_w, grad_up_w = unpack_rows(*take(gu, held), 2)
    for _ in range(4):
        small = next(sums)
    held = take(chain, (grad_gate_w, small))
    go(chain)
    grad_down_w = unpack_cols(*take(dw, held))
    take(chain, grad_down_w)
    take_extra(chain)
    go(chain)
    depth = x.shape[1]
    small = small.reshape(-1)
    norms = small[:4 * depth].reshape(4, depth)
    bias_sum = jnp.sum(jnp.where(tp_row, small[4 * depth:].reshape(n_tp, -1), 0.0), axis=0)
    grad_query_w, grad_key_w, grad_value_w, grad_output_w = unpack_rows(*take(chain), 4, True)
    norm_one, _, _ = layer_back(grad_one.astype(F32), unit_one, inverse_one, gain_one)
    grad_tokens = (grad_mixed + norm_one).astype(BF16)
    return (
        out_tokens, grad_tokens, norms[0], norms[1], grad_query_w, grad_key_w, grad_value_w,
        bias_sum[:width], bias_sum[width:2 * width].reshape(heads, HEAD_DIM)[:, :ROT], bias_sum[2 * width:],
        grad_output_w, norms[2], norms[3], grad_gate_w, grad_up_w, grad_down_w,
    )


def solution(mesh):
    rows, cols, depth, flat = P(("ctx", "tp"), None), P(None, "tp"), P("tp", None), P("tp")
    in_specs = (rows, rows, P(), P(), P(), cols, cols, cols, flat, depth, flat, depth, P(), P(), cols, cols, depth)
    out_specs = (rows, rows, P(), P(), cols, cols, cols, flat, depth, flat, depth, P(), P(), cols, cols, depth)
    return jax.shard_map(local, mesh=mesh, in_specs=in_specs, out_specs=out_specs, check_vma=False)
```

```python
import functools
import jax, jax.numpy as jnp
from jax import lax
from jax.experimental import pallas as pl
from jax.experimental.pallas import tpu as pltpu

BLK = 128
CB = 8
CH = BLK * CB
NEG = -1e30
SCALE = 0.125


def nt(a, b):
    return lax.dot_general(a, b, (((1,), (1,)), ((), ())), preferred_element_type=jnp.float32)


def nn(a, b):
    return lax.dot_general(a, b, (((1,), (0,)), ((), ())), preferred_element_type=jnp.float32)


def lane_of(shape):
    return lax.broadcasted_iota(jnp.int32, shape, 1)


def row_of(shape):
    return lax.broadcasted_iota(jnp.int32, shape, 0)


def split_heads(x):
    low = lane_of(x.shape) < 64
    zero = jnp.zeros_like(x)
    return jnp.concatenate([jnp.where(low, x, zero), jnp.where(low, zero, x)], axis=0)


def join_heads(x):
    low = lane_of((BLK, 128)) < 64
    return jnp.where(low, x[:BLK], x[BLK:])


def own_lanes(pair):
    shape = (2 * BLK, 128)
    return lane_of(shape) // 3 == 2 * pair + row_of(shape) // BLK


def lanes_of(pair):
    return slice(pair * 128, (pair + 1) * 128)


def terms(x, lane):
    first = x.astype(jnp.bfloat16).astype(jnp.float32)
    second = (x - first).astype(jnp.bfloat16).astype(jnp.float32)
    return jnp.where(lane % 3 == 0, first, jnp.where(lane % 3 == 1, second, x - first - second))


def place_rows(place_ref, s, refs, dst_ref, ext=False):
    pairs = dst_ref.shape[0]
    at = 0
    for ref in refs:
        for j in range(ref.shape[0]):
            for w in range(2):
                rows = pl.ds(pl.multiple_of(place_ref[s, at] * BLK, BLK), BLK)
                for p in range(pairs):
                    dst_ref[p, rows, 0:128] = ref[j, 0, w, :, p * 128:(p + 1) * 128]
                    if ext:
                        dst_ref[p, rows, 128:256] = ref[j, 0, w, :, pairs * 128:]
                at += 1


def sweep(full, step):
    def one(c, carry):
        step(c, False)
        return carry

    lax.fori_loop(0, full, one, 0)
    step(full, True)


def span(c):
    return pl.ds(pl.multiple_of(c * CH, CH), CH)


def may_see(query_block, c):
    shape = (2 * BLK, CH)
    return c * CH + lane_of(shape) <= query_block * BLK + row_of(shape) % BLK


def fwd_kernel(place_ref, own_ref, q_ref, *refs, pairs, n):
    k_refs, v_refs, (o_ref, ext_ref, ks, vs, qs, scr, run, acc) = refs[:n], refs[n:2 * n], refs[2 * n:]
    s = pl.program_id(0)

    @pl.when(s == 0)
    def _():
        for p in range(pairs):
            vs[p, :, 128:256] = jnp.ones((vs.shape[1], 128), jnp.bfloat16)

    place_rows(place_ref, s, k_refs, ks)
    place_rows(place_ref, s, v_refs, vs)

    for w in range(2):
        rows = slice(w * BLK, (w + 1) * BLK)
        pos = own_ref[s, w]
        for p in range(pairs):
            qs[p] = split_heads(q_ref[0, rows, lanes_of(p)] * jnp.bfloat16(SCALE))
        run[...] = jnp.full_like(run, NEG)
        acc[...] = jnp.zeros_like(acc)

        def score(c, masked):
            for p in range(pairs):
                sc = nt(qs[p], ks[p, span(c), :])
                if masked:
                    sc = jnp.where(may_see(pos, c), sc, NEG)
                scr[p, :, span(c)] = sc
                top = run[p]
                for t in range(CB):
                    top = jnp.maximum(top, sc[:, t * 128:(t + 1) * 128])
                run[p] = top

        sweep(pos // CB, score)
        for p in range(pairs):
            run[p] = jnp.broadcast_to(jnp.max(run[p], axis=1, keepdims=True), (2 * BLK, 128))

        def weigh(c, masked):
            for p in range(pairs):
                weight = jnp.exp(scr[p, :, span(c)] - jnp.concatenate([run[p]] * CB, axis=1)).astype(jnp.bfloat16)
                acc[p] += nn(weight, vs[p, span(c), :])

        sweep(pos // CB, weigh)
        lane = lane_of((2 * BLK, 128))
        ext = jnp.zeros((BLK, 128), jnp.float32)
        for p in range(pairs):
            total = acc[p, :, 128:256]
            o_ref[0, rows, lanes_of(p)] = join_heads(acc[p, :, 0:128] / total).astype(jnp.bfloat16)
            mine = jnp.where(own_lanes(p), terms(-(run[p] + jnp.log(total)), lane), 0.0)
            ext = ext + mine[:BLK] + mine[BLK:]
        ext_ref[0, rows, :] = ext.astype(jnp.bfloat16)


def dq_kernel(place_ref, own_ref, q_ref, do_ref, qx_ref, dox_ref, c_ref, a_ref, b_ref, *refs, pairs, n):
    k_refs, v_refs, (dq_ref, ks, vs, qs, dos, acc) = refs[:n], refs[n:2 * n], refs[2 * n:]
    s = pl.program_id(0)

    @pl.when(s == 0)
    def _():
        for ref in (ks, vs):
            for p in range(pairs):
                ref[p, :, 128:256] = jnp.ones((ref.shape[1], 128), jnp.bfloat16)

    place_rows(place_ref, s, k_refs, ks)
    place_rows(place_ref, s, v_refs, vs)

    for w in range(2):
        rows = slice(w * BLK, (w + 1) * BLK)
        pos = own_ref[s, w]

        def extend(tile, ext, p):
            both = jnp.concatenate([ext, ext], axis=0)
            return jnp.concatenate([split_heads(tile), jnp.where(own_lanes(p), both, jnp.zeros_like(both))], axis=1)

        for p in range(pairs):
            qs[p] = extend(q_ref[0, rows, lanes_of(p)] * jnp.bfloat16(SCALE), qx_ref[0, rows, :], p)
            dos[p] = extend(do_ref[0, rows, lanes_of(p)], dox_ref[0, rows, :], p)
        acc[...] = jnp.zeros_like(acc)

        def step(c, masked):
            for p in range(pairs):
                prob = jnp.exp(nt(qs[p], ks[p, span(c), :]))
                if masked:
                    prob = jnp.where(may_see(pos, c), prob, 0.0)
                ds = (prob * nt(dos[p], vs[p, span(c), :])).astype(jnp.bfloat16)
                acc[p] += nn(ds, ks[p, span(c), 0:128])

        sweep(pos // CB, step)
        for p in range(pairs):
            grad = join_heads(acc[p]) * SCALE
            dq_ref[0, rows, lanes_of(p)] = turn(grad, c_ref[rows], a_ref[rows], b_ref[rows], -1.0).astype(jnp.bfloat16)


def dkv_kernel(place_ref, own_ref, kv_ref, c_ref, a_ref, b_ref, *refs, pairs, n, lead):
    q_refs, do_refs, (dk_ref, dv_ref, qs, dos, kw, vw, acck, accv) = refs[:n], refs[n:2 * n], refs[2 * n:]
    s = pl.program_id(0) + lead
    place_rows(place_ref, s, q_refs, qs, True)
    place_rows(place_ref, s, do_refs, dos, True)
    chunks = qs.shape[1] // CH

    for w in range(2):
        rows = slice(w * BLK, (w + 1) * BLK)
        pos = own_ref[s, w]
        first = pos // CB
        for p in range(pairs):
            ones = own_lanes(p).astype(jnp.bfloat16)
            kw[p] = jnp.concatenate([split_heads(kv_ref[0, 0, rows, lanes_of(p)] * jnp.bfloat16(SCALE)), ones], axis=1)
            vw[p] = jnp.concatenate([split_heads(kv_ref[1, 0, rows, lanes_of(p)]), ones], axis=1)
        acck[...] = jnp.zeros_like(acck)
        accv[...] = jnp.zeros_like(accv)

        def step(c, masked):
            for p in range(pairs):
                prob = jnp.exp(nt(kw[p], qs[p, span(c), :]))
                if masked:
                    shape = (2 * BLK, CH)
                    prob = jnp.where(pos * BLK + row_of(shape) % BLK <= c * CH + lane_of(shape), prob, 0.0)
                accv[p] += nn(prob.astype(jnp.bfloat16), dos[p, span(c), 0:128])
                ds = (prob * nt(vw[p], dos[p, span(c), :])).astype(jnp.bfloat16)
                acck[p] += nn(ds, qs[p, span(c), 0:128])

        def one(c, carry):
            step(c, False)
            return carry

        step(first, True)
        lax.fori_loop(first + 1, chunks, one, 0)
        for p in range(pairs):
            grad = join_heads(acck[p]) * SCALE
            dk_ref[0, rows, lanes_of(p)] = turn(grad, c_ref[rows], a_ref[rows], b_ref[rows], -1.0).astype(jnp.bfloat16)
            dv_ref[0, rows, lanes_of(p)] = join_heads(accv[p]).astype(jnp.bfloat16)


def own(width):
    return pl.BlockSpec((1, 2 * BLK, width), lambda s, *_: (s, 0, 0))


def table(lead=0):
    return pl.BlockSpec((2 * BLK, 128), lambda s, *_: (s + lead, 0))


def piece(x, first=0, lead=0):
    return pl.BlockSpec((1, 1, 2, BLK, x.shape[4]), lambda s, *_: (first, s + lead, 0, 0, 0))


def attention_call(kernel, name, mats, seqs, pairs, blocks, in_specs, out_specs, out_shape, scratch, args):
    work = seqs * pairs * 2 * 2 * BLK * blocks * BLK // 2
    return pl.pallas_call(
        kernel,
        grid_spec=pltpu.PrefetchScalarGridSpec(
            num_scalar_prefetch=2, grid=(seqs,), in_specs=in_specs, out_specs=out_specs, scratch_shapes=scratch),
        out_shape=out_shape,
        compiler_params=pltpu.CompilerParams(vmem_limit_bytes=60 * 2**20),
        cost_estimate=pl.CostEstimate(flops=work * 64 * mats, bytes_accessed=seqs * pairs * blocks * BLK * 128, transcendentals=0),
        name=name,
    )(*args)


def rows_of(pairs, blocks, lanes):
    return pltpu.VMEM((pairs, blocks * BLK, lanes), jnp.bfloat16)


def acc_of(pairs, lanes, dtype=jnp.float32):
    return pltpu.VMEM((pairs, 2 * BLK, lanes), dtype)


def attend(place, own_blocks, q, keys, values):
    seqs, width, blocks = q.shape[0], q.shape[2], place.shape[1]
    pairs = width // 128
    return attention_call(
        functools.partial(fwd_kernel, pairs=pairs, n=len(keys)), "attend", 2, seqs, pairs, blocks,
        [own(width)] + [piece(*e) for e in keys + values], [own(width), own(128)],
        [jax.ShapeDtypeStruct(q.shape, jnp.bfloat16), jax.ShapeDtypeStruct(q.shape[:2] + (128,), jnp.bfloat16)],
        [rows_of(pairs, blocks, 128), rows_of(pairs, blocks, 256), acc_of(pairs, 128, jnp.bfloat16), acc_of(pairs, blocks * BLK),
         acc_of(pairs, 128), acc_of(pairs, 256)],
        [place, own_blocks, q] + [e[0] for e in keys + values])


def query_grad(place, own_blocks, q, do, q_ext, do_ext, tabs, keys, values):
    seqs, width, blocks = q.shape[0], q.shape[2], place.shape[1]
    pairs = width // 128
    return attention_call(
        functools.partial(dq_kernel, pairs=pairs, n=len(keys)), "query_grad", 3, seqs, pairs, blocks,
        [own(width), own(width), own(128), own(128)] + [table()] * 3 + [piece(*e) for e in keys + values], own(width),
        jax.ShapeDtypeStruct(q.shape, jnp.bfloat16),
        [rows_of(pairs, blocks, 256), rows_of(pairs, blocks, 256), acc_of(pairs, 256, jnp.bfloat16), acc_of(pairs, 256, jnp.bfloat16),
         acc_of(pairs, 128)],
        [place, own_blocks, q, do, q_ext, do_ext, *tabs] + [e[0] for e in keys + values])


def key_value_grad(place, own_blocks, kv, tabs, queries, grads, lead, count):
    width, blocks = kv.shape[3], place.shape[1]
    pairs = width // 128
    shape = (count,) + kv.shape[2:]
    return attention_call(
        functools.partial(dkv_kernel, pairs=pairs, n=len(queries), lead=lead), "key_value_grad", 4, count, pairs, blocks,
        [pl.BlockSpec((2, 1, 2 * BLK, width), lambda s, *_: (0, s + lead, 0, 0))] + [table(lead)] * 3
        + [piece(x, lead=lead) for x in queries + grads], [own(width)] * 2,
        [jax.ShapeDtypeStruct(shape, jnp.bfloat16)] * 2,
        [rows_of(pairs, blocks, 256), rows_of(pairs, blocks, 256), acc_of(pairs, 256, jnp.bfloat16), acc_of(pairs, 256, jnp.bfloat16),
         acc_of(pairs, 128), acc_of(pairs, 128)],
        [place, own_blocks, kv, *tabs] + queries + grads)


import math
from jax.sharding import PartitionSpec as P

HEAD_DIM = 64
ROT = 16
SEQS = 4
EPS = 1e-05
F32 = jnp.float32
BF16 = jnp.bfloat16


def rc(left, right):
    return lax.dot_general(left, right, (((0,), (0,)), ((), ())), preferred_element_type=F32)


def layer_stats(values, gain, shift):
    mean = jnp.mean(values, axis=-1, keepdims=True)
    centred = values - mean
    inverse = lax.rsqrt(jnp.mean(centred * centred, axis=-1, keepdims=True) + EPS)
    unit = centred * inverse
    return unit * gain + shift, unit, inverse


def layer_back(grad, unit, inverse, gain):
    scaled = grad * gain
    grad_in = inverse * (
        scaled
        - jnp.mean(scaled, axis=-1, keepdims=True)
        - unit * jnp.mean(scaled * unit, axis=-1, keepdims=True)
    )
    return grad_in, jnp.sum(grad * unit, axis=0), jnp.sum(grad, axis=0)


def rotary_tables(positions):
    half = ROT // 2
    dim = jnp.arange(2 * HEAD_DIM) % HEAD_DIM
    freq = jnp.where(dim < ROT, 10000.0 ** (-2.0 * (dim % half).astype(F32) / ROT), 0.0)
    angles = positions.astype(F32)[:, None] * freq[None, :]
    sin = jnp.sin(angles)
    return jnp.cos(angles), jnp.where(dim < half, sin, 0.0), jnp.where(dim < half, 0.0, sin)


def turn(x, ctab, above, below, sign):
    up = pltpu.roll(x, 128 - ROT // 2, axis=1)
    down = pltpu.roll(x, ROT // 2, axis=1)
    return x * ctab + sign * (down * below - up * above)


def project_kernel(h_ref, wq_ref, wk_ref, wv_ref, bias_ref, c_ref, a_ref, b_ref, q_ref, kv_ref):
    h = h_ref[...]
    width = wq_ref.shape[1]
    tabs = c_ref[...], a_ref[...], b_ref[...]
    for at, (w_ref, out) in enumerate(((wq_ref, q_ref.at[0]), (wk_ref, kv_ref.at[0, 0]), (wv_ref, kv_ref.at[1, 0]))):
        lin = nn(h, w_ref[...]) + bias_ref[at:at + 1, :]
        for p in range(width // 128):
            part = lin[:, p * 128:(p + 1) * 128]
            if at < 2:
                part = turn(part, *tabs, 1.0)
            out[:, p * 128:(p + 1) * 128] = part.astype(BF16)


def project(rows, wq, wk, wv, bias, tabs):
    total, depth = rows.shape
    width = wq.shape[1]
    step = total // SEQS
    weight = pl.BlockSpec((depth, width), lambda i: (0, 0))
    table = pl.BlockSpec((step, 128), lambda i: (i, 0))
    return pl.pallas_call(
        project_kernel,
        grid=(SEQS,),
        in_specs=[pl.BlockSpec((step, depth), lambda i: (i, 0)), weight, weight, weight,
                  pl.BlockSpec((3, width), lambda i: (0, 0)), table, table, table],
        out_specs=[pl.BlockSpec((1, step, width), lambda i: (i, 0, 0)),
                   pl.BlockSpec((2, 1, step, width), lambda i: (0, i, 0, 0))],
        out_shape=[jax.ShapeDtypeStruct((SEQS, step, width), BF16), jax.ShapeDtypeStruct((2, SEQS, step, width), BF16)],
        compiler_params=pltpu.CompilerParams(vmem_limit_bytes=48 * 2**20),
        cost_estimate=pl.CostEstimate(flops=6 * total * depth * width, bytes_accessed=6 * depth * width, transcendentals=0),
        name="project",
    )(rows, wq, wk, wv, bias, *tabs)


def mlp_kernel(h_ref, dy_ref, gate_ref, up_ref, down_ref, act_ref, *grad_refs):
    width = gate_ref.shape[1]
    gate = nn(h_ref[...], gate_ref[...])
    up = nn(h_ref[...], up_ref[...])
    grad = nt(dy_ref[...], down_ref[...])
    sig = 1.0 / (1.0 + jnp.exp(-gate))
    silu = gate * sig
    act_ref[...] = (silu * up).astype(BF16)
    outs = grad_refs if len(grad_refs) == 2 else (grad_refs[0].at[:, :width], grad_refs[0].at[:, width:])
    outs[0][...] = (grad * up * (sig + silu * (1.0 - sig))).astype(BF16)
    outs[1][...] = (grad * silu).astype(BF16)


def mlp(rows, dy, gate_w, up_w, down_w, step=256):
    total, depth = rows.shape
    width = gate_w.shape[1]
    joined = width % 128 == 0
    block = pl.BlockSpec((step, depth), lambda i: (i, 0))

    def whole(x):
        return pl.BlockSpec(x.shape, lambda i: (0, 0), pipeline_mode=pl.Buffered(1))

    def out(n):
        return pl.BlockSpec((step, n), lambda i: (i, 0)), jax.ShapeDtypeStruct((total, n), BF16)

    outs = [out(width), out(2 * width)] if joined else [out(width)] * 3
    act, *grads = pl.pallas_call(
        mlp_kernel,
        grid=(total // step,),
        in_specs=[block, block, whole(gate_w), whole(up_w), whole(down_w)],
        out_specs=[o[0] for o in outs],
        out_shape=[o[1] for o in outs],
        compiler_params=pltpu.CompilerParams(vmem_limit_bytes=56 * 2**20),
        cost_estimate=pl.CostEstimate(flops=6 * total * depth * width, bytes_accessed=6 * depth * width + 10 * total * depth,
                                      transcendentals=total * width),
        name="mlp",
    )(rows, dy, gate_w, up_w, down_w)
    return act, grads[0] if joined else jnp.concatenate(grads, axis=1)


def ctx_swap(x, mask):
    n = lax.axis_size("ctx")
    return lax.ppermute(x, "ctx", [(i, i ^ mask) for i in range(n)])


def add16(a, b):
    return (a.astype(F32) + b.astype(F32)).astype(BF16)


def after(x, *deps):
    if not jax.tree.leaves(deps):
        return x
    return lax.optimization_barrier((x, deps))[0]


def half_of(x, bit, mine):
    side = (lax.axis_index("ctx") >> bit) & 1
    r = x.shape[0] // 2
    return lax.dynamic_slice_in_dim(x, (side if mine else 1 - side) * r, r, 0)


def weight_grad(part, flying):
    core = lax.axis_index("ctx") & 1
    got = ctx_swap(part(1 - core).astype(BF16), 1)
    flying[:] = [got]
    gate = yield
    half = (part(core) + after(got, gate).astype(F32)).astype(BF16)
    bits = list(range(1, int(math.log2(lax.axis_size("ctx")))))
    orders = [bits, bits[::-1]]
    r = half.shape[0] // 2
    streams = [half[:r], half[r:]]
    gate = yield streams
    for i in range(len(bits)):
        streams = after(streams, gate)
        got = [ctx_swap(half_of(x, o[i], False), 1 << o[i]) for x, o in zip(streams, orders)]
        flying[:] = got
        gate = yield
        streams, got = after((streams, got), gate)
        streams = [add16(half_of(x, o[i], True), g) for x, o, g in zip(streams, orders, got)]
        gate = yield streams
    for i in reversed(range(len(bits))):
        streams = after(streams, gate)
        got = [ctx_swap(x, 1 << o[i]) for x, o in zip(streams, orders)]
        flying[:] = got
        gate = yield
        streams, got = after((streams, got), gate)
        streams = [
            jnp.where(((lax.axis_index("ctx") >> o[i]) & 1) == 0, jnp.concatenate([x, g]), jnp.concatenate([g, x]))
            for x, o, g in zip(streams, orders, got)
        ]
        if i == 0:
            streams = jnp.concatenate(streams)
        gate = yield streams
    streams = after(streams, gate)
    other = ctx_swap(streams, 1)
    gate = yield
    yield after((streams, other), gate)


def begin(part, flying=None):
    chain = weight_grad(part, [] if flying is None else flying)
    next(chain)
    return chain


def take(chain, gate=None):
    return chain.send(gate)


def go(chain, gate=None):
    chain.send(gate)


def take_extra(chain):
    for _ in range(2 * int(math.log2(lax.axis_size("ctx"))) - 6):
        go(chain)
        take(chain)


def unpack_rows_kernel(core_ref, half_ref, other_ref, *out_refs, turned):
    def put(src):
        at = 0
        for i, out in enumerate(out_refs):
            if turned and i == len(out_refs) - 1:
                out[...] = src[:, at:].astype(F32).T
            else:
                out[...] = src[:, at:at + out.shape[1]].astype(F32)
                at += out.shape[1]

    @pl.when(pl.program_id(0) == core_ref[0])
    def _():
        put(half_ref)

    @pl.when(pl.program_id(0) != core_ref[0])
    def _():
        put(other_ref)


def unpack_rows(half, other, parts, turned=False):
    r, c = half.shape
    step = math.gcd(r, 256)
    blocks = r // step
    w = c // parts
    core = lax.axis_index("ctx") & 1

    def mine(i, j, core_ref):
        return jnp.where(i == core_ref[0], j, jnp.where(core_ref[0] == 0, blocks - 1, 0)), 0

    def theirs(i, j, core_ref):
        return jnp.where(i != core_ref[0], j, jnp.where(core_ref[0] == 1, blocks - 1, 0)), 0

    specs = [pl.BlockSpec((step, w), lambda i, j, _: (i * blocks + j, 0))] * parts
    shapes = [jax.ShapeDtypeStruct((2 * r, w), F32)] * parts
    if turned:
        specs[-1] = pl.BlockSpec((w, step), lambda i, j, _: (0, i * blocks + j))
        shapes[-1] = jax.ShapeDtypeStruct((w, 2 * r), F32)
    return pl.pallas_call(
        functools.partial(unpack_rows_kernel, turned=turned),
        grid_spec=pltpu.PrefetchScalarGridSpec(
            num_scalar_prefetch=1, grid=(2, blocks),
            in_specs=[pl.BlockSpec((step, c), mine), pl.BlockSpec((step, c), theirs)], out_specs=specs),
        out_shape=shapes,
        compiler_params=pltpu.CompilerParams(vmem_limit_bytes=40 * 2**20),
        cost_estimate=pl.CostEstimate(flops=0, bytes_accessed=12 * r * c, transcendentals=0),
        name="unpack_rows",
    )(core[None], half, other)


def columns(x, which):
    w = x.shape[1] // 2
    return lax.dynamic_slice_in_dim(x, which * w, w, 1)


def unpack_cols_kernel(core_ref, half_ref, other_ref, out_ref):
    c = half_ref.shape[1]
    core = core_ref[0]
    out_ref[:, pl.ds(pl.multiple_of(core * c, 128), c)] = half_ref[...].astype(F32)
    out_ref[:, pl.ds(pl.multiple_of((1 - core) * c, 128), c)] = other_ref[...].astype(F32)


def unpack_cols(half, other):
    r, c = half.shape
    step = math.gcd(r, 256)
    block = pl.BlockSpec((step, c), lambda i, _: (i, 0))
    return pl.pallas_call(
        unpack_cols_kernel,
        grid_spec=pltpu.PrefetchScalarGridSpec(
            num_scalar_prefetch=1, grid=(r // step,), in_specs=[block, block],
            out_specs=pl.BlockSpec((step, 2 * c), lambda i, _: (i, 0))),
        out_shape=jax.ShapeDtypeStruct((r, 2 * c), F32),
        compiler_params=pltpu.CompilerParams(vmem_limit_bytes=40 * 2**20),
        cost_estimate=pl.CostEstimate(flops=0, bytes_accessed=12 * r * c, transcendentals=0),
        name="unpack_cols",
    )((lax.axis_index("ctx") & 1)[None], half, other)


def all_rows(x):
    return lax.all_gather(x, "tp", axis=0, tiled=True)


def tp_shift(x, d):
    n = lax.axis_size("tp")
    return lax.ppermute(x, "tp", [(i, (i + d) % n) for i in range(n)])


def part_of(x, d, axis):
    n = lax.axis_size("tp")
    w = x.shape[axis] // n
    return lax.dynamic_slice_in_dim(x, (lax.axis_index("tp") + d) % n * w, w, axis)


def exchange(x, split, join):
    n, me = lax.axis_size("tp"), lax.axis_index("tp")
    w = x.shape[join]
    shape = list(x.shape)
    shape[split] //= n
    shape[join] *= n
    out = jnp.zeros(shape, x.dtype)
    for d in range(n):
        got = tp_shift(part_of(x, d, split), d) if d else part_of(x, 0, split)
        out = lax.dynamic_update_slice_in_dim(out, got, (me + n - d) % n * w, join)
    return out


def sum_rows(x):
    return lax.psum_scatter(x, "tp", scatter_dimension=0, tiled=True)


def gather_pair(kv):
    n = lax.axis_size("ctx")
    held = {0: ((kv, 0), (kv, 1))}
    for bit in range(1, int(math.log2(n))):
        mask = 1 << bit
        for j in list(held):
            if j == 0:
                got = ctx_swap(kv, mask)
                held[mask] = (got, 0), (got, 1)
            elif mask == 4 and j == 2:
                held[6] = (ctx_swap(held[2][0][0][0:1], 4), 0), (ctx_swap(held[4][1][0][1:2], 2), 0)
            else:
                (k, i), (v, t) = held[j]
                if k is v:
                    got = ctx_swap(k, mask)
                    held[j | mask] = (got, i), (got, t)
                else:
                    held[j | mask] = (ctx_swap(k, mask), i), (ctx_swap(v, mask), t)
    for j in list(held):
        (k, i), (v, t) = held[j]
        got = ctx_swap(k, 1)
        held[j | 1] = (got, i), (got if k is v else ctx_swap(v, 1), t)
    return [held[j][0] for j in range(n)], [held[j][1] for j in range(n)]


def gather_other(x):
    held = {0: x, 1: ctx_swap(x, 1)}
    for j in range(2, lax.axis_size("ctx"), 2):
        held[j] = ctx_swap(x, j)
    return held


def gather_cores(held, gate=None):
    n = lax.axis_size("ctx")
    for j in range(2, n, 2):
        held[j + 1] = ctx_swap(after(held[j], gate), 1)
    return [held[j] for j in range(n)]


def sum_over_all(x):
    steps = [(axis, bit) for axis in ("ctx", "tp") for bit in range(int(math.log2(lax.axis_size(axis))))]
    for axis, bit in sorted(steps, key=lambda step: step[0] == "ctx" and step[1] > 0):
        x = x + lax.ppermute(x, axis, [(i, i ^ (1 << bit)) for i in range(lax.axis_size(axis))])
        yield x
    while True:
        yield x


def gather_tp(x):
    n, me = lax.axis_size("tp"), lax.axis_index("tp")
    out = jnp.zeros((n,) + x.shape, x.dtype)
    for d in range(n):
        got = lax.ppermute(x, "tp", [(i, (i + d) % n) for i in range(n)]) if d else x
        out = lax.dynamic_update_index_in_dim(out, got, (me + n - d) % n, 0)
    return out


def local(tokens, cotangent, block_order, gain_one, shift_one, query_w, key_w, value_w, query_b, key_b, value_b,
          output_w, gain_two, shift_two, gate_w, up_w, down_w):
    heads = key_b.shape[0]
    width = heads * HEAD_DIM
    n_ctx, n_tp = lax.axis_size("ctx"), lax.axis_size("tp")
    ctx = lax.axis_index("ctx")
    own = lax.dynamic_slice_in_dim(block_order, 2 * ctx, 2, 1)
    picked = (jnp.arange(n_ctx, dtype=jnp.int32) ^ ctx)[:, None] == jnp.arange(n_ctx, dtype=jnp.int32)[None, :]
    by_ctx = block_order.reshape(SEQS, 1, n_ctx, 2)
    place = jnp.sum(jnp.where(picked[None, :, :, None], by_ctx, 0), axis=2).astype(jnp.int32).reshape(SEQS, 2 * n_ctx)
    positions = (own[:, :, None] * BLK + jnp.arange(BLK, dtype=jnp.int32)).reshape(-1)
    tabs = rotary_tables(positions)

    x = tokens.astype(F32)
    normed_one, unit_one, inverse_one = layer_stats(x, gain_one, shift_one)
    rows_one = all_rows(normed_one.astype(BF16))
    key_bias = jnp.concatenate([key_b, jnp.zeros((heads, HEAD_DIM - ROT), F32)], axis=1).reshape(-1)
    bias = jnp.stack([query_b, key_bias, value_b])
    q, kv = project(rows_one, query_w, key_w, value_w, bias, tabs)
    keys, values = gather_pair(kv.reshape(2, SEQS, 2, BLK, width))
    arrived = [e[0] for e in keys + values]

    rows_w = output_w.shape[0] // n_ctx
    part = lax.dynamic_slice_in_dim(output_w, ctx * rows_w, rows_w, 0)
    part = gather_tp(after(part, kv))
    dy_rows = all_rows(after(cotangent, rows_one))
    whole_w = lax.all_gather(after(part, arrived, dy_rows), "ctx", axis=1).reshape(n_tp * output_w.shape[0], -1)

    attn, q_ext = attend(place, own, q, keys, values)
    attn_rows = attn.reshape(-1, width)
    attn_own = exchange(attn_rows, 0, 1)
    mixed = x + nn(attn_own, whole_w)
    normed_two, unit_two, inverse_two = layer_stats(mixed, gain_two, shift_two)
    rows_two = all_rows(after(normed_two.astype(BF16), dy_rows, whole_w))
    shape = (1, SEQS, 2, BLK, width + 128)
    queries = gather_cores(gather_other(after(jnp.concatenate([q, q_ext], axis=2).reshape(shape), attn_own)))
    rows_two = after(rows_two, queries)

    act, grad_gu = mlp(rows_two, dy_rows, gate_w, up_w, down_w)
    ff = gate_w.shape[1]
    part_two = (nt(grad_gu[:, :ff], gate_w) + nt(grad_gu[:, ff:], up_w)).astype(BF16)
    grad_two = sum_rows(part_two)
    act, rows_two, dy_rows, grad_gu = after((act, rows_two, dy_rows, grad_gu), part_two)
    gu_fly, dw_fly = [], []
    gu = begin(lambda core: rc(columns(rows_two, core), grad_gu), gu_fly)
    dw = begin(lambda core: rc(act, columns(dy_rows, core)), dw_fly)
    held = take(gu)
    go(gu)
    down = nn(after(act, held), down_w).astype(BF16)
    held = take(dw), take(gu, down)
    go(gu)
    go(dw, held)
    grad_two = after(grad_two, held)

    norm_two, grad_gain_two, grad_shift_two = layer_back(grad_two.astype(F32), unit_two, inverse_two, gain_two)
    grad_mixed = cotangent.astype(F32) + norm_two
    branch_own = grad_mixed.astype(BF16)
    grad_attn = nt(branch_own, whole_w).astype(BF16)
    held = take(gu, grad_attn)
    go(gu)
    grad_attn = exchange(grad_attn, 1, 0)
    lane = jnp.arange(128)[None, :]
    ind = ((jnp.arange(width) // HEAD_DIM)[:, None] == lane // 3).astype(F32)
    delta = lax.dot_general(grad_attn.astype(F32) * attn_rows.astype(F32), ind, (((1,), (0,)), ((), ())),
                            precision=lax.Precision.HIGHEST, preferred_element_type=F32)
    do_ext = terms(-delta, lane).astype(BF16)
    do_sent = jnp.concatenate([grad_attn, do_ext], axis=1).reshape(shape)
    do_sent = after(do_sent, held)
    branch = all_rows(after(branch_own, do_sent))
    out_sum = sum_rows(after(down, do_sent))
    grads = gather_other(do_sent)
    grad_q = query_grad(place, own, q, grad_attn.reshape(q.shape), q_ext, do_ext.reshape(q_ext.shape), tabs, keys, values)
    grad_q = after(grad_q.reshape(-1, width), [grads[j] for j in grads if j > 1])
    grads = gather_cores(grads, grad_q)
    q_part = nt(grad_q, query_w)
    first = key_value_grad(place, own, kv, tabs, queries, grads, 0, SEQS // 2)
    grads = after(grads, take(gu, first), take(dw, first))
    go(gu)
    go(dw)
    second = key_value_grad(place, own, kv, tabs, queries, grads, SEQS // 2, SEQS // 2)
    second = after(second, dw_fly)
    grad_k, grad_v = (jnp.concatenate(pair).reshape(-1, width) for pair in zip(first, second))
    part_one = q_part + nt(grad_k, key_w) + nt(grad_v, value_w)
    part_sent = after(part_one.astype(BF16), branch)
    grad_one = sum_rows(part_sent)

    rows_one, branch, grad_q, grad_k, grad_v = after((rows_one, branch, grad_q, grad_k, grad_v), part_sent, gu_fly)
    grad_qkv = jnp.concatenate([grad_q, grad_k, grad_v], axis=1)
    chain = begin(lambda core: jnp.concatenate([rc(columns(rows_one, core), grad_qkv), rc(columns(branch, core), attn_rows)], axis=1))
    held = take(chain)
    go(chain)
    take(gu, held)
    take_extra(gu)
    go(gu)
    take(dw, held)
    go(dw)
    unit_rows = (rows_one.astype(F32) - shift_one) / gain_one
    bias_grad = jnp.sum(grad_qkv.astype(F32), axis=0)
    tp_row = (jnp.arange(n_tp) == lax.axis_index("tp"))[:, None]
    small = jnp.concatenate([
        jnp.sum(part_one * unit_rows, axis=0), jnp.sum(part_one, axis=0), grad_gain_two, grad_shift_two,
        jnp.where(tp_row, bias_grad[None, :], 0.0).reshape(-1)])
    held = take(chain)
    go(chain)
    take(dw, held)
    go(dw)
    held = take(chain)
    go(chain)
    take(dw, held)
    take_extra(dw)
    go(dw)
    mixed_late, out_sum = after((mixed, out_sum), held)
    out_tokens = (mixed_late + out_sum.astype(F32)).astype(BF16)
    grad_gate_w, grad_up_w = unpack_rows(*take(gu, held), 2)
    held = take(chain, grad_gate_w)
    go(chain)
    sums = sum_over_all(after(small, held).reshape(-1, 1024))
    small = [next(sums) for _ in range(1 + int(math.log2(n_tp)))]
    grad_down_w = unpack_cols(*take(dw, held))
    take(chain, (grad_down_w, small))
    take_extra(chain)
    go(chain)
    for _ in range(4):
        small = next(sums)
    depth = x.shape[1]
    small = small.reshape(-1)
    norms = small[:4 * depth].reshape(4, depth)
    bias_sum = jnp.sum(jnp.where(tp_row, small[4 * depth:].reshape(n_tp, -1), 0.0), axis=0)
    grad_query_w, grad_key_w, grad_value_w, grad_output_w = unpack_rows(*take(chain), 4, True)
    norm_one, _, _ = layer_back(grad_one.astype(F32), unit_one, inverse_one, gain_one)
    grad_tokens = (grad_mixed + norm_one).astype(BF16)
    return (
        out_tokens, grad_tokens, norms[0], norms[1], grad_query_w, grad_key_w, grad_value_w,
        bias_sum[:width], bias_sum[width:2 * width].reshape(heads, HEAD_DIM)[:, :ROT], bias_sum[2 * width:],
        grad_output_w, norms[2], norms[3], grad_gate_w, grad_up_w, grad_down_w,
    )


def solution(mesh):
    rows, cols, depth, flat = P(("ctx", "tp"), None), P(None, "tp"), P("tp", None), P("tp")
    in_specs = (rows, rows, P(), P(), P(), cols, cols, cols, flat, depth, flat, depth, P(), P(), cols, cols, depth)
    out_specs = (rows, rows, P(), P(), cols, cols, cols, flat, depth, flat, depth, P(), P(), cols, cols, depth)
    return jax.shard_map(local, mesh=mesh, in_specs=in_specs, out_specs=out_specs, check_vma=False)
```

```python
import functools
import jax, jax.numpy as jnp
from jax import lax
from jax.experimental import pallas as pl
from jax.experimental.pallas import tpu as pltpu

BLK = 128
CB = 8
CH = BLK * CB
NEG = -1e30
SCALE = 0.125


def nt(a, b):
    return lax.dot_general(a, b, (((1,), (1,)), ((), ())), preferred_element_type=jnp.float32)


def nn(a, b):
    return lax.dot_general(a, b, (((1,), (0,)), ((), ())), preferred_element_type=jnp.float32)


def lane_of(shape):
    return lax.broadcasted_iota(jnp.int32, shape, 1)


def row_of(shape):
    return lax.broadcasted_iota(jnp.int32, shape, 0)


def split_heads(x):
    low = lane_of(x.shape) < 64
    zero = jnp.zeros_like(x)
    return jnp.concatenate([jnp.where(low, x, zero), jnp.where(low, zero, x)], axis=0)


def join_heads(x):
    low = lane_of((BLK, 128)) < 64
    return jnp.where(low, x[:BLK], x[BLK:])


def own_lanes(pair):
    shape = (2 * BLK, 128)
    return lane_of(shape) // 3 == 2 * pair + row_of(shape) // BLK


def lanes_of(pair):
    return slice(pair * 128, (pair + 1) * 128)


def terms(x, lane):
    first = x.astype(jnp.bfloat16).astype(jnp.float32)
    second = (x - first).astype(jnp.bfloat16).astype(jnp.float32)
    return jnp.where(lane % 3 == 0, first, jnp.where(lane % 3 == 1, second, x - first - second))


def place_rows(place_ref, s, refs, dst_ref, ext=False):
    pairs = dst_ref.shape[0]
    at = 0
    for ref in refs:
        for j in range(ref.shape[0]):
            for w in range(2):
                rows = pl.ds(pl.multiple_of(place_ref[s, at] * BLK, BLK), BLK)
                for p in range(pairs):
                    dst_ref[p, rows, 0:128] = ref[j, 0, w, :, p * 128:(p + 1) * 128]
                    if ext:
                        dst_ref[p, rows, 128:256] = ref[j, 0, w, :, pairs * 128:]
                at += 1


def sweep(full, step):
    def one(c, carry):
        step(c, False)
        return carry

    lax.fori_loop(0, full, one, 0)
    step(full, True)


def span(c):
    return pl.ds(pl.multiple_of(c * CH, CH), CH)


def may_see(query_block, c):
    shape = (2 * BLK, CH)
    return c * CH + lane_of(shape) <= query_block * BLK + row_of(shape) % BLK


def fwd_kernel(place_ref, own_ref, q_ref, *refs, pairs, n):
    k_refs, v_refs, (o_ref, ext_ref, ks, vs, qs, scr, run, acc) = refs[:n], refs[n:2 * n], refs[2 * n:]
    s = pl.program_id(0)

    @pl.when(s == 0)
    def _():
        for p in range(pairs):
            vs[p, :, 128:256] = jnp.ones((vs.shape[1], 128), jnp.bfloat16)

    place_rows(place_ref, s, k_refs, ks)
    place_rows(place_ref, s, v_refs, vs)

    for w in range(2):
        rows = slice(w * BLK, (w + 1) * BLK)
        pos = own_ref[s, w]
        for p in range(pairs):
            qs[p] = split_heads(q_ref[0, rows, lanes_of(p)] * jnp.bfloat16(SCALE))
        run[...] = jnp.full_like(run, NEG)
        acc[...] = jnp.zeros_like(acc)

        def score(c, masked):
            for p in range(pairs):
                sc = nt(qs[p], ks[p, span(c), :])
                if masked:
                    sc = jnp.where(may_see(pos, c), sc, NEG)
                scr[p, :, span(c)] = sc
                top = run[p]
                for t in range(CB):
                    top = jnp.maximum(top, sc[:, t * 128:(t + 1) * 128])
                run[p] = top

        sweep(pos // CB, score)
        for p in range(pairs):
            run[p] = jnp.broadcast_to(jnp.max(run[p], axis=1, keepdims=True), (2 * BLK, 128))

        def weigh(c, masked):
            for p in range(pairs):
                weight = jnp.exp(scr[p, :, span(c)] - jnp.concatenate([run[p]] * CB, axis=1)).astype(jnp.bfloat16)
                acc[p] += nn(weight, vs[p, span(c), :])

        sweep(pos // CB, weigh)
        lane = lane_of((2 * BLK, 128))
        ext = jnp.zeros((BLK, 128), jnp.float32)
        for p in range(pairs):
            total = acc[p, :, 128:256]
            o_ref[0, rows, lanes_of(p)] = join_heads(acc[p, :, 0:128] / total).astype(jnp.bfloat16)
            mine = jnp.where(own_lanes(p), terms(-(run[p] + jnp.log(total)), lane), 0.0)
            ext = ext + mine[:BLK] + mine[BLK:]
        ext_ref[0, rows, :] = ext.astype(jnp.bfloat16)


def dq_kernel(place_ref, own_ref, q_ref, do_ref, qx_ref, dox_ref, c_ref, a_ref, b_ref, *refs, pairs, n):
    k_refs, v_refs, (dq_ref, ks, vs, qs, dos, acc) = refs[:n], refs[n:2 * n], refs[2 * n:]
    s = pl.program_id(0)

    @pl.when(s == 0)
    def _():
        for ref in (ks, vs):
            for p in range(pairs):
                ref[p, :, 128:256] = jnp.ones((ref.shape[1], 128), jnp.bfloat16)

    place_rows(place_ref, s, k_refs, ks)
    place_rows(place_ref, s, v_refs, vs)

    for w in range(2):
        rows = slice(w * BLK, (w + 1) * BLK)
        pos = own_ref[s, w]

        def extend(tile, ext, p):
            both = jnp.concatenate([ext, ext], axis=0)
            return jnp.concatenate([split_heads(tile), jnp.where(own_lanes(p), both, jnp.zeros_like(both))], axis=1)

        for p in range(pairs):
            qs[p] = extend(q_ref[0, rows, lanes_of(p)] * jnp.bfloat16(SCALE), qx_ref[0, rows, :], p)
            dos[p] = extend(do_ref[0, rows, lanes_of(p)], dox_ref[0, rows, :], p)
        acc[...] = jnp.zeros_like(acc)

        def step(c, masked):
            for p in range(pairs):
                prob = jnp.exp(nt(qs[p], ks[p, span(c), :]))
                if masked:
                    prob = jnp.where(may_see(pos, c), prob, 0.0)
                ds = (prob * nt(dos[p], vs[p, span(c), :])).astype(jnp.bfloat16)
                acc[p] += nn(ds, ks[p, span(c), 0:128])

        sweep(pos // CB, step)
        for p in range(pairs):
            grad = join_heads(acc[p]) * SCALE
            dq_ref[0, rows, lanes_of(p)] = turn(grad, c_ref[rows], a_ref[rows], b_ref[rows], -1.0).astype(jnp.bfloat16)


def dkv_kernel(place_ref, own_ref, kv_ref, c_ref, a_ref, b_ref, *refs, pairs, n, lead):
    q_refs, do_refs, (dk_ref, dv_ref, qs, dos, kw, vw, acck, accv) = refs[:n], refs[n:2 * n], refs[2 * n:]
    s = pl.program_id(0) + lead
    place_rows(place_ref, s, q_refs, qs, True)
    place_rows(place_ref, s, do_refs, dos, True)
    chunks = qs.shape[1] // CH

    for w in range(2):
        rows = slice(w * BLK, (w + 1) * BLK)
        pos = own_ref[s, w]
        first = pos // CB
        for p in range(pairs):
            ones = own_lanes(p).astype(jnp.bfloat16)
            kw[p] = jnp.concatenate([split_heads(kv_ref[0, 0, rows, lanes_of(p)] * jnp.bfloat16(SCALE)), ones], axis=1)
            vw[p] = jnp.concatenate([split_heads(kv_ref[1, 0, rows, lanes_of(p)]), ones], axis=1)
        acck[...] = jnp.zeros_like(acck)
        accv[...] = jnp.zeros_like(accv)

        def step(c, masked):
            for p in range(pairs):
                prob = jnp.exp(nt(kw[p], qs[p, span(c), :]))
                if masked:
                    shape = (2 * BLK, CH)
                    prob = jnp.where(pos * BLK + row_of(shape) % BLK <= c * CH + lane_of(shape), prob, 0.0)
                accv[p] += nn(prob.astype(jnp.bfloat16), dos[p, span(c), 0:128])
                ds = (prob * nt(vw[p], dos[p, span(c), :])).astype(jnp.bfloat16)
                acck[p] += nn(ds, qs[p, span(c), 0:128])

        def one(c, carry):
            step(c, False)
            return carry

        step(first, True)
        lax.fori_loop(first + 1, chunks, one, 0)
        for p in range(pairs):
            grad = join_heads(acck[p]) * SCALE
            dk_ref[0, rows, lanes_of(p)] = turn(grad, c_ref[rows], a_ref[rows], b_ref[rows], -1.0).astype(jnp.bfloat16)
            dv_ref[0, rows, lanes_of(p)] = join_heads(accv[p]).astype(jnp.bfloat16)


def own(width):
    return pl.BlockSpec((1, 2 * BLK, width), lambda s, *_: (s, 0, 0))


def table(lead=0):
    return pl.BlockSpec((2 * BLK, 128), lambda s, *_: (s + lead, 0))


def piece(x, first=0, lead=0):
    return pl.BlockSpec((1, 1, 2, BLK, x.shape[4]), lambda s, *_: (first, s + lead, 0, 0, 0))


def attention_call(kernel, name, mats, seqs, pairs, blocks, in_specs, out_specs, out_shape, scratch, args):
    work = seqs * pairs * 2 * 2 * BLK * blocks * BLK // 2
    return pl.pallas_call(
        kernel,
        grid_spec=pltpu.PrefetchScalarGridSpec(
            num_scalar_prefetch=2, grid=(seqs,), in_specs=in_specs, out_specs=out_specs, scratch_shapes=scratch),
        out_shape=out_shape,
        compiler_params=pltpu.CompilerParams(vmem_limit_bytes=60 * 2**20),
        cost_estimate=pl.CostEstimate(flops=work * 64 * mats, bytes_accessed=seqs * pairs * blocks * BLK * 128, transcendentals=0),
        name=name,
    )(*args)


def rows_of(pairs, blocks, lanes):
    return pltpu.VMEM((pairs, blocks * BLK, lanes), jnp.bfloat16)


def acc_of(pairs, lanes, dtype=jnp.float32):
    return pltpu.VMEM((pairs, 2 * BLK, lanes), dtype)


def attend(place, own_blocks, q, keys, values):
    seqs, width, blocks = q.shape[0], q.shape[2], place.shape[1]
    pairs = width // 128
    return attention_call(
        functools.partial(fwd_kernel, pairs=pairs, n=len(keys)), "attend", 2, seqs, pairs, blocks,
        [own(width)] + [piece(*e) for e in keys + values], [own(width), own(128)],
        [jax.ShapeDtypeStruct(q.shape, jnp.bfloat16), jax.ShapeDtypeStruct(q.shape[:2] + (128,), jnp.bfloat16)],
        [rows_of(pairs, blocks, 128), rows_of(pairs, blocks, 256), acc_of(pairs, 128, jnp.bfloat16), acc_of(pairs, blocks * BLK),
         acc_of(pairs, 128), acc_of(pairs, 256)],
        [place, own_blocks, q] + [e[0] for e in keys + values])


def query_grad(place, own_blocks, q, do, q_ext, do_ext, tabs, keys, values):
    seqs, width, blocks = q.shape[0], q.shape[2], place.shape[1]
    pairs = width // 128
    return attention_call(
        functools.partial(dq_kernel, pairs=pairs, n=len(keys)), "query_grad", 3, seqs, pairs, blocks,
        [own(width), own(width), own(128), own(128)] + [table()] * 3 + [piece(*e) for e in keys + values], own(width),
        jax.ShapeDtypeStruct(q.shape, jnp.bfloat16),
        [rows_of(pairs, blocks, 256), rows_of(pairs, blocks, 256), acc_of(pairs, 256, jnp.bfloat16), acc_of(pairs, 256, jnp.bfloat16),
         acc_of(pairs, 128)],
        [place, own_blocks, q, do, q_ext, do_ext, *tabs] + [e[0] for e in keys + values])


def key_value_grad(place, own_blocks, kv, tabs, queries, grads, lead, count):
    width, blocks = kv.shape[3], place.shape[1]
    pairs = width // 128
    shape = (count,) + kv.shape[2:]
    return attention_call(
        functools.partial(dkv_kernel, pairs=pairs, n=len(queries), lead=lead), "key_value_grad", 4, count, pairs, blocks,
        [pl.BlockSpec((2, 1, 2 * BLK, width), lambda s, *_: (0, s + lead, 0, 0))] + [table(lead)] * 3
        + [piece(x, lead=lead) for x in queries + grads], [own(width)] * 2,
        [jax.ShapeDtypeStruct(shape, jnp.bfloat16)] * 2,
        [rows_of(pairs, blocks, 256), rows_of(pairs, blocks, 256), acc_of(pairs, 256, jnp.bfloat16), acc_of(pairs, 256, jnp.bfloat16),
         acc_of(pairs, 128), acc_of(pairs, 128)],
        [place, own_blocks, kv, *tabs] + queries + grads)


import math
from jax.sharding import PartitionSpec as P

HEAD_DIM = 64
ROT = 16
SEQS = 4
EPS = 1e-05
F32 = jnp.float32
BF16 = jnp.bfloat16


def rc(left, right):
    return lax.dot_general(left, right, (((0,), (0,)), ((), ())), preferred_element_type=F32)


def layer_stats(values, gain, shift):
    mean = jnp.mean(values, axis=-1, keepdims=True)
    centred = values - mean
    inverse = lax.rsqrt(jnp.mean(centred * centred, axis=-1, keepdims=True) + EPS)
    unit = centred * inverse
    return unit * gain + shift, unit, inverse


def layer_back(grad, unit, inverse, gain):
    scaled = grad * gain
    grad_in = inverse * (
        scaled
        - jnp.mean(scaled, axis=-1, keepdims=True)
        - unit * jnp.mean(scaled * unit, axis=-1, keepdims=True)
    )
    return grad_in, jnp.sum(grad * unit, axis=0), jnp.sum(grad, axis=0)


def rotary_tables(positions):
    half = ROT // 2
    dim = jnp.arange(2 * HEAD_DIM) % HEAD_DIM
    freq = jnp.where(dim < ROT, 10000.0 ** (-2.0 * (dim % half).astype(F32) / ROT), 0.0)
    angles = positions.astype(F32)[:, None] * freq[None, :]
    sin = jnp.sin(angles)
    return jnp.cos(angles), jnp.where(dim < half, sin, 0.0), jnp.where(dim < half, 0.0, sin)


def turn(x, ctab, above, below, sign):
    up = pltpu.roll(x, 128 - ROT // 2, axis=1)
    down = pltpu.roll(x, ROT // 2, axis=1)
    return x * ctab + sign * (down * below - up * above)


def project_kernel(h_ref, wq_ref, wk_ref, wv_ref, bias_ref, c_ref, a_ref, b_ref, q_ref, kv_ref):
    h = h_ref[...]
    width = wq_ref.shape[1]
    tabs = c_ref[...], a_ref[...], b_ref[...]
    for at, (w_ref, out) in enumerate(((wq_ref, q_ref.at[0]), (wk_ref, kv_ref.at[0, 0]), (wv_ref, kv_ref.at[1, 0]))):
        lin = nn(h, w_ref[...]) + bias_ref[at:at + 1, :]
        for p in range(width // 128):
            part = lin[:, p * 128:(p + 1) * 128]
            if at < 2:
                part = turn(part, *tabs, 1.0)
            out[:, p * 128:(p + 1) * 128] = part.astype(BF16)


def project(rows, wq, wk, wv, bias, tabs):
    total, depth = rows.shape
    width = wq.shape[1]
    step = total // SEQS
    weight = pl.BlockSpec((depth, width), lambda i: (0, 0))
    table = pl.BlockSpec((step, 128), lambda i: (i, 0))
    return pl.pallas_call(
        project_kernel,
        grid=(SEQS,),
        in_specs=[pl.BlockSpec((step, depth), lambda i: (i, 0)), weight, weight, weight,
                  pl.BlockSpec((3, width), lambda i: (0, 0)), table, table, table],
        out_specs=[pl.BlockSpec((1, step, width), lambda i: (i, 0, 0)),
                   pl.BlockSpec((2, 1, step, width), lambda i: (0, i, 0, 0))],
        out_shape=[jax.ShapeDtypeStruct((SEQS, step, width), BF16), jax.ShapeDtypeStruct((2, SEQS, step, width), BF16)],
        compiler_params=pltpu.CompilerParams(vmem_limit_bytes=48 * 2**20),
        cost_estimate=pl.CostEstimate(flops=6 * total * depth * width, bytes_accessed=6 * depth * width, transcendentals=0),
        name="project",
    )(rows, wq, wk, wv, bias, *tabs)


def mlp_kernel(h_ref, dy_ref, gate_ref, up_ref, down_ref, act_ref, *grad_refs):
    width = gate_ref.shape[1]
    gate = nn(h_ref[...], gate_ref[...])
    up = nn(h_ref[...], up_ref[...])
    grad = nt(dy_ref[...], down_ref[...])
    sig = 1.0 / (1.0 + jnp.exp(-gate))
    silu = gate * sig
    act_ref[...] = (silu * up).astype(BF16)
    outs = grad_refs if len(grad_refs) == 2 else (grad_refs[0].at[:, :width], grad_refs[0].at[:, width:])
    outs[0][...] = (grad * up * (sig + silu * (1.0 - sig))).astype(BF16)
    outs[1][...] = (grad * silu).astype(BF16)


def mlp(rows, dy, gate_w, up_w, down_w, step=256):
    total, depth = rows.shape
    width = gate_w.shape[1]
    joined = width % 128 == 0
    block = pl.BlockSpec((step, depth), lambda i: (i, 0))

    def whole(x):
        return pl.BlockSpec(x.shape, lambda i: (0, 0), pipeline_mode=pl.Buffered(1))

    def out(n):
        return pl.BlockSpec((step, n), lambda i: (i, 0)), jax.ShapeDtypeStruct((total, n), BF16)

    outs = [out(width), out(2 * width)] if joined else [out(width)] * 3
    act, *grads = pl.pallas_call(
        mlp_kernel,
        grid=(total // step,),
        in_specs=[block, block, whole(gate_w), whole(up_w), whole(down_w)],
        out_specs=[o[0] for o in outs],
        out_shape=[o[1] for o in outs],
        compiler_params=pltpu.CompilerParams(vmem_limit_bytes=56 * 2**20),
        cost_estimate=pl.CostEstimate(flops=6 * total * depth * width, bytes_accessed=6 * depth * width + 10 * total * depth,
                                      transcendentals=total * width),
        name="mlp",
    )(rows, dy, gate_w, up_w, down_w)
    return act, grads[0] if joined else jnp.concatenate(grads, axis=1)


def ctx_swap(x, mask):
    n = lax.axis_size("ctx")
    return lax.ppermute(x, "ctx", [(i, i ^ mask) for i in range(n)])


def add16(a, b):
    return (a.astype(F32) + b.astype(F32)).astype(BF16)


def after(x, *deps):
    if not jax.tree.leaves(deps):
        return x
    return lax.optimization_barrier((x, deps))[0]


def half_of(x, bit, mine):
    side = (lax.axis_index("ctx") >> bit) & 1
    r = x.shape[0] // 2
    return lax.dynamic_slice_in_dim(x, (side if mine else 1 - side) * r, r, 0)


def weight_grad(part, flying):
    core = lax.axis_index("ctx") & 1
    got = ctx_swap(part(1 - core).astype(BF16), 1)
    flying[:] = [got]
    gate = yield
    half = (part(core) + after(got, gate).astype(F32)).astype(BF16)
    bits = list(range(1, int(math.log2(lax.axis_size("ctx")))))
    orders = [bits, bits[::-1]]
    r = half.shape[0] // 2
    streams = [half[:r], half[r:]]
    gate = yield streams
    for i in range(len(bits)):
        streams = after(streams, gate)
        got = [ctx_swap(half_of(x, o[i], False), 1 << o[i]) for x, o in zip(streams, orders)]
        flying[:] = got
        gate = yield
        streams, got = after((streams, got), gate)
        streams = [add16(half_of(x, o[i], True), g) for x, o, g in zip(streams, orders, got)]
        gate = yield streams
    for i in reversed(range(len(bits))):
        streams = after(streams, gate)
        got = [ctx_swap(x, 1 << o[i]) for x, o in zip(streams, orders)]
        flying[:] = got
        gate = yield
        streams, got = after((streams, got), gate)
        streams = [
            jnp.where(((lax.axis_index("ctx") >> o[i]) & 1) == 0, jnp.concatenate([x, g]), jnp.concatenate([g, x]))
            for x, o, g in zip(streams, orders, got)
        ]
        if i == 0:
            streams = jnp.concatenate(streams)
        gate = yield streams
    streams = after(streams, gate)
    other = ctx_swap(streams, 1)
    gate = yield
    yield after((streams, other), gate)


def begin(part, flying=None):
    chain = weight_grad(part, [] if flying is None else flying)
    next(chain)
    return chain


def take(chain, gate=None):
    return chain.send(gate)


def go(chain, gate=None):
    chain.send(gate)


def take_extra(chain):
    for _ in range(2 * int(math.log2(lax.axis_size("ctx"))) - 6):
        go(chain)
        take(chain)


def unpack_rows_kernel(core_ref, half_ref, other_ref, *out_refs, turned):
    def put(src):
        at = 0
        for i, out in enumerate(out_refs):
            if turned and i == len(out_refs) - 1:
                out[...] = src[:, at:].astype(F32).T
            else:
                out[...] = src[:, at:at + out.shape[1]].astype(F32)
                at += out.shape[1]

    @pl.when(pl.program_id(0) == core_ref[0])
    def _():
        put(half_ref)

    @pl.when(pl.program_id(0) != core_ref[0])
    def _():
        put(other_ref)


def unpack_rows(half, other, parts, turned=False):
    r, c = half.shape
    step = math.gcd(r, 256)
    blocks = r // step
    w = c // parts
    core = lax.axis_index("ctx") & 1

    def mine(i, j, core_ref):
        return jnp.where(i == core_ref[0], j, jnp.where(core_ref[0] == 0, blocks - 1, 0)), 0

    def theirs(i, j, core_ref):
        return jnp.where(i != core_ref[0], j, jnp.where(core_ref[0] == 1, blocks - 1, 0)), 0

    specs = [pl.BlockSpec((step, w), lambda i, j, _: (i * blocks + j, 0))] * parts
    shapes = [jax.ShapeDtypeStruct((2 * r, w), F32)] * parts
    if turned:
        specs[-1] = pl.BlockSpec((w, step), lambda i, j, _: (0, i * blocks + j))
        shapes[-1] = jax.ShapeDtypeStruct((w, 2 * r), F32)
    return pl.pallas_call(
        functools.partial(unpack_rows_kernel, turned=turned),
        grid_spec=pltpu.PrefetchScalarGridSpec(
            num_scalar_prefetch=1, grid=(2, blocks),
            in_specs=[pl.BlockSpec((step, c), mine), pl.BlockSpec((step, c), theirs)], out_specs=specs),
        out_shape=shapes,
        compiler_params=pltpu.CompilerParams(vmem_limit_bytes=40 * 2**20),
        cost_estimate=pl.CostEstimate(flops=0, bytes_accessed=12 * r * c, transcendentals=0),
        name="unpack_rows",
    )(core[None], half, other)


def columns(x, which):
    w = x.shape[1] // 2
    return lax.dynamic_slice_in_dim(x, which * w, w, 1)


def unpack_cols_kernel(core_ref, half_ref, other_ref, out_ref):
    c = half_ref.shape[1]
    core = core_ref[0]
    out_ref[:, pl.ds(pl.multiple_of(core * c, 128), c)] = half_ref[...].astype(F32)
    out_ref[:, pl.ds(pl.multiple_of((1 - core) * c, 128), c)] = other_ref[...].astype(F32)


def unpack_cols(half, other):
    r, c = half.shape
    step = math.gcd(r, 256)
    block = pl.BlockSpec((step, c), lambda i, _: (i, 0))
    return pl.pallas_call(
        unpack_cols_kernel,
        grid_spec=pltpu.PrefetchScalarGridSpec(
            num_scalar_prefetch=1, grid=(r // step,), in_specs=[block, block],
            out_specs=pl.BlockSpec((step, 2 * c), lambda i, _: (i, 0))),
        out_shape=jax.ShapeDtypeStruct((r, 2 * c), F32),
        compiler_params=pltpu.CompilerParams(vmem_limit_bytes=40 * 2**20),
        cost_estimate=pl.CostEstimate(flops=0, bytes_accessed=12 * r * c, transcendentals=0),
        name="unpack_cols",
    )((lax.axis_index("ctx") & 1)[None], half, other)


def all_rows(x):
    return lax.all_gather(x, "tp", axis=0, tiled=True)


def tp_shift(x, d):
    n = lax.axis_size("tp")
    return lax.ppermute(x, "tp", [(i, (i + d) % n) for i in range(n)])


def part_of(x, d, axis):
    n = lax.axis_size("tp")
    w = x.shape[axis] // n
    return lax.dynamic_slice_in_dim(x, (lax.axis_index("tp") + d) % n * w, w, axis)


def exchange(x, split, join):
    n, me = lax.axis_size("tp"), lax.axis_index("tp")
    w = x.shape[join]
    shape = list(x.shape)
    shape[split] //= n
    shape[join] *= n
    out = jnp.zeros(shape, x.dtype)
    for d in range(n):
        got = tp_shift(part_of(x, d, split), d) if d else part_of(x, 0, split)
        out = lax.dynamic_update_slice_in_dim(out, got, (me + n - d) % n * w, join)
    return out


def sum_rows(x):
    return lax.psum_scatter(x, "tp", scatter_dimension=0, tiled=True)


def gather_pair(kv):
    n = lax.axis_size("ctx")
    held = {0: ((kv, 0), (kv, 1))}
    for bit in range(1, int(math.log2(n))):
        mask = 1 << bit
        for j in list(held):
            if j == 0:
                got = ctx_swap(kv, mask)
                held[mask] = (got, 0), (got, 1)
            elif mask == 4 and j == 2:
                held[6] = (ctx_swap(held[2][0][0][0:1], 4), 0), (ctx_swap(held[4][1][0][1:2], 2), 0)
            else:
                (k, i), (v, t) = held[j]
                if k is v:
                    got = ctx_swap(k, mask)
                    held[j | mask] = (got, i), (got, t)
                else:
                    held[j | mask] = (ctx_swap(k, mask), i), (ctx_swap(v, mask), t)
    for j in list(held):
        (k, i), (v, t) = held[j]
        got = ctx_swap(k, 1)
        held[j | 1] = (got, i), (got if k is v else ctx_swap(v, 1), t)
    return [held[j][0] for j in range(n)], [held[j][1] for j in range(n)]


def gather_other(x):
    held = {0: x, 1: ctx_swap(x, 1)}
    for j in range(2, lax.axis_size("ctx"), 2):
        held[j] = ctx_swap(x, j)
    return held


def gather_cores(held, gate=None):
    n = lax.axis_size("ctx")
    for j in range(2, n, 2):
        held[j + 1] = ctx_swap(after(held[j], gate), 1)
    return [held[j] for j in range(n)]


def sum_over_all(x):
    steps = [(axis, bit) for axis in ("ctx", "tp") for bit in range(int(math.log2(lax.axis_size(axis))))]
    for axis, bit in sorted(steps, key=lambda step: step[0] == "ctx" and step[1] > 0):
        x = x + lax.ppermute(x, axis, [(i, i ^ (1 << bit)) for i in range(lax.axis_size(axis))])
        yield x
    while True:
        yield x


def gather_tp(x):
    n, me = lax.axis_size("tp"), lax.axis_index("tp")
    out = jnp.zeros((n,) + x.shape, x.dtype)
    for d in range(n):
        got = lax.ppermute(x, "tp", [(i, (i + d) % n) for i in range(n)]) if d else x
        out = lax.dynamic_update_index_in_dim(out, got, (me + n - d) % n, 0)
    return out


def local(tokens, cotangent, block_order, gain_one, shift_one, query_w, key_w, value_w, query_b, key_b, value_b,
          output_w, gain_two, shift_two, gate_w, up_w, down_w):
    heads = key_b.shape[0]
    width = heads * HEAD_DIM
    n_ctx, n_tp = lax.axis_size("ctx"), lax.axis_size("tp")
    ctx = lax.axis_index("ctx")
    own = lax.dynamic_slice_in_dim(block_order, 2 * ctx, 2, 1)
    picked = (jnp.arange(n_ctx, dtype=jnp.int32) ^ ctx)[:, None] == jnp.arange(n_ctx, dtype=jnp.int32)[None, :]
    by_ctx = block_order.reshape(SEQS, 1, n_ctx, 2)
    place = jnp.sum(jnp.where(picked[None, :, :, None], by_ctx, 0), axis=2).astype(jnp.int32).reshape(SEQS, 2 * n_ctx)
    positions = (own[:, :, None] * BLK + jnp.arange(BLK, dtype=jnp.int32)).reshape(-1)
    tabs = rotary_tables(positions)

    x = tokens.astype(F32)
    normed_one, unit_one, inverse_one = layer_stats(x, gain_one, shift_one)
    rows_one = all_rows(normed_one.astype(BF16))
    key_bias = jnp.concatenate([key_b, jnp.zeros((heads, HEAD_DIM - ROT), F32)], axis=1).reshape(-1)
    bias = jnp.stack([query_b, key_bias, value_b])
    q, kv = project(rows_one, query_w, key_w, value_w, bias, tabs)
    keys, values = gather_pair(kv.reshape(2, SEQS, 2, BLK, width))
    arrived = [e[0] for e in keys + values]

    rows_w = output_w.shape[0] // n_ctx
    part = lax.dynamic_slice_in_dim(output_w, ctx * rows_w, rows_w, 0)
    part = gather_tp(after(part, kv))
    dy_rows = all_rows(after(cotangent, rows_one))
    whole_w = lax.all_gather(after(part, arrived, dy_rows), "ctx", axis=1).reshape(n_tp * output_w.shape[0], -1)

    attn, q_ext = attend(place, own, q, keys, values)
    attn_rows = attn.reshape(-1, width)
    attn_own = exchange(attn_rows, 0, 1)
    mixed = x + nn(attn_own, whole_w)
    normed_two, unit_two, inverse_two = layer_stats(mixed, gain_two, shift_two)
    rows_two = all_rows(after(normed_two.astype(BF16), dy_rows, whole_w))
    shape = (1, SEQS, 2, BLK, width + 128)
    queries = gather_cores(gather_other(after(jnp.concatenate([q, q_ext], axis=2).reshape(shape), attn_own)))
    rows_two = after(rows_two, queries)

    act, grad_gu = mlp(rows_two, dy_rows, gate_w, up_w, down_w)
    ff = gate_w.shape[1]
    part_two = (nt(grad_gu[:, :ff], gate_w) + nt(grad_gu[:, ff:], up_w)).astype(BF16)
    grad_two = sum_rows(part_two)
    act, rows_two, dy_rows, grad_gu = after((act, rows_two, dy_rows, grad_gu), part_two)
    gu_fly, dw_fly = [], []
    gu = begin(lambda core: rc(columns(rows_two, core), grad_gu), gu_fly)
    dw = begin(lambda core: rc(act, columns(dy_rows, core)), dw_fly)
    held = take(gu)
    go(gu)
    down = nn(after(act, held), down_w).astype(BF16)
    held = take(dw), take(gu, down)
    go(gu)
    go(dw, held)
    grad_two = after(grad_two, held)

    norm_two, grad_gain_two, grad_shift_two = layer_back(grad_two.astype(F32), unit_two, inverse_two, gain_two)
    grad_mixed = cotangent.astype(F32) + norm_two
    branch_own = grad_mixed.astype(BF16)
    grad_attn = nt(branch_own, whole_w).astype(BF16)
    held = take(gu, grad_attn)
    go(gu)
    grad_attn = exchange(grad_attn, 1, 0)
    lane = jnp.arange(128)[None, :]
    ind = ((jnp.arange(width) // HEAD_DIM)[:, None] == lane // 3).astype(F32)
    delta = lax.dot_general(grad_attn.astype(F32) * attn_rows.astype(F32), ind, (((1,), (0,)), ((), ())),
                            precision=lax.Precision.HIGHEST, preferred_element_type=F32)
    do_ext = terms(-delta, lane).astype(BF16)
    do_sent = jnp.concatenate([grad_attn, do_ext], axis=1).reshape(shape)
    do_sent = after(do_sent, held, gu_fly)
    branch = all_rows(after(branch_own, do_sent))
    out_sum = sum_rows(after(down, do_sent))
    grads = gather_other(do_sent)
    grad_q = query_grad(place, own, q, grad_attn.reshape(q.shape), q_ext, do_ext.reshape(q_ext.shape), tabs, keys, values)
    grad_q = after(grad_q.reshape(-1, width), [grads[j] for j in grads if j > 1])
    grads = gather_cores(grads, grad_q)
    q_part = nt(grad_q, query_w)
    take(gu, grad_q)
    go(gu, grads)
    first = key_value_grad(place, own, kv, tabs, queries, grads, 0, SEQS // 2)
    grads = after(grads, take(dw, first))
    go(dw)
    second = key_value_grad(place, own, kv, tabs, queries, grads, SEQS // 2, SEQS // 2)
    second = after(second, dw_fly)
    grad_k, grad_v = (jnp.concatenate(pair).reshape(-1, width) for pair in zip(first, second))
    part_one = q_part + nt(grad_k, key_w) + nt(grad_v, value_w)
    part_sent = after(part_one.astype(BF16), branch)
    grad_one = sum_rows(part_sent)

    rows_one, branch, grad_q, grad_k, grad_v = after((rows_one, branch, grad_q, grad_k, grad_v), part_sent, gu_fly)
    grad_qkv = jnp.concatenate([grad_q, grad_k, grad_v], axis=1)
    chain = begin(lambda core: jnp.concatenate([rc(columns(rows_one, core), grad_qkv), rc(columns(branch, core), attn_rows)], axis=1))
    held = take(chain)
    go(chain)
    take(gu, held)
    take_extra(gu)
    go(gu)
    unit_rows = (rows_one.astype(F32) - shift_one) / gain_one
    bias_grad = jnp.sum(grad_qkv.astype(F32), axis=0)
    tp_row = (jnp.arange(n_tp) == lax.axis_index("tp"))[:, None]
    small = jnp.concatenate([
        jnp.sum(part_one * unit_rows, axis=0), jnp.sum(part_one, axis=0), grad_gain_two, grad_shift_two,
        jnp.where(tp_row, bias_grad[None, :], 0.0).reshape(-1)])
    take(dw, held)
    go(dw)
    held = take(chain)
    go(chain)
    held = take(chain, list(dw_fly))
    go(chain)
    take(dw, held)
    take_extra(dw)
    go(dw)
    sums = sum_over_all(after(small, held).reshape(-1, 1024))
    small = [next(sums) for _ in range(1 + int(math.log2(n_tp)))]
    grad_gate_w, grad_up_w = unpack_rows(*take(gu, held), 2)
    held = take(chain, (small, grad_gate_w, list(dw_fly)))
    take_extra(chain)
    go(chain)
    mixed_late, out_sum = after((mixed, out_sum), held)
    out_tokens = (mixed_late + out_sum.astype(F32)).astype(BF16)
    take(dw, held)
    go(dw)
    grad_down_w = unpack_cols(*take(dw))
    take(chain, grad_down_w)
    go(chain)
    for _ in range(4):
        small = next(sums)
    depth = x.shape[1]
    small = small.reshape(-1)
    norms = small[:4 * depth].reshape(4, depth)
    bias_sum = jnp.sum(jnp.where(tp_row, small[4 * depth:].reshape(n_tp, -1), 0.0), axis=0)
    grad_query_w, grad_key_w, grad_value_w, grad_output_w = unpack_rows(*take(chain), 4, True)
    norm_one, _, _ = layer_back(grad_one.astype(F32), unit_one, inverse_one, gain_one)
    grad_tokens = (grad_mixed + norm_one).astype(BF16)
    return (
        out_tokens, grad_tokens, norms[0], norms[1], grad_query_w, grad_key_w, grad_value_w,
        bias_sum[:width], bias_sum[width:2 * width].reshape(heads, HEAD_DIM)[:, :ROT], bias_sum[2 * width:],
        grad_output_w, norms[2], norms[3], grad_gate_w, grad_up_w, grad_down_w,
    )


def solution(mesh):
    rows, cols, depth, flat = P(("ctx", "tp"), None), P(None, "tp"), P("tp", None), P("tp")
    in_specs = (rows, rows, P(), P(), P(), cols, cols, cols, flat, depth, flat, depth, P(), P(), cols, cols, depth)
    out_specs = (rows, rows, P(), P(), cols, cols, cols, flat, depth, flat, depth, P(), P(), cols, cols, depth)
    return jax.shard_map(local, mesh=mesh, in_specs=in_specs, out_specs=out_specs, check_vma=False)
```

```python
import functools
import jax, jax.numpy as jnp
from jax import lax
from jax.experimental import pallas as pl
from jax.experimental.pallas import tpu as pltpu

BLK = 128
CB = 8
CH = BLK * CB
NEG = -1e30
SCALE = 0.125


def nt(a, b):
    return lax.dot_general(a, b, (((1,), (1,)), ((), ())), preferred_element_type=jnp.float32)


def nn(a, b):
    return lax.dot_general(a, b, (((1,), (0,)), ((), ())), preferred_element_type=jnp.float32)


def lane_of(shape):
    return lax.broadcasted_iota(jnp.int32, shape, 1)


def row_of(shape):
    return lax.broadcasted_iota(jnp.int32, shape, 0)


def split_heads(x):
    low = lane_of(x.shape) < 64
    zero = jnp.zeros_like(x)
    return jnp.concatenate([jnp.where(low, x, zero), jnp.where(low, zero, x)], axis=0)


def join_heads(x):
    low = lane_of((BLK, 128)) < 64
    return jnp.where(low, x[:BLK], x[BLK:])


def own_lanes(pair):
    shape = (2 * BLK, 128)
    return lane_of(shape) // 3 == 2 * pair + row_of(shape) // BLK


def lanes_of(pair):
    return slice(pair * 128, (pair + 1) * 128)


def terms(x, lane):
    first = x.astype(jnp.bfloat16).astype(jnp.float32)
    second = (x - first).astype(jnp.bfloat16).astype(jnp.float32)
    return jnp.where(lane % 3 == 0, first, jnp.where(lane % 3 == 1, second, x - first - second))


def place_rows(place_ref, s, refs, dst_ref, ext=False):
    pairs = dst_ref.shape[0]
    at = 0
    for ref in refs:
        for j in range(ref.shape[0]):
            for w in range(2):
                rows = pl.ds(pl.multiple_of(place_ref[s, at] * BLK, BLK), BLK)
                for p in range(pairs):
                    dst_ref[p, rows, 0:128] = ref[j, 0, w, :, p * 128:(p + 1) * 128]
                    if ext:
                        dst_ref[p, rows, 128:256] = ref[j, 0, w, :, pairs * 128:]
                at += 1


def sweep(full, step):
    def one(c, carry):
        step(c, False)
        return carry

    lax.fori_loop(0, full, one, 0)
    step(full, True)


def span(c):
    return pl.ds(pl.multiple_of(c * CH, CH), CH)


def may_see(query_block, c):
    shape = (2 * BLK, CH)
    return c * CH + lane_of(shape) <= query_block * BLK + row_of(shape) % BLK


def fwd_kernel(place_ref, own_ref, q_ref, *refs, pairs, n):
    k_refs, v_refs, (o_ref, ext_ref, ks, vs, qs, scr, run, acc) = refs[:n], refs[n:2 * n], refs[2 * n:]
    s = pl.program_id(0)

    @pl.when(s == 0)
    def _():
        for p in range(pairs):
            vs[p, :, 128:256] = jnp.ones((vs.shape[1], 128), jnp.bfloat16)

    place_rows(place_ref, s, k_refs, ks)
    place_rows(place_ref, s, v_refs, vs)

    for w in range(2):
        rows = slice(w * BLK, (w + 1) * BLK)
        pos = own_ref[s, w]
        for p in range(pairs):
            qs[p] = split_heads(q_ref[0, rows, lanes_of(p)] * jnp.bfloat16(SCALE))
        run[...] = jnp.full_like(run, NEG)
        acc[...] = jnp.zeros_like(acc)

        def score(c, masked):
            for p in range(pairs):
                sc = nt(qs[p], ks[p, span(c), :])
                if masked:
                    sc = jnp.where(may_see(pos, c), sc, NEG)
                scr[p, :, span(c)] = sc
                top = run[p]
                for t in range(CB):
                    top = jnp.maximum(top, sc[:, t * 128:(t + 1) * 128])
                run[p] = top

        sweep(pos // CB, score)
        for p in range(pairs):
            run[p] = jnp.broadcast_to(jnp.max(run[p], axis=1, keepdims=True), (2 * BLK, 128))

        def weigh(c, masked):
            for p in range(pairs):
                weight = jnp.exp(scr[p, :, span(c)] - jnp.concatenate([run[p]] * CB, axis=1)).astype(jnp.bfloat16)
                acc[p] += nn(weight, vs[p, span(c), :])

        sweep(pos // CB, weigh)
        lane = lane_of((2 * BLK, 128))
        ext = jnp.zeros((BLK, 128), jnp.float32)
        for p in range(pairs):
            total = acc[p, :, 128:256]
            o_ref[0, rows, lanes_of(p)] = join_heads(acc[p, :, 0:128] / total).astype(jnp.bfloat16)
            mine = jnp.where(own_lanes(p), terms(-(run[p] + jnp.log(total)), lane), 0.0)
            ext = ext + mine[:BLK] + mine[BLK:]
        ext_ref[0, rows, :] = ext.astype(jnp.bfloat16)


def dq_kernel(place_ref, own_ref, q_ref, do_ref, qx_ref, dox_ref, c_ref, a_ref, b_ref, *refs, pairs, n):
    k_refs, v_refs, (dq_ref, ks, vs, qs, dos, acc) = refs[:n], refs[n:2 * n], refs[2 * n:]
    s = pl.program_id(0)

    @pl.when(s == 0)
    def _():
        for ref in (ks, vs):
            for p in range(pairs):
                ref[p, :, 128:256] = jnp.ones((ref.shape[1], 128), jnp.bfloat16)

    place_rows(place_ref, s, k_refs, ks)
    place_rows(place_ref, s, v_refs, vs)

    for w in range(2):
        rows = slice(w * BLK, (w + 1) * BLK)
        pos = own_ref[s, w]

        def extend(tile, ext, p):
            both = jnp.concatenate([ext, ext], axis=0)
            return jnp.concatenate([split_heads(tile), jnp.where(own_lanes(p), both, jnp.zeros_like(both))], axis=1)

        for p in range(pairs):
            qs[p] = extend(q_ref[0, rows, lanes_of(p)] * jnp.bfloat16(SCALE), qx_ref[0, rows, :], p)
            dos[p] = extend(do_ref[0, rows, lanes_of(p)], dox_ref[0, rows, :], p)
        acc[...] = jnp.zeros_like(acc)

        def step(c, masked):
            for p in range(pairs):
                prob = jnp.exp(nt(qs[p], ks[p, span(c), :]))
                if masked:
                    prob = jnp.where(may_see(pos, c), prob, 0.0)
                ds = (prob * nt(dos[p], vs[p, span(c), :])).astype(jnp.bfloat16)
                acc[p] += nn(ds, ks[p, span(c), 0:128])

        sweep(pos // CB, step)
        for p in range(pairs):
            grad = join_heads(acc[p]) * SCALE
            dq_ref[0, rows, lanes_of(p)] = turn(grad, c_ref[rows], a_ref[rows], b_ref[rows], -1.0).astype(jnp.bfloat16)


def dkv_kernel(place_ref, own_ref, kv_ref, c_ref, a_ref, b_ref, *refs, pairs, n, lead):
    q_refs, do_refs, (dk_ref, dv_ref, qs, dos, kw, vw, acck, accv) = refs[:n], refs[n:2 * n], refs[2 * n:]
    s = pl.program_id(0) + lead
    place_rows(place_ref, s, q_refs, qs, True)
    place_rows(place_ref, s, do_refs, dos, True)
    chunks = qs.shape[1] // CH

    for w in range(2):
        rows = slice(w * BLK, (w + 1) * BLK)
        pos = own_ref[s, w]
        first = pos // CB
        for p in range(pairs):
            ones = own_lanes(p).astype(jnp.bfloat16)
            kw[p] = jnp.concatenate([split_heads(kv_ref[0, 0, rows, lanes_of(p)] * jnp.bfloat16(SCALE)), ones], axis=1)
            vw[p] = jnp.concatenate([split_heads(kv_ref[1, 0, rows, lanes_of(p)]), ones], axis=1)
        acck[...] = jnp.zeros_like(acck)
        accv[...] = jnp.zeros_like(accv)

        def step(c, masked):
            for p in range(pairs):
                prob = jnp.exp(nt(kw[p], qs[p, span(c), :]))
                if masked:
                    shape = (2 * BLK, CH)
                    prob = jnp.where(pos * BLK + row_of(shape) % BLK <= c * CH + lane_of(shape), prob, 0.0)
                accv[p] += nn(prob.astype(jnp.bfloat16), dos[p, span(c), 0:128])
                ds = (prob * nt(vw[p], dos[p, span(c), :])).astype(jnp.bfloat16)
                acck[p] += nn(ds, qs[p, span(c), 0:128])

        def one(c, carry):
            step(c, False)
            return carry

        step(first, True)
        lax.fori_loop(first + 1, chunks, one, 0)
        for p in range(pairs):
            grad = join_heads(acck[p]) * SCALE
            dk_ref[0, rows, lanes_of(p)] = turn(grad, c_ref[rows], a_ref[rows], b_ref[rows], -1.0).astype(jnp.bfloat16)
            dv_ref[0, rows, lanes_of(p)] = join_heads(accv[p]).astype(jnp.bfloat16)


def own(width):
    return pl.BlockSpec((1, 2 * BLK, width), lambda s, *_: (s, 0, 0))


def table(lead=0):
    return pl.BlockSpec((2 * BLK, 128), lambda s, *_: (s + lead, 0))


def piece(x, first=0, lead=0):
    return pl.BlockSpec((1, 1, 2, BLK, x.shape[4]), lambda s, *_: (first, s + lead, 0, 0, 0))


def attention_call(kernel, name, mats, seqs, pairs, blocks, in_specs, out_specs, out_shape, scratch, args):
    work = seqs * pairs * 2 * 2 * BLK * blocks * BLK // 2
    return pl.pallas_call(
        kernel,
        grid_spec=pltpu.PrefetchScalarGridSpec(
            num_scalar_prefetch=2, grid=(seqs,), in_specs=in_specs, out_specs=out_specs, scratch_shapes=scratch),
        out_shape=out_shape,
        compiler_params=pltpu.CompilerParams(vmem_limit_bytes=60 * 2**20),
        cost_estimate=pl.CostEstimate(flops=work * 64 * mats, bytes_accessed=seqs * pairs * blocks * BLK * 128, transcendentals=0),
        name=name,
    )(*args)


def rows_of(pairs, blocks, lanes):
    return pltpu.VMEM((pairs, blocks * BLK, lanes), jnp.bfloat16)


def acc_of(pairs, lanes, dtype=jnp.float32):
    return pltpu.VMEM((pairs, 2 * BLK, lanes), dtype)


def attend(place, own_blocks, q, keys, values):
    seqs, width, blocks = q.shape[0], q.shape[2], place.shape[1]
    pairs = width // 128
    return attention_call(
        functools.partial(fwd_kernel, pairs=pairs, n=len(keys)), "attend", 2, seqs, pairs, blocks,
        [own(width)] + [piece(*e) for e in keys + values], [own(width), own(128)],
        [jax.ShapeDtypeStruct(q.shape, jnp.bfloat16), jax.ShapeDtypeStruct(q.shape[:2] + (128,), jnp.bfloat16)],
        [rows_of(pairs, blocks, 128), rows_of(pairs, blocks, 256), acc_of(pairs, 128, jnp.bfloat16), acc_of(pairs, blocks * BLK),
         acc_of(pairs, 128), acc_of(pairs, 256)],
        [place, own_blocks, q] + [e[0] for e in keys + values])


def query_grad(place, own_blocks, q, do, q_ext, do_ext, tabs, keys, values):
    seqs, width, blocks = q.shape[0], q.shape[2], place.shape[1]
    pairs = width // 128
    return attention_call(
        functools.partial(dq_kernel, pairs=pairs, n=len(keys)), "query_grad", 3, seqs, pairs, blocks,
        [own(width), own(width), own(128), own(128)] + [table()] * 3 + [piece(*e) for e in keys + values], own(width),
        jax.ShapeDtypeStruct(q.shape, jnp.bfloat16),
        [rows_of(pairs, blocks, 256), rows_of(pairs, blocks, 256), acc_of(pairs, 256, jnp.bfloat16), acc_of(pairs, 256, jnp.bfloat16),
         acc_of(pairs, 128)],
        [place, own_blocks, q, do, q_ext, do_ext, *tabs] + [e[0] for e in keys + values])


def key_value_grad(place, own_blocks, kv, tabs, queries, grads, lead, count):
    width, blocks = kv.shape[3], place.shape[1]
    pairs = width // 128
    shape = (count,) + kv.shape[2:]
    return attention_call(
        functools.partial(dkv_kernel, pairs=pairs, n=len(queries), lead=lead), "key_value_grad", 4, count, pairs, blocks,
        [pl.BlockSpec((2, 1, 2 * BLK, width), lambda s, *_: (0, s + lead, 0, 0))] + [table(lead)] * 3
        + [piece(x, lead=lead) for x in queries + grads], [own(width)] * 2,
        [jax.ShapeDtypeStruct(shape, jnp.bfloat16)] * 2,
        [rows_of(pairs, blocks, 256), rows_of(pairs, blocks, 256), acc_of(pairs, 256, jnp.bfloat16), acc_of(pairs, 256, jnp.bfloat16),
         acc_of(pairs, 128), acc_of(pairs, 128)],
        [place, own_blocks, kv, *tabs] + queries + grads)


import math
from jax.sharding import PartitionSpec as P

HEAD_DIM = 64
ROT = 16
SEQS = 4
EPS = 1e-05
F32 = jnp.float32
BF16 = jnp.bfloat16


def rc(left, right):
    return lax.dot_general(left, right, (((0,), (0,)), ((), ())), preferred_element_type=F32)


def layer_stats(values, gain, shift):
    mean = jnp.mean(values, axis=-1, keepdims=True)
    centred = values - mean
    inverse = lax.rsqrt(jnp.mean(centred * centred, axis=-1, keepdims=True) + EPS)
    unit = centred * inverse
    return unit * gain + shift, unit, inverse


def layer_back(grad, unit, inverse, gain):
    scaled = grad * gain
    grad_in = inverse * (
        scaled
        - jnp.mean(scaled, axis=-1, keepdims=True)
        - unit * jnp.mean(scaled * unit, axis=-1, keepdims=True)
    )
    return grad_in, jnp.sum(grad * unit, axis=0), jnp.sum(grad, axis=0)


def rotary_tables(positions):
    half = ROT // 2
    dim = jnp.arange(2 * HEAD_DIM) % HEAD_DIM
    freq = jnp.where(dim < ROT, 10000.0 ** (-2.0 * (dim % half).astype(F32) / ROT), 0.0)
    angles = positions.astype(F32)[:, None] * freq[None, :]
    sin = jnp.sin(angles)
    return jnp.cos(angles), jnp.where(dim < half, sin, 0.0), jnp.where(dim < half, 0.0, sin)


def turn(x, ctab, above, below, sign):
    up = pltpu.roll(x, 128 - ROT // 2, axis=1)
    down = pltpu.roll(x, ROT // 2, axis=1)
    return x * ctab + sign * (down * below - up * above)


def project_kernel(h_ref, wq_ref, wk_ref, wv_ref, bias_ref, c_ref, a_ref, b_ref, q_ref, kv_ref):
    h = h_ref[...]
    width = wq_ref.shape[1]
    tabs = c_ref[...], a_ref[...], b_ref[...]
    for at, (w_ref, out) in enumerate(((wq_ref, q_ref.at[0]), (wk_ref, kv_ref.at[0, 0]), (wv_ref, kv_ref.at[1, 0]))):
        lin = nn(h, w_ref[...]) + bias_ref[at:at + 1, :]
        for p in range(width // 128):
            part = lin[:, p * 128:(p + 1) * 128]
            if at < 2:
                part = turn(part, *tabs, 1.0)
            out[:, p * 128:(p + 1) * 128] = part.astype(BF16)


def project(rows, wq, wk, wv, bias, tabs):
    total, depth = rows.shape
    width = wq.shape[1]
    step = total // SEQS
    weight = pl.BlockSpec((depth, width), lambda i: (0, 0))
    table = pl.BlockSpec((step, 128), lambda i: (i, 0))
    return pl.pallas_call(
        project_kernel,
        grid=(SEQS,),
        in_specs=[pl.BlockSpec((step, depth), lambda i: (i, 0)), weight, weight, weight,
                  pl.BlockSpec((3, width), lambda i: (0, 0)), table, table, table],
        out_specs=[pl.BlockSpec((1, step, width), lambda i: (i, 0, 0)),
                   pl.BlockSpec((2, 1, step, width), lambda i: (0, i, 0, 0))],
        out_shape=[jax.ShapeDtypeStruct((SEQS, step, width), BF16), jax.ShapeDtypeStruct((2, SEQS, step, width), BF16)],
        compiler_params=pltpu.CompilerParams(vmem_limit_bytes=48 * 2**20),
        cost_estimate=pl.CostEstimate(flops=6 * total * depth * width, bytes_accessed=6 * depth * width, transcendentals=0),
        name="project",
    )(rows, wq, wk, wv, bias, *tabs)


def mlp_kernel(h_ref, dy_ref, gate_ref, up_ref, down_ref, act_ref, *grad_refs):
    width = gate_ref.shape[1]
    gate = nn(h_ref[...], gate_ref[...])
    up = nn(h_ref[...], up_ref[...])
    grad = nt(dy_ref[...], down_ref[...])
    sig = 1.0 / (1.0 + jnp.exp(-gate))
    silu = gate * sig
    act_ref[...] = (silu * up).astype(BF16)
    outs = grad_refs if len(grad_refs) == 2 else (grad_refs[0].at[:, :width], grad_refs[0].at[:, width:])
    outs[0][...] = (grad * up * (sig + silu * (1.0 - sig))).astype(BF16)
    outs[1][...] = (grad * silu).astype(BF16)


def mlp(rows, dy, gate_w, up_w, down_w, step=256):
    total, depth = rows.shape
    width = gate_w.shape[1]
    joined = width % 128 == 0
    block = pl.BlockSpec((step, depth), lambda i: (i, 0))

    def whole(x):
        return pl.BlockSpec(x.shape, lambda i: (0, 0), pipeline_mode=pl.Buffered(1))

    def out(n):
        return pl.BlockSpec((step, n), lambda i: (i, 0)), jax.ShapeDtypeStruct((total, n), BF16)

    outs = [out(width), out(2 * width)] if joined else [out(width)] * 3
    act, *grads = pl.pallas_call(
        mlp_kernel,
        grid=(total // step,),
        in_specs=[block, block, whole(gate_w), whole(up_w), whole(down_w)],
        out_specs=[o[0] for o in outs],
        out_shape=[o[1] for o in outs],
        compiler_params=pltpu.CompilerParams(vmem_limit_bytes=56 * 2**20),
        cost_estimate=pl.CostEstimate(flops=6 * total * depth * width, bytes_accessed=6 * depth * width + 10 * total * depth,
                                      transcendentals=total * width),
        name="mlp",
    )(rows, dy, gate_w, up_w, down_w)
    return act, grads[0] if joined else jnp.concatenate(grads, axis=1)


def ctx_swap(x, mask):
    n = lax.axis_size("ctx")
    return lax.ppermute(x, "ctx", [(i, i ^ mask) for i in range(n)])


def add16(a, b):
    return (a.astype(F32) + b.astype(F32)).astype(BF16)


def after(x, *deps):
    if not jax.tree.leaves(deps):
        return x
    return lax.optimization_barrier((x, deps))[0]


def half_of(x, bit, mine):
    side = (lax.axis_index("ctx") >> bit) & 1
    r = x.shape[0] // 2
    return lax.dynamic_slice_in_dim(x, (side if mine else 1 - side) * r, r, 0)


def assemble_kernel(source_ref, *refs):
    *in_refs, out_ref = refs
    for k, ref in enumerate(in_refs):

        @pl.when(source_ref[pl.program_id(0)] == k)
        def _(ref=ref):
            out_ref[...] = ref[...]


def assemble(pieces, source):
    r, c = pieces[0].shape
    count = len(pieces)
    return pl.pallas_call(
        assemble_kernel,
        grid_spec=pltpu.PrefetchScalarGridSpec(
            num_scalar_prefetch=1, grid=(count,),
            in_specs=[pl.BlockSpec((r, c), lambda j, _: (0, 0), pipeline_mode=pl.Buffered(1))] * count,
            out_specs=pl.BlockSpec((r, c), lambda j, _: (j, 0))),
        out_shape=jax.ShapeDtypeStruct((count * r, c), BF16),
        compiler_params=pltpu.CompilerParams(vmem_limit_bytes=40 * 2**20),
        cost_estimate=pl.CostEstimate(flops=0, bytes_accessed=1024, transcendentals=0),
        name="assemble",
    )(source, *pieces)


def weight_grad(part, flying):
    core = lax.axis_index("ctx") & 1
    got = ctx_swap(part(1 - core).astype(BF16), 1)
    flying[:] = [got]
    gate = yield
    half = (part(core) + after(got, gate).astype(F32)).astype(BF16)
    bits = list(range(1, int(math.log2(lax.axis_size("ctx")))))
    orders = [bits, bits[::-1]]
    r = half.shape[0] // 2
    streams = [half[:r], half[r:]]
    gate = yield streams
    for i in range(len(bits)):
        streams = after(streams, gate)
        got = [ctx_swap(half_of(x, o[i], False), 1 << o[i]) for x, o in zip(streams, orders)]
        flying[:] = got
        gate = yield
        streams, got = after((streams, got), gate)
        streams = [add16(half_of(x, o[i], True), g) for x, o, g in zip(streams, orders, got)]
        gate = yield streams
    for i in reversed(range(len(bits))):
        streams = after(streams, gate)
        got = [ctx_swap(x, 1 << o[i]) for x, o in zip(streams, orders)]
        flying[:] = got
        gate = yield
        streams, got = after((streams, got), gate)
        sides = [(lax.axis_index("ctx") >> o[i]) & 1 for o in orders]
        if i == 0:
            source = jnp.stack([sides[0], 1 - sides[0], 2 + sides[1], 3 - sides[1]])
            streams = assemble([streams[0], got[0], streams[1], got[1]], source)
        else:
            streams = [
                jnp.where(side == 0, jnp.concatenate([x, g]), jnp.concatenate([g, x]))
                for x, side, g in zip(streams, sides, got)
            ]
        gate = yield streams
    streams = after(streams, gate)
    other = ctx_swap(streams, 1)
    gate = yield
    yield after((streams, other), gate)


def begin(part, flying=None):
    chain = weight_grad(part, [] if flying is None else flying)
    next(chain)
    return chain


def take(chain, gate=None):
    return chain.send(gate)


def go(chain, gate=None):
    chain.send(gate)


def take_extra(chain):
    for _ in range(2 * int(math.log2(lax.axis_size("ctx"))) - 6):
        go(chain)
        take(chain)


def unpack_rows_kernel(core_ref, half_ref, other_ref, *out_refs, turned):
    def put(src):
        at = 0
        for i, out in enumerate(out_refs):
            if turned and i == len(out_refs) - 1:
                out[...] = src[:, at:].astype(F32).T
            else:
                out[...] = src[:, at:at + out.shape[1]].astype(F32)
                at += out.shape[1]

    @pl.when(pl.program_id(0) == core_ref[0])
    def _():
        put(half_ref)

    @pl.when(pl.program_id(0) != core_ref[0])
    def _():
        put(other_ref)


def unpack_rows(half, other, parts, turned=False):
    r, c = half.shape
    step = math.gcd(r, 256)
    blocks = r // step
    w = c // parts
    core = lax.axis_index("ctx") & 1

    def mine(i, j, core_ref):
        return jnp.where(i == core_ref[0], j, jnp.where(core_ref[0] == 0, blocks - 1, 0)), 0

    def theirs(i, j, core_ref):
        return jnp.where(i != core_ref[0], j, jnp.where(core_ref[0] == 1, blocks - 1, 0)), 0

    specs = [pl.BlockSpec((step, w), lambda i, j, _: (i * blocks + j, 0))] * parts
    shapes = [jax.ShapeDtypeStruct((2 * r, w), F32)] * parts
    if turned:
        specs[-1] = pl.BlockSpec((w, step), lambda i, j, _: (0, i * blocks + j))
        shapes[-1] = jax.ShapeDtypeStruct((w, 2 * r), F32)
    return pl.pallas_call(
        functools.partial(unpack_rows_kernel, turned=turned),
        grid_spec=pltpu.PrefetchScalarGridSpec(
            num_scalar_prefetch=1, grid=(2, blocks),
            in_specs=[pl.BlockSpec((step, c), mine), pl.BlockSpec((step, c), theirs)], out_specs=specs),
        out_shape=shapes,
        compiler_params=pltpu.CompilerParams(vmem_limit_bytes=40 * 2**20),
        cost_estimate=pl.CostEstimate(flops=0, bytes_accessed=1024, transcendentals=0),
        name="unpack_rows",
    )(core[None], half, other)


def columns(x, which):
    w = x.shape[1] // 2
    return lax.dynamic_slice_in_dim(x, which * w, w, 1)


def unpack_cols_kernel(core_ref, half_ref, other_ref, out_ref):
    c = half_ref.shape[1]
    core = core_ref[0]
    out_ref[:, pl.ds(pl.multiple_of(core * c, 128), c)] = half_ref[...].astype(F32)
    out_ref[:, pl.ds(pl.multiple_of((1 - core) * c, 128), c)] = other_ref[...].astype(F32)


def unpack_cols(half, other):
    r, c = half.shape
    step = math.gcd(r, 256)
    block = pl.BlockSpec((step, c), lambda i, _: (i, 0))
    return pl.pallas_call(
        unpack_cols_kernel,
        grid_spec=pltpu.PrefetchScalarGridSpec(
            num_scalar_prefetch=1, grid=(r // step,), in_specs=[block, block],
            out_specs=pl.BlockSpec((step, 2 * c), lambda i, _: (i, 0))),
        out_shape=jax.ShapeDtypeStruct((r, 2 * c), F32),
        compiler_params=pltpu.CompilerParams(vmem_limit_bytes=40 * 2**20),
        cost_estimate=pl.CostEstimate(flops=0, bytes_accessed=1024, transcendentals=0),
        name="unpack_cols",
    )((lax.axis_index("ctx") & 1)[None], half, other)


def all_rows(x):
    return lax.all_gather(x, "tp", axis=0, tiled=True)


def tp_shift(x, d):
    n = lax.axis_size("tp")
    return lax.ppermute(x, "tp", [(i, (i + d) % n) for i in range(n)])


def part_of(x, d, axis):
    n = lax.axis_size("tp")
    w = x.shape[axis] // n
    return lax.dynamic_slice_in_dim(x, (lax.axis_index("tp") + d) % n * w, w, axis)


def exchange(x, split, join):
    n, me = lax.axis_size("tp"), lax.axis_index("tp")
    w = x.shape[join]
    shape = list(x.shape)
    shape[split] //= n
    shape[join] *= n
    out = jnp.zeros(shape, x.dtype)
    for d in range(n):
        got = tp_shift(part_of(x, d, split), d) if d else part_of(x, 0, split)
        out = lax.dynamic_update_slice_in_dim(out, got, (me + n - d) % n * w, join)
    return out


def sum_rows(x):
    return lax.psum_scatter(x, "tp", scatter_dimension=0, tiled=True)


def gather_pair(kv):
    n = lax.axis_size("ctx")
    held = {0: ((kv, 0), (kv, 1))}
    for bit in range(1, int(math.log2(n))):
        mask = 1 << bit
        for j in list(held):
            if j == 0:
                got = ctx_swap(kv, mask)
                held[mask] = (got, 0), (got, 1)
            elif mask == 4 and j == 2:
                held[6] = (ctx_swap(held[2][0][0][0:1], 4), 0), (ctx_swap(held[4][1][0][1:2], 2), 0)
            else:
                (k, i), (v, t) = held[j]
                if k is v:
                    got = ctx_swap(k, mask)
                    held[j | mask] = (got, i), (got, t)
                else:
                    held[j | mask] = (ctx_swap(k, mask), i), (ctx_swap(v, mask), t)
    for j in list(held):
        (k, i), (v, t) = held[j]
        got = ctx_swap(k, 1)
        held[j | 1] = (got, i), (got if k is v else ctx_swap(v, 1), t)
    return [held[j][0] for j in range(n)], [held[j][1] for j in range(n)]


def gather_other(x):
    held = {0: x, 1: ctx_swap(x, 1)}
    for j in range(2, lax.axis_size("ctx"), 2):
        held[j] = ctx_swap(x, j)
    return held


def gather_cores(held, gate=None):
    n = lax.axis_size("ctx")
    for j in range(2, n, 2):
        held[j + 1] = ctx_swap(after(held[j], gate), 1)
    return [held[j] for j in range(n)]


def sum_over_all(x):
    steps = [(axis, bit) for axis in ("ctx", "tp") for bit in range(int(math.log2(lax.axis_size(axis))))]
    for axis, bit in sorted(steps, key=lambda step: step[0] == "ctx" and step[1] > 0):
        x = x + lax.ppermute(x, axis, [(i, i ^ (1 << bit)) for i in range(lax.axis_size(axis))])
        yield x
    while True:
        yield x


def gather_tp(x):
    n, me = lax.axis_size("tp"), lax.axis_index("tp")
    out = jnp.zeros((n,) + x.shape, x.dtype)
    for d in range(n):
        got = lax.ppermute(x, "tp", [(i, (i + d) % n) for i in range(n)]) if d else x
        out = lax.dynamic_update_index_in_dim(out, got, (me + n - d) % n, 0)
    return out


def local(tokens, cotangent, block_order, gain_one, shift_one, query_w, key_w, value_w, query_b, key_b, value_b,
          output_w, gain_two, shift_two, gate_w, up_w, down_w):
    heads = key_b.shape[0]
    width = heads * HEAD_DIM
    n_ctx, n_tp = lax.axis_size("ctx"), lax.axis_size("tp")
    ctx = lax.axis_index("ctx")
    own = lax.dynamic_slice_in_dim(block_order, 2 * ctx, 2, 1)
    picked = (jnp.arange(n_ctx, dtype=jnp.int32) ^ ctx)[:, None] == jnp.arange(n_ctx, dtype=jnp.int32)[None, :]
    by_ctx = block_order.reshape(SEQS, 1, n_ctx, 2)
    place = jnp.sum(jnp.where(picked[None, :, :, None], by_ctx, 0), axis=2).astype(jnp.int32).reshape(SEQS, 2 * n_ctx)
    positions = (own[:, :, None] * BLK + jnp.arange(BLK, dtype=jnp.int32)).reshape(-1)
    tabs = rotary_tables(positions)

    x = tokens.astype(F32)
    normed_one, unit_one, inverse_one = layer_stats(x, gain_one, shift_one)
    rows_one = all_rows(normed_one.astype(BF16))
    key_bias = jnp.concatenate([key_b, jnp.zeros((heads, HEAD_DIM - ROT), F32)], axis=1).reshape(-1)
    bias = jnp.stack([query_b, key_bias, value_b])
    q, kv = project(rows_one, query_w, key_w, value_w, bias, tabs)
    keys, values = gather_pair(kv.reshape(2, SEQS, 2, BLK, width))
    arrived = [e[0] for e in keys + values]

    rows_w = output_w.shape[0] // n_ctx
    part = lax.dynamic_slice_in_dim(output_w, ctx * rows_w, rows_w, 0)
    part = gather_tp(after(part, kv))
    dy_rows = all_rows(after(cotangent, rows_one))
    whole_w = lax.all_gather(after(part, arrived, dy_rows), "ctx", axis=1).reshape(n_tp * output_w.shape[0], -1)

    attn, q_ext = attend(place, own, q, keys, values)
    attn_rows = attn.reshape(-1, width)
    attn_own = exchange(attn_rows, 0, 1)
    mixed = x + nn(attn_own, whole_w)
    normed_two, unit_two, inverse_two = layer_stats(mixed, gain_two, shift_two)
    rows_two = all_rows(after(normed_two.astype(BF16), dy_rows, whole_w))
    shape = (1, SEQS, 2, BLK, width + 128)
    queries = gather_cores(gather_other(after(jnp.concatenate([q, q_ext], axis=2).reshape(shape), attn_own)))
    rows_two = after(rows_two, queries)

    act, grad_gu = mlp(rows_two, dy_rows, gate_w, up_w, down_w)
    ff = gate_w.shape[1]
    part_two = (nt(grad_gu[:, :ff], gate_w) + nt(grad_gu[:, ff:], up_w)).astype(BF16)
    grad_two = sum_rows(part_two)
    act, rows_two, dy_rows, grad_gu = after((act, rows_two, dy_rows, grad_gu), part_two)
    gu_fly, dw_fly = [], []
    gu = begin(lambda core: rc(columns(rows_two, core), grad_gu), gu_fly)
    dw = begin(lambda core: rc(act, columns(dy_rows, core)), dw_fly)
    held = take(gu)
    go(gu)
    down = nn(after(act, held), down_w).astype(BF16)
    held = take(dw), take(gu, down)
    go(gu)
    go(dw, held)
    grad_two = after(grad_two, held)

    norm_two, grad_gain_two, grad_shift_two = layer_back(grad_two.astype(F32), unit_two, inverse_two, gain_two)
    grad_mixed = cotangent.astype(F32) + norm_two
    branch_own = grad_mixed.astype(BF16)
    grad_attn = nt(branch_own, whole_w).astype(BF16)
    held = take(gu, grad_attn)
    go(gu)
    grad_attn = exchange(grad_attn, 1, 0)
    lane = jnp.arange(128)[None, :]
    ind = ((jnp.arange(width) // HEAD_DIM)[:, None] == lane // 3).astype(F32)
    delta = lax.dot_general(grad_attn.astype(F32) * attn_rows.astype(F32), ind, (((1,), (0,)), ((), ())),
                            precision=lax.Precision.HIGHEST, preferred_element_type=F32)
    do_ext = terms(-delta, lane).astype(BF16)
    do_sent = jnp.concatenate([grad_attn, do_ext], axis=1).reshape(shape)
    do_sent = after(do_sent, held, gu_fly)
    branch = all_rows(after(branch_own, do_sent))
    out_sum = sum_rows(after(down, do_sent))
    grads = gather_other(do_sent)
    grad_q = query_grad(place, own, q, grad_attn.reshape(q.shape), q_ext, do_ext.reshape(q_ext.shape), tabs, keys, values)
    grad_q = after(grad_q.reshape(-1, width), [grads[j] for j in grads if j > 1])
    grads = gather_cores(grads, grad_q)
    q_part = nt(grad_q, query_w)
    grads = after(grads, take(gu, grad_q))
    go(gu, grads)
    first = key_value_grad(place, own, kv, tabs, queries, grads, 0, SEQS // 2)
    grads = after(grads, take(dw, first))
    go(dw)
    second = key_value_grad(place, own, kv, tabs, queries, grads, SEQS // 2, SEQS // 2)
    second = after(second, dw_fly)
    grad_k, grad_v = (jnp.concatenate(pair).reshape(-1, width) for pair in zip(first, second))
    part_one = q_part + nt(grad_k, key_w) + nt(grad_v, value_w)
    part_sent = after(part_one.astype(BF16), branch)
    rows_one, branch, grad_q, grad_k, grad_v = after((rows_one, branch, grad_q, grad_k, grad_v), part_sent, gu_fly)
    grad_qkv = jnp.concatenate([grad_q, grad_k, grad_v], axis=1)
    chain = begin(lambda core: jnp.concatenate([rc(columns(rows_one, core), grad_qkv), rc(columns(branch, core), attn_rows)], axis=1))
    held = take(chain)
    go(chain)
    grad_one = sum_rows(after(part_sent, out_sum, held))
    take(gu, held)
    take_extra(gu)
    go(gu)
    unit_rows = (rows_one.astype(F32) - shift_one) / gain_one
    bias_grad = jnp.sum(grad_qkv.astype(F32), axis=0)
    tp_row = (jnp.arange(n_tp) == lax.axis_index("tp"))[:, None]
    small = jnp.concatenate([
        jnp.sum(part_one * unit_rows, axis=0), jnp.sum(part_one, axis=0), grad_gain_two, grad_shift_two,
        jnp.where(tp_row, bias_grad[None, :], 0.0).reshape(-1)])
    take(dw, held)
    go(dw)
    held = take(chain, out_sum)
    go(chain)
    held = take(chain, list(dw_fly))
    go(chain)
    take(dw, held)
    take_extra(dw)
    go(dw)
    grad_gate_w, grad_up_w = unpack_rows(*take(gu, held), 2)
    held = take(chain, (grad_gate_w, list(dw_fly)))
    take_extra(chain)
    go(chain)
    mixed_late, out_sum = after((mixed, out_sum), held)
    out_tokens = (mixed_late + out_sum.astype(F32)).astype(BF16)
    take(dw, held)
    go(dw)
    sums = sum_over_all(after(small, held).reshape(-1, 1024))
    small = [next(sums) for _ in range(1 + int(math.log2(n_tp)))]
    grad_down_w = unpack_cols(*take(dw))
    take(chain, (grad_down_w, small))
    go(chain)
    for _ in range(4):
        small = next(sums)
    depth = x.shape[1]
    small = small.reshape(-1)
    norms = small[:4 * depth].reshape(4, depth)
    bias_sum = jnp.sum(jnp.where(tp_row, small[4 * depth:].reshape(n_tp, -1), 0.0), axis=0)
    grad_query_w, grad_key_w, grad_value_w, grad_output_w = unpack_rows(*take(chain), 4, True)
    norm_one, _, _ = layer_back(grad_one.astype(F32), unit_one, inverse_one, gain_one)
    grad_tokens = (grad_mixed + norm_one).astype(BF16)
    return (
        out_tokens, grad_tokens, norms[0], norms[1], grad_query_w, grad_key_w, grad_value_w,
        bias_sum[:width], bias_sum[width:2 * width].reshape(heads, HEAD_DIM)[:, :ROT], bias_sum[2 * width:],
        grad_output_w, norms[2], norms[3], grad_gate_w, grad_up_w, grad_down_w,
    )


def solution(mesh):
    rows, cols, depth, flat = P(("ctx", "tp"), None), P(None, "tp"), P("tp", None), P("tp")
    in_specs = (rows, rows, P(), P(), P(), cols, cols, cols, flat, depth, flat, depth, P(), P(), cols, cols, depth)
    out_specs = (rows, rows, P(), P(), cols, cols, cols, flat, depth, flat, depth, P(), P(), cols, cols, depth)
    return jax.shard_map(local, mesh=mesh, in_specs=in_specs, out_specs=out_specs, check_vma=False)
```

```python
import functools
import jax, jax.numpy as jnp
from jax import lax
from jax.experimental import pallas as pl
from jax.experimental.pallas import tpu as pltpu

BLK = 128
CB = 8
CH = BLK * CB
NEG = -1e30
SCALE = 0.125


def nt(a, b):
    return lax.dot_general(a, b, (((1,), (1,)), ((), ())), preferred_element_type=jnp.float32)


def nn(a, b):
    return lax.dot_general(a, b, (((1,), (0,)), ((), ())), preferred_element_type=jnp.float32)


def lane_of(shape):
    return lax.broadcasted_iota(jnp.int32, shape, 1)


def row_of(shape):
    return lax.broadcasted_iota(jnp.int32, shape, 0)


def split_heads(x):
    low = lane_of(x.shape) < 64
    zero = jnp.zeros_like(x)
    return jnp.concatenate([jnp.where(low, x, zero), jnp.where(low, zero, x)], axis=0)


def join_heads(x):
    low = lane_of((BLK, 128)) < 64
    return jnp.where(low, x[:BLK], x[BLK:])


def own_lanes(pair):
    shape = (2 * BLK, 128)
    return lane_of(shape) // 3 == 2 * pair + row_of(shape) // BLK


def lanes_of(pair):
    return slice(pair * 128, (pair + 1) * 128)


def terms(x, lane):
    first = x.astype(jnp.bfloat16).astype(jnp.float32)
    second = (x - first).astype(jnp.bfloat16).astype(jnp.float32)
    return jnp.where(lane % 3 == 0, first, jnp.where(lane % 3 == 1, second, x - first - second))


def place_rows(place_ref, s, refs, dst_ref, ext=False):
    pairs = dst_ref.shape[0]
    at = 0
    for ref in refs:
        for j in range(ref.shape[0]):
            for w in range(2):
                rows = pl.ds(pl.multiple_of(place_ref[s, at] * BLK, BLK), BLK)
                for p in range(pairs):
                    dst_ref[p, rows, 0:128] = ref[j, 0, w, :, p * 128:(p + 1) * 128]
                    if ext:
                        dst_ref[p, rows, 128:256] = ref[j, 0, w, :, pairs * 128:]
                at += 1


def sweep(full, step):
    def one(c, carry):
        step(c, False)
        return carry

    lax.fori_loop(0, full, one, 0)
    step(full, True)


def span(c):
    return pl.ds(pl.multiple_of(c * CH, CH), CH)


def may_see(query_block, c):
    shape = (2 * BLK, CH)
    return c * CH + lane_of(shape) <= query_block * BLK + row_of(shape) % BLK


def fwd_kernel(place_ref, own_ref, q_ref, *refs, pairs, n):
    k_refs, v_refs, (o_ref, ext_ref, ks, vs, qs, scr, run, acc) = refs[:n], refs[n:2 * n], refs[2 * n:]
    s = pl.program_id(0)

    @pl.when(s == 0)
    def _():
        for p in range(pairs):
            vs[p, :, 128:256] = jnp.ones((vs.shape[1], 128), jnp.bfloat16)

    place_rows(place_ref, s, k_refs, ks)
    place_rows(place_ref, s, v_refs, vs)

    for w in range(2):
        rows = slice(w * BLK, (w + 1) * BLK)
        pos = own_ref[s, w]
        for p in range(pairs):
            qs[p] = split_heads(q_ref[0, rows, lanes_of(p)] * jnp.bfloat16(SCALE))
        run[...] = jnp.full_like(run, NEG)
        acc[...] = jnp.zeros_like(acc)

        def score(c, masked):
            for p in range(pairs):
                sc = nt(qs[p], ks[p, span(c), :])
                if masked:
                    sc = jnp.where(may_see(pos, c), sc, NEG)
                scr[p, :, span(c)] = sc
                top = run[p]
                for t in range(CB):
                    top = jnp.maximum(top, sc[:, t * 128:(t + 1) * 128])
                run[p] = top

        sweep(pos // CB, score)
        for p in range(pairs):
            run[p] = jnp.broadcast_to(jnp.max(run[p], axis=1, keepdims=True), (2 * BLK, 128))

        def weigh(c, masked):
            for p in range(pairs):
                weight = jnp.exp(scr[p, :, span(c)] - jnp.concatenate([run[p]] * CB, axis=1)).astype(jnp.bfloat16)
                acc[p] += nn(weight, vs[p, span(c), :])

        sweep(pos // CB, weigh)
        lane = lane_of((2 * BLK, 128))
        ext = jnp.zeros((BLK, 128), jnp.float32)
        for p in range(pairs):
            total = acc[p, :, 128:256]
            o_ref[0, rows, lanes_of(p)] = join_heads(acc[p, :, 0:128] / total).astype(jnp.bfloat16)
            mine = jnp.where(own_lanes(p), terms(-(run[p] + jnp.log(total)), lane), 0.0)
            ext = ext + mine[:BLK] + mine[BLK:]
        ext_ref[0, rows, :] = ext.astype(jnp.bfloat16)


def dq_kernel(place_ref, own_ref, q_ref, do_ref, qx_ref, dox_ref, c_ref, a_ref, b_ref, *refs, pairs, n):
    k_refs, v_refs, (dq_ref, ks, vs, qs, dos, acc) = refs[:n], refs[n:2 * n], refs[2 * n:]
    s = pl.program_id(0)

    @pl.when(s == 0)
    def _():
        for ref in (ks, vs):
            for p in range(pairs):
                ref[p, :, 128:256] = jnp.ones((ref.shape[1], 128), jnp.bfloat16)

    place_rows(place_ref, s, k_refs, ks)
    place_rows(place_ref, s, v_refs, vs)

    for w in range(2):
        rows = slice(w * BLK, (w + 1) * BLK)
        pos = own_ref[s, w]

        def extend(tile, ext, p):
            both = jnp.concatenate([ext, ext], axis=0)
            return jnp.concatenate([split_heads(tile), jnp.where(own_lanes(p), both, jnp.zeros_like(both))], axis=1)

        for p in range(pairs):
            qs[p] = extend(q_ref[0, rows, lanes_of(p)] * jnp.bfloat16(SCALE), qx_ref[0, rows, :], p)
            dos[p] = extend(do_ref[0, rows, lanes_of(p)], dox_ref[0, rows, :], p)
        acc[...] = jnp.zeros_like(acc)

        def step(c, masked):
            for p in range(pairs):
                prob = jnp.exp(nt(qs[p], ks[p, span(c), :]))
                if masked:
                    prob = jnp.where(may_see(pos, c), prob, 0.0)
                ds = (prob * nt(dos[p], vs[p, span(c), :])).astype(jnp.bfloat16)
                acc[p] += nn(ds, ks[p, span(c), 0:128])

        sweep(pos // CB, step)
        for p in range(pairs):
            grad = join_heads(acc[p]) * SCALE
            dq_ref[0, rows, lanes_of(p)] = turn(grad, c_ref[rows], a_ref[rows], b_ref[rows], -1.0).astype(jnp.bfloat16)


def dkv_kernel(place_ref, own_ref, kv_ref, c_ref, a_ref, b_ref, *refs, pairs, n, lead):
    q_refs, do_refs, (dk_ref, dv_ref, qs, dos, kw, vw, acck, accv) = refs[:n], refs[n:2 * n], refs[2 * n:]
    s = pl.program_id(0) + lead
    place_rows(place_ref, s, q_refs, qs, True)
    place_rows(place_ref, s, do_refs, dos, True)
    chunks = qs.shape[1] // CH

    for w in range(2):
        rows = slice(w * BLK, (w + 1) * BLK)
        pos = own_ref[s, w]
        first = pos // CB
        for p in range(pairs):
            ones = own_lanes(p).astype(jnp.bfloat16)
            kw[p] = jnp.concatenate([split_heads(kv_ref[0, 0, rows, lanes_of(p)] * jnp.bfloat16(SCALE)), ones], axis=1)
            vw[p] = jnp.concatenate([split_heads(kv_ref[1, 0, rows, lanes_of(p)]), ones], axis=1)
        acck[...] = jnp.zeros_like(acck)
        accv[...] = jnp.zeros_like(accv)

        def step(c, masked):
            for p in range(pairs):
                prob = jnp.exp(nt(kw[p], qs[p, span(c), :]))
                if masked:
                    shape = (2 * BLK, CH)
                    prob = jnp.where(pos * BLK + row_of(shape) % BLK <= c * CH + lane_of(shape), prob, 0.0)
                accv[p] += nn(prob.astype(jnp.bfloat16), dos[p, span(c), 0:128])
                ds = (prob * nt(vw[p], dos[p, span(c), :])).astype(jnp.bfloat16)
                acck[p] += nn(ds, qs[p, span(c), 0:128])

        def one(c, carry):
            step(c, False)
            return carry

        step(first, True)
        lax.fori_loop(first + 1, chunks, one, 0)
        for p in range(pairs):
            grad = join_heads(acck[p]) * SCALE
            dk_ref[0, rows, lanes_of(p)] = turn(grad, c_ref[rows], a_ref[rows], b_ref[rows], -1.0).astype(jnp.bfloat16)
            dv_ref[0, rows, lanes_of(p)] = join_heads(accv[p]).astype(jnp.bfloat16)


def own(width):
    return pl.BlockSpec((1, 2 * BLK, width), lambda s, *_: (s, 0, 0))


def table(lead=0):
    return pl.BlockSpec((2 * BLK, 128), lambda s, *_: (s + lead, 0))


def piece(x, first=0, lead=0):
    return pl.BlockSpec((1, 1, 2, BLK, x.shape[4]), lambda s, *_: (first, s + lead, 0, 0, 0))


def attention_call(kernel, name, mats, seqs, pairs, blocks, in_specs, out_specs, out_shape, scratch, args):
    work = seqs * pairs * 2 * 2 * BLK * blocks * BLK // 2
    return pl.pallas_call(
        kernel,
        grid_spec=pltpu.PrefetchScalarGridSpec(
            num_scalar_prefetch=2, grid=(seqs,), in_specs=in_specs, out_specs=out_specs, scratch_shapes=scratch),
        out_shape=out_shape,
        compiler_params=pltpu.CompilerParams(vmem_limit_bytes=60 * 2**20),
        cost_estimate=pl.CostEstimate(flops=work * 64 * mats, bytes_accessed=seqs * pairs * blocks * BLK * 128, transcendentals=0),
        name=name,
    )(*args)


def rows_of(pairs, blocks, lanes):
    return pltpu.VMEM((pairs, blocks * BLK, lanes), jnp.bfloat16)


def acc_of(pairs, lanes, dtype=jnp.float32):
    return pltpu.VMEM((pairs, 2 * BLK, lanes), dtype)


def attend(place, own_blocks, q, keys, values):
    seqs, width, blocks = q.shape[0], q.shape[2], place.shape[1]
    pairs = width // 128
    return attention_call(
        functools.partial(fwd_kernel, pairs=pairs, n=len(keys)), "attend", 2, seqs, pairs, blocks,
        [own(width)] + [piece(*e) for e in keys + values], [own(width), own(128)],
        [jax.ShapeDtypeStruct(q.shape, jnp.bfloat16), jax.ShapeDtypeStruct(q.shape[:2] + (128,), jnp.bfloat16)],
        [rows_of(pairs, blocks, 128), rows_of(pairs, blocks, 256), acc_of(pairs, 128, jnp.bfloat16), acc_of(pairs, blocks * BLK),
         acc_of(pairs, 128), acc_of(pairs, 256)],
        [place, own_blocks, q] + [e[0] for e in keys + values])


def query_grad(place, own_blocks, q, do, q_ext, do_ext, tabs, keys, values):
    seqs, width, blocks = q.shape[0], q.shape[2], place.shape[1]
    pairs = width // 128
    return attention_call(
        functools.partial(dq_kernel, pairs=pairs, n=len(keys)), "query_grad", 3, seqs, pairs, blocks,
        [own(width), own(width), own(128), own(128)] + [table()] * 3 + [piece(*e) for e in keys + values], own(width),
        jax.ShapeDtypeStruct(q.shape, jnp.bfloat16),
        [rows_of(pairs, blocks, 256), rows_of(pairs, blocks, 256), acc_of(pairs, 256, jnp.bfloat16), acc_of(pairs, 256, jnp.bfloat16),
         acc_of(pairs, 128)],
        [place, own_blocks, q, do, q_ext, do_ext, *tabs] + [e[0] for e in keys + values])


def key_value_grad(place, own_blocks, kv, tabs, queries, grads, lead, count):
    width, blocks = kv.shape[3], place.shape[1]
    pairs = width // 128
    shape = (count,) + kv.shape[2:]
    return attention_call(
        functools.partial(dkv_kernel, pairs=pairs, n=len(queries), lead=lead), "key_value_grad", 4, count, pairs, blocks,
        [pl.BlockSpec((2, 1, 2 * BLK, width), lambda s, *_: (0, s + lead, 0, 0))] + [table(lead)] * 3
        + [piece(x, lead=lead) for x in queries + grads], [own(width)] * 2,
        [jax.ShapeDtypeStruct(shape, jnp.bfloat16)] * 2,
        [rows_of(pairs, blocks, 256), rows_of(pairs, blocks, 256), acc_of(pairs, 256, jnp.bfloat16), acc_of(pairs, 256, jnp.bfloat16),
         acc_of(pairs, 128), acc_of(pairs, 128)],
        [place, own_blocks, kv, *tabs] + queries + grads)


import math
from jax.sharding import PartitionSpec as P

HEAD_DIM = 64
ROT = 16
SEQS = 4
EPS = 1e-05
F32 = jnp.float32
BF16 = jnp.bfloat16


def rc(left, right):
    return lax.dot_general(left, right, (((0,), (0,)), ((), ())), preferred_element_type=F32)


def layer_stats(values, gain, shift):
    mean = jnp.mean(values, axis=-1, keepdims=True)
    centred = values - mean
    inverse = lax.rsqrt(jnp.mean(centred * centred, axis=-1, keepdims=True) + EPS)
    unit = centred * inverse
    return unit * gain + shift, unit, inverse


def layer_back(grad, unit, inverse, gain):
    scaled = grad * gain
    grad_in = inverse * (
        scaled
        - jnp.mean(scaled, axis=-1, keepdims=True)
        - unit * jnp.mean(scaled * unit, axis=-1, keepdims=True)
    )
    return grad_in, jnp.sum(grad * unit, axis=0), jnp.sum(grad, axis=0)


def rotary_tables(positions):
    half = ROT // 2
    dim = jnp.arange(2 * HEAD_DIM) % HEAD_DIM
    freq = jnp.where(dim < ROT, 10000.0 ** (-2.0 * (dim % half).astype(F32) / ROT), 0.0)
    angles = positions.astype(F32)[:, None] * freq[None, :]
    sin = jnp.sin(angles)
    return jnp.cos(angles), jnp.where(dim < half, sin, 0.0), jnp.where(dim < half, 0.0, sin)


def turn(x, ctab, above, below, sign):
    up = pltpu.roll(x, 128 - ROT // 2, axis=1)
    down = pltpu.roll(x, ROT // 2, axis=1)
    return x * ctab + sign * (down * below - up * above)


def project_kernel(h_ref, wq_ref, wk_ref, wv_ref, bias_ref, c_ref, a_ref, b_ref, q_ref, kv_ref):
    h = h_ref[...]
    width = wq_ref.shape[1]
    tabs = c_ref[...], a_ref[...], b_ref[...]
    for at, (w_ref, out) in enumerate(((wq_ref, q_ref.at[0]), (wk_ref, kv_ref.at[0, 0]), (wv_ref, kv_ref.at[1, 0]))):
        lin = nn(h, w_ref[...]) + bias_ref[at:at + 1, :]
        for p in range(width // 128):
            part = lin[:, p * 128:(p + 1) * 128]
            if at < 2:
                part = turn(part, *tabs, 1.0)
            out[:, p * 128:(p + 1) * 128] = part.astype(BF16)


def project(rows, wq, wk, wv, bias, tabs):
    total, depth = rows.shape
    width = wq.shape[1]
    step = total // SEQS
    weight = pl.BlockSpec((depth, width), lambda i: (0, 0))
    table = pl.BlockSpec((step, 128), lambda i: (i, 0))
    return pl.pallas_call(
        project_kernel,
        grid=(SEQS,),
        in_specs=[pl.BlockSpec((step, depth), lambda i: (i, 0)), weight, weight, weight,
                  pl.BlockSpec((3, width), lambda i: (0, 0)), table, table, table],
        out_specs=[pl.BlockSpec((1, step, width), lambda i: (i, 0, 0)),
                   pl.BlockSpec((2, 1, step, width), lambda i: (0, i, 0, 0))],
        out_shape=[jax.ShapeDtypeStruct((SEQS, step, width), BF16), jax.ShapeDtypeStruct((2, SEQS, step, width), BF16)],
        compiler_params=pltpu.CompilerParams(vmem_limit_bytes=48 * 2**20),
        cost_estimate=pl.CostEstimate(flops=6 * total * depth * width, bytes_accessed=6 * depth * width, transcendentals=0),
        name="project",
    )(rows, wq, wk, wv, bias, *tabs)


def mlp_kernel(h_ref, dy_ref, gate_ref, up_ref, down_ref, act_ref, *grad_refs):
    width = gate_ref.shape[1]
    gate = nn(h_ref[...], gate_ref[...])
    up = nn(h_ref[...], up_ref[...])
    grad = nt(dy_ref[...], down_ref[...])
    sig = 1.0 / (1.0 + jnp.exp(-gate))
    silu = gate * sig
    act_ref[...] = (silu * up).astype(BF16)
    outs = grad_refs if len(grad_refs) == 2 else (grad_refs[0].at[:, :width], grad_refs[0].at[:, width:])
    outs[0][...] = (grad * up * (sig + silu * (1.0 - sig))).astype(BF16)
    outs[1][...] = (grad * silu).astype(BF16)


def mlp(rows, dy, gate_w, up_w, down_w, step=256):
    total, depth = rows.shape
    width = gate_w.shape[1]
    joined = width % 128 == 0
    block = pl.BlockSpec((step, depth), lambda i: (i, 0))

    def whole(x):
        return pl.BlockSpec(x.shape, lambda i: (0, 0), pipeline_mode=pl.Buffered(1))

    def out(n):
        return pl.BlockSpec((step, n), lambda i: (i, 0)), jax.ShapeDtypeStruct((total, n), BF16)

    outs = [out(width), out(2 * width)] if joined else [out(width)] * 3
    act, *grads = pl.pallas_call(
        mlp_kernel,
        grid=(total // step,),
        in_specs=[block, block, whole(gate_w), whole(up_w), whole(down_w)],
        out_specs=[o[0] for o in outs],
        out_shape=[o[1] for o in outs],
        compiler_params=pltpu.CompilerParams(vmem_limit_bytes=56 * 2**20),
        cost_estimate=pl.CostEstimate(flops=6 * total * depth * width, bytes_accessed=6 * depth * width + 10 * total * depth,
                                      transcendentals=total * width),
        name="mlp",
    )(rows, dy, gate_w, up_w, down_w)
    return act, grads[0] if joined else jnp.concatenate(grads, axis=1)


def ctx_swap(x, mask):
    n = lax.axis_size("ctx")
    return lax.ppermute(x, "ctx", [(i, i ^ mask) for i in range(n)])


def add16(a, b):
    return (a.astype(F32) + b.astype(F32)).astype(BF16)


def after(x, *deps):
    if not jax.tree.leaves(deps):
        return x
    return lax.optimization_barrier((x, deps))[0]


def half_of(x, bit, mine):
    side = (lax.axis_index("ctx") >> bit) & 1
    r = x.shape[0] // 2
    return lax.dynamic_slice_in_dim(x, (side if mine else 1 - side) * r, r, 0)


def assemble_kernel(source_ref, *refs):
    *in_refs, out_ref = refs
    for k, ref in enumerate(in_refs):

        @pl.when(source_ref[pl.program_id(0)] == k)
        def _(ref=ref):
            out_ref[...] = ref[...]


def assemble(pieces, source):
    r, c = pieces[0].shape
    count = len(pieces)
    return pl.pallas_call(
        assemble_kernel,
        grid_spec=pltpu.PrefetchScalarGridSpec(
            num_scalar_prefetch=1, grid=(count,),
            in_specs=[pl.BlockSpec((r, c), lambda j, _: (0, 0), pipeline_mode=pl.Buffered(1))] * count,
            out_specs=pl.BlockSpec((r, c), lambda j, _: (j, 0))),
        out_shape=jax.ShapeDtypeStruct((count * r, c), BF16),
        compiler_params=pltpu.CompilerParams(vmem_limit_bytes=40 * 2**20),
        cost_estimate=pl.CostEstimate(flops=0, bytes_accessed=1024, transcendentals=0),
        name="assemble",
    )(source, *pieces)


def weight_grad(part, flying):
    core = lax.axis_index("ctx") & 1
    got = ctx_swap(part(1 - core).astype(BF16), 1)
    flying[:] = [got]
    gate = yield
    half = (part(core) + after(got, gate).astype(F32)).astype(BF16)
    bits = list(range(1, int(math.log2(lax.axis_size("ctx")))))
    orders = [bits, bits[::-1]]
    r = half.shape[0] // 2
    streams = [half[:r], half[r:]]
    gate = yield streams
    for i in range(len(bits)):
        streams = after(streams, gate)
        got = [ctx_swap(half_of(x, o[i], False), 1 << o[i]) for x, o in zip(streams, orders)]
        flying[:] = got
        gate = yield
        streams, got = after((streams, got), gate)
        streams = [add16(half_of(x, o[i], True), g) for x, o, g in zip(streams, orders, got)]
        gate = yield streams
    for i in reversed(range(len(bits))):
        streams = after(streams, gate)
        got = [ctx_swap(x, 1 << o[i]) for x, o in zip(streams, orders)]
        flying[:] = got
        gate = yield
        streams, got = after((streams, got), gate)
        sides = [(lax.axis_index("ctx") >> o[i]) & 1 for o in orders]
        if i == 0:
            source = jnp.stack([sides[0], 1 - sides[0], 2 + sides[1], 3 - sides[1]])
            streams = assemble([streams[0], got[0], streams[1], got[1]], source)
        else:
            streams = [
                jnp.where(side == 0, jnp.concatenate([x, g]), jnp.concatenate([g, x]))
                for x, side, g in zip(streams, sides, got)
            ]
        gate = yield streams
    streams = after(streams, gate)
    other = ctx_swap(streams, 1)
    gate = yield
    yield after((streams, other), gate)


def begin(part, flying=None):
    chain = weight_grad(part, [] if flying is None else flying)
    next(chain)
    return chain


def take(chain, gate=None):
    return chain.send(gate)


def go(chain, gate=None):
    chain.send(gate)


def take_extra(chain):
    for _ in range(2 * int(math.log2(lax.axis_size("ctx"))) - 6):
        go(chain)
        take(chain)


def unpack_rows_kernel(core_ref, half_ref, other_ref, *out_refs, turned):
    def put(src):
        at = 0
        for i, out in enumerate(out_refs):
            if turned and i == len(out_refs) - 1:
                out[...] = src[:, at:].astype(F32).T
            else:
                out[...] = src[:, at:at + out.shape[1]].astype(F32)
                at += out.shape[1]

    @pl.when(pl.program_id(0) == core_ref[0])
    def _():
        put(half_ref)

    @pl.when(pl.program_id(0) != core_ref[0])
    def _():
        put(other_ref)


def unpack_rows(half, other, parts, turned=False):
    r, c = half.shape
    step = math.gcd(r, 256)
    blocks = r // step
    w = c // parts
    core = lax.axis_index("ctx") & 1

    def mine(i, j, core_ref):
        return jnp.where(i == core_ref[0], j, jnp.where(core_ref[0] == 0, blocks - 1, 0)), 0

    def theirs(i, j, core_ref):
        return jnp.where(i != core_ref[0], j, jnp.where(core_ref[0] == 1, blocks - 1, 0)), 0

    specs = [pl.BlockSpec((step, w), lambda i, j, _: (i * blocks + j, 0))] * parts
    shapes = [jax.ShapeDtypeStruct((2 * r, w), F32)] * parts
    if turned:
        specs[-1] = pl.BlockSpec((w, step), lambda i, j, _: (0, i * blocks + j))
        shapes[-1] = jax.ShapeDtypeStruct((w, 2 * r), F32)
    return pl.pallas_call(
        functools.partial(unpack_rows_kernel, turned=turned),
        grid_spec=pltpu.PrefetchScalarGridSpec(
            num_scalar_prefetch=1, grid=(2, blocks),
            in_specs=[pl.BlockSpec((step, c), mine), pl.BlockSpec((step, c), theirs)], out_specs=specs),
        out_shape=shapes,
        compiler_params=pltpu.CompilerParams(vmem_limit_bytes=40 * 2**20),
        cost_estimate=pl.CostEstimate(flops=0, bytes_accessed=1024, transcendentals=0),
        name="unpack_rows",
    )(core[None], half, other)


def columns(x, which):
    w = x.shape[1] // 2
    return lax.dynamic_slice_in_dim(x, which * w, w, 1)


def unpack_cols_kernel(core_ref, half_ref, other_ref, out_ref):
    c = half_ref.shape[1]
    core = core_ref[0]
    out_ref[:, pl.ds(pl.multiple_of(core * c, 128), c)] = half_ref[...].astype(F32)
    out_ref[:, pl.ds(pl.multiple_of((1 - core) * c, 128), c)] = other_ref[...].astype(F32)


def unpack_cols(half, other):
    r, c = half.shape
    step = math.gcd(r, 256)
    block = pl.BlockSpec((step, c), lambda i, _: (i, 0))
    return pl.pallas_call(
        unpack_cols_kernel,
        grid_spec=pltpu.PrefetchScalarGridSpec(
            num_scalar_prefetch=1, grid=(r // step,), in_specs=[block, block],
            out_specs=pl.BlockSpec((step, 2 * c), lambda i, _: (i, 0))),
        out_shape=jax.ShapeDtypeStruct((r, 2 * c), F32),
        compiler_params=pltpu.CompilerParams(vmem_limit_bytes=40 * 2**20),
        cost_estimate=pl.CostEstimate(flops=0, bytes_accessed=1024, transcendentals=0),
        name="unpack_cols",
    )((lax.axis_index("ctx") & 1)[None], half, other)


def all_rows(x):
    return lax.all_gather(x, "tp", axis=0, tiled=True)


def tp_shift(x, d):
    n = lax.axis_size("tp")
    return lax.ppermute(x, "tp", [(i, (i + d) % n) for i in range(n)])


def part_of(x, d, axis):
    n = lax.axis_size("tp")
    w = x.shape[axis] // n
    return lax.dynamic_slice_in_dim(x, (lax.axis_index("tp") + d) % n * w, w, axis)


def exchange(x, split, join):
    n, me = lax.axis_size("tp"), lax.axis_index("tp")
    w = x.shape[join]
    shape = list(x.shape)
    shape[split] //= n
    shape[join] *= n
    out = jnp.zeros(shape, x.dtype)
    for d in range(n):
        got = tp_shift(part_of(x, d, split), d) if d else part_of(x, 0, split)
        out = lax.dynamic_update_slice_in_dim(out, got, (me + n - d) % n * w, join)
    return out


def sum_rows(x):
    return lax.psum_scatter(x, "tp", scatter_dimension=0, tiled=True)


def gather_pair(kv):
    n = lax.axis_size("ctx")
    held = {0: ((kv, 0), (kv, 1))}
    for bit in range(1, int(math.log2(n))):
        mask = 1 << bit
        for j in list(held):
            if j == 0:
                got = ctx_swap(kv, mask)
                held[mask] = (got, 0), (got, 1)
            elif mask == 4 and j == 2:
                held[6] = (ctx_swap(held[2][0][0][0:1], 4), 0), (ctx_swap(held[4][1][0][1:2], 2), 0)
            else:
                (k, i), (v, t) = held[j]
                if k is v:
                    got = ctx_swap(k, mask)
                    held[j | mask] = (got, i), (got, t)
                else:
                    held[j | mask] = (ctx_swap(k, mask), i), (ctx_swap(v, mask), t)
    for j in list(held):
        (k, i), (v, t) = held[j]
        got = ctx_swap(k, 1)
        held[j | 1] = (got, i), (got if k is v else ctx_swap(v, 1), t)
    return [held[j][0] for j in range(n)], [held[j][1] for j in range(n)]


def gather_other(x):
    held = {0: x, 1: ctx_swap(x, 1)}
    for j in range(2, lax.axis_size("ctx"), 2):
        held[j] = ctx_swap(x, j)
    return held


def gather_cores(held, gate=None):
    n = lax.axis_size("ctx")
    for j in range(2, n, 2):
        held[j + 1] = ctx_swap(after(held[j], gate), 1)
    return [held[j] for j in range(n)]


def sum_over_all(x):
    steps = [(axis, bit) for axis in ("ctx", "tp") for bit in range(int(math.log2(lax.axis_size(axis))))]
    for axis, bit in sorted(steps, key=lambda step: step[0] == "ctx" and step[1] > 0):
        x = x + lax.ppermute(x, axis, [(i, i ^ (1 << bit)) for i in range(lax.axis_size(axis))])
        yield x
    while True:
        yield x


def gather_tp(x):
    n, me = lax.axis_size("tp"), lax.axis_index("tp")
    out = jnp.zeros((n,) + x.shape, x.dtype)
    for d in range(n):
        got = lax.ppermute(x, "tp", [(i, (i + d) % n) for i in range(n)]) if d else x
        out = lax.dynamic_update_index_in_dim(out, got, (me + n - d) % n, 0)
    return out


def local(tokens, cotangent, block_order, gain_one, shift_one, query_w, key_w, value_w, query_b, key_b, value_b,
          output_w, gain_two, shift_two, gate_w, up_w, down_w):
    heads = key_b.shape[0]
    width = heads * HEAD_DIM
    n_ctx, n_tp = lax.axis_size("ctx"), lax.axis_size("tp")
    ctx = lax.axis_index("ctx")
    own = lax.dynamic_slice_in_dim(block_order, 2 * ctx, 2, 1)
    picked = (jnp.arange(n_ctx, dtype=jnp.int32) ^ ctx)[:, None] == jnp.arange(n_ctx, dtype=jnp.int32)[None, :]
    by_ctx = block_order.reshape(SEQS, 1, n_ctx, 2)
    place = jnp.sum(jnp.where(picked[None, :, :, None], by_ctx, 0), axis=2).astype(jnp.int32).reshape(SEQS, 2 * n_ctx)
    positions = (own[:, :, None] * BLK + jnp.arange(BLK, dtype=jnp.int32)).reshape(-1)
    tabs = rotary_tables(positions)

    x = tokens.astype(F32)
    normed_one, unit_one, inverse_one = layer_stats(x, gain_one, shift_one)
    rows_one = all_rows(normed_one.astype(BF16))
    key_bias = jnp.concatenate([key_b, jnp.zeros((heads, HEAD_DIM - ROT), F32)], axis=1).reshape(-1)
    bias = jnp.stack([query_b, key_bias, value_b])
    q, kv = project(rows_one, query_w, key_w, value_w, bias, tabs)
    keys, values = gather_pair(kv.reshape(2, SEQS, 2, BLK, width))
    arrived = [e[0] for e in keys + values]

    rows_w = output_w.shape[0] // n_ctx
    part = lax.dynamic_slice_in_dim(output_w, ctx * rows_w, rows_w, 0)
    part = gather_tp(after(part, kv))
    dy_rows = all_rows(after(cotangent, rows_one))
    whole_w = lax.all_gather(after(part, arrived, dy_rows), "ctx", axis=1).reshape(n_tp * output_w.shape[0], -1)

    attn, q_ext = attend(place, own, q, keys, values)
    attn_rows = attn.reshape(-1, width)
    attn_own = exchange(attn_rows, 0, 1)
    mixed = x + nn(attn_own, whole_w)
    normed_two, unit_two, inverse_two = layer_stats(mixed, gain_two, shift_two)
    rows_two = all_rows(after(normed_two.astype(BF16), dy_rows, whole_w))
    shape = (1, SEQS, 2, BLK, width + 128)
    queries = gather_cores(gather_other(after(jnp.concatenate([q, q_ext], axis=2).reshape(shape), attn_own)))
    rows_two = after(rows_two, queries)

    act, grad_gu = mlp(rows_two, dy_rows, gate_w, up_w, down_w)
    ff = gate_w.shape[1]
    part_two = (nt(grad_gu[:, :ff], gate_w) + nt(grad_gu[:, ff:], up_w)).astype(BF16)
    grad_two = sum_rows(part_two)
    act, rows_two, dy_rows, grad_gu = after((act, rows_two, dy_rows, grad_gu), part_two)
    gu_fly, dw_fly = [], []
    gu = begin(lambda core: rc(columns(rows_two, core), grad_gu), gu_fly)
    dw = begin(lambda core: rc(act, columns(dy_rows, core)), dw_fly)
    held = take(gu)
    go(gu)
    down = nn(after(act, held), down_w).astype(BF16)
    held = take(dw), take(gu, down)
    go(gu)
    go(dw, held)
    grad_two = after(grad_two, held)

    norm_two, grad_gain_two, grad_shift_two = layer_back(grad_two.astype(F32), unit_two, inverse_two, gain_two)
    grad_mixed = cotangent.astype(F32) + norm_two
    branch_own = grad_mixed.astype(BF16)
    grad_attn = nt(branch_own, whole_w).astype(BF16)
    held = take(gu, grad_attn)
    go(gu)
    grad_attn = exchange(grad_attn, 1, 0)
    lane = jnp.arange(128)[None, :]
    ind = ((jnp.arange(width) // HEAD_DIM)[:, None] == lane // 3).astype(F32)
    delta = lax.dot_general(grad_attn.astype(F32) * attn_rows.astype(F32), ind, (((1,), (0,)), ((), ())),
                            precision=lax.Precision.HIGHEST, preferred_element_type=F32)
    do_ext = terms(-delta, lane).astype(BF16)
    do_sent = jnp.concatenate([grad_attn, do_ext], axis=1).reshape(shape)
    do_sent = after(do_sent, held, gu_fly)
    branch = all_rows(after(branch_own, do_sent))
    out_sum = sum_rows(after(down, do_sent))
    grads = gather_other(do_sent)
    grad_q = query_grad(place, own, q, grad_attn.reshape(q.shape), q_ext, do_ext.reshape(q_ext.shape), tabs, keys, values)
    grad_q = after(grad_q.reshape(-1, width), [grads[j] for j in grads if j > 1])
    grads = gather_cores(grads, grad_q)
    q_part = nt(grad_q, query_w)
    grads = after(grads, take(gu, grad_q))
    go(gu, grads)
    first = key_value_grad(place, own, kv, tabs, queries, grads, 0, SEQS // 2)
    grads = after(grads, take(dw, first))
    go(dw)
    second = key_value_grad(place, own, kv, tabs, queries, grads, SEQS // 2, SEQS // 2)
    second = after(second, take(dw, second))
    go(dw)
    grad_k, grad_v = (jnp.concatenate(pair).reshape(-1, width) for pair in zip(first, second))
    part_one = q_part + nt(grad_k, key_w) + nt(grad_v, value_w)
    part_sent = after(part_one.astype(BF16), branch)
    rows_one, branch, grad_q, grad_k, grad_v = after((rows_one, branch, grad_q, grad_k, grad_v), part_sent, gu_fly, dw_fly)
    grad_qkv = jnp.concatenate([grad_q, grad_k, grad_v], axis=1)
    chain = begin(lambda core: jnp.concatenate([rc(columns(rows_one, core), grad_qkv), rc(columns(branch, core), attn_rows)], axis=1))
    take(dw, part_sent)
    go(dw)
    held = take(chain, (list(dw_fly), out_sum))
    go(chain)
    grad_one = sum_rows(after(part_sent, out_sum, held))
    take(gu, held)
    take_extra(gu)
    go(gu)
    take(dw, held)
    take_extra(dw)
    go(dw)
    unit_rows = (rows_one.astype(F32) - shift_one) / gain_one
    bias_grad = jnp.sum(grad_qkv.astype(F32), axis=0)
    tp_row = (jnp.arange(n_tp) == lax.axis_index("tp"))[:, None]
    small = jnp.concatenate([
        jnp.sum(part_one * unit_rows, axis=0), jnp.sum(part_one, axis=0), grad_gain_two, grad_shift_two,
        jnp.where(tp_row, bias_grad[None, :], 0.0).reshape(-1)])
    held = take(chain)
    go(chain)
    held = take(chain)
    go(chain)
    grad_down_w = unpack_cols(*take(dw, held))
    held = take(chain, grad_down_w)
    take_extra(chain)
    go(chain)
    mixed_late, out_sum = after((mixed, out_sum), held)
    out_tokens = (mixed_late + out_sum.astype(F32)).astype(BF16)
    grad_gate_w, grad_up_w = unpack_rows(*take(gu, held), 2)
    sums = sum_over_all(after(small, held).reshape(-1, 1024))
    small = [next(sums) for _ in range(1 + int(math.log2(n_tp)))]
    take(chain, (grad_gate_w, small))
    go(chain)
    for _ in range(4):
        small = next(sums)
    depth = x.shape[1]
    small = small.reshape(-1)
    norms = small[:4 * depth].reshape(4, depth)
    bias_sum = jnp.sum(jnp.where(tp_row, small[4 * depth:].reshape(n_tp, -1), 0.0), axis=0)
    grad_query_w, grad_key_w, grad_value_w, grad_output_w = unpack_rows(*take(chain), 4, True)
    norm_one, _, _ = layer_back(grad_one.astype(F32), unit_one, inverse_one, gain_one)
    grad_tokens = (grad_mixed + norm_one).astype(BF16)
    return (
        out_tokens, grad_tokens, norms[0], norms[1], grad_query_w, grad_key_w, grad_value_w,
        bias_sum[:width], bias_sum[width:2 * width].reshape(heads, HEAD_DIM)[:, :ROT], bias_sum[2 * width:],
        grad_output_w, norms[2], norms[3], grad_gate_w, grad_up_w, grad_down_w,
    )


def solution(mesh):
    rows, cols, depth, flat = P(("ctx", "tp"), None), P(None, "tp"), P("tp", None), P("tp")
    in_specs = (rows, rows, P(), P(), P(), cols, cols, cols, flat, depth, flat, depth, P(), P(), cols, cols, depth)
    out_specs = (rows, rows, P(), P(), cols, cols, cols, flat, depth, flat, depth, P(), P(), cols, cols, depth)
    return jax.shard_map(local, mesh=mesh, in_specs=in_specs, out_specs=out_specs, check_vma=False)
```

```python
import functools
import jax, jax.numpy as jnp
from jax import lax
from jax.experimental import pallas as pl
from jax.experimental.pallas import tpu as pltpu

BLK = 128
CB = 8
CH = BLK * CB
NEG = -1e30
SCALE = 0.125


def nt(a, b):
    return lax.dot_general(a, b, (((1,), (1,)), ((), ())), preferred_element_type=jnp.float32)


def nn(a, b):
    return lax.dot_general(a, b, (((1,), (0,)), ((), ())), preferred_element_type=jnp.float32)


def lane_of(shape):
    return lax.broadcasted_iota(jnp.int32, shape, 1)


def row_of(shape):
    return lax.broadcasted_iota(jnp.int32, shape, 0)


def split_heads(x):
    low = lane_of(x.shape) < 64
    zero = jnp.zeros_like(x)
    return jnp.concatenate([jnp.where(low, x, zero), jnp.where(low, zero, x)], axis=0)


def join_heads(x):
    low = lane_of((BLK, 128)) < 64
    return jnp.where(low, x[:BLK], x[BLK:])


def own_lanes(pair):
    shape = (2 * BLK, 128)
    return lane_of(shape) // 3 == 2 * pair + row_of(shape) // BLK


def lanes_of(pair):
    return slice(pair * 128, (pair + 1) * 128)


def terms(x, lane):
    first = x.astype(jnp.bfloat16).astype(jnp.float32)
    second = (x - first).astype(jnp.bfloat16).astype(jnp.float32)
    return jnp.where(lane % 3 == 0, first, jnp.where(lane % 3 == 1, second, x - first - second))


def place_rows(place_ref, s, refs, dst_ref, ext=False):
    pairs = dst_ref.shape[0]
    at = 0
    for ref in refs:
        for j in range(ref.shape[0]):
            for w in range(2):
                rows = pl.ds(pl.multiple_of(place_ref[s, at] * BLK, BLK), BLK)
                for p in range(pairs):
                    dst_ref[p, rows, 0:128] = ref[j, 0, w, :, p * 128:(p + 1) * 128]
                    if ext:
                        dst_ref[p, rows, 128:256] = ref[j, 0, w, :, pairs * 128:]
                at += 1


def sweep(full, step):
    def one(c, carry):
        step(c, False)
        return carry

    lax.fori_loop(0, full, one, 0)
    step(full, True)


def span(c):
    return pl.ds(pl.multiple_of(c * CH, CH), CH)


def may_see(query_block, c):
    shape = (2 * BLK, CH)
    return c * CH + lane_of(shape) <= query_block * BLK + row_of(shape) % BLK


def fwd_kernel(place_ref, own_ref, q_ref, *refs, pairs, n):
    k_refs, v_refs, (o_ref, ext_ref, ks, vs, qs, scr, run, acc) = refs[:n], refs[n:2 * n], refs[2 * n:]
    s = pl.program_id(0)

    @pl.when(s == 0)
    def _():
        for p in range(pairs):
            vs[p, :, 128:256] = jnp.ones((vs.shape[1], 128), jnp.bfloat16)

    place_rows(place_ref, s, k_refs, ks)
    place_rows(place_ref, s, v_refs, vs)

    for w in range(2):
        rows = slice(w * BLK, (w + 1) * BLK)
        pos = own_ref[s, w]
        for p in range(pairs):
            qs[p] = split_heads(q_ref[0, rows, lanes_of(p)] * jnp.bfloat16(SCALE))
        run[...] = jnp.full_like(run, NEG)
        acc[...] = jnp.zeros_like(acc)

        def score(c, masked):
            for p in range(pairs):
                sc = nt(qs[p], ks[p, span(c), :])
                if masked:
                    sc = jnp.where(may_see(pos, c), sc, NEG)
                scr[p, :, span(c)] = sc
                top = run[p]
                for t in range(CB):
                    top = jnp.maximum(top, sc[:, t * 128:(t + 1) * 128])
                run[p] = top

        sweep(pos // CB, score)
        for p in range(pairs):
            run[p] = jnp.broadcast_to(jnp.max(run[p], axis=1, keepdims=True), (2 * BLK, 128))

        def weigh(c, masked):
            for p in range(pairs):
                weight = jnp.exp(scr[p, :, span(c)] - jnp.concatenate([run[p]] * CB, axis=1)).astype(jnp.bfloat16)
                acc[p] += nn(weight, vs[p, span(c), :])

        sweep(pos // CB, weigh)
        lane = lane_of((2 * BLK, 128))
        ext = jnp.zeros((BLK, 128), jnp.float32)
        for p in range(pairs):
            total = acc[p, :, 128:256]
            o_ref[0, rows, lanes_of(p)] = join_heads(acc[p, :, 0:128] / total).astype(jnp.bfloat16)
            mine = jnp.where(own_lanes(p), terms(-(run[p] + jnp.log(total)), lane), 0.0)
            ext = ext + mine[:BLK] + mine[BLK:]
        ext_ref[0, rows, :] = ext.astype(jnp.bfloat16)


def dq_kernel(place_ref, own_ref, q_ref, do_ref, qx_ref, dox_ref, c_ref, a_ref, b_ref, *refs, pairs, n):
    k_refs, v_refs, (dq_ref, ks, vs, qs, dos, acc) = refs[:n], refs[n:2 * n], refs[2 * n:]
    s = pl.program_id(0)

    @pl.when(s == 0)
    def _():
        for ref in (ks, vs):
            for p in range(pairs):
                ref[p, :, 128:256] = jnp.ones((ref.shape[1], 128), jnp.bfloat16)

    place_rows(place_ref, s, k_refs, ks)
    place_rows(place_ref, s, v_refs, vs)

    for w in range(2):
        rows = slice(w * BLK, (w + 1) * BLK)
        pos = own_ref[s, w]

        def extend(tile, ext, p):
            both = jnp.concatenate([ext, ext], axis=0)
            return jnp.concatenate([split_heads(tile), jnp.where(own_lanes(p), both, jnp.zeros_like(both))], axis=1)

        for p in range(pairs):
            qs[p] = extend(q_ref[0, rows, lanes_of(p)] * jnp.bfloat16(SCALE), qx_ref[0, rows, :], p)
            dos[p] = extend(do_ref[0, rows, lanes_of(p)], dox_ref[0, rows, :], p)
        acc[...] = jnp.zeros_like(acc)

        def step(c, masked):
            for p in range(pairs):
                prob = jnp.exp(nt(qs[p], ks[p, span(c), :]))
                if masked:
                    prob = jnp.where(may_see(pos, c), prob, 0.0)
                ds = (prob * nt(dos[p], vs[p, span(c), :])).astype(jnp.bfloat16)
                acc[p] += nn(ds, ks[p, span(c), 0:128])

        sweep(pos // CB, step)
        for p in range(pairs):
            grad = join_heads(acc[p]) * SCALE
            dq_ref[0, rows, lanes_of(p)] = turn(grad, c_ref[rows], a_ref[rows], b_ref[rows], -1.0).astype(jnp.bfloat16)


def dkv_kernel(place_ref, own_ref, kv_ref, c_ref, a_ref, b_ref, *refs, pairs, n, lead):
    q_refs, do_refs, (dk_ref, dv_ref, qs, dos, kw, vw, acck, accv) = refs[:n], refs[n:2 * n], refs[2 * n:]
    s = pl.program_id(0) + lead
    place_rows(place_ref, s, q_refs, qs, True)
    place_rows(place_ref, s, do_refs, dos, True)
    chunks = qs.shape[1] // CH

    for w in range(2):
        rows = slice(w * BLK, (w + 1) * BLK)
        pos = own_ref[s, w]
        first = pos // CB
        for p in range(pairs):
            ones = own_lanes(p).astype(jnp.bfloat16)
            kw[p] = jnp.concatenate([split_heads(kv_ref[0, 0, rows, lanes_of(p)] * jnp.bfloat16(SCALE)), ones], axis=1)
            vw[p] = jnp.concatenate([split_heads(kv_ref[1, 0, rows, lanes_of(p)]), ones], axis=1)
        acck[...] = jnp.zeros_like(acck)
        accv[...] = jnp.zeros_like(accv)

        def step(c, masked):
            for p in range(pairs):
                prob = jnp.exp(nt(kw[p], qs[p, span(c), :]))
                if masked:
                    shape = (2 * BLK, CH)
                    prob = jnp.where(pos * BLK + row_of(shape) % BLK <= c * CH + lane_of(shape), prob, 0.0)
                accv[p] += nn(prob.astype(jnp.bfloat16), dos[p, span(c), 0:128])
                ds = (prob * nt(vw[p], dos[p, span(c), :])).astype(jnp.bfloat16)
                acck[p] += nn(ds, qs[p, span(c), 0:128])

        def one(c, carry):
            step(c, False)
            return carry

        step(first, True)
        lax.fori_loop(first + 1, chunks, one, 0)
        for p in range(pairs):
            grad = join_heads(acck[p]) * SCALE
            dk_ref[0, rows, lanes_of(p)] = turn(grad, c_ref[rows], a_ref[rows], b_ref[rows], -1.0).astype(jnp.bfloat16)
            dv_ref[0, rows, lanes_of(p)] = join_heads(accv[p]).astype(jnp.bfloat16)


def own(width):
    return pl.BlockSpec((1, 2 * BLK, width), lambda s, *_: (s, 0, 0))


def table(lead=0):
    return pl.BlockSpec((2 * BLK, 128), lambda s, *_: (s + lead, 0))


def piece(x, first=0, lead=0):
    return pl.BlockSpec((1, 1, 2, BLK, x.shape[4]), lambda s, *_: (first, s + lead, 0, 0, 0))


def attention_call(kernel, name, mats, seqs, pairs, blocks, in_specs, out_specs, out_shape, scratch, args):
    work = seqs * pairs * 2 * 2 * BLK * blocks * BLK // 2
    return pl.pallas_call(
        kernel,
        grid_spec=pltpu.PrefetchScalarGridSpec(
            num_scalar_prefetch=2, grid=(seqs,), in_specs=in_specs, out_specs=out_specs, scratch_shapes=scratch),
        out_shape=out_shape,
        compiler_params=pltpu.CompilerParams(vmem_limit_bytes=60 * 2**20),
        cost_estimate=pl.CostEstimate(flops=work * 64 * mats, bytes_accessed=seqs * pairs * blocks * BLK * 128, transcendentals=0),
        name=name,
    )(*args)


def rows_of(pairs, blocks, lanes):
    return pltpu.VMEM((pairs, blocks * BLK, lanes), jnp.bfloat16)


def acc_of(pairs, lanes, dtype=jnp.float32):
    return pltpu.VMEM((pairs, 2 * BLK, lanes), dtype)


def attend(place, own_blocks, q, keys, values):
    seqs, width, blocks = q.shape[0], q.shape[2], place.shape[1]
    pairs = width // 128
    return attention_call(
        functools.partial(fwd_kernel, pairs=pairs, n=len(keys)), "attend", 2, seqs, pairs, blocks,
        [own(width)] + [piece(*e) for e in keys + values], [own(width), own(128)],
        [jax.ShapeDtypeStruct(q.shape, jnp.bfloat16), jax.ShapeDtypeStruct(q.shape[:2] + (128,), jnp.bfloat16)],
        [rows_of(pairs, blocks, 128), rows_of(pairs, blocks, 256), acc_of(pairs, 128, jnp.bfloat16), acc_of(pairs, blocks * BLK),
         acc_of(pairs, 128), acc_of(pairs, 256)],
        [place, own_blocks, q] + [e[0] for e in keys + values])


def query_grad(place, own_blocks, q, do, q_ext, do_ext, tabs, keys, values):
    seqs, width, blocks = q.shape[0], q.shape[2], place.shape[1]
    pairs = width // 128
    return attention_call(
        functools.partial(dq_kernel, pairs=pairs, n=len(keys)), "query_grad", 3, seqs, pairs, blocks,
        [own(width), own(width), own(128), own(128)] + [table()] * 3 + [piece(*e) for e in keys + values], own(width),
        jax.ShapeDtypeStruct(q.shape, jnp.bfloat16),
        [rows_of(pairs, blocks, 256), rows_of(pairs, blocks, 256), acc_of(pairs, 256, jnp.bfloat16), acc_of(pairs, 256, jnp.bfloat16),
         acc_of(pairs, 128)],
        [place, own_blocks, q, do, q_ext, do_ext, *tabs] + [e[0] for e in keys + values])


def key_value_grad(place, own_blocks, kv, tabs, queries, grads, lead, count):
    width, blocks = kv.shape[3], place.shape[1]
    pairs = width // 128
    shape = (count,) + kv.shape[2:]
    return attention_call(
        functools.partial(dkv_kernel, pairs=pairs, n=len(queries), lead=lead), "key_value_grad", 4, count, pairs, blocks,
        [pl.BlockSpec((2, 1, 2 * BLK, width), lambda s, *_: (0, s + lead, 0, 0))] + [table(lead)] * 3
        + [piece(x, lead=lead) for x in queries + grads], [own(width)] * 2,
        [jax.ShapeDtypeStruct(shape, jnp.bfloat16)] * 2,
        [rows_of(pairs, blocks, 256), rows_of(pairs, blocks, 256), acc_of(pairs, 256, jnp.bfloat16), acc_of(pairs, 256, jnp.bfloat16),
         acc_of(pairs, 128), acc_of(pairs, 128)],
        [place, own_blocks, kv, *tabs] + queries + grads)


import math
from jax.sharding import PartitionSpec as P

HEAD_DIM = 64
ROT = 16
SEQS = 4
EPS = 1e-05
F32 = jnp.float32
BF16 = jnp.bfloat16


def rc(left, right):
    return lax.dot_general(left, right, (((0,), (0,)), ((), ())), preferred_element_type=F32)


def layer_stats(values, gain, shift):
    mean = jnp.mean(values, axis=-1, keepdims=True)
    centred = values - mean
    inverse = lax.rsqrt(jnp.mean(centred * centred, axis=-1, keepdims=True) + EPS)
    unit = centred * inverse
    return unit * gain + shift, unit, inverse


def layer_back(grad, unit, inverse, gain):
    scaled = grad * gain
    grad_in = inverse * (
        scaled
        - jnp.mean(scaled, axis=-1, keepdims=True)
        - unit * jnp.mean(scaled * unit, axis=-1, keepdims=True)
    )
    return grad_in, jnp.sum(grad * unit, axis=0), jnp.sum(grad, axis=0)


def rotary_tables(positions):
    half = ROT // 2
    dim = jnp.arange(2 * HEAD_DIM) % HEAD_DIM
    freq = jnp.where(dim < ROT, 10000.0 ** (-2.0 * (dim % half).astype(F32) / ROT), 0.0)
    angles = positions.astype(F32)[:, None] * freq[None, :]
    sin = jnp.sin(angles)
    return jnp.cos(angles), jnp.where(dim < half, sin, 0.0), jnp.where(dim < half, 0.0, sin)


def turn(x, ctab, above, below, sign):
    up = pltpu.roll(x, 128 - ROT // 2, axis=1)
    down = pltpu.roll(x, ROT // 2, axis=1)
    return x * ctab + sign * (down * below - up * above)


def project_kernel(h_ref, wq_ref, wk_ref, wv_ref, bias_ref, c_ref, a_ref, b_ref, q_ref, kv_ref):
    h = h_ref[...]
    width = wq_ref.shape[1]
    tabs = c_ref[...], a_ref[...], b_ref[...]
    for at, (w_ref, out) in enumerate(((wq_ref, q_ref.at[0]), (wk_ref, kv_ref.at[0, 0]), (wv_ref, kv_ref.at[1, 0]))):
        lin = nn(h, w_ref[...]) + bias_ref[at:at + 1, :]
        for p in range(width // 128):
            part = lin[:, p * 128:(p + 1) * 128]
            if at < 2:
                part = turn(part, *tabs, 1.0)
            out[:, p * 128:(p + 1) * 128] = part.astype(BF16)


def project(rows, wq, wk, wv, bias, tabs):
    total, depth = rows.shape
    width = wq.shape[1]
    step = total // SEQS
    weight = pl.BlockSpec((depth, width), lambda i: (0, 0))
    table = pl.BlockSpec((step, 128), lambda i: (i, 0))
    return pl.pallas_call(
        project_kernel,
        grid=(SEQS,),
        in_specs=[pl.BlockSpec((step, depth), lambda i: (i, 0)), weight, weight, weight,
                  pl.BlockSpec((3, width), lambda i: (0, 0)), table, table, table],
        out_specs=[pl.BlockSpec((1, step, width), lambda i: (i, 0, 0)),
                   pl.BlockSpec((2, 1, step, width), lambda i: (0, i, 0, 0))],
        out_shape=[jax.ShapeDtypeStruct((SEQS, step, width), BF16), jax.ShapeDtypeStruct((2, SEQS, step, width), BF16)],
        compiler_params=pltpu.CompilerParams(vmem_limit_bytes=48 * 2**20),
        cost_estimate=pl.CostEstimate(flops=6 * total * depth * width, bytes_accessed=6 * depth * width, transcendentals=0),
        name="project",
    )(rows, wq, wk, wv, bias, *tabs)


def mlp_kernel(h_ref, dy_ref, gate_ref, up_ref, down_ref, act_ref, *grad_refs):
    width = gate_ref.shape[1]
    gate = nn(h_ref[...], gate_ref[...])
    up = nn(h_ref[...], up_ref[...])
    grad = nt(dy_ref[...], down_ref[...])
    sig = 1.0 / (1.0 + jnp.exp(-gate))
    silu = gate * sig
    act_ref[...] = (silu * up).astype(BF16)
    outs = grad_refs if len(grad_refs) == 2 else (grad_refs[0].at[:, :width], grad_refs[0].at[:, width:])
    outs[0][...] = (grad * up * (sig + silu * (1.0 - sig))).astype(BF16)
    outs[1][...] = (grad * silu).astype(BF16)


def mlp(rows, dy, gate_w, up_w, down_w, step=256):
    total, depth = rows.shape
    width = gate_w.shape[1]
    joined = width % 128 == 0
    block = pl.BlockSpec((step, depth), lambda i: (i, 0))

    def whole(x):
        return pl.BlockSpec(x.shape, lambda i: (0, 0), pipeline_mode=pl.Buffered(1))

    def out(n):
        return pl.BlockSpec((step, n), lambda i: (i, 0)), jax.ShapeDtypeStruct((total, n), BF16)

    outs = [out(width), out(2 * width)] if joined else [out(width)] * 3
    act, *grads = pl.pallas_call(
        mlp_kernel,
        grid=(total // step,),
        in_specs=[block, block, whole(gate_w), whole(up_w), whole(down_w)],
        out_specs=[o[0] for o in outs],
        out_shape=[o[1] for o in outs],
        compiler_params=pltpu.CompilerParams(vmem_limit_bytes=56 * 2**20),
        cost_estimate=pl.CostEstimate(flops=6 * total * depth * width, bytes_accessed=6 * depth * width + 10 * total * depth,
                                      transcendentals=total * width),
        name="mlp",
    )(rows, dy, gate_w, up_w, down_w)
    return act, grads[0] if joined else jnp.concatenate(grads, axis=1)


def ctx_swap(x, mask):
    n = lax.axis_size("ctx")
    return lax.ppermute(x, "ctx", [(i, i ^ mask) for i in range(n)])


def add16(a, b):
    return (a.astype(F32) + b.astype(F32)).astype(BF16)


def after(x, *deps):
    if not jax.tree.leaves(deps):
        return x
    return lax.optimization_barrier((x, deps))[0]


def half_of(x, bit, mine):
    side = (lax.axis_index("ctx") >> bit) & 1
    r = x.shape[0] // 2
    return lax.dynamic_slice_in_dim(x, (side if mine else 1 - side) * r, r, 0)


def assemble_kernel(source_ref, *refs):
    *in_refs, out_ref = refs
    for k, ref in enumerate(in_refs):

        @pl.when(source_ref[pl.program_id(0)] == k)
        def _(ref=ref):
            out_ref[...] = ref[...]


def assemble(pieces, source):
    r, c = pieces[0].shape
    count = len(pieces)
    return pl.pallas_call(
        assemble_kernel,
        grid_spec=pltpu.PrefetchScalarGridSpec(
            num_scalar_prefetch=1, grid=(count,),
            in_specs=[pl.BlockSpec((r, c), lambda j, _: (0, 0), pipeline_mode=pl.Buffered(1))] * count,
            out_specs=pl.BlockSpec((r, c), lambda j, _: (j, 0))),
        out_shape=jax.ShapeDtypeStruct((count * r, c), BF16),
        compiler_params=pltpu.CompilerParams(vmem_limit_bytes=40 * 2**20),
        cost_estimate=pl.CostEstimate(flops=0, bytes_accessed=1024, transcendentals=0),
        name="assemble",
    )(source, *pieces)


def weight_grad(part, flying):
    core = lax.axis_index("ctx") & 1
    got = ctx_swap(part(1 - core).astype(BF16), 1)
    flying[:] = [got]
    gate = yield
    half = (part(core) + after(got, gate).astype(F32)).astype(BF16)
    bits = list(range(1, int(math.log2(lax.axis_size("ctx")))))
    orders = [bits, bits[::-1]]
    r = half.shape[0] // 2
    streams = [half[:r], half[r:]]
    gate = yield streams
    for i in range(len(bits)):
        streams = after(streams, gate)
        got = [ctx_swap(half_of(x, o[i], False), 1 << o[i]) for x, o in zip(streams, orders)]
        flying[:] = got
        gate = yield
        streams, got = after((streams, got), gate)
        streams = [add16(half_of(x, o[i], True), g) for x, o, g in zip(streams, orders, got)]
        gate = yield streams
    for i in reversed(range(len(bits))):
        streams = after(streams, gate)
        got = [ctx_swap(x, 1 << o[i]) for x, o in zip(streams, orders)]
        flying[:] = got
        gate = yield
        streams, got = after((streams, got), gate)
        sides = [(lax.axis_index("ctx") >> o[i]) & 1 for o in orders]
        if i == 0:
            source = jnp.stack([sides[0], 1 - sides[0], 2 + sides[1], 3 - sides[1]])
            streams = assemble([streams[0], got[0], streams[1], got[1]], source)
        else:
            streams = [
                jnp.where(side == 0, jnp.concatenate([x, g]), jnp.concatenate([g, x]))
                for x, side, g in zip(streams, sides, got)
            ]
        gate = yield streams
    streams = after(streams, gate)
    other = ctx_swap(streams, 1)
    gate = yield
    yield after((streams, other), gate)


def begin(part, flying=None):
    chain = weight_grad(part, [] if flying is None else flying)
    next(chain)
    return chain


def take(chain, gate=None):
    return chain.send(gate)


def go(chain, gate=None):
    chain.send(gate)


def take_extra(chain):
    for _ in range(2 * int(math.log2(lax.axis_size("ctx"))) - 6):
        go(chain)
        take(chain)


def unpack_rows_kernel(core_ref, half_ref, other_ref, *out_refs, turned):
    def put(src):
        at = 0
        for i, out in enumerate(out_refs):
            if turned and i == len(out_refs) - 1:
                out[...] = src[:, at:].astype(F32).T
            else:
                out[...] = src[:, at:at + out.shape[1]].astype(F32)
                at += out.shape[1]

    @pl.when(pl.program_id(0) == core_ref[0])
    def _():
        put(half_ref)

    @pl.when(pl.program_id(0) != core_ref[0])
    def _():
        put(other_ref)


def unpack_rows(half, other, parts, turned=False):
    r, c = half.shape
    step = math.gcd(r, 256)
    blocks = r // step
    w = c // parts
    core = lax.axis_index("ctx") & 1

    def mine(i, j, core_ref):
        return jnp.where(i == core_ref[0], j, jnp.where(core_ref[0] == 0, blocks - 1, 0)), 0

    def theirs(i, j, core_ref):
        return jnp.where(i != core_ref[0], j, jnp.where(core_ref[0] == 1, blocks - 1, 0)), 0

    specs = [pl.BlockSpec((step, w), lambda i, j, _: (i * blocks + j, 0))] * parts
    shapes = [jax.ShapeDtypeStruct((2 * r, w), F32)] * parts
    if turned:
        specs[-1] = pl.BlockSpec((w, step), lambda i, j, _: (0, i * blocks + j))
        shapes[-1] = jax.ShapeDtypeStruct((w, 2 * r), F32)
    return pl.pallas_call(
        functools.partial(unpack_rows_kernel, turned=turned),
        grid_spec=pltpu.PrefetchScalarGridSpec(
            num_scalar_prefetch=1, grid=(2, blocks),
            in_specs=[pl.BlockSpec((step, c), mine), pl.BlockSpec((step, c), theirs)], out_specs=specs),
        out_shape=shapes,
        compiler_params=pltpu.CompilerParams(vmem_limit_bytes=40 * 2**20),
        cost_estimate=pl.CostEstimate(flops=0, bytes_accessed=1024, transcendentals=0),
        name="unpack_rows",
    )(core[None], half, other)


def columns(x, which):
    w = x.shape[1] // 2
    return lax.dynamic_slice_in_dim(x, which * w, w, 1)


def unpack_cols_kernel(core_ref, half_ref, other_ref, out_ref):
    c = half_ref.shape[1]
    core = core_ref[0]
    out_ref[:, pl.ds(pl.multiple_of(core * c, 128), c)] = half_ref[...].astype(F32)
    out_ref[:, pl.ds(pl.multiple_of((1 - core) * c, 128), c)] = other_ref[...].astype(F32)


def unpack_cols(half, other):
    r, c = half.shape
    step = math.gcd(r, 256)
    block = pl.BlockSpec((step, c), lambda i, _: (i, 0))
    return pl.pallas_call(
        unpack_cols_kernel,
        grid_spec=pltpu.PrefetchScalarGridSpec(
            num_scalar_prefetch=1, grid=(r // step,), in_specs=[block, block],
            out_specs=pl.BlockSpec((step, 2 * c), lambda i, _: (i, 0))),
        out_shape=jax.ShapeDtypeStruct((r, 2 * c), F32),
        compiler_params=pltpu.CompilerParams(vmem_limit_bytes=40 * 2**20),
        cost_estimate=pl.CostEstimate(flops=0, bytes_accessed=1024, transcendentals=0),
        name="unpack_cols",
    )((lax.axis_index("ctx") & 1)[None], half, other)


def all_rows(x):
    return lax.all_gather(x, "tp", axis=0, tiled=True)


def tp_shift(x, d):
    n = lax.axis_size("tp")
    return lax.ppermute(x, "tp", [(i, (i + d) % n) for i in range(n)])


def part_of(x, d, axis):
    n = lax.axis_size("tp")
    w = x.shape[axis] // n
    return lax.dynamic_slice_in_dim(x, (lax.axis_index("tp") + d) % n * w, w, axis)


def exchange(x, split, join):
    n, me = lax.axis_size("tp"), lax.axis_index("tp")
    w = x.shape[join]
    shape = list(x.shape)
    shape[split] //= n
    shape[join] *= n
    out = jnp.zeros(shape, x.dtype)
    for d in range(n):
        got = tp_shift(part_of(x, d, split), d) if d else part_of(x, 0, split)
        out = lax.dynamic_update_slice_in_dim(out, got, (me + n - d) % n * w, join)
    return out


def sum_rows(x):
    return lax.psum_scatter(x, "tp", scatter_dimension=0, tiled=True)


def gather_pair(kv):
    n = lax.axis_size("ctx")
    held = {0: ((kv, 0), (kv, 1))}
    for bit in range(1, int(math.log2(n))):
        mask = 1 << bit
        for j in list(held):
            if j == 0:
                got = ctx_swap(kv, mask)
                held[mask] = (got, 0), (got, 1)
            elif mask == 4 and j == 2:
                held[6] = (ctx_swap(held[2][0][0][0:1], 4), 0), (ctx_swap(held[4][1][0][1:2], 2), 0)
            else:
                (k, i), (v, t) = held[j]
                if k is v:
                    got = ctx_swap(k, mask)
                    held[j | mask] = (got, i), (got, t)
                else:
                    held[j | mask] = (ctx_swap(k, mask), i), (ctx_swap(v, mask), t)
    for j in list(held):
        (k, i), (v, t) = held[j]
        got = ctx_swap(k, 1)
        held[j | 1] = (got, i), (got if k is v else ctx_swap(v, 1), t)
    return [held[j][0] for j in range(n)], [held[j][1] for j in range(n)]


def gather_other(x):
    held = {0: x, 1: ctx_swap(x, 1)}
    for j in range(2, lax.axis_size("ctx"), 2):
        held[j] = ctx_swap(x, j)
    return held


def gather_cores(held, gate=None):
    n = lax.axis_size("ctx")
    for j in range(2, n, 2):
        held[j + 1] = ctx_swap(after(held[j], gate), 1)
    return [held[j] for j in range(n)]


def sum_over_all(x):
    steps = [(axis, bit) for axis in ("ctx", "tp") for bit in range(int(math.log2(lax.axis_size(axis))))]
    for axis, bit in sorted(steps, key=lambda step: step[0] == "ctx" and step[1] > 0):
        x = x + lax.ppermute(x, axis, [(i, i ^ (1 << bit)) for i in range(lax.axis_size(axis))])
        yield x
    while True:
        yield x


def gather_tp(x):
    n, me = lax.axis_size("tp"), lax.axis_index("tp")
    out = jnp.zeros((n,) + x.shape, x.dtype)
    for d in range(n):
        got = lax.ppermute(x, "tp", [(i, (i + d) % n) for i in range(n)]) if d else x
        out = lax.dynamic_update_index_in_dim(out, got, (me + n - d) % n, 0)
    return out


def local(tokens, cotangent, block_order, gain_one, shift_one, query_w, key_w, value_w, query_b, key_b, value_b,
          output_w, gain_two, shift_two, gate_w, up_w, down_w):
    heads = key_b.shape[0]
    width = heads * HEAD_DIM
    n_ctx, n_tp = lax.axis_size("ctx"), lax.axis_size("tp")
    ctx = lax.axis_index("ctx")
    own = lax.dynamic_slice_in_dim(block_order, 2 * ctx, 2, 1)
    picked = (jnp.arange(n_ctx, dtype=jnp.int32) ^ ctx)[:, None] == jnp.arange(n_ctx, dtype=jnp.int32)[None, :]
    by_ctx = block_order.reshape(SEQS, 1, n_ctx, 2)
    place = jnp.sum(jnp.where(picked[None, :, :, None], by_ctx, 0), axis=2).astype(jnp.int32).reshape(SEQS, 2 * n_ctx)
    positions = (own[:, :, None] * BLK + jnp.arange(BLK, dtype=jnp.int32)).reshape(-1)
    tabs = rotary_tables(positions)

    x = tokens.astype(F32)
    normed_one, unit_one, inverse_one = layer_stats(x, gain_one, shift_one)
    rows_one = all_rows(normed_one.astype(BF16))
    key_bias = jnp.concatenate([key_b, jnp.zeros((heads, HEAD_DIM - ROT), F32)], axis=1).reshape(-1)
    bias = jnp.stack([query_b, key_bias, value_b])
    q, kv = project(rows_one, query_w, key_w, value_w, bias, tabs)
    keys, values = gather_pair(kv.reshape(2, SEQS, 2, BLK, width))
    arrived = [e[0] for e in keys + values]

    rows_w = output_w.shape[0] // n_ctx
    part = lax.dynamic_slice_in_dim(output_w, ctx * rows_w, rows_w, 0)
    part = gather_tp(after(part, kv))
    dy_rows = all_rows(after(cotangent, rows_one))
    whole_w = lax.all_gather(after(part, arrived, dy_rows), "ctx", axis=1).reshape(n_tp * output_w.shape[0], -1)

    attn, q_ext = attend(place, own, q, keys, values)
    attn_rows = attn.reshape(-1, width)
    attn_own = exchange(attn_rows, 0, 1)
    mixed = x + nn(attn_own, whole_w)
    normed_two, unit_two, inverse_two = layer_stats(mixed, gain_two, shift_two)
    rows_two = all_rows(after(normed_two.astype(BF16), dy_rows, whole_w))
    shape = (1, SEQS, 2, BLK, width + 128)
    queries = gather_cores(gather_other(after(jnp.concatenate([q, q_ext], axis=2).reshape(shape), attn_own)))
    rows_two = after(rows_two, queries)

    act, grad_gu = mlp(rows_two, dy_rows, gate_w, up_w, down_w)
    ff = gate_w.shape[1]
    part_two = (nt(grad_gu[:, :ff], gate_w) + nt(grad_gu[:, ff:], up_w)).astype(BF16)
    grad_two = sum_rows(part_two)
    act, rows_two, dy_rows, grad_gu = after((act, rows_two, dy_rows, grad_gu), part_two)
    gu_fly, dw_fly = [], []
    gu = begin(lambda core: rc(columns(rows_two, core), grad_gu), gu_fly)
    dw = begin(lambda core: rc(act, columns(dy_rows, core)), dw_fly)
    held = take(gu)
    go(gu)
    down = nn(after(act, held), down_w).astype(BF16)
    held = take(dw), take(gu, down)
    go(gu)
    go(dw, held)
    grad_two = after(grad_two, held)

    norm_two, grad_gain_two, grad_shift_two = layer_back(grad_two.astype(F32), unit_two, inverse_two, gain_two)
    grad_mixed = cotangent.astype(F32) + norm_two
    branch_own = grad_mixed.astype(BF16)
    grad_attn = nt(branch_own, whole_w).astype(BF16)
    held = take(gu, grad_attn)
    go(gu)
    grad_attn = exchange(grad_attn, 1, 0)
    lane = jnp.arange(128)[None, :]
    ind = ((jnp.arange(width) // HEAD_DIM)[:, None] == lane // 3).astype(F32)
    delta = lax.dot_general(grad_attn.astype(F32) * attn_rows.astype(F32), ind, (((1,), (0,)), ((), ())),
                            precision=lax.Precision.HIGHEST, preferred_element_type=F32)
    do_ext = terms(-delta, lane).astype(BF16)
    do_sent = jnp.concatenate([grad_attn, do_ext], axis=1).reshape(shape)
    do_sent = after(do_sent, held, gu_fly)
    branch = all_rows(after(branch_own, do_sent))
    out_sum = sum_rows(after(down, do_sent))
    grads = gather_other(do_sent)
    grad_q = query_grad(place, own, q, grad_attn.reshape(q.shape), q_ext, do_ext.reshape(q_ext.shape), tabs, keys, values)
    grad_q = after(grad_q.reshape(-1, width), [grads[j] for j in grads if j > 1])
    grads = gather_cores(grads, grad_q)
    q_part = nt(grad_q, query_w)
    grads = after(grads, take(gu, grad_q))
    go(gu, grads)
    first = key_value_grad(place, own, kv, tabs, queries, grads, 0, SEQS // 2)
    grads = after(grads, take(dw, first))
    go(dw)
    second = key_value_grad(place, own, kv, tabs, queries, grads, SEQS // 2, SEQS // 2)
    second = after(second, take(dw, second))
    go(dw)
    grad_k, grad_v = (jnp.concatenate(pair).reshape(-1, width) for pair in zip(first, second))
    part_one = q_part + nt(grad_k, key_w) + nt(grad_v, value_w)
    part_sent = after(part_one.astype(BF16), branch)
    rows_one, branch, grad_q, grad_k, grad_v = after((rows_one, branch, grad_q, grad_k, grad_v), part_sent, gu_fly, dw_fly)
    grad_qkv = jnp.concatenate([grad_q, grad_k, grad_v], axis=1)
    chain = begin(lambda core: jnp.concatenate([rc(columns(rows_one, core), grad_qkv), rc(columns(branch, core), attn_rows)], axis=1))
    take(dw, part_sent)
    go(dw)
    held = take(chain, (list(dw_fly), out_sum))
    go(chain)
    grad_one = sum_rows(after(part_sent, out_sum, held))
    take(gu, held)
    take_extra(gu)
    go(gu)
    take(dw, held)
    take_extra(dw)
    go(dw)
    unit_rows = (rows_one.astype(F32) - shift_one) / gain_one
    bias_grad = jnp.sum(grad_qkv.astype(F32), axis=0)
    tp_row = (jnp.arange(n_tp) == lax.axis_index("tp"))[:, None]
    small = jnp.concatenate([
        jnp.sum(part_one * unit_rows, axis=0), jnp.sum(part_one, axis=0), grad_gain_two, grad_shift_two,
        jnp.where(tp_row, bias_grad[None, :], 0.0).reshape(-1)])
    sums = sum_over_all(after(small, held).reshape(-1, 1024))
    small = [next(sums) for _ in range(1 + int(math.log2(n_tp)))]
    held = take(chain)
    go(chain)
    held = take(chain, small)
    go(chain)
    grad_down_w = unpack_cols(*take(dw, held))
    held = take(chain, grad_down_w)
    take_extra(chain)
    go(chain)
    mixed_late, out_sum = after((mixed, out_sum), held)
    out_tokens = (mixed_late + out_sum.astype(F32)).astype(BF16)
    grad_gate_w, grad_up_w = unpack_rows(*take(gu, held), 2)
    take(chain, grad_gate_w)
    go(chain)
    for _ in range(4):
        small = next(sums)
    depth = x.shape[1]
    small = small.reshape(-1)
    norms = small[:4 * depth].reshape(4, depth)
    bias_sum = jnp.sum(jnp.where(tp_row, small[4 * depth:].reshape(n_tp, -1), 0.0), axis=0)
    grad_query_w, grad_key_w, grad_value_w, grad_output_w = unpack_rows(*take(chain), 4, True)
    norm_one, _, _ = layer_back(grad_one.astype(F32), unit_one, inverse_one, gain_one)
    grad_tokens = (grad_mixed + norm_one).astype(BF16)
    return (
        out_tokens, grad_tokens, norms[0], norms[1], grad_query_w, grad_key_w, grad_value_w,
        bias_sum[:width], bias_sum[width:2 * width].reshape(heads, HEAD_DIM)[:, :ROT], bias_sum[2 * width:],
        grad_output_w, norms[2], norms[3], grad_gate_w, grad_up_w, grad_down_w,
    )


def solution(mesh):
    rows, cols, depth, flat = P(("ctx", "tp"), None), P(None, "tp"), P("tp", None), P("tp")
    in_specs = (rows, rows, P(), P(), P(), cols, cols, cols, flat, depth, flat, depth, P(), P(), cols, cols, depth)
    out_specs = (rows, rows, P(), P(), cols, cols, cols, flat, depth, flat, depth, P(), P(), cols, cols, depth)
    return jax.shard_map(local, mesh=mesh, in_specs=in_specs, out_specs=out_specs, check_vma=False)
```
